32 devices in a mesh: ctx: 4 (over y, x), fsdp: 8 (over z, core).
Axes of the slice: x: 2, y: 2, z: 4, core: 2. Of those that a mesh axis runs over, the one named last changes fastest.
Arguments:
- activations: bfloat16 [8, 1536, 768], P('fsdp', 'ctx'), may hold values from -6 to 6
- cotangent: bfloat16 [8, 1536, 768], P('fsdp', 'ctx'), may hold values from -6 to 6
- doc_start: int32 [8, 1536], P('fsdp', 'ctx'), may hold values from 0 to 1535, as said below
- deal: int32 [4], replicated, may hold values from 0 to 3, as said below
- attend_in: bfloat16 [2, 768, 2304], P(None, 'fsdp'), may hold values from -0.21875 to 0.21875
- query_bias: bfloat16 [2, 768], P(None, 'fsdp'), may hold values from -3 to 3
- value_bias: bfloat16 [2, 768], P(None, 'fsdp'), may hold values from -3 to 3
- attend_out: bfloat16 [2, 768, 768], P(None, 'fsdp'), may hold values from -1.25 to 1.25
- attend_bias: bfloat16 [2, 768], P(None, 'fsdp'), may hold values from -3 to 3
- first_gain: bfloat16 [2, 768], P(None, 'fsdp'), may hold values from 0.099609375 to 1.8984375
- first_shift: bfloat16 [2, 768], P(None, 'fsdp'), may hold values from -3 to 3
- expand_proj: bfloat16 [2, 768, 3072], P(None, 'fsdp'), may hold values from -0.21875 to 0.21875
- expand_bias: bfloat16 [2, 3072], P(None, 'fsdp'), may hold values from -3 to 3
- reduce_proj: bfloat16 [2, 3072, 768], P(None, 'fsdp'), may hold values from -0.109375 to 0.109375
- reduce_bias: bfloat16 [2, 768], P(None, 'fsdp'), may hold values from -3 to 3
- second_gain: bfloat16 [2, 768], P(None, 'fsdp'), may hold values from 0.099609375 to 1.8984375
- second_shift: bfloat16 [2, 768], P(None, 'fsdp'), may hold values from -3 to 3
Outputs:
- out_act: bfloat16 [8, 1536, 768], P('fsdp', 'ctx')
- in_grad: float32 [8, 1536, 768], P('fsdp', 'ctx')
- attend_in_grad: float32 [2, 768, 2304], P(None, 'fsdp')
- query_bias_grad: float32 [2, 768], P(None, 'fsdp')
- value_bias_grad: float32 [2, 768], P(None, 'fsdp')
- attend_out_grad: float32 [2, 768, 768], P(None, 'fsdp')
- attend_bias_grad: float32 [2, 768], P(None, 'fsdp')
- first_gain_grad: float32 [2, 768], P(None, 'fsdp')
- first_shift_grad: float32 [2, 768], P(None, 'fsdp')
- expand_proj_grad: float32 [2, 768, 3072], P(None, 'fsdp')
- expand_bias_grad: float32 [2, 3072], P(None, 'fsdp')
- reduce_proj_grad: float32 [2, 3072, 768], P(None, 'fsdp')
- reduce_bias_grad: float32 [2, 768], P(None, 'fsdp')
- second_gain_grad: float32 [2, 768], P(None, 'fsdp')
- second_shift_grad: float32 [2, 768], P(None, 'fsdp')
The draws below stay inside these ranges and needn't reach their ends.
Inputs may be any that keep to these rules, and one draw needn't show every extreme that they name: `doc_start`: rows of one document share the position where it begins; each sequence's first document begins at 0 and covers its first half or more; the last position of a sequence is a document of its own. A permutation of 0 to 3; index c of ctx holds blocks deal[c] and 7 - deal[c].
All inputs are finite; a program needn't handle non-finite values.
Results may differ from the reference program's by a relative error of at most 0.022.
Values may be sent and summed in bfloat16 or wider, within the bound.
No kernel may reach another device: no remote copies, remote signals or barrier semaphores. Data moves between devices by JAX's collectives and lax.ppermute only.
A program may use at most 192 MiB of HBM per device.

```python
import jax
import jax.numpy as jnp
from jax import lax

D = 768
HEADS = 12
HEAD_DIM = 64
FF = 3072
LAYERS = 2
BLK = 192
PAIRS = 4
SEQ_LEN = 1536
SEQS = 8


def layout(key):
    dealing = jax.random.permutation(jax.random.fold_in(key, 11), PAIRS).astype(jnp.int32)
    extra = jax.random.randint(jax.random.fold_in(key, 12), (SEQS, 1), 0, SEQ_LEN // 4, dtype=jnp.int32)
    long_end = SEQ_LEN // 2 + extra
    marks = jax.random.randint(jax.random.fold_in(key, 13), (SEQS, SEQ_LEN), 0, 48, dtype=jnp.int32)
    place = jnp.arange(SEQ_LEN, dtype=jnp.int32)[None, :]
    begins = (place == 0) | (place == long_end) | (place == SEQ_LEN - 1) | (place > long_end) & (marks == 0)
    starts = lax.cummax(jnp.where(begins, place, 0), axis=1)
    blocks = starts.reshape(SEQS, 2 * PAIRS, BLK)
    order = jnp.stack([dealing, 2 * PAIRS - 1 - dealing], axis=1).reshape(2 * PAIRS)
    stored = jnp.take(blocks, order, axis=1).reshape(SEQS, SEQ_LEN)
    return (dealing, stored.astype(jnp.int32))


def draw_doc_start(key, part):
    return layout(key)[1]


def draw_deal(key, part):
    return layout(key)[0]


def with_spikes(values, stream_key, source, target, shards_of, factor):
    owner, partner = [(jnp.arange(values.shape[position]) // (values.shape[position] // shards_of)).reshape([-1 if axis == position else 1 for axis in range(values.ndim)]) for position in (source, target)]
    chosen = jax.random.permutation(stream_key, shards_of)[partner]
    strong = (owner == chosen) | (owner == (partner + shards_of // 2) % shards_of)
    return jnp.where(strong, factor * values, values)


def block_levels(own_key, shape, cuts, least, largest):
    level = 1.0
    for axis_at, blocks in cuts:
        heights = jax.random.uniform(jax.random.fold_in(jax.random.fold_in(own_key, 6), axis_at), (blocks,), jnp.float32, least / len(cuts), largest / len(cuts))
        level = level * jnp.repeat(jnp.exp(heights), shape[axis_at] // blocks).reshape((-1,) + (1,) * (len(shape) - 1 - axis_at))
    return level


def gaussian(stream_key, shape, scale, limit, split=(), kind=jnp.bfloat16):
    array = jax.random.normal(stream_key, shape, jnp.float32) * scale
    if len(split) > 0:
        array = block_levels(stream_key, shape, split, -0.22, 0.18) * array
    return jnp.clip(array, min=-limit, max=limit).astype(kind)


def gaussian_with(rng, shape, scale, bound, cuts, heavy, kind=jnp.bfloat16):
    values = scale * jax.random.normal(rng, shape, jnp.float32)
    if cuts:
        values = values * block_levels(rng, shape, cuts, -0.22, 0.18)
    return jnp.clip(with_spikes(values, jax.random.fold_in(rng, 3), *heavy), -bound, bound).astype(kind)


def setup_inputs(seed: int = 0) -> dict:
    splits = jax.random.split(jax.random.key(seed), 18)
    return {
        "activations": gaussian_with(splits[0], (SEQS, SEQ_LEN, D), 1.0, 6.0, ((0, 8), (1, 4)), (0, 2, 8, 2.0)),
        "cotangent": gaussian(splits[1], (SEQS, SEQ_LEN, D), 1.0, 6.0, ((0, 8), (1, 4))),
        "doc_start": draw_doc_start(jax.random.fold_in(splits[17], 71), 0),
        "deal": draw_deal(jax.random.fold_in(splits[17], 71), 0),
        "attend_in": gaussian(splits[4], (LAYERS, D, 3 * D), D ** -0.5, 0.21875, ((1, 8),)),
        "query_bias": gaussian(splits[5], (LAYERS, D), 0.5, 3.0, ((1, 8),)),
        "value_bias": gaussian(splits[6], (LAYERS, D), 0.5, 3.0, ((1, 8),)),
        "attend_out": gaussian(splits[7], (LAYERS, D, D), (D // 32) ** -0.5, 1.25, ((1, 8),)),
        "attend_bias": gaussian(splits[8], (LAYERS, D), 0.5, 3.0, ((1, 8),)),
        "first_gain": jnp.clip(1.0 + 0.18 * jax.random.normal(splits[9], (LAYERS, D), jnp.float32), 0.099609375, 1.8984375).astype(jnp.bfloat16),
        "first_shift": gaussian(splits[10], (LAYERS, D), 0.5, 3.0, ((1, 8),)),
        "expand_proj": gaussian(splits[11], (LAYERS, D, FF), D ** -0.5, 0.21875, ((1, 8),)),
        "expand_bias": gaussian(splits[12], (LAYERS, FF), 0.5, 3.0, ((1, 8),)),
        "reduce_proj": gaussian(splits[13], (LAYERS, FF, D), FF ** -0.5, 0.109375, ((1, 8),)),
        "reduce_bias": gaussian(splits[14], (LAYERS, D), 0.5, 3.0, ((1, 8),)),
        "second_gain": jnp.clip(1.0 + 0.18 * jax.random.normal(splits[15], (LAYERS, D), jnp.float32), 0.099609375, 1.8984375).astype(jnp.bfloat16),
        "second_shift": gaussian(splits[16], (LAYERS, D), 0.5, 3.0, ((1, 8),)),
    }


@jax.custom_vjp
def low(v):
    return lax.optimization_barrier(v.astype(jnp.bfloat16)).astype(jnp.float32)

@jax.custom_vjp
def low_back(v):
    return v

def low_keep(v):
    return (low(v), None)

def low_pass(kept, grad):
    return (grad,)

def back_keep(v):
    return (v, None)

def back_low(kept, grad):
    return (low(grad),)
low.defvjp(low_keep, low_pass)
low_back.defvjp(back_keep, back_low)
norm_eps = 1e-05
HIGHEST = lax.Precision.HIGHEST

def layer_norm(values, gain, shift):
    centre = values - lax.optimization_barrier(jnp.mean(values, axis=-1, keepdims=True))
    spread = lax.optimization_barrier(jnp.mean(centre * centre, axis=-1, keepdims=True))
    return centre * lax.rsqrt(spread + norm_eps) * gain + shift

def gelu_exact(inputs):
    return 0.5 * inputs * (1.0 + jax.scipy.special.erf(inputs * 0.7071067811865476))

def stored_positions(deal):
    offsets = jnp.arange(BLK, dtype=jnp.int32)
    first = deal[:, None] * BLK + offsets[None, :]
    second = (2 * PAIRS - 1 - deal)[:, None] * BLK + offsets[None, :]
    return jnp.concatenate([first, second], axis=1).reshape(-1).astype(jnp.int32)

def split_heads(matrix):
    return matrix.reshape(matrix.shape[0], HEADS, HEAD_DIM).transpose(1, 0, 2)

def attend_heads(queries, keys_all, values_all, allowed):

    def one_head(items):
        head_q, head_k, head_v = items
        raw = jnp.dot(head_q, head_k.T, precision=HIGHEST)
        scores = low_back(raw * HEAD_DIM ** (-0.5))
        scores = jnp.where(allowed, scores, -1e+30)
        top = lax.optimization_barrier(jnp.max(scores, axis=-1, keepdims=True))
        weights = jnp.exp(scores - top)
        probs = weights / lax.optimization_barrier(jnp.sum(weights, axis=-1, keepdims=True))
        return jnp.dot(low(probs), head_v, precision=HIGHEST)
    outputs = lax.map(jax.checkpoint(one_head), (split_heads(queries), split_heads(keys_all), split_heads(values_all)))
    return outputs.transpose(1, 0, 2).reshape(queries.shape[0], D)

def forward(inputs, params, allowed):
    hidden = inputs
    for layer_index in range(LAYERS):
        attend_in, query_bias, value_bias, attend_out, attend_bias, first_gain, first_shift, expand_proj, expand_bias, reduce_proj, reduce_bias, second_gain, second_shift = [tensor[layer_index] for tensor in params]
        low_hidden = low(hidden)
        projected = jnp.dot(low_hidden, attend_in, precision=HIGHEST)
        queries = low_back(low(projected[:, :D] + query_bias))
        keys_all = low_back(low(projected[:, D:2 * D]))
        values_all = low_back(low(projected[:, 2 * D:] + value_bias))
        context = low_back(low(attend_heads(queries, keys_all, values_all, allowed)))
        branch = low_back(jnp.dot(context, attend_out, precision=HIGHEST) + attend_bias)
        normed = layer_norm(hidden + branch, first_gain, first_shift)
        inner_act = low_back(jnp.dot(low(normed), expand_proj, precision=HIGHEST) + expand_bias)
        active = low(gelu_exact(inner_act))
        output_branch = low_back(jnp.dot(active, reduce_proj, precision=HIGHEST) + reduce_bias)
        hidden = layer_norm(normed + output_branch, second_gain, second_shift)
    return hidden

def reference(activations, cotangent, doc_start, deal, attend_in, query_bias, value_bias, attend_out, attend_bias, first_gain, first_shift, expand_proj, expand_bias, reduce_proj, reduce_bias, second_gain, second_shift):
    params = tuple((tensor.astype(jnp.float32) for tensor in (attend_in, query_bias, value_bias, attend_out, attend_bias, first_gain, first_shift, expand_proj, expand_bias, reduce_proj, reduce_bias, second_gain, second_shift)))
    positions = stored_positions(deal)
    causal = positions[None, :] <= positions[:, None]

    def one_sequence(totals, items):
        inputs, seed_grad, starts = items
        allowed = causal & (starts[:, None] == starts[None, :])

        def run(rows_in, weights):
            return forward(rows_in, weights, allowed)
        result, pullback = jax.vjp(run, inputs.astype(jnp.float32), params)
        row_grad, weight_grads = pullback(seed_grad.astype(jnp.float32))
        totals = jax.tree.map(jnp.add, totals, weight_grads)
        return (totals, (result.astype(jnp.bfloat16), row_grad))
    zeros = jax.tree.map(jnp.zeros_like, params)
    totals, outputs = lax.scan(one_sequence, zeros, (activations, cotangent, doc_start))
    out_act, in_grad = outputs
    return (out_act, in_grad, totals[0], totals[1], totals[2], totals[3], totals[4], totals[5], totals[6], totals[7], totals[8], totals[9], totals[10], totals[11], totals[12])
```

```python
import functools

import jax
import jax.numpy as jnp
from jax import lax
from jax.experimental import pallas as pl
from jax.experimental.pallas import tpu as pltpu
from jax.sharding import PartitionSpec as P

HEADS = 12
HEAD_DIM = 64
LAYERS = 2
BLK = 192


norm_eps = 1e-05


def for_sending(x):
    return jax.tree.map(lambda a: a.astype(jnp.bfloat16) if a.dtype == jnp.float32 else a, x)


def layer_norm(values, gain, shift):
    centre = values - jnp.mean(values, axis=-1, keepdims=True)
    spread = jnp.mean(centre * centre, axis=-1, keepdims=True)
    return centre * lax.rsqrt(spread + norm_eps) * gain + shift


def gelu_exact(inputs):
    return 0.5 * inputs * (1.0 + jax.scipy.special.erf(inputs * 0.7071067811865476))


def key_positions(deal):
    pairs = deal.shape[0]
    offsets = jnp.arange(BLK, dtype=jnp.int32)
    first = deal[:, None] * BLK + offsets[None, :]
    second = (2 * pairs - 1 - deal)[:, None] * BLK + offsets[None, :]
    return jnp.concatenate([first, second], axis=1).reshape(-1)


def split_heads(matrix):
    return matrix.reshape(matrix.shape[0], HEADS, HEAD_DIM).transpose(1, 0, 2)


def join_heads(stacked):
    return stacked.transpose(1, 0, 2).reshape(stacked.shape[1], HEADS * HEAD_DIM)


def attend_forward(queries, keys_full, values_full, allowed):

    def one_head(items):
        head_q, head_k, head_v = items
        scores = jnp.einsum(
            "qd,kd->qk", head_q, head_k, preferred_element_type=jnp.float32
        ) * HEAD_DIM ** (-0.5)
        scores = jnp.where(allowed, scores, -1e30)
        top = jnp.max(scores, axis=-1, keepdims=True)
        weights = jnp.exp(scores - top)
        total = jnp.sum(weights, axis=-1, keepdims=True)
        probs = (weights / total).astype(jnp.bfloat16)
        output = jnp.einsum("qk,kd->qd", probs, head_v, preferred_element_type=jnp.float32)
        return (output, top[:, 0] + jnp.log(total[:, 0]))

    outputs, log_totals = lax.map(
        one_head, (split_heads(queries), split_heads(keys_full), split_heads(values_full))
    )
    return (join_heads(outputs), log_totals)


def attend_backward(queries, keys_full, values_full, log_totals, grad_context, allowed):

    def one_head(items):
        head_q, head_k, head_v, head_lse, head_grad = items
        scores = jnp.einsum(
            "qd,kd->qk", head_q, head_k, preferred_element_type=jnp.float32
        ) * HEAD_DIM ** (-0.5)
        scores = jnp.where(allowed, scores, -1e30)
        probs = jnp.exp(scores - head_lse[:, None])
        grad_probs = jnp.einsum("qd,kd->qk", head_grad, head_v, preferred_element_type=jnp.float32)
        inner_sum = jnp.sum(probs * grad_probs, axis=-1, keepdims=True)
        grad_scores = (probs * (grad_probs - inner_sum)).astype(jnp.bfloat16)
        grad_q = jnp.einsum(
            "qk,kd->qd", grad_scores, head_k, preferred_element_type=jnp.float32
        ) * HEAD_DIM ** (-0.5)
        grad_k = jnp.einsum(
            "qk,qd->kd", grad_scores, head_q, preferred_element_type=jnp.float32
        ) * HEAD_DIM ** (-0.5)
        grad_v = jnp.einsum(
            "qk,qd->kd", probs.astype(jnp.bfloat16), head_grad, preferred_element_type=jnp.float32
        )
        return (grad_q, grad_k, grad_v)

    grads = lax.map(
        one_head,
        (
            split_heads(queries),
            split_heads(keys_full),
            split_heads(values_full),
            log_totals,
            split_heads(grad_context),
        ),
    )
    return (join_heads(grads[0]), join_heads(grads[1]), join_heads(grads[2]))


def forward_layer(hidden, weights, allowed):
    (
        attend_in,
        query_bias,
        value_bias,
        attend_out,
        attend_bias,
        first_gain,
        first_shift,
        expand_proj,
        expand_bias,
        reduce_proj,
        reduce_bias,
        second_gain,
        second_shift,
    ) = weights
    width = hidden.shape[1]
    low_hidden = hidden.astype(jnp.bfloat16)
    projected = jnp.dot(low_hidden, attend_in, preferred_element_type=jnp.float32)
    queries = (projected[:, :width] + query_bias.astype(jnp.float32)).astype(jnp.bfloat16)
    keys_own = projected[:, width : 2 * width].astype(jnp.bfloat16)
    values_own = (projected[:, 2 * width :] + value_bias.astype(jnp.float32)).astype(jnp.bfloat16)
    keys_full, values_full = (
        lax.all_gather(keys_own, "ctx", axis=0, tiled=True),
        lax.all_gather(values_own, "ctx", axis=0, tiled=True),
    )
    context, log_totals = attend_forward(queries, keys_full, values_full, allowed)
    low_context = context.astype(jnp.bfloat16)
    branch = jnp.dot(
        low_context, attend_out, preferred_element_type=jnp.float32
    ) + attend_bias.astype(jnp.float32)
    first_sum = hidden + branch
    normed = layer_norm(first_sum, first_gain.astype(jnp.float32), first_shift.astype(jnp.float32))
    low_normed = normed.astype(jnp.bfloat16)
    inner_pre = jnp.dot(
        low_normed, expand_proj, preferred_element_type=jnp.float32
    ) + expand_bias.astype(jnp.float32)
    active = gelu_exact(inner_pre).astype(jnp.bfloat16)
    output_branch = jnp.dot(
        active, reduce_proj, preferred_element_type=jnp.float32
    ) + reduce_bias.astype(jnp.float32)
    second_sum = normed + output_branch
    output = layer_norm(
        second_sum, second_gain.astype(jnp.float32), second_shift.astype(jnp.float32)
    )
    saved = (
        low_hidden,
        queries,
        keys_full,
        values_full,
        log_totals,
        low_context,
        first_sum,
        low_normed,
        inner_pre,
        active,
        second_sum,
    )
    return (output, saved)


def column_sum(matrix):
    return jnp.sum(matrix.astype(jnp.float32), axis=0)


def backward_layer(grad_hidden, weights, saved, allowed):
    (
        attend_in,
        query_bias,
        value_bias,
        attend_out,
        attend_bias,
        first_gain,
        first_shift,
        expand_proj,
        expand_bias,
        reduce_proj,
        reduce_bias,
        second_gain,
        second_shift,
    ) = weights
    (
        low_hidden,
        queries,
        keys_full,
        values_full,
        log_totals,
        low_context,
        first_sum,
        low_normed,
        inner_pre,
        active,
        second_sum,
    ) = saved
    width = low_hidden.shape[1]
    second_pull = jax.vjp(
        layer_norm, second_sum, second_gain.astype(jnp.float32), second_shift.astype(jnp.float32)
    )[1]
    grad_second_sum, grad_second_gain, grad_second_shift = second_pull(grad_hidden)
    grad_branch = grad_second_sum.astype(jnp.bfloat16)
    grad_reduce_bias = column_sum(grad_branch)
    grad_reduce = jnp.einsum("tf,td->fd", active, grad_branch, preferred_element_type=jnp.float32)
    grad_active = jnp.einsum(
        "td,fd->tf", grad_branch, reduce_proj, preferred_element_type=jnp.float32
    )
    gelu_pull = jax.vjp(gelu_exact, inner_pre)[1]
    grad_inner = gelu_pull(grad_active)[0].astype(jnp.bfloat16)
    grad_expand_bias = column_sum(grad_inner)
    grad_expand = jnp.einsum(
        "td,tf->df", low_normed, grad_inner, preferred_element_type=jnp.float32
    )
    grad_normed = grad_second_sum + jnp.einsum(
        "tf,df->td", grad_inner, expand_proj, preferred_element_type=jnp.float32
    )
    first_pull = jax.vjp(
        layer_norm, first_sum, first_gain.astype(jnp.float32), first_shift.astype(jnp.float32)
    )[1]
    grad_first_sum, grad_first_gain, grad_first_shift = first_pull(grad_normed)
    grad_attn = grad_first_sum.astype(jnp.bfloat16)
    grad_attend_bias = column_sum(grad_attn)
    grad_attend_out = jnp.einsum(
        "td,te->de", low_context, grad_attn, preferred_element_type=jnp.float32
    )
    grad_context = jnp.einsum(
        "te,de->td", grad_attn, attend_out, preferred_element_type=jnp.float32
    ).astype(jnp.bfloat16)
    grad_queries, grad_keys_full, grad_values_full = attend_backward(
        queries, keys_full, values_full, log_totals, grad_context, allowed
    )
    grad_keys, grad_values = (
        lax.psum_scatter(
            grad_keys_full.astype(jnp.bfloat16), "ctx", scatter_dimension=0, tiled=True
        ).astype(jnp.float32),
        lax.psum_scatter(
            grad_values_full.astype(jnp.bfloat16), "ctx", scatter_dimension=0, tiled=True
        ).astype(jnp.float32),
    )
    grad_proj = jnp.concatenate(
        [
            grad_queries.astype(jnp.bfloat16),
            grad_keys.astype(jnp.bfloat16),
            grad_values.astype(jnp.bfloat16),
        ],
        axis=1,
    )
    grad_query_bias = column_sum(grad_proj[:, :width])
    grad_value_bias = column_sum(grad_proj[:, 2 * width :])
    grad_attend_in = jnp.einsum(
        "td,te->de", low_hidden, grad_proj, preferred_element_type=jnp.float32
    )
    grad_input = grad_first_sum + jnp.einsum(
        "te,de->td", grad_proj, attend_in, preferred_element_type=jnp.float32
    )
    grads = (
        grad_attend_in,
        grad_query_bias,
        grad_value_bias,
        grad_attend_out,
        grad_attend_bias,
        grad_first_gain,
        grad_first_shift,
        grad_expand,
        grad_expand_bias,
        grad_reduce,
        grad_reduce_bias,
        grad_second_gain,
        grad_second_shift,
    )
    return (grad_input, grads)


def reduce_grads(grads):
    shards = (
        lax.psum_scatter(
            grads[0].astype(jnp.bfloat16), "fsdp", scatter_dimension=0, tiled=True
        ).astype(jnp.float32),
        lax.psum_scatter(
            grads[1].astype(jnp.bfloat16), "fsdp", scatter_dimension=0, tiled=True
        ).astype(jnp.float32),
        lax.psum_scatter(
            grads[2].astype(jnp.bfloat16), "fsdp", scatter_dimension=0, tiled=True
        ).astype(jnp.float32),
        lax.psum_scatter(
            grads[3].astype(jnp.bfloat16), "fsdp", scatter_dimension=0, tiled=True
        ).astype(jnp.float32),
        lax.psum_scatter(
            grads[4].astype(jnp.bfloat16), "fsdp", scatter_dimension=0, tiled=True
        ).astype(jnp.float32),
        lax.psum_scatter(
            grads[5].astype(jnp.bfloat16), "fsdp", scatter_dimension=0, tiled=True
        ).astype(jnp.float32),
        lax.psum_scatter(
            grads[6].astype(jnp.bfloat16), "fsdp", scatter_dimension=0, tiled=True
        ).astype(jnp.float32),
        lax.psum_scatter(
            grads[7].astype(jnp.bfloat16), "fsdp", scatter_dimension=0, tiled=True
        ).astype(jnp.float32),
        lax.psum_scatter(
            grads[8].astype(jnp.bfloat16), "fsdp", scatter_dimension=0, tiled=True
        ).astype(jnp.float32),
        lax.psum_scatter(
            grads[9].astype(jnp.bfloat16), "fsdp", scatter_dimension=0, tiled=True
        ).astype(jnp.float32),
        lax.psum_scatter(
            grads[10].astype(jnp.bfloat16), "fsdp", scatter_dimension=0, tiled=True
        ).astype(jnp.float32),
        lax.psum_scatter(
            grads[11].astype(jnp.bfloat16), "fsdp", scatter_dimension=0, tiled=True
        ).astype(jnp.float32),
        lax.psum_scatter(
            grads[12].astype(jnp.bfloat16), "fsdp", scatter_dimension=0, tiled=True
        ).astype(jnp.float32),
    )
    return (
        lax.psum(shards[0].astype(jnp.bfloat16), "ctx").astype(jnp.float32),
        lax.psum(shards[1].astype(jnp.bfloat16), "ctx").astype(jnp.float32),
        lax.psum(shards[2].astype(jnp.bfloat16), "ctx").astype(jnp.float32),
        lax.psum(shards[3].astype(jnp.bfloat16), "ctx").astype(jnp.float32),
        lax.psum(shards[4].astype(jnp.bfloat16), "ctx").astype(jnp.float32),
        lax.psum(shards[5].astype(jnp.bfloat16), "ctx").astype(jnp.float32),
        lax.psum(shards[6].astype(jnp.bfloat16), "ctx").astype(jnp.float32),
        lax.psum(shards[7].astype(jnp.bfloat16), "ctx").astype(jnp.float32),
        lax.psum(shards[8].astype(jnp.bfloat16), "ctx").astype(jnp.float32),
        lax.psum(shards[9].astype(jnp.bfloat16), "ctx").astype(jnp.float32),
        lax.psum(shards[10].astype(jnp.bfloat16), "ctx").astype(jnp.float32),
        lax.psum(shards[11].astype(jnp.bfloat16), "ctx").astype(jnp.float32),
        lax.psum(shards[12].astype(jnp.bfloat16), "ctx").astype(jnp.float32),
    )


def layer_slices(sharded, layer_index):
    return tuple((tensor[layer_index] for tensor in sharded))


def on_device_plain(
    activations,
    cotangent,
    doc_start,
    deal,
    attend_in,
    query_bias,
    value_bias,
    attend_out,
    attend_bias,
    first_gain,
    first_shift,
    expand_proj,
    expand_bias,
    reduce_proj,
    reduce_bias,
    second_gain,
    second_shift,
):
    sharded = (
        attend_in,
        query_bias,
        value_bias,
        attend_out,
        attend_bias,
        first_gain,
        first_shift,
        expand_proj,
        expand_bias,
        reduce_proj,
        reduce_bias,
        second_gain,
        second_shift,
    )
    row_count = activations.shape[1]
    positions = key_positions(deal)
    own_rank = lax.axis_index("ctx")
    own_positions = lax.dynamic_slice_in_dim(positions, own_rank * row_count, row_count)
    own_starts = doc_start[0]
    key_starts = lax.all_gather(own_starts, "ctx", axis=0, tiled=True)
    allowed = (positions[None, :] <= own_positions[:, None]) & (
        key_starts[None, :] == own_starts[:, None]
    )
    hidden = activations[0].astype(jnp.float32)
    kept_weights = []
    kept_saved = []
    for layer_index in range(LAYERS):
        weights = lax.all_gather(
            for_sending(layer_slices(sharded, layer_index)), "fsdp", axis=0, tiled=True
        )
        hidden, saved = forward_layer(hidden, weights, allowed)
        kept_weights.append(weights)
        kept_saved.append(saved)
    out_act = hidden.astype(jnp.bfloat16)[None]
    grad_hidden = cotangent[0].astype(jnp.float32)
    reduced = [None] * LAYERS
    for layer_index in reversed(range(LAYERS)):
        weights = lax.all_gather(
            for_sending(layer_slices(sharded, layer_index)), "fsdp", axis=0, tiled=True
        )
        grad_hidden, grads = backward_layer(grad_hidden, weights, kept_saved[layer_index], allowed)
        reduced[layer_index] = reduce_grads(grads)
    stacked = [
        jnp.stack([reduced[layer_index][member] for layer_index in range(LAYERS)])
        for member in range(13)
    ]
    return (
        out_act,
        grad_hidden[None],
        stacked[0],
        stacked[1],
        stacked[2],
        stacked[3],
        stacked[4],
        stacked[5],
        stacked[6],
        stacked[7],
        stacked[8],
        stacked[9],
        stacked[10],
        stacked[11],
        stacked[12],
    )


F32 = jnp.float32
BF = jnp.bfloat16
WIDTH = HEADS * HEAD_DIM
QB = 256
SCORE_SCALE = HEAD_DIM ** (-0.5) * 1.4426950408889634
NEG = -1e30
VMEM_LIMIT = 60 * 1024 * 1024


def mm_nn(a, b):
    return lax.dot_general(a, b, (((1,), (0,)), ((), ())), preferred_element_type=F32)


def mm_nt(a, b):
    return lax.dot_general(a, b, (((1,), (1,)), ((), ())), preferred_element_type=F32)


def mm_tn(a, b):
    return lax.dot_general(a, b, (((0,), (0,)), ((), ())), preferred_element_type=F32)


def call(kernel, outs, args, specs, scratch, name, flops, nbytes):
    return pl.pallas_call(
        kernel,
        out_shape=[jax.ShapeDtypeStruct(shape, dtype) for shape, dtype in outs],
        in_specs=[pl.BlockSpec(memory_space=space) for space in specs],
        out_specs=[pl.BlockSpec(memory_space=pltpu.VMEM) for _ in outs],
        scratch_shapes=scratch,
        compiler_params=pltpu.CompilerParams(vmem_limit_bytes=VMEM_LIMIT),
        cost_estimate=pl.CostEstimate(flops=flops, bytes_accessed=nbytes, transcendentals=0),
        name=name,
    )(*args)


def block_of(block, blocks):
    half = 0 if 2 * block < blocks else 1
    return (block if half == 0 else blocks - 1 - block), half


def attn_fwd_kernel(
    jmap, inv, jmin, h0, h1, h2, h3, w, bias, qrow, kcol, qkv, ctx, lse, q_s, k_s, vt_s, o_s, *, heads, tokens
):
    blocks = tokens // BLK
    hw = heads * HEAD_DIM
    for j, piece in enumerate((h0, h1, h2, h3)):
        qkv[j] = (mm_nn(piece[...], w[...]) + bias[...]).astype(BF)
    for pair in range(blocks // 2):
        rows = []
        for block in (2 * pair, 2 * pair + 1):
            at, half = block_of(block, blocks)
            rows.append(qkv[jmap[at], half * BLK : (half + 1) * BLK, :])
        both = jnp.concatenate(rows, axis=0)
        lo, hi = 2 * pair * BLK, 2 * (pair + 1) * BLK
        for h in range(heads):
            q_s[h, lo:hi, :] = both[:, h * HEAD_DIM : (h + 1) * HEAD_DIM]
            k_s[h, lo:hi, :] = both[:, hw + h * HEAD_DIM : hw + (h + 1) * HEAD_DIM]
        vt_s[:, lo:hi] = both[:, 2 * hw :].T
    iota_k = lax.broadcasted_iota(jnp.int32, (QB, QB), 0)
    iota_q = lax.broadcasted_iota(jnp.int32, (QB, QB), 1)
    causal = iota_k <= iota_q
    for h in range(heads):
        for i in range(tokens // QB):
            lo = i * QB
            q = q_s[h, lo : lo + QB, :]
            starts_q = qrow[0:1, lo : lo + QB]

            def scores(at, diagonal):
                s = mm_nt(k_s[h, pl.ds(at, QB), :], q) * SCORE_SCALE
                col = kcol[pl.ds(at, QB), :]
                allowed = jnp.concatenate([col, col], axis=1) == starts_q
                if diagonal:
                    allowed = allowed & causal
                return jnp.where(allowed, s, NEG)

            s = scores(lo, True)
            top = jnp.max(s, axis=0, keepdims=True)
            p = jnp.exp2(s - top)
            total = jnp.sum(p, axis=0, keepdims=True)
            out = mm_nn(vt_s[h * HEAD_DIM : (h + 1) * HEAD_DIM, lo : lo + QB], p.astype(BF))

            def step(jb, carry):
                top, total, out = carry
                at = pl.multiple_of(jb * QB, QB)
                s = scores(at, False)
                new_top = jnp.maximum(top, jnp.max(s, axis=0, keepdims=True))
                p = jnp.exp2(s - new_top)
                alpha = jnp.exp2(top - new_top)
                total = total * alpha + jnp.sum(p, axis=0, keepdims=True)
                out = out * alpha + mm_nn(
                    vt_s[h * HEAD_DIM : (h + 1) * HEAD_DIM, pl.ds(at, QB)], p.astype(BF)
                )
                return (new_top, total, out)

            if i > 0:
                top, total, out = lax.fori_loop(jmin[i], i, step, (top, total, out))
            o_s[h * HEAD_DIM : (h + 1) * HEAD_DIM, lo : lo + QB] = out / total
            lse[h : h + 1, lo : lo + QB] = top + jnp.log2(total)
    for pair in range(blocks // 2):
        lo, hi = 2 * pair * BLK, 2 * (pair + 1) * BLK
        both = o_s[:, lo:hi].T.astype(BF)
        for n, block in enumerate((2 * pair, 2 * pair + 1)):
            at, half = block_of(block, blocks)
            ctx[inv[at], :, half * hw : (half + 1) * hw] = both[n * BLK : (n + 1) * BLK, :]


def attn_bwd_kernel(
    jmap, inv, jmin, h0, h1, h2, h3, w, qrow, kcol, qkv, ctx, gctx, lse,
    g_own, g_a, g_bd, dw,
    q_s, k_s, v_s, do_s, kt_s, delta_s, dk_s, dv_s, dqt_s, g_s, *, heads, tokens
):
    blocks = tokens // BLK
    hw = heads * HEAD_DIM
    scale = HEAD_DIM ** (-0.5)
    for pair in range(blocks // 2):
        rows, grads, outs = [], [], []
        for block in (2 * pair, 2 * pair + 1):
            at, half = block_of(block, blocks)
            rows.append(qkv[jmap[at], half * BLK : (half + 1) * BLK, :])
            grads.append(gctx[inv[at], :, half * hw : (half + 1) * hw])
            outs.append(ctx[inv[at], :, half * hw : (half + 1) * hw])
        both = jnp.concatenate(rows, axis=0)
        grad = jnp.concatenate(grads, axis=0)
        out = jnp.concatenate(outs, axis=0)
        lo, hi = 2 * pair * BLK, 2 * (pair + 1) * BLK
        prod = (grad.astype(F32) * out.astype(F32)).T
        kt_s[:, lo:hi] = both[:, hw : 2 * hw].T
        for h in range(heads):
            c0, c1 = h * HEAD_DIM, (h + 1) * HEAD_DIM
            q_s[h, lo:hi, :] = both[:, c0:c1]
            k_s[h, lo:hi, :] = both[:, hw + c0 : hw + c1]
            v_s[h, lo:hi, :] = both[:, 2 * hw + c0 : 2 * hw + c1]
            do_s[h, lo:hi, :] = grad[:, c0:c1]
            delta_s[h : h + 1, lo:hi] = jnp.sum(prod[c0:c1, :], axis=0, keepdims=True)
    dk_s[...] = jnp.zeros_like(dk_s)
    dv_s[...] = jnp.zeros_like(dv_s)
    iota_k = lax.broadcasted_iota(jnp.int32, (QB, QB), 0)
    iota_q = lax.broadcasted_iota(jnp.int32, (QB, QB), 1)
    causal = iota_k <= iota_q
    for h in range(heads):
        for i in range(tokens // QB):
            lo = i * QB
            q = q_s[h, lo : lo + QB, :]
            do = do_s[h, lo : lo + QB, :]
            starts_q = qrow[0:1, lo : lo + QB]
            lse_q = lse[h : h + 1, lo : lo + QB]
            delta_q = delta_s[h : h + 1, lo : lo + QB]

            def block(at, diagonal):
                s = mm_nt(k_s[h, pl.ds(at, QB), :], q) * SCORE_SCALE
                col = kcol[pl.ds(at, QB), :]
                allowed = jnp.concatenate([col, col], axis=1) == starts_q
                if diagonal:
                    allowed = allowed & causal
                p = jnp.exp2(jnp.where(allowed, s, NEG) - lse_q)
                dp = mm_nt(v_s[h, pl.ds(at, QB), :], do)
                ds = (p * (dp - delta_q)).astype(BF)
                dv_s[h, pl.ds(at, QB), :] += mm_nn(p.astype(BF), do)
                dk_s[h, pl.ds(at, QB), :] += mm_nn(ds, q)
                return mm_nn(kt_s[h * HEAD_DIM : (h + 1) * HEAD_DIM, pl.ds(at, QB)], ds)

            dq = block(lo, True)
            if i > 0:
                dq = lax.fori_loop(
                    jmin[i], i, lambda jb, acc: acc + block(pl.multiple_of(jb * QB, QB), False), dq
                )
            dqt_s[h * HEAD_DIM : (h + 1) * HEAD_DIM, lo : lo + QB] = dq * scale
    for pair in range(blocks // 2):
        lo, hi = 2 * pair * BLK, 2 * (pair + 1) * BLK
        parts = [dqt_s[:, lo:hi].T.astype(BF)]
        parts += [(dk_s[h, lo:hi, :] * scale).astype(BF) for h in range(heads)]
        parts += [dv_s[h, lo:hi, :].astype(BF) for h in range(heads)]
        both = jnp.concatenate(parts, axis=1)
        for n, block_at in enumerate((2 * pair, 2 * pair + 1)):
            at, half = block_of(block_at, blocks)
            g_s[jmap[at], half * BLK : (half + 1) * BLK, :] = both[n * BLK : (n + 1) * BLK, :]
    total = None
    sums = None
    for j, piece in enumerate((h0, h1, h2, h3)):
        g = g_s[j]
        back = mm_nt(g, w[...])
        if j == 0:
            g_own[...] = back
        elif j == 1:
            g_a[...] = back.astype(BF)
        else:
            g_bd[j - 2] = back.astype(BF)
        part = mm_tn(piece[...], g)
        col = jnp.sum(g.astype(F32), axis=0, keepdims=True)
        total = part if total is None else total + part
        sums = col if sums is None else sums + col
    shards, rows_out, cols = dw.shape
    rows = WIDTH // shards
    dw[:, 0:rows, :] = total.reshape(shards, rows, cols).astype(BF)
    dw[:, rows:rows_out, :] = jnp.broadcast_to(sums[None], (shards, rows_out - rows, cols)).astype(BF)


def start_ffn_copies(core, own, other, e_s, r_s, sems):
    copies = []
    for p, (mine, theirs) in enumerate(zip(own, (other[0], other[2], other[1], other[3]))):
        group = []
        for n, (src, parity) in enumerate(((mine, core), (theirs, 1 - core))):
            for k, dst in enumerate((e_s, r_s)):
                copy = pltpu.make_async_copy(src.at[:, k], dst.at[p, :, parity], sems.at[p, 2 * n + k])
                copy.start()
                group.append(copy)
        copies.append(group)
    return copies


def ffn_scratch():
    return [
        pltpu.VMEM((4, 4, 2, 96, WIDTH), BF),
        pltpu.VMEM((4, 4, 2, 96, WIDTH), BF),
        pltpu.SemaphoreType.DMA((4, 4)),
    ]


def norm_parts(values):
    centre = values - jnp.mean(values, axis=-1, keepdims=True)
    spread = jnp.mean(centre * centre, axis=-1, keepdims=True)
    rstd = lax.rsqrt(spread + norm_eps)
    return centre * rstd, rstd


def mlp_fwd_kernel(
    core_ref, rk, cx, hid, wo, vec, eb, t, a, b, d, ct, ca, cb, cd,
    lowctx, xhat1, rstd1, lown, act, gp, xhat2, rstd2, hnext, hlow,
    e_s, r_s, sems,
):
    core = core_ref[0]
    copies = start_ffn_copies(core, (t, a, b, d), (ct, ca, cb, cd), e_s, r_s, sems)
    ranks, _, cols = cx.shape
    hw = cols // 2
    for s in range(ranks):
        for half in range(2):
            lowctx[half * BLK : (half + 1) * BLK, s * hw : (s + 1) * hw] = cx[s, :, half * hw : (half + 1) * hw]
    first_sum = hid[...] + (mm_nn(lowctx[...], wo[...].reshape(WIDTH, WIDTH)) + vec[0:1, :])
    x1, r1 = norm_parts(first_sum)
    xhat1[...] = x1
    rstd1[...] = r1
    normed = x1 * vec[1:2, :] + vec[2:3, :]
    lown[...] = normed.astype(BF)
    out = normed + vec[3:4, :]
    for p in range(4):
        for copy in copies[p]:
            copy.wait()
        bias = eb[pl.ds(rk[p], 1), :]
        u = mm_nn(lown[...], e_s[p].reshape(WIDTH, WIDTH)) + bias
        cdf = 0.5 * (1.0 + lax.erf(u * 0.7071067811865476))
        pdf = jnp.exp(-0.5 * u * u) * 0.3989422804014327
        low = (u * cdf).astype(BF)
        act[:, p * WIDTH : (p + 1) * WIDTH] = low
        gp[:, p * WIDTH : (p + 1) * WIDTH] = (cdf + u * pdf).astype(BF)
        out = out + mm_nn(low, r_s[p].reshape(WIDTH, WIDTH))
    x2, r2 = norm_parts(out)
    xhat2[...] = x2
    rstd2[...] = r2
    nxt = x2 * vec[4:5, :] + vec[5:6, :]
    hnext[...] = nxt
    hlow[...] = nxt.astype(BF)


def norm_back(gy, gain, xhat, rstd):
    g = gy * gain
    return rstd * (g - jnp.mean(g, axis=-1, keepdims=True) - xhat * jnp.mean(g * xhat, axis=-1, keepdims=True))


def rows_sum(x):
    return jnp.sum(x, axis=0, keepdims=True)


def mlp_bwd_kernel(
    core_ref, rk, gh, xhat1, rstd1, xhat2, rstd2, gp, vec, wo, t, a, b, d, ct, ca, cb, cd,
    gfs, gb, gat, di, gctx, ext,
    e_s, r_s, sems, eb_s,
):
    core = core_ref[0]
    copies = start_ffn_copies(core, (t, a, b, d), (ct, ca, cb, cd), e_s, r_s, sems)
    grad = gh[...]
    x2 = xhat2[...]
    gss = norm_back(grad, vec[4:5, :], x2, rstd2[...])
    low = gss.astype(BF)
    gb[...] = low
    sums = [None] * 8
    sums[4] = rows_sum(grad * x2)
    sums[5] = rows_sum(grad)
    sums[3] = rows_sum(low.astype(F32))
    gn = gss
    eb_s[...] = jnp.zeros_like(eb_s)
    for p in range(4):
        for copy in copies[p]:
            copy.wait()
        ga = mm_nt(low, r_s[p].reshape(WIDTH, WIDTH))
        dip = (ga * gp[:, p * WIDTH : (p + 1) * WIDTH].astype(F32)).astype(BF)
        di[:, p * WIDTH : (p + 1) * WIDTH] = dip
        eb_s[pl.ds(rk[p], 1), :] = rows_sum(dip.astype(F32))
        gn = gn + mm_nt(dip, e_s[p].reshape(WIDTH, WIDTH))
    x1 = xhat1[...]
    gf = norm_back(gn, vec[1:2, :], x1, rstd1[...])
    sums[1] = rows_sum(gn * x1)
    sums[2] = rows_sum(gn)
    gfs[...] = gf
    lowa = gf.astype(BF)
    gat[...] = lowa
    sums[0] = rows_sum(lowa.astype(F32))
    sums[6] = jnp.zeros_like(sums[0])
    sums[7] = sums[6]
    gc = mm_nt(lowa, wo[...].reshape(WIDTH, WIDTH)).astype(BF)
    ranks, _, cols = gctx.shape
    hw = cols // 2
    for s in range(ranks):
        for half in range(2):
            gctx[s, :, half * hw : (half + 1) * hw] = gc[half * BLK : (half + 1) * BLK, s * hw : (s + 1) * hw]
    vecs = jnp.concatenate(sums + [eb_s[...]], axis=0)
    ext[...] = jnp.zeros_like(ext)
    shards = ext.shape[0]
    cut = WIDTH // shards
    for f in range(shards):
        ext[f, :, 0:cut] = vecs[:, f * cut : (f + 1) * cut].astype(BF)


def wgrad_kernel(
    core_ref, lown, di, act, gb, lowctx, gat, ext, mine_ta, mine_bd, other_ta, other_bd, dwo
):
    core = core_ref[0]
    shards, rows_out, _ = dwo.shape
    rows = WIDTH // shards
    dwo[:, 0:rows, :] = mm_tn(lowctx[...], gat[...]).reshape(shards, rows, WIDTH).astype(BF)
    dwo[:, rows:rows_out, :] = ext[...]
    mine = ((mine_ta, 0), (mine_ta, 1), (mine_bd, 0), (mine_bd, 1))
    other = ((other_ta, 0), (other_bd, 0), (other_ta, 1), (other_bd, 1))
    for p in (2, 3, 1, 0):
        cut = slice(p * WIDTH, (p + 1) * WIDTH)
        for k, (left, right) in enumerate(((lown[...], di[:, cut]), (act[:, cut], gb[...]))):
            x = mm_tn(left, right).reshape(4, 2, 96, WIDTH).astype(BF)
            for parity in range(2):

                @pl.when(core == parity)
                def _():
                    ref, at = mine[p]
                    ref[at, :, k] = x[:, parity]

                @pl.when(core != parity)
                def _():
                    ref, at = other[p]
                    ref[at, :, k] = x[:, parity]


def place_kernel(rk, ffn0, ffn1, ffn2, ffn3, win0, win1, win2, win3, dwo, e_out, r_out, i_out, o_out, e_s, i_s):
    for p, (ffn, win) in enumerate(((ffn0, win0), (ffn1, win1), (ffn2, win2), (ffn3, win3))):
        r_out[pl.ds(pl.multiple_of(rk[p] * 96, 96), 96), :] = ffn[1].astype(F32)
        e_s[rk[p]] = ffn[0].astype(F32)
        i_s[rk[p]] = win[0:96, :].astype(F32)
    for f in range(8):
        e_out[:, f * 384 : (f + 1) * 384] = jnp.concatenate(
            [e_s[c, :, f * 96 : (f + 1) * 96] for c in range(4)], axis=1
        )
    hw = WIDTH // 4
    for k in range(3):
        i_out[:, k * WIDTH : (k + 1) * WIDTH] = jnp.concatenate(
            [i_s[c, :, k * hw : (k + 1) * hw] for c in range(4)], axis=1
        )
    o_out[...] = dwo[0:96, :].astype(F32)


def permutations(ctx, fsdp):
    first, second, cores = [], [], []
    for c in range(ctx):
        for f in range(fsdp):
            m1, m2 = (1, 2) if f % 2 == 0 else (2, 1)
            first.append((c * fsdp + f, (c ^ m1) * fsdp + f))
            second.append((c * fsdp + f, (c ^ m2) * fsdp + f))
            cores.append((c * fsdp + f, c * fsdp + (f ^ 1)))
    return first, second, cores


def on_device_fast(
    activations, cotangent, doc_start, deal,
    attend_in, query_bias, value_bias, attend_out, attend_bias, first_gain, first_shift,
    expand_proj, expand_bias, reduce_proj, reduce_bias, second_gain, second_shift,
    *, ctx, fsdp,
):
    S = pltpu.SMEM
    V = pltpu.VMEM
    A = pl.ANY
    first, second, cores = permutations(ctx, fsdp)
    both_axes = ("ctx", "fsdp")

    def via_first(x):
        return lax.ppermute(x, both_axes, first)

    def via_second(x):
        return lax.ppermute(x, both_axes, second)

    def via_core(x):
        return lax.ppermute(x, both_axes, cores)

    def gather_ctx(x):
        a, b = via_first(x), via_second(x)
        return (x, a, b, via_second(a))

    heads = HEADS // ctx
    hw = heads * HEAD_DIM
    rows = activations.shape[1]
    tokens = rows * ctx
    c = lax.axis_index("ctx").astype(jnp.int32)
    core = (lax.axis_index("fsdp") % 2).astype(jnp.int32)
    core1 = core.reshape(1)
    m1 = 1 + core
    rk = jnp.stack([c, c ^ m1, c ^ (3 - m1), c ^ 3])
    inv = jnp.sum(
        jnp.where(deal[None, :] == jnp.arange(ctx)[:, None], jnp.arange(ctx)[None, :], 0), axis=1
    ).astype(jnp.int32)
    mask = inv ^ c
    jmap = jnp.where((core == 1) & (mask > 0) & (mask < 3), 3 - mask, mask).astype(jnp.int32)

    zgroups = [[2 * z + k for z in range(fsdp // 2)] for k in range(2)]
    hidden = activations[0].astype(F32)
    hlow = activations[0]

    small = [attend_bias, first_gain, first_shift, reduce_bias, second_gain, second_shift, query_bias, value_bias]
    packed = jnp.concatenate([jnp.stack(small, axis=1).reshape(LAYERS, -1), expand_bias], axis=1)
    packed = lax.all_gather(packed.reshape(1, -1), "fsdp", axis=0, tiled=True).reshape(fsdp, LAYERS, -1)
    cut = WIDTH // fsdp
    vec = packed[:, :, : 8 * cut].reshape(fsdp, LAYERS, 8, cut).transpose(1, 2, 0, 3).reshape(LAYERS, 8, WIDTH)
    vec = vec.astype(F32)
    ebias = packed[:, :, 8 * cut :].reshape(fsdp, LAYERS, ctx, cut).transpose(1, 2, 0, 3)
    ebias = ebias.reshape(LAYERS, ctx, WIDTH).astype(F32)

    starts = lax.all_gather(doc_start[0], "ctx", axis=0, tiled=True).reshape(ctx, 2, BLK)
    chosen = inv[:, None, None, None] == jnp.arange(ctx, dtype=jnp.int32)[None, :, None, None]
    starts = jnp.sum(jnp.where(chosen, starts[None], 0), axis=1)
    logical = jnp.concatenate([starts[:, 0], starts[::-1, 1]], axis=0).reshape(-1)
    qrow = jnp.broadcast_to(logical[None, :], (8, tokens))
    kcol = jnp.broadcast_to(logical[:, None], (tokens, 128))
    jmin = jnp.min(logical.reshape(tokens // QB, QB), axis=1) // QB

    def ffn_piece(layer):
        e = expand_proj[layer].reshape(cut, fsdp, ctx, cut)
        e = lax.dynamic_index_in_dim(e, c, axis=2, keepdims=False).reshape(cut, WIDTH)
        r = lax.dynamic_slice_in_dim(reduce_proj[layer], c * cut, cut, axis=0)
        x = lax.all_gather(
            jnp.concatenate([e, r], axis=0), "fsdp", axis=0, tiled=True, axis_index_groups=zgroups
        ).reshape(fsdp // 2, 2, cut, WIDTH)
        own = gather_ctx(x)
        return own + tuple(via_core(piece) for piece in own)

    win = attend_in.reshape(LAYERS, cut, 3, WIDTH)
    win = lax.dynamic_slice_in_dim(win, c * hw, hw, axis=3).reshape(LAYERS * cut, 3 * hw)
    win = lax.all_gather(win, "fsdp", axis=0, tiled=True).reshape(fsdp, LAYERS, cut, 3 * hw)
    win = [win[:, layer].reshape(WIDTH, 3 * hw) for layer in range(LAYERS)]
    wout = lax.all_gather(attend_out.reshape(LAYERS * cut, WIDTH), "fsdp", axis=0, tiled=True)
    wout = wout.reshape(fsdp, LAYERS, cut, WIDTH)
    wout = [wout[:, layer] for layer in range(LAYERS)]
    pieces = [ffn_piece(layer) for layer in range(LAYERS)]
    qkv_bias = []
    for layer in range(LAYERS):
        qb = lax.dynamic_slice_in_dim(vec[layer, 6], c * hw, hw)
        vb = lax.dynamic_slice_in_dim(vec[layer, 7], c * hw, hw)
        qkv_bias.append(jnp.concatenate([qb, jnp.zeros_like(qb), vb])[None, :])

    mac = 2
    kept = []
    for layer in range(LAYERS):
        gathered = gather_ctx(hlow)
        qkv, ctx_own, lse = call(
            functools.partial(attn_fwd_kernel, heads=heads, tokens=tokens),
            [((ctx, rows, 3 * hw), BF), ((ctx, BLK, 2 * hw), BF), ((8, tokens), F32)],
            (jmap, inv, jmin) + gathered + (win[layer], qkv_bias[layer], qrow, kcol),
            [S] * 3 + [V] * 8,
            [
                pltpu.VMEM((heads, tokens, HEAD_DIM), BF),
                pltpu.VMEM((heads, tokens, HEAD_DIM), BF),
                pltpu.VMEM((hw, tokens), BF),
                pltpu.VMEM((hw, tokens), F32),
            ],
            "attn_fwd",
            mac * tokens * WIDTH * 3 * hw * 4,
            10 * 1024 * 1024,
        )
        cx = lax.all_to_all(ctx_own, "ctx", 0, 0, tiled=True)
        lowctx, xhat1, rstd1, lown, act, gp, xhat2, rstd2, hidden, hlow = call(
            mlp_fwd_kernel,
            [
                ((rows, WIDTH), BF), ((rows, WIDTH), F32), ((rows, 1), F32), ((rows, WIDTH), BF),
                ((rows, 4 * WIDTH), BF), ((rows, 4 * WIDTH), BF), ((rows, WIDTH), F32), ((rows, 1), F32),
                ((rows, WIDTH), F32), ((rows, WIDTH), BF),
            ],
            (core1, rk, cx, hidden, wout[layer], vec[layer], ebias[layer]) + pieces[layer],
            [S] * 2 + [V] * 5 + [A] * 8,
            ffn_scratch(),
            "mlp_fwd",
            mac * rows * WIDTH * WIDTH * 9,
            20 * 1024 * 1024,
        )
        kept.append((gathered, qkv, ctx_own, lse, lowctx, xhat1, rstd1, lown, act, gp, xhat2, rstd2))
    out_act = hlow[None]

    grad = cotangent[0].astype(F32)
    results = [None] * LAYERS
    for layer in reversed(range(LAYERS)):
        gathered, qkv, ctx_own, lse, lowctx, xhat1, rstd1, lown, act, gp, xhat2, rstd2 = kept[layer]
        gfs, gb, gat, di, gctx, ext = call(
            mlp_bwd_kernel,
            [
                ((rows, WIDTH), F32), ((rows, WIDTH), BF), ((rows, WIDTH), BF), ((rows, 4 * WIDTH), BF),
                ((ctx, BLK, 2 * hw), BF), ((fsdp, 16, WIDTH), BF),
            ],
            (core1, rk, grad, xhat1, rstd1, xhat2, rstd2, gp, vec[layer], wout[layer]) + pieces[layer],
            [S] * 2 + [V] * 8 + [A] * 8,
            ffn_scratch() + [pltpu.VMEM((8, WIDTH), F32)],
            "mlp_bwd",
            mac * rows * WIDTH * WIDTH * 9,
            20 * 1024 * 1024,
        )
        gcx = lax.all_to_all(gctx, "ctx", 0, 0, tiled=True)
        pair = ((2, 4, 2, cut, WIDTH), BF)
        mine_ta, mine_bd, other_ta, other_bd, dwo = call(
            wgrad_kernel,
            [pair, pair, pair, pair, ((fsdp, cut + 16, WIDTH), BF)],
            (core1, lown, di, act, gb, lowctx, gat, ext),
            [S] + [V] * 7,
            [],
            "wgrad",
            mac * rows * WIDTH * WIDTH * 9,
            20 * 1024 * 1024,
        )
        g_own, g_a, g_bd, dw = call(
            functools.partial(attn_bwd_kernel, heads=heads, tokens=tokens),
            [
                ((rows, WIDTH), F32), ((rows, WIDTH), BF), ((2, rows, WIDTH), BF),
                ((fsdp, cut + 16, 3 * hw), BF),
            ],
            (jmap, inv, jmin) + gathered + (win[layer], qrow, kcol, qkv, ctx_own, gcx, lse),
            [S] * 3 + [V] * 11,
            [
                pltpu.VMEM((heads, tokens, HEAD_DIM), BF),
                pltpu.VMEM((heads, tokens, HEAD_DIM), BF),
                pltpu.VMEM((heads, tokens, HEAD_DIM), BF),
                pltpu.VMEM((heads, tokens, HEAD_DIM), BF),
                pltpu.VMEM((hw, tokens), BF),
                pltpu.VMEM((8, tokens), F32),
                pltpu.VMEM((heads, tokens, HEAD_DIM), F32),
                pltpu.VMEM((heads, tokens, HEAD_DIM), F32),
                pltpu.VMEM((hw, tokens), F32),
                pltpu.VMEM((ctx, rows, 3 * hw), BF),
            ],
            "attn_bwd",
            mac * tokens * WIDTH * 3 * hw * 8,
            10 * 1024 * 1024,
        )
        back = via_second(g_bd).astype(F32)
        over = via_first((g_a.astype(F32) + back[1]).astype(BF)).astype(F32)
        grad = gfs + (g_own + (back[0] + over))
        sum_bd = (mine_bd.astype(F32) + via_core(other_bd).astype(F32)).astype(BF)
        back = via_second(sum_bd).astype(F32)
        sum_ta = mine_ta.astype(F32) + via_core(other_ta).astype(F32) + back
        over = via_first(sum_ta[1].astype(BF)).astype(F32)
        ffn = lax.psum_scatter(
            (sum_ta[0] + over).astype(BF), "fsdp", scatter_dimension=0, tiled=True, axis_index_groups=zgroups
        ).reshape(2, cut, WIDTH)
        dw = lax.psum_scatter(dw, "fsdp", scatter_dimension=0, tiled=True).reshape(cut + 16, 3 * hw)
        dwo = lax.psum_scatter(dwo, "fsdp", scatter_dimension=0, tiled=True).reshape(cut + 16, WIDTH)
        dwo = (dwo.astype(F32) + via_first(dwo).astype(F32)).astype(BF)
        dwo = dwo.astype(F32) + via_second(dwo).astype(F32)
        ffn_all = gather_ctx(ffn)
        dw_all = gather_ctx(dw)
        e_out, r_out, i_out, o_out = call(
            place_kernel,
            [((cut, 4 * WIDTH), F32), ((4 * cut, WIDTH), F32), ((cut, 3 * WIDTH), F32), ((cut, WIDTH), F32)],
            (rk,) + ffn_all + dw_all + (dwo,),
            [S] + [V] * 9,
            [pltpu.VMEM((ctx, cut, WIDTH), F32), pltpu.VMEM((ctx, cut, 3 * hw), F32)],
            "place",
            0,
            10 * 1024 * 1024,
        )
        shard = lax.axis_index("fsdp").astype(jnp.int32)
        bias_rows = jnp.stack([piece[cut : cut + 1] for piece in dw_all])
        owner = (shard * cut) // hw
        holder = owner ^ c
        holder = jnp.where((core == 1) & (holder > 0) & (holder < 3), 3 - holder, holder)
        row = lax.dynamic_index_in_dim(bias_rows, holder, axis=0, keepdims=False)[0]
        offset = shard * cut - owner * hw
        qb = lax.dynamic_slice_in_dim(row, offset, cut).astype(F32)
        vb = lax.dynamic_slice_in_dim(row, 2 * hw + offset, cut).astype(F32)
        v = dwo[cut:, :cut]
        results[layer] = (
            i_out, qb, vb, o_out, v[0], v[1], v[2], e_out, v[8 : 8 + ctx].reshape(-1), r_out, v[3], v[4], v[5]
        )
    stacked = [jnp.stack([results[layer][n] for layer in range(LAYERS)]) for n in range(13)]
    return (out_act, grad[None]) + tuple(stacked)


def on_device(*args, ctx, fsdp):
    if ctx == 4 and fsdp == 8 and args[0].shape[1] == 2 * BLK:
        return on_device_fast(*args, ctx=ctx, fsdp=fsdp)
    return on_device_plain(*args)


def solution(mesh):
    placed = (
        P("fsdp", "ctx", None),
        P("fsdp", "ctx", None),
        P("fsdp", "ctx"),
        P(),
        P(None, "fsdp", None),
        P(None, "fsdp"),
        P(None, "fsdp"),
        P(None, "fsdp", None),
        P(None, "fsdp"),
        P(None, "fsdp"),
        P(None, "fsdp"),
        P(None, "fsdp", None),
        P(None, "fsdp"),
        P(None, "fsdp", None),
        P(None, "fsdp"),
        P(None, "fsdp"),
        P(None, "fsdp"),
    )
    return jax.shard_map(
        functools.partial(on_device, ctx=mesh.shape["ctx"], fsdp=mesh.shape["fsdp"]),
        mesh=mesh,
        in_specs=placed,
        out_specs=(
            P("fsdp", "ctx", None),
            P("fsdp", "ctx", None),
            P(None, "fsdp", None),
            P(None, "fsdp"),
            P(None, "fsdp"),
            P(None, "fsdp", None),
            P(None, "fsdp"),
            P(None, "fsdp"),
            P(None, "fsdp"),
            P(None, "fsdp", None),
            P(None, "fsdp"),
            P(None, "fsdp", None),
            P(None, "fsdp"),
            P(None, "fsdp"),
            P(None, "fsdp"),
        ),
        check_vma=False,
    )
```

```python
import functools

import jax
import jax.numpy as jnp
from jax import lax
from jax.experimental import pallas as pl
from jax.experimental.pallas import tpu as pltpu
from jax.sharding import PartitionSpec as P

HEADS = 12
HEAD_DIM = 64
LAYERS = 2
BLK = 192


norm_eps = 1e-05


def for_sending(x):
    return jax.tree.map(lambda a: a.astype(jnp.bfloat16) if a.dtype == jnp.float32 else a, x)


def layer_norm(values, gain, shift):
    centre = values - jnp.mean(values, axis=-1, keepdims=True)
    spread = jnp.mean(centre * centre, axis=-1, keepdims=True)
    return centre * lax.rsqrt(spread + norm_eps) * gain + shift


def gelu_exact(inputs):
    return 0.5 * inputs * (1.0 + jax.scipy.special.erf(inputs * 0.7071067811865476))


def key_positions(deal):
    pairs = deal.shape[0]
    offsets = jnp.arange(BLK, dtype=jnp.int32)
    first = deal[:, None] * BLK + offsets[None, :]
    second = (2 * pairs - 1 - deal)[:, None] * BLK + offsets[None, :]
    return jnp.concatenate([first, second], axis=1).reshape(-1)


def split_heads(matrix):
    return matrix.reshape(matrix.shape[0], HEADS, HEAD_DIM).transpose(1, 0, 2)


def join_heads(stacked):
    return stacked.transpose(1, 0, 2).reshape(stacked.shape[1], HEADS * HEAD_DIM)


def attend_forward(queries, keys_full, values_full, allowed):

    def one_head(items):
        head_q, head_k, head_v = items
        scores = jnp.einsum(
            "qd,kd->qk", head_q, head_k, preferred_element_type=jnp.float32
        ) * HEAD_DIM ** (-0.5)
        scores = jnp.where(allowed, scores, -1e30)
        top = jnp.max(scores, axis=-1, keepdims=True)
        weights = jnp.exp(scores - top)
        total = jnp.sum(weights, axis=-1, keepdims=True)
        probs = (weights / total).astype(jnp.bfloat16)
        output = jnp.einsum("qk,kd->qd", probs, head_v, preferred_element_type=jnp.float32)
        return (output, top[:, 0] + jnp.log(total[:, 0]))

    outputs, log_totals = lax.map(
        one_head, (split_heads(queries), split_heads(keys_full), split_heads(values_full))
    )
    return (join_heads(outputs), log_totals)


def attend_backward(queries, keys_full, values_full, log_totals, grad_context, allowed):

    def one_head(items):
        head_q, head_k, head_v, head_lse, head_grad = items
        scores = jnp.einsum(
            "qd,kd->qk", head_q, head_k, preferred_element_type=jnp.float32
        ) * HEAD_DIM ** (-0.5)
        scores = jnp.where(allowed, scores, -1e30)
        probs = jnp.exp(scores - head_lse[:, None])
        grad_probs = jnp.einsum("qd,kd->qk", head_grad, head_v, preferred_element_type=jnp.float32)
        inner_sum = jnp.sum(probs * grad_probs, axis=-1, keepdims=True)
        grad_scores = (probs * (grad_probs - inner_sum)).astype(jnp.bfloat16)
        grad_q = jnp.einsum(
            "qk,kd->qd", grad_scores, head_k, preferred_element_type=jnp.float32
        ) * HEAD_DIM ** (-0.5)
        grad_k = jnp.einsum(
            "qk,qd->kd", grad_scores, head_q, preferred_element_type=jnp.float32
        ) * HEAD_DIM ** (-0.5)
        grad_v = jnp.einsum(
            "qk,qd->kd", probs.astype(jnp.bfloat16), head_grad, preferred_element_type=jnp.float32
        )
        return (grad_q, grad_k, grad_v)

    grads = lax.map(
        one_head,
        (
            split_heads(queries),
            split_heads(keys_full),
            split_heads(values_full),
            log_totals,
            split_heads(grad_context),
        ),
    )
    return (join_heads(grads[0]), join_heads(grads[1]), join_heads(grads[2]))


def forward_layer(hidden, weights, allowed):
    (
        attend_in,
        query_bias,
        value_bias,
        attend_out,
        attend_bias,
        first_gain,
        first_shift,
        expand_proj,
        expand_bias,
        reduce_proj,
        reduce_bias,
        second_gain,
        second_shift,
    ) = weights
    width = hidden.shape[1]
    low_hidden = hidden.astype(jnp.bfloat16)
    projected = jnp.dot(low_hidden, attend_in, preferred_element_type=jnp.float32)
    queries = (projected[:, :width] + query_bias.astype(jnp.float32)).astype(jnp.bfloat16)
    keys_own = projected[:, width : 2 * width].astype(jnp.bfloat16)
    values_own = (projected[:, 2 * width :] + value_bias.astype(jnp.float32)).astype(jnp.bfloat16)
    keys_full, values_full = (
        lax.all_gather(keys_own, "ctx", axis=0, tiled=True),
        lax.all_gather(values_own, "ctx", axis=0, tiled=True),
    )
    context, log_totals = attend_forward(queries, keys_full, values_full, allowed)
    low_context = context.astype(jnp.bfloat16)
    branch = jnp.dot(
        low_context, attend_out, preferred_element_type=jnp.float32
    ) + attend_bias.astype(jnp.float32)
    first_sum = hidden + branch
    normed = layer_norm(first_sum, first_gain.astype(jnp.float32), first_shift.astype(jnp.float32))
    low_normed = normed.astype(jnp.bfloat16)
    inner_pre = jnp.dot(
        low_normed, expand_proj, preferred_element_type=jnp.float32
    ) + expand_bias.astype(jnp.float32)
    active = gelu_exact(inner_pre).astype(jnp.bfloat16)
    output_branch = jnp.dot(
        active, reduce_proj, preferred_element_type=jnp.float32
    ) + reduce_bias.astype(jnp.float32)
    second_sum = normed + output_branch
    output = layer_norm(
        second_sum, second_gain.astype(jnp.float32), second_shift.astype(jnp.float32)
    )
    saved = (
        low_hidden,
        queries,
        keys_full,
        values_full,
        log_totals,
        low_context,
        first_sum,
        low_normed,
        inner_pre,
        active,
        second_sum,
    )
    return (output, saved)


def column_sum(matrix):
    return jnp.sum(matrix.astype(jnp.float32), axis=0)


def backward_layer(grad_hidden, weights, saved, allowed):
    (
        attend_in,
        query_bias,
        value_bias,
        attend_out,
        attend_bias,
        first_gain,
        first_shift,
        expand_proj,
        expand_bias,
        reduce_proj,
        reduce_bias,
        second_gain,
        second_shift,
    ) = weights
    (
        low_hidden,
        queries,
        keys_full,
        values_full,
        log_totals,
        low_context,
        first_sum,
        low_normed,
        inner_pre,
        active,
        second_sum,
    ) = saved
    width = low_hidden.shape[1]
    second_pull = jax.vjp(
        layer_norm, second_sum, second_gain.astype(jnp.float32), second_shift.astype(jnp.float32)
    )[1]
    grad_second_sum, grad_second_gain, grad_second_shift = second_pull(grad_hidden)
    grad_branch = grad_second_sum.astype(jnp.bfloat16)
    grad_reduce_bias = column_sum(grad_branch)
    grad_reduce = jnp.einsum("tf,td->fd", active, grad_branch, preferred_element_type=jnp.float32)
    grad_active = jnp.einsum(
        "td,fd->tf", grad_branch, reduce_proj, preferred_element_type=jnp.float32
    )
    gelu_pull = jax.vjp(gelu_exact, inner_pre)[1]
    grad_inner = gelu_pull(grad_active)[0].astype(jnp.bfloat16)
    grad_expand_bias = column_sum(grad_inner)
    grad_expand = jnp.einsum(
        "td,tf->df", low_normed, grad_inner, preferred_element_type=jnp.float32
    )
    grad_normed = grad_second_sum + jnp.einsum(
        "tf,df->td", grad_inner, expand_proj, preferred_element_type=jnp.float32
    )
    first_pull = jax.vjp(
        layer_norm, first_sum, first_gain.astype(jnp.float32), first_shift.astype(jnp.float32)
    )[1]
    grad_first_sum, grad_first_gain, grad_first_shift = first_pull(grad_normed)
    grad_attn = grad_first_sum.astype(jnp.bfloat16)
    grad_attend_bias = column_sum(grad_attn)
    grad_attend_out = jnp.einsum(
        "td,te->de", low_context, grad_attn, preferred_element_type=jnp.float32
    )
    grad_context = jnp.einsum(
        "te,de->td", grad_attn, attend_out, preferred_element_type=jnp.float32
    ).astype(jnp.bfloat16)
    grad_queries, grad_keys_full, grad_values_full = attend_backward(
        queries, keys_full, values_full, log_totals, grad_context, allowed
    )
    grad_keys, grad_values = (
        lax.psum_scatter(
            grad_keys_full.astype(jnp.bfloat16), "ctx", scatter_dimension=0, tiled=True
        ).astype(jnp.float32),
        lax.psum_scatter(
            grad_values_full.astype(jnp.bfloat16), "ctx", scatter_dimension=0, tiled=True
        ).astype(jnp.float32),
    )
    grad_proj = jnp.concatenate(
        [
            grad_queries.astype(jnp.bfloat16),
            grad_keys.astype(jnp.bfloat16),
            grad_values.astype(jnp.bfloat16),
        ],
        axis=1,
    )
    grad_query_bias = column_sum(grad_proj[:, :width])
    grad_value_bias = column_sum(grad_proj[:, 2 * width :])
    grad_attend_in = jnp.einsum(
        "td,te->de", low_hidden, grad_proj, preferred_element_type=jnp.float32
    )
    grad_input = grad_first_sum + jnp.einsum(
        "te,de->td", grad_proj, attend_in, preferred_element_type=jnp.float32
    )
    grads = (
        grad_attend_in,
        grad_query_bias,
        grad_value_bias,
        grad_attend_out,
        grad_attend_bias,
        grad_first_gain,
        grad_first_shift,
        grad_expand,
        grad_expand_bias,
        grad_reduce,
        grad_reduce_bias,
        grad_second_gain,
        grad_second_shift,
    )
    return (grad_input, grads)


def reduce_grads(grads):
    shards = (
        lax.psum_scatter(
            grads[0].astype(jnp.bfloat16), "fsdp", scatter_dimension=0, tiled=True
        ).astype(jnp.float32),
        lax.psum_scatter(
            grads[1].astype(jnp.bfloat16), "fsdp", scatter_dimension=0, tiled=True
        ).astype(jnp.float32),
        lax.psum_scatter(
            grads[2].astype(jnp.bfloat16), "fsdp", scatter_dimension=0, tiled=True
        ).astype(jnp.float32),
        lax.psum_scatter(
            grads[3].astype(jnp.bfloat16), "fsdp", scatter_dimension=0, tiled=True
        ).astype(jnp.float32),
        lax.psum_scatter(
            grads[4].astype(jnp.bfloat16), "fsdp", scatter_dimension=0, tiled=True
        ).astype(jnp.float32),
        lax.psum_scatter(
            grads[5].astype(jnp.bfloat16), "fsdp", scatter_dimension=0, tiled=True
        ).astype(jnp.float32),
        lax.psum_scatter(
            grads[6].astype(jnp.bfloat16), "fsdp", scatter_dimension=0, tiled=True
        ).astype(jnp.float32),
        lax.psum_scatter(
            grads[7].astype(jnp.bfloat16), "fsdp", scatter_dimension=0, tiled=True
        ).astype(jnp.float32),
        lax.psum_scatter(
            grads[8].astype(jnp.bfloat16), "fsdp", scatter_dimension=0, tiled=True
        ).astype(jnp.float32),
        lax.psum_scatter(
            grads[9].astype(jnp.bfloat16), "fsdp", scatter_dimension=0, tiled=True
        ).astype(jnp.float32),
        lax.psum_scatter(
            grads[10].astype(jnp.bfloat16), "fsdp", scatter_dimension=0, tiled=True
        ).astype(jnp.float32),
        lax.psum_scatter(
            grads[11].astype(jnp.bfloat16), "fsdp", scatter_dimension=0, tiled=True
        ).astype(jnp.float32),
        lax.psum_scatter(
            grads[12].astype(jnp.bfloat16), "fsdp", scatter_dimension=0, tiled=True
        ).astype(jnp.float32),
    )
    return (
        lax.psum(shards[0].astype(jnp.bfloat16), "ctx").astype(jnp.float32),
        lax.psum(shards[1].astype(jnp.bfloat16), "ctx").astype(jnp.float32),
        lax.psum(shards[2].astype(jnp.bfloat16), "ctx").astype(jnp.float32),
        lax.psum(shards[3].astype(jnp.bfloat16), "ctx").astype(jnp.float32),
        lax.psum(shards[4].astype(jnp.bfloat16), "ctx").astype(jnp.float32),
        lax.psum(shards[5].astype(jnp.bfloat16), "ctx").astype(jnp.float32),
        lax.psum(shards[6].astype(jnp.bfloat16), "ctx").astype(jnp.float32),
        lax.psum(shards[7].astype(jnp.bfloat16), "ctx").astype(jnp.float32),
        lax.psum(shards[8].astype(jnp.bfloat16), "ctx").astype(jnp.float32),
        lax.psum(shards[9].astype(jnp.bfloat16), "ctx").astype(jnp.float32),
        lax.psum(shards[10].astype(jnp.bfloat16), "ctx").astype(jnp.float32),
        lax.psum(shards[11].astype(jnp.bfloat16), "ctx").astype(jnp.float32),
        lax.psum(shards[12].astype(jnp.bfloat16), "ctx").astype(jnp.float32),
    )


def layer_slices(sharded, layer_index):
    return tuple((tensor[layer_index] for tensor in sharded))


def on_device_plain(
    activations,
    cotangent,
    doc_start,
    deal,
    attend_in,
    query_bias,
    value_bias,
    attend_out,
    attend_bias,
    first_gain,
    first_shift,
    expand_proj,
    expand_bias,
    reduce_proj,
    reduce_bias,
    second_gain,
    second_shift,
):
    sharded = (
        attend_in,
        query_bias,
        value_bias,
        attend_out,
        attend_bias,
        first_gain,
        first_shift,
        expand_proj,
        expand_bias,
        reduce_proj,
        reduce_bias,
        second_gain,
        second_shift,
    )
    row_count = activations.shape[1]
    positions = key_positions(deal)
    own_rank = lax.axis_index("ctx")
    own_positions = lax.dynamic_slice_in_dim(positions, own_rank * row_count, row_count)
    own_starts = doc_start[0]
    key_starts = lax.all_gather(own_starts, "ctx", axis=0, tiled=True)
    allowed = (positions[None, :] <= own_positions[:, None]) & (
        key_starts[None, :] == own_starts[:, None]
    )
    hidden = activations[0].astype(jnp.float32)
    kept_weights = []
    kept_saved = []
    for layer_index in range(LAYERS):
        weights = lax.all_gather(
            for_sending(layer_slices(sharded, layer_index)), "fsdp", axis=0, tiled=True
        )
        hidden, saved = forward_layer(hidden, weights, allowed)
        kept_weights.append(weights)
        kept_saved.append(saved)
    out_act = hidden.astype(jnp.bfloat16)[None]
    grad_hidden = cotangent[0].astype(jnp.float32)
    reduced = [None] * LAYERS
    for layer_index in reversed(range(LAYERS)):
        weights = lax.all_gather(
            for_sending(layer_slices(sharded, layer_index)), "fsdp", axis=0, tiled=True
        )
        grad_hidden, grads = backward_layer(grad_hidden, weights, kept_saved[layer_index], allowed)
        reduced[layer_index] = reduce_grads(grads)
    stacked = [
        jnp.stack([reduced[layer_index][member] for layer_index in range(LAYERS)])
        for member in range(13)
    ]
    return (
        out_act,
        grad_hidden[None],
        stacked[0],
        stacked[1],
        stacked[2],
        stacked[3],
        stacked[4],
        stacked[5],
        stacked[6],
        stacked[7],
        stacked[8],
        stacked[9],
        stacked[10],
        stacked[11],
        stacked[12],
    )


F32 = jnp.float32
BF = jnp.bfloat16
WIDTH = HEADS * HEAD_DIM
QB = 256
SCORE_SCALE = HEAD_DIM ** (-0.5) * 1.4426950408889634
NEG = -1e30
VMEM_LIMIT = 60 * 1024 * 1024


def mm_nn(a, b):
    return lax.dot_general(a, b, (((1,), (0,)), ((), ())), preferred_element_type=F32)


def mm_nt(a, b):
    return lax.dot_general(a, b, (((1,), (1,)), ((), ())), preferred_element_type=F32)


def mm_tn(a, b):
    return lax.dot_general(a, b, (((0,), (0,)), ((), ())), preferred_element_type=F32)


def call(kernel, outs, args, specs, scratch, name, flops, nbytes):
    return pl.pallas_call(
        kernel,
        out_shape=[jax.ShapeDtypeStruct(shape, dtype) for shape, dtype in outs],
        in_specs=[pl.BlockSpec(memory_space=space) for space in specs],
        out_specs=[pl.BlockSpec(memory_space=pltpu.VMEM) for _ in outs],
        scratch_shapes=scratch,
        compiler_params=pltpu.CompilerParams(vmem_limit_bytes=VMEM_LIMIT),
        cost_estimate=pl.CostEstimate(flops=0, bytes_accessed=0, transcendentals=0),
        name=name,
    )(*args)


def block_of(block, blocks):
    half = 0 if 2 * block < blocks else 1
    return (block if half == 0 else blocks - 1 - block), half


CORE, SHARD, RANK, JMAP, INV, JMIN = 0, 1, 2, 6, 10, 14
SWAPPED = (0, 2, 1, 3)
VEC_AT = 640


def started_copies(sems, *pairs):
    copies = []
    for n, (src, dst) in enumerate(pairs):
        copy = pltpu.make_async_copy(src, dst, sems.at[n])
        copy.start()
        copies.append(copy)
    return copies


def prep_kernel(
    expand, reduce, attend_in, attend_out, expand_bias, v0, v1, v2, v3, v4, v5, v6, v7,
    t0, d0, t1, d1,
):
    rank = lax.axis_index("ctx")
    cut = expand.shape[1]
    hw = WIDTH // 4
    for layer, (t, d) in enumerate(((t0, d0), (t1, d1))):
        bias = expand_bias[layer : layer + 1, :].astype(F32)
        rows = [v[layer : layer + 1, :].astype(F32) for v in (v0, v1, v2, v3, v4, v5, v6, v7)]
        rows += [bias[:, k * cut : (k + 1) * cut] for k in range(4)]
        rows.append(jnp.zeros((4, cut), F32))
        d[2 * cut :, :] = attend_out[layer]
        t[2 * cut :, 3 * hw :] = jnp.zeros((cut, WIDTH - 3 * hw), BF)
        t[2 * cut : 2 * cut + 16, VEC_AT : VEC_AT + cut] = jnp.concatenate(rows, axis=0).astype(BF)
        for k in range(4):

            @pl.when(rank == k)
            def _():
                for out, at in ((t, k), (d, k ^ 3)):
                    out[0:cut, :] = jnp.concatenate(
                        [
                            expand[layer, :, (2 * z + h) * 4 * cut + at * cut : (2 * z + h) * 4 * cut + (at + 1) * cut]
                            for h in range(2)
                            for z in range(4)
                        ],
                        axis=1,
                    )
                    out[cut : 2 * cut, :] = reduce[layer, at * cut : (at + 1) * cut, :]
                t[2 * cut :, 0 : 3 * hw] = jnp.concatenate(
                    [attend_in[layer, :, n * WIDTH + k * hw : n * WIDTH + (k + 1) * hw] for n in range(3)], axis=1
                )


def nothing_kernel(*refs):
    pass


def after(xs, *others):
    return pl.pallas_call(
        nothing_kernel,
        out_shape=[jax.ShapeDtypeStruct(x.shape, x.dtype) for x in xs],
        in_specs=[pl.BlockSpec(memory_space=pl.ANY)] * (len(xs) + len(others)),
        out_specs=[pl.BlockSpec(memory_space=pl.ANY)] * len(xs),
        input_output_aliases={n: n for n in range(len(xs))},
        name="after",
    )(*xs, *others)


def token_kernel(*refs):
    refs[-1][...] = jnp.zeros_like(refs[-1])


def token(*others):
    return call(token_kernel, [((8, 128), F32)], others, [pl.ANY] * len(others), [], "token", 0, 0)[0]


def pack_kernel(a, b, *rest):
    out = rest[-1]
    out[0] = a[...]
    out[1] = b[...]


def pack(a, b, *others):
    return call(
        pack_kernel, [((2,) + a.shape, a.dtype)], (a, b) + others, [pltpu.VMEM] * 2 + [pl.ANY] * len(others), [],
        "pack", 0, 0,
    )[0]


def half_kernel(meta, t, *rest):
    out, sem = rest[-2:]
    copy = pltpu.make_async_copy(t.at[:, meta[CORE], 0:2], out, sem)
    copy.start()
    copy.wait()


def half_of(meta, t, *others):
    shape = (t.shape[0], 2) + t.shape[3:]
    return call(
        half_kernel, [(shape, t.dtype)], (meta, t) + others, [pltpu.SMEM] + [pl.ANY] * (1 + len(others)),
        [pltpu.SemaphoreType.DMA(())], "half", 0, 0,
    )[0]


def sums_kernel(*refs, layout, count, split):
    outs = refs[-len(layout) :]
    at = 0
    for out, parts in zip(outs, layout):
        lane = 0
        for n in parts:
            total = refs[at][...].astype(F32)
            for ref in refs[at + 1 : at + n]:
                total = total + ref[...].astype(F32)
            at += n
            if split:
                for k in range(len(outs)):
                    outs[k][...] = total[k].astype(BF)
            else:
                out[..., lane : lane + total.shape[-1]] = total.astype(BF)
            lane += total.shape[-1]
        if split:
            break


def sums(outputs, *others, split=0):
    args = tuple(x for groups in outputs for group in groups for x in group)
    layout = tuple(tuple(len(group) for group in groups) for groups in outputs)
    if split:
        shapes = [(args[0].shape[1:], BF)] * split
        layout = layout * split
    else:
        shapes = [
            (groups[0][0].shape[:-1] + (sum(group[0].shape[-1] for group in groups),), BF) for groups in outputs
        ]
    return call(
        functools.partial(sums_kernel, layout=layout, count=len(args), split=split),
        shapes, args + others, [pltpu.VMEM] * len(args) + [pl.ANY] * len(others), [], "sums", 0, 0,
    )


def merge_kernel(dwo, own, other, *rest):
    out = rest[-1]
    out[:, :, 0:WIDTH] = dwo[...]
    out[:, :, WIDTH:] = (own[...].astype(F32) + other[...].astype(F32)).astype(BF)


def vectors_of(shards, order):
    return jnp.concatenate([shards[f // 2, f % 2, :, 0:96] for f in order], axis=1).astype(F32)


NATURAL = tuple(range(8))
CORE_MAJOR = (0, 2, 4, 6, 1, 3, 5, 7)


def attn_fwd_kernel(
    meta, h0, h1, h2, h3, qrow, kcol, t, *rest, heads, tokens
):
    qkv, c0, c1, c2, c3, lse, q_s, k_s, vt_s, o_s, ctx, w_s, b_s, sems = rest[-14:]
    blocks = tokens // BLK
    hw = heads * HEAD_DIM
    copies = started_copies(
        sems, (t.at[:, :, 2, :, 0:VEC_AT], w_s), (t.at[:, :, 2, 0:16, VEC_AT : VEC_AT + 128], b_s)
    )
    for copy in copies:
        copy.wait()
    w = w_s[...].reshape(WIDTH, VEC_AT)[:, 0 : 3 * hw]
    vec = vectors_of(b_s, NATURAL)
    bias = jnp.zeros((1, 3 * hw), F32)
    for k in range(4):
        part = jnp.concatenate(
            [vec[6:7, k * hw : (k + 1) * hw], jnp.zeros((1, hw), F32), vec[7:8, k * hw : (k + 1) * hw]], axis=1
        )
        bias = jnp.where(meta[RANK] == k, part, bias)
    for j, piece in enumerate((h0, h1, h2, h3)):
        qkv[j] = (mm_nn(piece[...], w) + bias).astype(BF)
    for pair in range(blocks // 2):
        rows = []
        for block in (2 * pair, 2 * pair + 1):
            at, half = block_of(block, blocks)
            rows.append(qkv[meta[JMAP + at], half * BLK : (half + 1) * BLK, :])
        both = jnp.concatenate(rows, axis=0)
        lo, hi = 2 * pair * BLK, 2 * (pair + 1) * BLK
        for h in range(heads):
            q_s[h, lo:hi, :] = both[:, h * HEAD_DIM : (h + 1) * HEAD_DIM]
            k_s[h, lo:hi, :] = both[:, hw + h * HEAD_DIM : hw + (h + 1) * HEAD_DIM]
        vt_s[:, lo:hi] = both[:, 2 * hw :].T
    iota_k = lax.broadcasted_iota(jnp.int32, (QB, QB), 0)
    iota_q = lax.broadcasted_iota(jnp.int32, (QB, QB), 1)
    causal = iota_k <= iota_q
    for h in range(heads):
        for i in range(tokens // QB):
            lo = i * QB
            q = q_s[h, lo : lo + QB, :]
            starts_q = qrow[0:1, lo : lo + QB]

            def scores(at, diagonal):
                s = mm_nt(k_s[h, pl.ds(at, QB), :], q) * SCORE_SCALE
                col = kcol[pl.ds(at, QB), :]
                allowed = jnp.concatenate([col, col], axis=1) == starts_q
                if diagonal:
                    allowed = allowed & causal
                return jnp.where(allowed, s, NEG)

            s = scores(lo, True)
            top = jnp.max(s, axis=0, keepdims=True)
            p = jnp.exp2(s - top)
            total = jnp.sum(p, axis=0, keepdims=True)
            out = mm_nn(vt_s[h * HEAD_DIM : (h + 1) * HEAD_DIM, lo : lo + QB], p.astype(BF))

            def step(jb, carry):
                top, total, out = carry
                at = pl.multiple_of(jb * QB, QB)
                s = scores(at, False)
                new_top = jnp.maximum(top, jnp.max(s, axis=0, keepdims=True))
                p = jnp.exp2(s - new_top)
                alpha = jnp.exp2(top - new_top)
                total = total * alpha + jnp.sum(p, axis=0, keepdims=True)
                out = out * alpha + mm_nn(
                    vt_s[h * HEAD_DIM : (h + 1) * HEAD_DIM, pl.ds(at, QB)], p.astype(BF)
                )
                return (new_top, total, out)

            if i > 0:
                top, total, out = lax.fori_loop(meta[JMIN + i], i, step, (top, total, out))
            o_s[h * HEAD_DIM : (h + 1) * HEAD_DIM, lo : lo + QB] = out / total
            lse[h : h + 1, lo : lo + QB] = top + jnp.log2(total)
    for pair in range(blocks // 2):
        lo, hi = 2 * pair * BLK, 2 * (pair + 1) * BLK
        both = o_s[:, lo:hi].T.astype(BF)
        for n, block in enumerate((2 * pair, 2 * pair + 1)):
            at, half = block_of(block, blocks)
            ctx[meta[JMAP + at], :, half * hw : (half + 1) * hw] = both[n * BLK : (n + 1) * BLK, :]
    for j, out in enumerate((c0, c1, c2, c3)):
        out[...] = ctx[j]


def attn_bwd_kernel(
    meta, h0, h1, h2, h3, qrow, kcol, qkv, c0, c1, c2, c3, gctx, lse, t, *rest, heads, tokens
):
    (
        g_own, g_a, g_b, g_d, dw_own, dw_other, q_s, k_s, v_s, do_s, kt_s, delta_s, dk_s, dv_s, dqt_s, g_s, w_s, ctx, dw, sems,
    ) = rest[-20:]
    blocks = tokens // BLK
    hw = heads * HEAD_DIM
    scale = HEAD_DIM ** (-0.5)
    copies = started_copies(sems, (t.at[:, :, 2, :, 0:VEC_AT], w_s))
    for j, c in enumerate((c0, c1, c2, c3)):
        ctx[j] = c[...]
    for pair in range(blocks // 2):
        rows, grads, outs = [], [], []
        for block in (2 * pair, 2 * pair + 1):
            at, half = block_of(block, blocks)
            rows.append(qkv[meta[JMAP + at], half * BLK : (half + 1) * BLK, :])
            grads.append(gctx[meta[INV + at], :, half * hw : (half + 1) * hw])
            outs.append(ctx[meta[JMAP + at], :, half * hw : (half + 1) * hw])
        both = jnp.concatenate(rows, axis=0)
        grad = jnp.concatenate(grads, axis=0)
        out = jnp.concatenate(outs, axis=0)
        lo, hi = 2 * pair * BLK, 2 * (pair + 1) * BLK
        prod = (grad.astype(F32) * out.astype(F32)).T
        kt_s[:, lo:hi] = both[:, hw : 2 * hw].T
        for h in range(heads):
            c0, c1 = h * HEAD_DIM, (h + 1) * HEAD_DIM
            q_s[h, lo:hi, :] = both[:, c0:c1]
            k_s[h, lo:hi, :] = both[:, hw + c0 : hw + c1]
            v_s[h, lo:hi, :] = both[:, 2 * hw + c0 : 2 * hw + c1]
            do_s[h, lo:hi, :] = grad[:, c0:c1]
            delta_s[h : h + 1, lo:hi] = jnp.sum(prod[c0:c1, :], axis=0, keepdims=True)
    dk_s[...] = jnp.zeros_like(dk_s)
    dv_s[...] = jnp.zeros_like(dv_s)
    iota_k = lax.broadcasted_iota(jnp.int32, (QB, QB), 0)
    iota_q = lax.broadcasted_iota(jnp.int32, (QB, QB), 1)
    causal = iota_k <= iota_q
    for h in range(heads):
        for i in range(tokens // QB):
            lo = i * QB
            q = q_s[h, lo : lo + QB, :]
            do = do_s[h, lo : lo + QB, :]
            starts_q = qrow[0:1, lo : lo + QB]
            lse_q = lse[h : h + 1, lo : lo + QB]
            delta_q = delta_s[h : h + 1, lo : lo + QB]

            def block(at, diagonal):
                s = mm_nt(k_s[h, pl.ds(at, QB), :], q) * SCORE_SCALE
                col = kcol[pl.ds(at, QB), :]
                allowed = jnp.concatenate([col, col], axis=1) == starts_q
                if diagonal:
                    allowed = allowed & causal
                p = jnp.exp2(jnp.where(allowed, s, NEG) - lse_q)
                dp = mm_nt(v_s[h, pl.ds(at, QB), :], do)
                ds = (p * (dp - delta_q)).astype(BF)
                dv_s[h, pl.ds(at, QB), :] += mm_nn(p.astype(BF), do)
                dk_s[h, pl.ds(at, QB), :] += mm_nn(ds, q)
                return mm_nn(kt_s[h * HEAD_DIM : (h + 1) * HEAD_DIM, pl.ds(at, QB)], ds)

            dq = block(lo, True)
            if i > 0:
                dq = lax.fori_loop(
                    meta[JMIN + i], i, lambda jb, acc: acc + block(pl.multiple_of(jb * QB, QB), False), dq
                )
            dqt_s[h * HEAD_DIM : (h + 1) * HEAD_DIM, lo : lo + QB] = dq * scale
    for pair in range(blocks // 2):
        lo, hi = 2 * pair * BLK, 2 * (pair + 1) * BLK
        parts = [dqt_s[:, lo:hi].T.astype(BF)]
        parts += [(dk_s[h, lo:hi, :] * scale).astype(BF) for h in range(heads)]
        parts += [dv_s[h, lo:hi, :].astype(BF) for h in range(heads)]
        both = jnp.concatenate(parts, axis=1)
        for n, block_at in enumerate((2 * pair, 2 * pair + 1)):
            at, half = block_of(block_at, blocks)
            g_s[meta[JMAP + at], half * BLK : (half + 1) * BLK, :] = both[n * BLK : (n + 1) * BLK, :]
    for copy in copies:
        copy.wait()
    w = w_s[...].reshape(WIDTH, VEC_AT)[:, 0 : 3 * hw]
    total = None
    sums = None
    for j, piece in enumerate((h0, h1, h2, h3)):
        g = g_s[j]
        back = mm_nt(g, w)
        if j == 0:
            g_own[...] = back
        else:
            (g_a, g_b, g_d)[j - 1][...] = back.astype(BF)
        part = mm_tn(piece[...], g)
        col = jnp.sum(g.astype(F32), axis=0, keepdims=True)
        total = part if total is None else total + part
        sums = col if sums is None else sums + col
    shards, rows_out, cols = dw.shape
    rows = WIDTH // shards
    dw[:, 0:rows, :] = total.reshape(shards, rows, cols).astype(BF)
    dw[:, rows:, :] = jnp.broadcast_to(sums[None], (shards, rows_out - rows, cols)).astype(BF)
    for k in range(4):
        dw_own[k] = dw[2 * k + meta[CORE]]
        dw_other[k] = dw[2 * k + 1 - meta[CORE]]


def start_ffn_copies(core, t, a, b, d, crossed, e_s, r_s, sems):
    ca, cb = crossed.at[0], crossed.at[1]
    groups = []
    for p, parts in enumerate(((t,), (a, cb), (b, ca), (d,))):
        pairs = []
        if len(parts) == 1:
            pairs.append((parts[0].at[:, :, 0], e_s.at[p]))
            for h in range(2):
                pairs.append((parts[0].at[:, h, 1], r_s.at[p, h]))
        else:
            for src, parity in ((parts[0], core), (parts[1], 1 - core)):
                pairs.append((src.at[:, 0], e_s.at[p, :, parity]))
                pairs.append((src.at[:, 1], r_s.at[p, parity]))
        group = []
        for n, (src, dst) in enumerate(pairs):
            copy = pltpu.make_async_copy(src, dst, sems.at[p, n])
            copy.start()
            group.append(copy)
        groups.append(group)
    return groups


def ffn_scratch():
    return [
        pltpu.VMEM((4, 4, 2, 96, WIDTH), BF),
        pltpu.VMEM((4, 2, 4, 96, WIDTH), BF),
        pltpu.SemaphoreType.DMA((4, 4)),
        pltpu.VMEM((4, 2, 96, WIDTH), BF),
        pltpu.VMEM((4, 2, 16, 128), BF),
        pltpu.SemaphoreType.DMA((2,)),
    ]


def norm_parts(values):
    centre = values - jnp.mean(values, axis=-1, keepdims=True)
    spread = jnp.mean(centre * centre, axis=-1, keepdims=True)
    rstd = lax.rsqrt(spread + norm_eps)
    return centre * rstd, rstd


def shard_columns(x, parity):
    return jnp.concatenate([x[:, (2 * z + parity) * 96 : (2 * z + parity + 1) * 96] for z in range(4)], axis=1)


def mlp_fwd_kernel(
    meta, c0, c1, c2, c3, hid, t, a, b, d, crossed,
    xhat1, rstd1, gp, xhat2, rstd2, l_mine, l_other, hlow, *rest,
):
    hnext, (e_s, r_s, sems, wo_s, b_s, wo_sems, ctx, eb) = rest[:-8], rest[-8:]
    core = meta[CORE]
    wo_copies = started_copies(
        wo_sems, (d.at[:, :, 2], wo_s), (t.at[:, :, 2, 0:16, VEC_AT : VEC_AT + 128], b_s)
    )
    copies = start_ffn_copies(core, t, a, b, d, crossed, e_s, r_s, sems)
    half_cols = WIDTH // 2
    hw = c0.shape[1] // 2
    for p, piece in enumerate((c0, c1, c2, c3)):
        for half in range(2):
            ctx[meta[RANK + p], half * BLK : (half + 1) * BLK, :] = piece[:, half * hw : (half + 1) * hw]

    def keep(parts, at):
        for parity in range(2):

            @pl.when(core == parity)
            def _():
                l_mine[:, at : at + half_cols] = parts[parity]

            @pl.when(core != parity)
            def _():
                l_other[:, at : at + half_cols] = parts[parity]

    low = jnp.concatenate([ctx[rank] for rank in range(4)], axis=1)
    keep([shard_columns(low, parity) for parity in range(2)], half_cols)
    for copy in wo_copies:
        copy.wait()
    vec = vectors_of(b_s, NATURAL)
    eb[...] = vectors_of(b_s, CORE_MAJOR)[8:16, :]
    wo = wo_s[...].reshape(WIDTH, WIDTH)
    first_sum = hid[...].astype(F32) + (mm_nn(low, wo) + vec[0:1, :])
    x1, r1 = norm_parts(first_sum)
    xhat1[...] = x1
    rstd1[...] = r1
    normed = x1 * vec[1:2, :] + vec[2:3, :]
    lown = normed.astype(BF)
    keep([shard_columns(lown, parity) for parity in range(2)], 0)
    out = normed + vec[3:4, :]
    for p in range(4):
        for copy in copies[p]:
            copy.wait()
        bias = eb[pl.ds(meta[RANK + p], 1), :]
        u = mm_nn(lown, e_s[p].reshape(WIDTH, WIDTH)) + bias
        cdf = 0.5 * (1.0 + lax.erf(u * 0.7071067811865476))
        pdf = jnp.exp(-0.5 * u * u) * 0.3989422804014327
        low = (u * cdf).astype(BF)
        gp[:, p * WIDTH : (p + 1) * WIDTH] = (cdf + u * pdf).astype(BF)
        keep([low[:, :half_cols], low[:, half_cols:]], WIDTH + p * half_cols)
        out = out + mm_nn(low, r_s[p].reshape(WIDTH, WIDTH))
    x2, r2 = norm_parts(out)
    xhat2[...] = x2
    rstd2[...] = r2
    nxt = x2 * vec[4:5, :] + vec[5:6, :]
    hlow[...] = nxt.astype(BF)
    if hnext:
        hnext[0][...] = nxt


def norm_back(gy, gain, xhat, rstd):
    g = gy * gain
    return rstd * (g - jnp.mean(g, axis=-1, keepdims=True) - xhat * jnp.mean(g * xhat, axis=-1, keepdims=True))


def rows_sum(x):
    return jnp.sum(x, axis=0, keepdims=True)


def mlp_bwd_kernel(
    meta, xhat1, rstd1, xhat2, rstd2, gp, *rest, parts
):
    t, a, b, d, crossed = rest[parts : parts + 5]
    gfs, dgg, gctx, e_s, r_s, sems, wo_s, b_s, wo_sems, eb_s = rest[-10:]
    rows = gfs.shape[0]
    core = meta[CORE]
    copies = start_ffn_copies(core, t, a, b, d, crossed, e_s, r_s, sems)
    wo_copies = started_copies(
        wo_sems, (d.at[:, :, 2], wo_s), (t.at[:, :, 2, 0:16, VEC_AT : VEC_AT + 128], b_s)
    )
    grad = rest[0][...].astype(F32)
    for ref in rest[1:parts]:
        grad = grad + ref[...].astype(F32)
    x2 = xhat2[...]
    for copy in wo_copies:
        copy.wait()
    vec = vectors_of(b_s, NATURAL)
    gss = norm_back(grad, vec[4:5, :], x2, rstd2[...])
    low = gss.astype(BF)
    dgg[0:rows, 4 * WIDTH : 5 * WIDTH] = low
    sums = [None] * 8
    sums[4] = rows_sum(grad * x2)
    sums[5] = rows_sum(grad)
    sums[3] = rows_sum(low.astype(F32))
    gn = gss
    eb_s[...] = jnp.zeros_like(eb_s)
    for p in range(4):
        for copy in copies[p]:
            copy.wait()
        ga = mm_nt(low, r_s[p].reshape(WIDTH, WIDTH))
        dip = (ga * gp[:, p * WIDTH : (p + 1) * WIDTH].astype(F32)).astype(BF)
        dgg[0:rows, p * WIDTH : (p + 1) * WIDTH] = dip
        eb_s[pl.ds(meta[RANK + p], 1), :] = rows_sum(dip.astype(F32))
        gn = gn + mm_nt(dip, e_s[p].reshape(WIDTH, WIDTH))
    x1 = xhat1[...]
    gf = norm_back(gn, vec[1:2, :], x1, rstd1[...])
    sums[1] = rows_sum(gn * x1)
    sums[2] = rows_sum(gn)
    gfs[...] = gf
    lowa = gf.astype(BF)
    dgg[0:rows, 5 * WIDTH :] = lowa
    sums[0] = rows_sum(lowa.astype(F32))
    sums[6] = jnp.zeros_like(sums[0])
    sums[7] = sums[6]
    gc = mm_nt(lowa, wo_s[...].reshape(WIDTH, WIDTH)).astype(BF)
    hw = gctx.shape[2] // 2
    for rank in range(4):
        for half in range(2):
            gctx[rank, :, half * hw : (half + 1) * hw] = gc[half * BLK : (half + 1) * BLK, rank * hw : (rank + 1) * hw]
    vecs = jnp.concatenate(sums, axis=0)
    ebs = jnp.concatenate([eb_s[:, (4 * (f % 2) + f // 2) * 96 : (4 * (f % 2) + f // 2 + 1) * 96] for f in range(8)], axis=1)
    dgg[rows:, 0:WIDTH] = jnp.concatenate([vecs, ebs], axis=0).astype(BF)
    dgg[rows:, WIDTH:] = jnp.zeros((16, 5 * WIDTH), BF)


def wgrad_kernel(
    meta, l_mine, l_other, dgg, dgg_other, *rest, by_z
):
    t, a, b, dwo = rest[-9:-5] if by_z else rest[-5:-1]
    d = rest[-1]
    half = WIDTH // 2
    rows = l_mine.shape[0]

    def grad(at, at_other, right, right_other):
        return mm_tn(l_mine[:, at : at + half], dgg[0:rows, right : right + WIDTH]) + mm_tn(
            l_other[:, at_other : at_other + half], dgg_other[0:rows, right_other : right_other + WIDTH]
        )

    for p, out in ((3, d), (1, a), (2, b), (0, t)):
        q = SWAPPED[p]
        out[:, 0] = grad(0, 0, p * WIDTH, q * WIDTH).reshape(4, 96, WIDTH).astype(BF)
        at, at_other = WIDTH + p * half, WIDTH + q * half
        out[:, 1] = grad(at, at_other, 4 * WIDTH, 4 * WIDTH).reshape(4, 96, WIDTH).astype(BF)
    dwo[:, 0:96, :] = grad(half, half, 5 * WIDTH, 5 * WIDTH).reshape(4, 96, WIDTH).astype(BF)
    vecs = dgg[rows:, 0:WIDTH].astype(F32) + dgg_other[rows:, 0:WIDTH].astype(F32)
    dwo[:, 96:, :] = jnp.zeros((4, 16, WIDTH), BF)
    for parity in range(2):

        @pl.when(meta[CORE] == parity)
        def _():
            for z in range(4):
                dwo[z, 96:, 0:96] = vecs[:, (2 * z + parity) * 96 : (2 * z + parity + 1) * 96].astype(BF)

    for k in range(4 if by_z else 0):
        rest[-5 + k][...] = d[lax.shift_right_logical(meta[SHARD], 1) ^ k]


def place_kernel(
    meta, ffn0, ffn1, ffn2, ffn3, att0, att1, att2, att3, *rest, layer, last
):
    if last:
        small_in, rest = rest[0], rest[5:]
    else:
        rest = rest[1:]
    e_hbm, r_hbm, i_hbm, o_hbm = rest[:4]
    smalls = rest[4:-10]
    e_s, i_s, b_s, e_out, r_out, i_out, o_out, small_s, eb_s, sems = rest[-10:]
    for p, (ffn, att) in enumerate(((ffn0, att0), (ffn1, att1), (ffn2, att2), (ffn3, att3))):
        rank = meta[RANK + p]
        r_out[pl.ds(pl.multiple_of(rank * 96, 96), 96), :] = ffn[1].astype(F32)
        e_s[rank] = ffn[0].astype(F32)
        i_s[rank] = att[0:96, WIDTH:].astype(F32)
        b_s[rank] = att[96:112, WIDTH:].astype(F32)
    copies = []

    def send(n, src, dst):
        copy = pltpu.make_async_copy(src, dst.at[layer], sems.at[n])
        copy.start()
        copies.append(copy)

    send(0, r_out, r_hbm)
    for f in range(8):
        at = (4 * (f % 2) + f // 2) * 96
        e_out[:, f * 384 : (f + 1) * 384] = jnp.concatenate([e_s[c, :, at : at + 96] for c in range(4)], axis=1)
    send(1, e_out, e_hbm)
    hw = WIDTH // 4
    for k in range(3):
        i_out[:, k * WIDTH : (k + 1) * WIDTH] = jnp.concatenate(
            [i_s[c, :, k * hw : (k + 1) * hw] for c in range(4)], axis=1
        )
    send(2, i_out, i_hbm)
    wo = [att[:, 0:WIDTH].astype(F32) for att in (att0, att1, att2, att3)]
    total = (wo[0] + wo[1]) + (wo[2] + wo[3])
    o_out[...] = total[0:96, :]
    send(3, o_out, o_hbm)
    bias = b_s[lax.shift_right_logical(meta[SHARD], 1)]
    low_half = (meta[SHARD] & 1) == 0
    qb = jnp.where(low_half, bias[:, 0:96], bias[:, 96:192])
    vb = jnp.where(low_half, bias[:, 2 * hw : 2 * hw + 96], bias[:, 2 * hw + 96 : 3 * hw])
    rows = jnp.concatenate([total[96:102, 0:96], qb[0:1], vb[0:1], total[104:112, 0:96]], axis=0)
    if last:
        for n, ref in enumerate(smalls[:-1]):
            ref[...] = jnp.concatenate([rows[n : n + 1], small_in[n : n + 1, 0:96]], axis=0)
        smalls[-1][...] = jnp.concatenate(
            [
                jnp.concatenate([x[8 + c : 9 + c, 0:96] for c in range(4)], axis=1)
                for x in (rows, small_in[...])
            ],
            axis=0,
        )
    else:
        smalls[0][...] = rows
    for copy in copies:
        copy.wait()


def permutation(ctx, fsdp, move):
    return [
        (c * fsdp + f, move(c, f)[0] * fsdp + move(c, f)[1]) for c in range(ctx) for f in range(fsdp)
    ]


def add(*parts):
    total = parts[0].astype(F32)
    for part in parts[1:]:
        total = total + part.astype(F32)
    return total


def on_device_fast(
    activations, cotangent, doc_start, deal,
    attend_in, query_bias, value_bias, attend_out, attend_bias, first_gain, first_shift,
    expand_proj, expand_bias, reduce_proj, reduce_bias, second_gain, second_shift,
    *, ctx, fsdp,
):
    S = [pltpu.SMEM]
    V = [pltpu.VMEM]
    A = [pl.ANY]
    axes = ("ctx", "fsdp")

    def via(move):
        perm = permutation(ctx, fsdp, move)
        return lambda x: lax.ppermute(x, axes, perm)

    via_first = via(lambda c, f: (c ^ (1 + f % 2), f))
    via_second = via(lambda c, f: (c ^ (2 - f % 2), f))
    via_diagonal = via(lambda c, f: (c ^ 3, f))
    via_core = via(lambda c, f: (c, f ^ 1))
    via_z = [None] + [via(lambda c, f, k=k: (c, f ^ (2 * k))) for k in range(1, 4)]

    def exchange_ctx(own, a, b, d):
        return (own, via_first(a), via_second(b), via_diagonal(d))

    def spread_ctx(x):
        return (x, via_first(x), via_second(x), via_diagonal(x))

    def reduce_z(x):
        return lax.psum_scatter(x, "fsdp", scatter_dimension=0, tiled=True, axis_index_groups=zgroups)

    def exchange_z(own, *others):
        return (own,) + tuple(via_z[k + 1](x) for k, x in enumerate(others))

    def gather_ctx(x):
        a, b = via_first(x), via_second(x)
        return (x, a, b, via_second(a))

    heads = HEADS // ctx
    hw = heads * HEAD_DIM
    rows = activations.shape[1]
    tokens = rows * ctx
    cut = WIDTH // fsdp
    c = lax.axis_index("ctx").astype(jnp.int32)
    shard = lax.axis_index("fsdp").astype(jnp.int32)
    core = shard % 2
    zgroups = [[2 * z + k for z in range(fsdp // 2)] for k in range(2)]

    hidden = activations[0]
    gathered = gather_ctx(hidden)
    small = (attend_bias, first_gain, first_shift, reduce_bias, second_gain, second_shift, query_bias, value_bias)
    sent = call(
        prep_kernel,
        [((3 * cut, WIDTH), BF)] * 4,
        (expand_proj, reduce_proj, attend_in, attend_out, expand_bias) + small,
        V * 13,
        [],
        "prep",
        0,
        8 * 1024 * 1024,
    )

    def gather_ffn(x):
        x = lax.all_gather(x, "fsdp", axis=0, tiled=True)
        return x.reshape(fsdp // 2, 2, 3, cut, WIDTH)

    ranks = jnp.arange(ctx, dtype=jnp.int32)
    inv = jnp.sum(jnp.where(deal[None, :] == ranks[:, None], ranks[None, :], 0), axis=1).astype(jnp.int32)
    starts = lax.all_gather(doc_start[0], "ctx", axis=0, tiled=True)
    by_rank = starts.reshape(ctx, 2, BLK)
    chosen = inv[:, None, None, None] == ranks[None, :, None, None]
    by_block = jnp.sum(jnp.where(chosen, by_rank[None], 0), axis=1)
    logical = jnp.concatenate([by_block[:, 0], by_block[::-1, 1]], axis=0).reshape(-1)
    qrow = jnp.broadcast_to(logical[None, :], (8, tokens))
    kcol = jnp.broadcast_to(logical[:, None], (tokens, 128))
    jmin = jnp.min(logical.reshape(tokens // QB, QB), axis=1) // QB

    m1 = 1 + core
    mask = inv ^ c
    jmap = jnp.where((core == 1) & (mask > 0) & (mask < 3), 3 - mask, mask)
    meta = jnp.concatenate(
        [jnp.stack([core, shard, c, c ^ m1, c ^ (3 - m1), c ^ 3]), jmap, inv, jmin]
    ).astype(jnp.int32)

    kept = []
    earlier = ()
    wide = [gather_ffn(sent[0]), gather_ffn(sent[1]), None, None]
    wide[0] = after((wide[0],), starts, *gathered[1:])[0]
    wide[2] = gather_ffn(*after(sent[2:3], wide[0]))
    pieces = []
    for layer in range(LAYERS):
        t, d = wide[2 * layer : 2 * layer + 2]
        mine = half_of(meta, t, *gathered[1:])
        a, b = via_first(mine), via_second(mine)
        qkv, *ctx_own, lse = call(
            functools.partial(attn_fwd_kernel, heads=heads, tokens=tokens),
            [((ctx, rows, 3 * hw), BF)] + [((BLK, 2 * hw), BF)] * 4 + [((8, tokens), F32)],
            (meta,) + gathered + (qrow, kcol, t, mine) + earlier,
            S + V * 6 + A * (2 + len(earlier)),
            [
                pltpu.VMEM((heads, tokens, HEAD_DIM), BF),
                pltpu.VMEM((heads, tokens, HEAD_DIM), BF),
                pltpu.VMEM((hw, tokens), BF),
                pltpu.VMEM((hw, tokens), F32),
                pltpu.VMEM((ctx, BLK, 2 * hw), BF),
                pltpu.VMEM((fsdp // 2, 2, cut, VEC_AT), BF),
                pltpu.VMEM((fsdp // 2, 2, 16, 128), BF),
                pltpu.SemaphoreType.DMA((2,)),
            ],
            "attn_fwd",
            2 * tokens * WIDTH * 3 * hw * 4,
            10 * 1024 * 1024,
        )
        cx = exchange_ctx(*ctx_own)
        if layer + 1 < LAYERS:
            wide[3] = gather_ffn(*after(sent[3:4], *cx[1:]))
        pieces.append((t, a, b, d, via_core(pack(a, b, lse))))
        outs = [
            ((rows, WIDTH), F32), ((rows, 1), F32), ((rows, 4 * WIDTH), BF), ((rows, WIDTH), F32), ((rows, 1), F32),
            ((rows, 3 * WIDTH), BF), ((rows, 3 * WIDTH), BF), ((rows, WIDTH), BF),
        ]
        if layer + 1 < LAYERS:
            outs.append(((rows, WIDTH), F32))
        xhat1, rstd1, gp, xhat2, rstd2, l_mine, l_other, hlow, *more = call(
            mlp_fwd_kernel,
            outs,
            (meta,) + cx + (hidden,) + pieces[layer],
            S + V * 5 + A * 5,
            ffn_scratch() + [pltpu.VMEM((ctx, rows, hw), BF), pltpu.VMEM((8, WIDTH), F32)],
            "mlp_fwd",
            2 * rows * WIDTH * WIDTH * 9,
            20 * 1024 * 1024,
        )
        l_other = via_core(l_other)
        earlier = (l_other,)
        kept.append((gathered, qkv, ctx_own, lse, xhat1, rstd1, gp, xhat2, rstd2, l_mine, l_other))
        if more:
            hidden = more[0]
            gathered = gather_ctx(hlow)
    out_act = hlow[None]

    grads = (cotangent[0],)
    order = ()
    for layer in reversed(range(LAYERS)):
        gathered, qkv, ctx_own, lse, xhat1, rstd1, gp, xhat2, rstd2, l_mine, l_other = kept[layer]
        gfs, dgg, gctx = call(
            functools.partial(mlp_bwd_kernel, parts=len(grads)),
            [
                ((rows, WIDTH), F32), ((rows + 16, 6 * WIDTH), BF), ((ctx, BLK, 2 * hw), BF),
            ],
            (meta, xhat1, rstd1, xhat2, rstd2, gp) + grads + pieces[layer] + order,
            S + V * (5 + len(grads)) + A * (5 + len(order)),
            ffn_scratch() + [pltpu.VMEM((8, WIDTH), F32)],
            "mlp_bwd",
            2 * rows * WIDTH * WIDTH * 9,
            20 * 1024 * 1024,
        )
        gcx = lax.all_to_all(gctx, "ctx", 0, 0, tiled=True)
        piece = ((4, 2, cut, WIDTH), BF)

        def weight_grads(by_z, *before):
            outs = [piece] * 3 + [((4, cut + 16, WIDTH), BF)]
            return call(
                functools.partial(wgrad_kernel, by_z=by_z),
                outs + ([((2, cut, WIDTH), BF)] * 4 if by_z else [piece]),
                (meta, l_mine, l_other, dgg, via_core(dgg)) + before,
                S + V * 4 + A * len(before),
                [pltpu.VMEM(*piece)] if by_z else [],
                "wgrad",
                2 * rows * WIDTH * WIDTH * 9,
                20 * 1024 * 1024,
            )

        def attention_grads(*before):
            return call(
                functools.partial(attn_bwd_kernel, heads=heads, tokens=tokens),
                [
                    ((rows, WIDTH), F32), ((rows, WIDTH), BF), ((rows, WIDTH), BF), ((rows, WIDTH), BF),
                    ((4, cut + 16, 3 * hw), BF), ((4, cut + 16, 3 * hw), BF),
                ],
                (meta,) + gathered + (qrow, kcol, qkv) + tuple(ctx_own) + (gcx, lse, wide[2 * layer]) + before,
                S + V * 13 + A * (1 + len(before)),
                [pltpu.VMEM((heads, tokens, HEAD_DIM), BF)] * 4
                + [
                    pltpu.VMEM((hw, tokens), BF),
                    pltpu.VMEM((8, tokens), F32),
                    pltpu.VMEM((heads, tokens, HEAD_DIM), F32),
                    pltpu.VMEM((heads, tokens, HEAD_DIM), F32),
                    pltpu.VMEM((hw, tokens), F32),
                    pltpu.VMEM((ctx, rows, 3 * hw), BF),
                    pltpu.VMEM((fsdp // 2, 2, cut, VEC_AT), BF),
                    pltpu.VMEM((ctx, BLK, 2 * hw), BF),
                    pltpu.VMEM((fsdp, cut + 16, 3 * hw), BF),
                    pltpu.SemaphoreType.DMA((1,)),
                ],
                "attn_bwd",
                2 * tokens * WIDTH * 3 * hw * 8,
                10 * 1024 * 1024,
            )

        def attention_shards(dwo, dw, crossed, *others):
            shape = (4, cut + 16, WIDTH + 3 * hw)
            (merged,) = call(
                merge_kernel, [(shape, BF)], (dwo, dw, crossed) + others, V * 3 + A * len(others), [], "merge", 0, 0
            )
            return merged, reduce_z(merged).reshape(shape[1:])

        if layer > 0:
            g_own, g_a, g_b, g_d, dw, dw_other = attention_grads(l_other)
            t, a, b, dwo, d = weight_grads(False, g_d)
            d1 = reduce_z(d)
            over = via_first(sums([[(g_a, via_second(g_d))]])[0])
            merged, att1 = attention_shards(dwo, dw, via_core(dw_other))
            grads = (gfs, g_own, via_second(g_b), over)
            (t1,) = sums([[(t, via_first(a), via_second(b))]])
            order = (t1, merged)
            t1 = reduce_z(t1)
        else:
            t, a, b, dwo, d = weight_grads(False, gcx)
            a, b = via_first(a), via_second(b)
            d0 = reduce_z(d)
            g_own, g_a, g_b, g_d, dw, dw_other = attention_grads(t)

    def shards(x):
        return x.reshape(2, cut, WIDTH)

    (t0,) = sums([[(t, a, b)]], g_d)
    merged, att0 = attention_shards(dwo, dw, via_core(dw_other), t0)
    t0 = reduce_z(t0)
    back = via_second(g_d), via_second(g_b)
    (ffn1,) = sums([[(shards(t1), shards(via_diagonal(d1)))]], merged)
    ffn1 = spread_ctx(ffn1)
    att1 = spread_ctx(att1)
    (over,) = sums([[(g_a, back[0])]], ffn1[0])
    over = via_first(over)

    finals = [None, (ffn1, att1)]
    small_out = None
    placed = []
    for layer in reversed(range(LAYERS)):
        if layer == 0:
            (ffn0,) = sums([[(shards(t0), shards(via_diagonal(d0)))]], small_out)
            finals[0] = (spread_ctx(ffn0), spread_ctx(att0))
        ffn, att = finals[layer]
        waits = (over,) if layer > 0 else ()
        last = layer == 0
        big = [
            ((LAYERS, cut, 4 * WIDTH), F32), ((LAYERS, 4 * cut, WIDTH), F32),
            ((LAYERS, cut, 3 * WIDTH), F32), ((LAYERS, cut, WIDTH), F32),
        ]
        if last:
            smalls = [((LAYERS, cut), F32)] * 8 + [((LAYERS, 4 * cut), F32)]
        else:
            smalls = [((16, cut), F32)]
        args = (meta,) + ffn + att + ((small_out,) + tuple(placed) if last else waits)
        spaces = S + V * 8 + (V + A * 4 if last else A)
        outs = pl.pallas_call(
            functools.partial(place_kernel, layer=layer, last=last),
            out_shape=[jax.ShapeDtypeStruct(shape, dtype) for shape, dtype in big + smalls],
            in_specs=[pl.BlockSpec(memory_space=space) for space in spaces],
            out_specs=[pl.BlockSpec(memory_space=space) for space in A * 4 + V * len(smalls)],
            scratch_shapes=[
                pltpu.VMEM((ctx, cut, WIDTH), F32), pltpu.VMEM((ctx, cut, 3 * hw), F32),
                pltpu.VMEM((ctx, 16, 3 * hw), F32),
                pltpu.VMEM((cut, 4 * WIDTH), F32), pltpu.VMEM((4 * cut, WIDTH), F32),
                pltpu.VMEM((cut, 3 * WIDTH), F32), pltpu.VMEM((cut, WIDTH), F32),
                pltpu.VMEM((16, 128), F32), pltpu.VMEM((8, 128), F32),
                pltpu.SemaphoreType.DMA((4,)),
            ],
            input_output_aliases={10 + n: n for n in range(4)} if last else {},
            compiler_params=pltpu.CompilerParams(vmem_limit_bytes=VMEM_LIMIT),
            cost_estimate=pl.CostEstimate(flops=0, bytes_accessed=10 * 1024 * 1024, transcendentals=0),
            name="place",
        )(*args)
        placed = outs[:4]
        small_out = outs[4]
        vectors = outs[4:]
    in_grad = add(gfs, g_own, back[1], over)[None]
    e_out, r_out, i_out, o_out = placed
    ab, fg, fs, rb, sg, ss, qb, vb, xb = vectors
    return (out_act, in_grad, i_out, qb, vb, o_out, ab, fg, fs, e_out, xb, r_out, rb, sg, ss)


def on_device(*args, ctx, fsdp):
    if ctx == 4 and fsdp == 8 and args[0].shape[1] == 2 * BLK:
        return on_device_fast(*args, ctx=ctx, fsdp=fsdp)
    return on_device_plain(*args)


def solution(mesh):
    placed = (
        P("fsdp", "ctx", None),
        P("fsdp", "ctx", None),
        P("fsdp", "ctx"),
        P(),
        P(None, "fsdp", None),
        P(None, "fsdp"),
        P(None, "fsdp"),
        P(None, "fsdp", None),
        P(None, "fsdp"),
        P(None, "fsdp"),
        P(None, "fsdp"),
        P(None, "fsdp", None),
        P(None, "fsdp"),
        P(None, "fsdp", None),
        P(None, "fsdp"),
        P(None, "fsdp"),
        P(None, "fsdp"),
    )
    return jax.shard_map(
        functools.partial(on_device, ctx=mesh.shape["ctx"], fsdp=mesh.shape["fsdp"]),
        mesh=mesh,
        in_specs=placed,
        out_specs=(
            P("fsdp", "ctx", None),
            P("fsdp", "ctx", None),
            P(None, "fsdp", None),
            P(None, "fsdp"),
            P(None, "fsdp"),
            P(None, "fsdp", None),
            P(None, "fsdp"),
            P(None, "fsdp"),
            P(None, "fsdp"),
            P(None, "fsdp", None),
            P(None, "fsdp"),
            P(None, "fsdp", None),
            P(None, "fsdp"),
            P(None, "fsdp"),
            P(None, "fsdp"),
        ),
        check_vma=False,
    )
```

```python
import functools

import jax
import jax.numpy as jnp
from jax import lax
from jax.experimental import pallas as pl
from jax.experimental.pallas import tpu as pltpu
from jax.sharding import PartitionSpec as P

HEADS = 12
HEAD_DIM = 64
LAYERS = 2
BLK = 192


norm_eps = 1e-05


def for_sending(x):
    return jax.tree.map(lambda a: a.astype(jnp.bfloat16) if a.dtype == jnp.float32 else a, x)


def layer_norm(values, gain, shift):
    centre = values - jnp.mean(values, axis=-1, keepdims=True)
    spread = jnp.mean(centre * centre, axis=-1, keepdims=True)
    return centre * lax.rsqrt(spread + norm_eps) * gain + shift


def gelu_exact(inputs):
    return 0.5 * inputs * (1.0 + jax.scipy.special.erf(inputs * 0.7071067811865476))


def key_positions(deal):
    pairs = deal.shape[0]
    offsets = jnp.arange(BLK, dtype=jnp.int32)
    first = deal[:, None] * BLK + offsets[None, :]
    second = (2 * pairs - 1 - deal)[:, None] * BLK + offsets[None, :]
    return jnp.concatenate([first, second], axis=1).reshape(-1)


def split_heads(matrix):
    return matrix.reshape(matrix.shape[0], HEADS, HEAD_DIM).transpose(1, 0, 2)


def join_heads(stacked):
    return stacked.transpose(1, 0, 2).reshape(stacked.shape[1], HEADS * HEAD_DIM)


def attend_forward(queries, keys_full, values_full, allowed):

    def one_head(items):
        head_q, head_k, head_v = items
        scores = jnp.einsum(
            "qd,kd->qk", head_q, head_k, preferred_element_type=jnp.float32
        ) * HEAD_DIM ** (-0.5)
        scores = jnp.where(allowed, scores, -1e30)
        top = jnp.max(scores, axis=-1, keepdims=True)
        weights = jnp.exp(scores - top)
        total = jnp.sum(weights, axis=-1, keepdims=True)
        probs = (weights / total).astype(jnp.bfloat16)
        output = jnp.einsum("qk,kd->qd", probs, head_v, preferred_element_type=jnp.float32)
        return (output, top[:, 0] + jnp.log(total[:, 0]))

    outputs, log_totals = lax.map(
        one_head, (split_heads(queries), split_heads(keys_full), split_heads(values_full))
    )
    return (join_heads(outputs), log_totals)


def attend_backward(queries, keys_full, values_full, log_totals, grad_context, allowed):

    def one_head(items):
        head_q, head_k, head_v, head_lse, head_grad = items
        scores = jnp.einsum(
            "qd,kd->qk", head_q, head_k, preferred_element_type=jnp.float32
        ) * HEAD_DIM ** (-0.5)
        scores = jnp.where(allowed, scores, -1e30)
        probs = jnp.exp(scores - head_lse[:, None])
        grad_probs = jnp.einsum("qd,kd->qk", head_grad, head_v, preferred_element_type=jnp.float32)
        inner_sum = jnp.sum(probs * grad_probs, axis=-1, keepdims=True)
        grad_scores = (probs * (grad_probs - inner_sum)).astype(jnp.bfloat16)
        grad_q = jnp.einsum(
            "qk,kd->qd", grad_scores, head_k, preferred_element_type=jnp.float32
        ) * HEAD_DIM ** (-0.5)
        grad_k = jnp.einsum(
            "qk,qd->kd", grad_scores, head_q, preferred_element_type=jnp.float32
        ) * HEAD_DIM ** (-0.5)
        grad_v = jnp.einsum(
            "qk,qd->kd", probs.astype(jnp.bfloat16), head_grad, preferred_element_type=jnp.float32
        )
        return (grad_q, grad_k, grad_v)

    grads = lax.map(
        one_head,
        (
            split_heads(queries),
            split_heads(keys_full),
            split_heads(values_full),
            log_totals,
            split_heads(grad_context),
        ),
    )
    return (join_heads(grads[0]), join_heads(grads[1]), join_heads(grads[2]))


def forward_layer(hidden, weights, allowed):
    (
        attend_in,
        query_bias,
        value_bias,
        attend_out,
        attend_bias,
        first_gain,
        first_shift,
        expand_proj,
        expand_bias,
        reduce_proj,
        reduce_bias,
        second_gain,
        second_shift,
    ) = weights
    width = hidden.shape[1]
    low_hidden = hidden.astype(jnp.bfloat16)
    projected = jnp.dot(low_hidden, attend_in, preferred_element_type=jnp.float32)
    queries = (projected[:, :width] + query_bias.astype(jnp.float32)).astype(jnp.bfloat16)
    keys_own = projected[:, width : 2 * width].astype(jnp.bfloat16)
    values_own = (projected[:, 2 * width :] + value_bias.astype(jnp.float32)).astype(jnp.bfloat16)
    keys_full, values_full = (
        lax.all_gather(keys_own, "ctx", axis=0, tiled=True),
        lax.all_gather(values_own, "ctx", axis=0, tiled=True),
    )
    context, log_totals = attend_forward(queries, keys_full, values_full, allowed)
    low_context = context.astype(jnp.bfloat16)
    branch = jnp.dot(
        low_context, attend_out, preferred_element_type=jnp.float32
    ) + attend_bias.astype(jnp.float32)
    first_sum = hidden + branch
    normed = layer_norm(first_sum, first_gain.astype(jnp.float32), first_shift.astype(jnp.float32))
    low_normed = normed.astype(jnp.bfloat16)
    inner_pre = jnp.dot(
        low_normed, expand_proj, preferred_element_type=jnp.float32
    ) + expand_bias.astype(jnp.float32)
    active = gelu_exact(inner_pre).astype(jnp.bfloat16)
    output_branch = jnp.dot(
        active, reduce_proj, preferred_element_type=jnp.float32
    ) + reduce_bias.astype(jnp.float32)
    second_sum = normed + output_branch
    output = layer_norm(
        second_sum, second_gain.astype(jnp.float32), second_shift.astype(jnp.float32)
    )
    saved = (
        low_hidden,
        queries,
        keys_full,
        values_full,
        log_totals,
        low_context,
        first_sum,
        low_normed,
        inner_pre,
        active,
        second_sum,
    )
    return (output, saved)


def column_sum(matrix):
    return jnp.sum(matrix.astype(jnp.float32), axis=0)


def backward_layer(grad_hidden, weights, saved, allowed):
    (
        attend_in,
        query_bias,
        value_bias,
        attend_out,
        attend_bias,
        first_gain,
        first_shift,
        expand_proj,
        expand_bias,
        reduce_proj,
        reduce_bias,
        second_gain,
        second_shift,
    ) = weights
    (
        low_hidden,
        queries,
        keys_full,
        values_full,
        log_totals,
        low_context,
        first_sum,
        low_normed,
        inner_pre,
        active,
        second_sum,
    ) = saved
    width = low_hidden.shape[1]
    second_pull = jax.vjp(
        layer_norm, second_sum, second_gain.astype(jnp.float32), second_shift.astype(jnp.float32)
    )[1]
    grad_second_sum, grad_second_gain, grad_second_shift = second_pull(grad_hidden)
    grad_branch = grad_second_sum.astype(jnp.bfloat16)
    grad_reduce_bias = column_sum(grad_branch)
    grad_reduce = jnp.einsum("tf,td->fd", active, grad_branch, preferred_element_type=jnp.float32)
    grad_active = jnp.einsum(
        "td,fd->tf", grad_branch, reduce_proj, preferred_element_type=jnp.float32
    )
    gelu_pull = jax.vjp(gelu_exact, inner_pre)[1]
    grad_inner = gelu_pull(grad_active)[0].astype(jnp.bfloat16)
    grad_expand_bias = column_sum(grad_inner)
    grad_expand = jnp.einsum(
        "td,tf->df", low_normed, grad_inner, preferred_element_type=jnp.float32
    )
    grad_normed = grad_second_sum + jnp.einsum(
        "tf,df->td", grad_inner, expand_proj, preferred_element_type=jnp.float32
    )
    first_pull = jax.vjp(
        layer_norm, first_sum, first_gain.astype(jnp.float32), first_shift.astype(jnp.float32)
    )[1]
    grad_first_sum, grad_first_gain, grad_first_shift = first_pull(grad_normed)
    grad_attn = grad_first_sum.astype(jnp.bfloat16)
    grad_attend_bias = column_sum(grad_attn)
    grad_attend_out = jnp.einsum(
        "td,te->de", low_context, grad_attn, preferred_element_type=jnp.float32
    )
    grad_context = jnp.einsum(
        "te,de->td", grad_attn, attend_out, preferred_element_type=jnp.float32
    ).astype(jnp.bfloat16)
    grad_queries, grad_keys_full, grad_values_full = attend_backward(
        queries, keys_full, values_full, log_totals, grad_context, allowed
    )
    grad_keys, grad_values = (
        lax.psum_scatter(
            grad_keys_full.astype(jnp.bfloat16), "ctx", scatter_dimension=0, tiled=True
        ).astype(jnp.float32),
        lax.psum_scatter(
            grad_values_full.astype(jnp.bfloat16), "ctx", scatter_dimension=0, tiled=True
        ).astype(jnp.float32),
    )
    grad_proj = jnp.concatenate(
        [
            grad_queries.astype(jnp.bfloat16),
            grad_keys.astype(jnp.bfloat16),
            grad_values.astype(jnp.bfloat16),
        ],
        axis=1,
    )
    grad_query_bias = column_sum(grad_proj[:, :width])
    grad_value_bias = column_sum(grad_proj[:, 2 * width :])
    grad_attend_in = jnp.einsum(
        "td,te->de", low_hidden, grad_proj, preferred_element_type=jnp.float32
    )
    grad_input = grad_first_sum + jnp.einsum(
        "te,de->td", grad_proj, attend_in, preferred_element_type=jnp.float32
    )
    grads = (
        grad_attend_in,
        grad_query_bias,
        grad_value_bias,
        grad_attend_out,
        grad_attend_bias,
        grad_first_gain,
        grad_first_shift,
        grad_expand,
        grad_expand_bias,
        grad_reduce,
        grad_reduce_bias,
        grad_second_gain,
        grad_second_shift,
    )
    return (grad_input, grads)


def reduce_grads(grads):
    shards = (
        lax.psum_scatter(
            grads[0].astype(jnp.bfloat16), "fsdp", scatter_dimension=0, tiled=True
        ).astype(jnp.float32),
        lax.psum_scatter(
            grads[1].astype(jnp.bfloat16), "fsdp", scatter_dimension=0, tiled=True
        ).astype(jnp.float32),
        lax.psum_scatter(
            grads[2].astype(jnp.bfloat16), "fsdp", scatter_dimension=0, tiled=True
        ).astype(jnp.float32),
        lax.psum_scatter(
            grads[3].astype(jnp.bfloat16), "fsdp", scatter_dimension=0, tiled=True
        ).astype(jnp.float32),
        lax.psum_scatter(
            grads[4].astype(jnp.bfloat16), "fsdp", scatter_dimension=0, tiled=True
        ).astype(jnp.float32),
        lax.psum_scatter(
            grads[5].astype(jnp.bfloat16), "fsdp", scatter_dimension=0, tiled=True
        ).astype(jnp.float32),
        lax.psum_scatter(
            grads[6].astype(jnp.bfloat16), "fsdp", scatter_dimension=0, tiled=True
        ).astype(jnp.float32),
        lax.psum_scatter(
            grads[7].astype(jnp.bfloat16), "fsdp", scatter_dimension=0, tiled=True
        ).astype(jnp.float32),
        lax.psum_scatter(
            grads[8].astype(jnp.bfloat16), "fsdp", scatter_dimension=0, tiled=True
        ).astype(jnp.float32),
        lax.psum_scatter(
            grads[9].astype(jnp.bfloat16), "fsdp", scatter_dimension=0, tiled=True
        ).astype(jnp.float32),
        lax.psum_scatter(
            grads[10].astype(jnp.bfloat16), "fsdp", scatter_dimension=0, tiled=True
        ).astype(jnp.float32),
        lax.psum_scatter(
            grads[11].astype(jnp.bfloat16), "fsdp", scatter_dimension=0, tiled=True
        ).astype(jnp.float32),
        lax.psum_scatter(
            grads[12].astype(jnp.bfloat16), "fsdp", scatter_dimension=0, tiled=True
        ).astype(jnp.float32),
    )
    return (
        lax.psum(shards[0].astype(jnp.bfloat16), "ctx").astype(jnp.float32),
        lax.psum(shards[1].astype(jnp.bfloat16), "ctx").astype(jnp.float32),
        lax.psum(shards[2].astype(jnp.bfloat16), "ctx").astype(jnp.float32),
        lax.psum(shards[3].astype(jnp.bfloat16), "ctx").astype(jnp.float32),
        lax.psum(shards[4].astype(jnp.bfloat16), "ctx").astype(jnp.float32),
        lax.psum(shards[5].astype(jnp.bfloat16), "ctx").astype(jnp.float32),
        lax.psum(shards[6].astype(jnp.bfloat16), "ctx").astype(jnp.float32),
        lax.psum(shards[7].astype(jnp.bfloat16), "ctx").astype(jnp.float32),
        lax.psum(shards[8].astype(jnp.bfloat16), "ctx").astype(jnp.float32),
        lax.psum(shards[9].astype(jnp.bfloat16), "ctx").astype(jnp.float32),
        lax.psum(shards[10].astype(jnp.bfloat16), "ctx").astype(jnp.float32),
        lax.psum(shards[11].astype(jnp.bfloat16), "ctx").astype(jnp.float32),
        lax.psum(shards[12].astype(jnp.bfloat16), "ctx").astype(jnp.float32),
    )


def layer_slices(sharded, layer_index):
    return tuple((tensor[layer_index] for tensor in sharded))


def on_device_plain(
    activations,
    cotangent,
    doc_start,
    deal,
    attend_in,
    query_bias,
    value_bias,
    attend_out,
    attend_bias,
    first_gain,
    first_shift,
    expand_proj,
    expand_bias,
    reduce_proj,
    reduce_bias,
    second_gain,
    second_shift,
):
    sharded = (
        attend_in,
        query_bias,
        value_bias,
        attend_out,
        attend_bias,
        first_gain,
        first_shift,
        expand_proj,
        expand_bias,
        reduce_proj,
        reduce_bias,
        second_gain,
        second_shift,
    )
    row_count = activations.shape[1]
    positions = key_positions(deal)
    own_rank = lax.axis_index("ctx")
    own_positions = lax.dynamic_slice_in_dim(positions, own_rank * row_count, row_count)
    own_starts = doc_start[0]
    key_starts = lax.all_gather(own_starts, "ctx", axis=0, tiled=True)
    allowed = (positions[None, :] <= own_positions[:, None]) & (
        key_starts[None, :] == own_starts[:, None]
    )
    hidden = activations[0].astype(jnp.float32)
    kept_weights = []
    kept_saved = []
    for layer_index in range(LAYERS):
        weights = lax.all_gather(
            for_sending(layer_slices(sharded, layer_index)), "fsdp", axis=0, tiled=True
        )
        hidden, saved = forward_layer(hidden, weights, allowed)
        kept_weights.append(weights)
        kept_saved.append(saved)
    out_act = hidden.astype(jnp.bfloat16)[None]
    grad_hidden = cotangent[0].astype(jnp.float32)
    reduced = [None] * LAYERS
    for layer_index in reversed(range(LAYERS)):
        weights = lax.all_gather(
            for_sending(layer_slices(sharded, layer_index)), "fsdp", axis=0, tiled=True
        )
        grad_hidden, grads = backward_layer(grad_hidden, weights, kept_saved[layer_index], allowed)
        reduced[layer_index] = reduce_grads(grads)
    stacked = [
        jnp.stack([reduced[layer_index][member] for layer_index in range(LAYERS)])
        for member in range(13)
    ]
    return (
        out_act,
        grad_hidden[None],
        stacked[0],
        stacked[1],
        stacked[2],
        stacked[3],
        stacked[4],
        stacked[5],
        stacked[6],
        stacked[7],
        stacked[8],
        stacked[9],
        stacked[10],
        stacked[11],
        stacked[12],
    )


F32 = jnp.float32
BF = jnp.bfloat16
WIDTH = HEADS * HEAD_DIM
QB = 256
SCORE_SCALE = HEAD_DIM ** (-0.5) * 1.4426950408889634
NEG = -1e30
VMEM_LIMIT = 60 * 1024 * 1024


def mm_nn(a, b):
    return lax.dot_general(a, b, (((1,), (0,)), ((), ())), preferred_element_type=F32)


def mm_nt(a, b):
    return lax.dot_general(a, b, (((1,), (1,)), ((), ())), preferred_element_type=F32)


def mm_tn(a, b):
    return lax.dot_general(a, b, (((0,), (0,)), ((), ())), preferred_element_type=F32)


def call(kernel, outs, args, specs, scratch, name, flops, nbytes):
    return pl.pallas_call(
        kernel,
        out_shape=[jax.ShapeDtypeStruct(shape, dtype) for shape, dtype in outs],
        in_specs=[pl.BlockSpec(memory_space=space) for space in specs],
        out_specs=[pl.BlockSpec(memory_space=pltpu.VMEM) for _ in outs],
        scratch_shapes=scratch,
        compiler_params=pltpu.CompilerParams(vmem_limit_bytes=VMEM_LIMIT),
        cost_estimate=pl.CostEstimate(flops=0, bytes_accessed=0, transcendentals=0),
        name=name,
    )(*args)


def block_of(block, blocks):
    half = 0 if 2 * block < blocks else 1
    return (block if half == 0 else blocks - 1 - block), half


CORE, SHARD, RANK, JMAP, INV, JMIN = 0, 1, 2, 6, 10, 14
SWAPPED = (0, 2, 1, 3)
VEC_AT = 640


def started_copies(sems, *pairs):
    copies = []
    for n, (src, dst) in enumerate(pairs):
        copy = pltpu.make_async_copy(src, dst, sems.at[n])
        copy.start()
        copies.append(copy)
    return copies


def last_kernel(
    writer, places, meta, c0, c1, c2, c3, hid, cot, t, a, b, d, crossed,
    l_mine, l_other, hlow, gfs, dgg, gctx,
    xhat1, rstd1, gp, xhat2, rstd2, e_s, r_s, sems, wo_s, b_s, wo_sems, ctx, eb, eb_s,
):
    loads = (e_s, r_s, sems, wo_s, b_s, wo_sems)
    mlp_fwd_kernel(
        writer, (None,) * 5 + tuple(places[:3]), meta, c0, c1, c2, c3, hid, t, a, b, d, crossed,
        xhat1, rstd1, gp, xhat2, rstd2, l_mine, l_other, hlow, *loads, ctx, eb, finish=False,
    )
    mlp_bwd_kernel(
        writer, places[3:], meta, xhat1, rstd1, xhat2, rstd2, gp, cot, t, a, b, d, crossed,
        gfs, dgg, gctx, *loads, eb_s, parts=1, loaded=True,
    )


class Writer:
    def __init__(self, sems):
        self.sems = sems
        self.copies = []

    def send(self, src, dst, *at):
        if dst is None:
            return
        if at:
            src, dst = src.at[at], dst.at[at]
        copy = pltpu.make_async_copy(src, dst, self.sems.at[len(self.copies)])
        copy.start()
        self.copies.append(copy)

    def finish(self):
        for copy in self.copies:
            copy.wait()


def writing(kernel, outs, copies):
    count = len(outs)

    def run(*refs, scratch, **keys):
        ins, places, rest = refs[: -count - scratch], refs[-count - scratch : -scratch], refs[-scratch:]
        buffers, sems, rest = rest[:count], rest[count], rest[count + 1 :]
        kernel(Writer(sems), places, *ins, *buffers, *rest, **keys)

    return run, [pltpu.VMEM(shape, dtype) for shape, dtype in outs] + [pltpu.SemaphoreType.DMA((copies,))]


def call_writing(kernel, outs, args, specs, scratch, name, copies, **keys):
    run, buffers = writing(kernel, outs, copies)
    scratch = buffers + scratch
    return pl.pallas_call(
        functools.partial(run, scratch=len(scratch), **keys),
        out_shape=[jax.ShapeDtypeStruct(shape, dtype) for shape, dtype in outs],
        in_specs=[pl.BlockSpec(memory_space=space) for space in specs],
        out_specs=[pl.BlockSpec(memory_space=pl.ANY) for _ in outs],
        scratch_shapes=scratch,
        compiler_params=pltpu.CompilerParams(vmem_limit_bytes=VMEM_LIMIT),
        cost_estimate=pl.CostEstimate(flops=0, bytes_accessed=0, transcendentals=0),
        name=name,
    )(*args)


def prep_kernel(
    expand, reduce, attend_in, attend_out, expand_bias, v0, v1, v2, v3, v4, v5, v6, v7,
    t0, d0, t1, d1,
):
    rank = lax.axis_index("ctx")
    cut = expand.shape[1]
    hw = WIDTH // 4
    for layer, (t, d) in enumerate(((t0, d0), (t1, d1))):
        bias = expand_bias[layer : layer + 1, :].astype(F32)
        rows = [v[layer : layer + 1, :].astype(F32) for v in (v0, v1, v2, v3, v4, v5, v6, v7)]
        rows += [bias[:, k * cut : (k + 1) * cut] for k in range(4)]
        rows.append(jnp.zeros((4, cut), F32))
        d[2 * cut :, :] = attend_out[layer]
        t[2 * cut :, 3 * hw :] = jnp.zeros((cut, WIDTH - 3 * hw), BF)
        t[2 * cut : 2 * cut + 16, VEC_AT : VEC_AT + cut] = jnp.concatenate(rows, axis=0).astype(BF)
        for k in range(4):

            @pl.when(rank == k)
            def _():
                for out, at in ((t, k), (d, k ^ 3)):
                    out[0:cut, :] = jnp.concatenate(
                        [
                            expand[layer, :, (2 * z + h) * 4 * cut + at * cut : (2 * z + h) * 4 * cut + (at + 1) * cut]
                            for h in range(2)
                            for z in range(4)
                        ],
                        axis=1,
                    )
                    out[cut : 2 * cut, :] = reduce[layer, at * cut : (at + 1) * cut, :]
                t[2 * cut :, 0 : 3 * hw] = jnp.concatenate(
                    [attend_in[layer, :, n * WIDTH + k * hw : n * WIDTH + (k + 1) * hw] for n in range(3)], axis=1
                )


def nothing_kernel(*refs):
    pass


def after(xs, *others):
    return pl.pallas_call(
        nothing_kernel,
        out_shape=[jax.ShapeDtypeStruct(x.shape, x.dtype) for x in xs],
        in_specs=[pl.BlockSpec(memory_space=pl.ANY)] * (len(xs) + len(others)),
        out_specs=[pl.BlockSpec(memory_space=pl.ANY)] * len(xs),
        input_output_aliases={n: n for n in range(len(xs))},
        name="after",
    )(*xs, *others)


def pack_kernel(a, b, *rest):
    out, held, ins, outs = rest[-4:]
    coming = [pltpu.make_async_copy((a, b)[n // 4].at[n % 4], held.at[n // 4, n % 4], ins.at[n]) for n in range(8)]
    going = [pltpu.make_async_copy(held.at[n // 4, n % 4], out.at[n // 4, n % 4], outs.at[n]) for n in range(8)]
    for copy in coming:
        copy.start()
    for arrive, leave in zip(coming, going):
        arrive.wait()
        leave.start()
    for copy in going:
        copy.wait()


def pack(a, b, *others):
    shape = (2,) + a.shape
    return pl.pallas_call(
        pack_kernel,
        out_shape=jax.ShapeDtypeStruct(shape, a.dtype),
        in_specs=[pl.BlockSpec(memory_space=pl.ANY)] * (2 + len(others)),
        out_specs=pl.BlockSpec(memory_space=pl.ANY),
        scratch_shapes=[pltpu.VMEM(shape, a.dtype), pltpu.SemaphoreType.DMA((8,)), pltpu.SemaphoreType.DMA((8,))],
        cost_estimate=pl.CostEstimate(flops=0, bytes_accessed=0, transcendentals=0),
        name="pack",
    )(a, b, *others)


def half_kernel(meta, t, *rest):
    out, held, ins, outs = rest[-4:]
    coming = [pltpu.make_async_copy(t.at[z, meta[CORE], 0:2], held.at[z], ins.at[z]) for z in range(4)]
    going = [pltpu.make_async_copy(held.at[z], out.at[z], outs.at[z]) for z in range(4)]
    for copy in coming:
        copy.start()
    for arrive, leave in zip(coming, going):
        arrive.wait()
        leave.start()
    for copy in going:
        copy.wait()


def half_of(meta, t, *others):
    shape = (4, 2) + t.shape[3:]
    return pl.pallas_call(
        half_kernel,
        out_shape=jax.ShapeDtypeStruct(shape, t.dtype),
        in_specs=[pl.BlockSpec(memory_space=space) for space in [pltpu.SMEM] + [pl.ANY] * (1 + len(others))],
        out_specs=pl.BlockSpec(memory_space=pl.ANY),
        scratch_shapes=[pltpu.VMEM(shape, t.dtype), pltpu.SemaphoreType.DMA((4,)), pltpu.SemaphoreType.DMA((4,))],
        cost_estimate=pl.CostEstimate(flops=0, bytes_accessed=0, transcendentals=0),
        name="half",
    )(meta, t, *others)


def sums_kernel(*refs, layout, count, split):
    outs = refs[-len(layout) :]
    at = 0
    for out, parts in zip(outs, layout):
        lane = 0
        for n in parts:
            total = refs[at][...].astype(F32)
            for ref in refs[at + 1 : at + n]:
                total = total + ref[...].astype(F32)
            at += n
            if split:
                for k in range(len(outs)):
                    outs[k][...] = total[k].astype(BF)
            else:
                out[..., lane : lane + total.shape[-1]] = total.astype(BF)
            lane += total.shape[-1]
        if split:
            break


def sums(outputs, *others, split=0):
    args = tuple(x for groups in outputs for group in groups for x in group)
    layout = tuple(tuple(len(group) for group in groups) for groups in outputs)
    if split:
        shapes = [(args[0].shape[1:], BF)] * split
        layout = layout * split
    else:
        shapes = [
            (groups[0][0].shape[:-1] + (sum(group[0].shape[-1] for group in groups),), BF) for groups in outputs
        ]
    return call(
        functools.partial(sums_kernel, layout=layout, count=len(args), split=split),
        shapes, args + others, [pltpu.VMEM] * len(args) + [pl.ANY] * len(others), [], "sums", 0, 0,
    )


def join_kernel(att, t, d, *rest):
    out = rest[-1]
    rows = att.shape[0]
    out[0:rows, 0 : att.shape[1]] = att[...]
    out[0:rows, att.shape[1] :] = jnp.zeros((rows, out.shape[1] - att.shape[1]), BF)
    for k in range(2):
        out[rows:, k * WIDTH : (k + 1) * WIDTH] = (t[k].astype(F32) + d[k].astype(F32)).astype(BF)


def merge_kernel(dwo, own, other, *rest):
    out = rest[-1]
    out[:, :, 0:WIDTH] = dwo[...]
    out[:, :, WIDTH:] = (own[...].astype(F32) + other[...].astype(F32)).astype(BF)


def vectors_of(shards, order):
    return jnp.concatenate([shards[f // 2, f % 2, :, 0:96] for f in order], axis=1).astype(F32)


NATURAL = tuple(range(8))
CORE_MAJOR = (0, 2, 4, 6, 1, 3, 5, 7)


def attn_fwd_kernel(
    meta, h0, h1, h2, h3, qrow, kcol, t, *rest, heads, tokens
):
    qkv, c0, c1, c2, c3, lse, q_s, k_s, vt_s, o_s, ctx, w_s, b_s, sems = rest[-14:]
    blocks = tokens // BLK
    hw = heads * HEAD_DIM
    copies = started_copies(
        sems, (t.at[:, :, 2, :, 0:VEC_AT], w_s), (t.at[:, :, 2, 0:16, VEC_AT : VEC_AT + 128], b_s)
    )
    for copy in copies:
        copy.wait()
    w = w_s[...].reshape(WIDTH, VEC_AT)[:, 0 : 3 * hw]
    vec = vectors_of(b_s, NATURAL)
    bias = jnp.zeros((1, 3 * hw), F32)
    for k in range(4):
        part = jnp.concatenate(
            [vec[6:7, k * hw : (k + 1) * hw], jnp.zeros((1, hw), F32), vec[7:8, k * hw : (k + 1) * hw]], axis=1
        )
        bias = jnp.where(meta[RANK] == k, part, bias)
    for j, piece in enumerate((h0, h1, h2, h3)):
        qkv[j] = (mm_nn(piece[...], w) + bias).astype(BF)
    for pair in range(blocks // 2):
        rows = []
        for block in (2 * pair, 2 * pair + 1):
            at, half = block_of(block, blocks)
            rows.append(qkv[meta[JMAP + at], half * BLK : (half + 1) * BLK, :])
        both = jnp.concatenate(rows, axis=0)
        lo, hi = 2 * pair * BLK, 2 * (pair + 1) * BLK
        for h in range(heads):
            q_s[h, lo:hi, :] = both[:, h * HEAD_DIM : (h + 1) * HEAD_DIM]
            k_s[h, lo:hi, :] = both[:, hw + h * HEAD_DIM : hw + (h + 1) * HEAD_DIM]
        vt_s[:, lo:hi] = both[:, 2 * hw :].T
    iota_k = lax.broadcasted_iota(jnp.int32, (QB, QB), 0)
    iota_q = lax.broadcasted_iota(jnp.int32, (QB, QB), 1)
    causal = iota_k <= iota_q
    head_rows = [slice(h * HEAD_DIM, (h + 1) * HEAD_DIM) for h in range(heads)]
    for i in range(tokens // QB):
        lo = i * QB
        starts_q = qrow[0:1, lo : lo + QB]

        def scores(at, diagonal):
            col = kcol[pl.ds(at, QB), :]
            allowed = jnp.concatenate([col, col], axis=1) == starts_q
            if diagonal:
                allowed = allowed & causal
            return [
                jnp.where(allowed, mm_nt(k_s[h, pl.ds(at, QB), :], q_s[h, lo : lo + QB, :]) * SCORE_SCALE, NEG)
                for h in range(heads)
            ]

        ss = scores(lo, True)
        tops = [jnp.max(s, axis=0, keepdims=True) for s in ss]
        ps = [jnp.exp2(s - top) for s, top in zip(ss, tops)]
        totals = [jnp.sum(p, axis=0, keepdims=True) for p in ps]
        outs = [mm_nn(vt_s[head_rows[h], lo : lo + QB], ps[h].astype(BF)) for h in range(heads)]

        def step(jb, carry):
            tops, totals, outs = carry
            at = pl.multiple_of(jb * QB, QB)
            ss = scores(at, False)
            new = [jnp.maximum(top, jnp.max(s, axis=0, keepdims=True)) for s, top in zip(ss, tops)]
            ps = [jnp.exp2(s - top) for s, top in zip(ss, new)]
            alphas = [jnp.exp2(top - n) for top, n in zip(tops, new)]
            totals = [
                total * alpha + jnp.sum(p, axis=0, keepdims=True) for total, alpha, p in zip(totals, alphas, ps)
            ]
            outs = [
                outs[h] * alphas[h] + mm_nn(vt_s[head_rows[h], pl.ds(at, QB)], ps[h].astype(BF)) for h in range(heads)
            ]
            return new, totals, outs

        if i > 0:
            tops, totals, outs = lax.fori_loop(meta[JMIN + i], i, step, (tops, totals, outs))
        for h in range(heads):
            o_s[head_rows[h], lo : lo + QB] = outs[h] / totals[h]
            lse[h : h + 1, lo : lo + QB] = tops[h] + jnp.log2(totals[h])
    for pair in range(blocks // 2):
        lo, hi = 2 * pair * BLK, 2 * (pair + 1) * BLK
        both = o_s[:, lo:hi].T.astype(BF)
        for n, block in enumerate((2 * pair, 2 * pair + 1)):
            at, half = block_of(block, blocks)
            ctx[meta[JMAP + at], :, half * hw : (half + 1) * hw] = both[n * BLK : (n + 1) * BLK, :]
    for j, out in enumerate((c0, c1, c2, c3)):
        out[...] = ctx[j]


def attn_bwd_kernel(
    meta, h0, h1, h2, h3, qrow, kcol, qkv, c0, c1, c2, c3, gctx, lse, t, *rest, heads, tokens
):
    (
        g_own, g_a, g_b, g_d, dw_own, dw_other, q_s, k_s, v_s, do_s, kt_s, delta_s, dk_s, dv_s, dqt_s, g_s, w_s, ctx, dw, sems,
    ) = rest[-20:]
    blocks = tokens // BLK
    hw = heads * HEAD_DIM
    scale = HEAD_DIM ** (-0.5)
    copies = started_copies(sems, (t.at[:, :, 2, :, 0:VEC_AT], w_s))
    for j, c in enumerate((c0, c1, c2, c3)):
        ctx[j] = c[...]
    for pair in range(blocks // 2):
        rows, grads, outs = [], [], []
        for block in (2 * pair, 2 * pair + 1):
            at, half = block_of(block, blocks)
            rows.append(qkv[meta[JMAP + at], half * BLK : (half + 1) * BLK, :])
            grads.append(gctx[meta[INV + at], :, half * hw : (half + 1) * hw])
            outs.append(ctx[meta[JMAP + at], :, half * hw : (half + 1) * hw])
        both = jnp.concatenate(rows, axis=0)
        grad = jnp.concatenate(grads, axis=0)
        out = jnp.concatenate(outs, axis=0)
        lo, hi = 2 * pair * BLK, 2 * (pair + 1) * BLK
        prod = (grad.astype(F32) * out.astype(F32)).T
        kt_s[:, lo:hi] = both[:, hw : 2 * hw].T
        for h in range(heads):
            c0, c1 = h * HEAD_DIM, (h + 1) * HEAD_DIM
            q_s[h, lo:hi, :] = both[:, c0:c1]
            k_s[h, lo:hi, :] = both[:, hw + c0 : hw + c1]
            v_s[h, lo:hi, :] = both[:, 2 * hw + c0 : 2 * hw + c1]
            do_s[h, lo:hi, :] = grad[:, c0:c1]
            delta_s[h : h + 1, lo:hi] = jnp.sum(prod[c0:c1, :], axis=0, keepdims=True)
    dk_s[...] = jnp.zeros_like(dk_s)
    dv_s[...] = jnp.zeros_like(dv_s)
    iota_k = lax.broadcasted_iota(jnp.int32, (QB, QB), 0)
    iota_q = lax.broadcasted_iota(jnp.int32, (QB, QB), 1)
    causal = iota_k <= iota_q
    head_rows = [slice(h * HEAD_DIM, (h + 1) * HEAD_DIM) for h in range(heads)]
    for i in range(tokens // QB):
        lo = i * QB
        starts_q = qrow[0:1, lo : lo + QB]

        def block(at, diagonal):
            col = kcol[pl.ds(at, QB), :]
            allowed = jnp.concatenate([col, col], axis=1) == starts_q
            if diagonal:
                allowed = allowed & causal
            dqs = []
            for h in range(heads):
                q, do = q_s[h, lo : lo + QB, :], do_s[h, lo : lo + QB, :]
                s = mm_nt(k_s[h, pl.ds(at, QB), :], q) * SCORE_SCALE
                p = jnp.exp2(jnp.where(allowed, s, NEG) - lse[h : h + 1, lo : lo + QB])
                dp = mm_nt(v_s[h, pl.ds(at, QB), :], do)
                ds = (p * (dp - delta_s[h : h + 1, lo : lo + QB])).astype(BF)
                dv_s[h, pl.ds(at, QB), :] += mm_nn(p.astype(BF), do)
                dk_s[h, pl.ds(at, QB), :] += mm_nn(ds, q)
                dqs.append(mm_nn(kt_s[head_rows[h], pl.ds(at, QB)], ds))
            return dqs

        dqs = block(lo, True)
        if i > 0:
            dqs = lax.fori_loop(
                meta[JMIN + i],
                i,
                lambda jb, acc: [x + y for x, y in zip(acc, block(pl.multiple_of(jb * QB, QB), False))],
                dqs,
            )
        for h in range(heads):
            dqt_s[head_rows[h], lo : lo + QB] = dqs[h] * scale
    for pair in range(blocks // 2):
        lo, hi = 2 * pair * BLK, 2 * (pair + 1) * BLK
        parts = [dqt_s[:, lo:hi].T.astype(BF)]
        parts += [(dk_s[h, lo:hi, :] * scale).astype(BF) for h in range(heads)]
        parts += [dv_s[h, lo:hi, :].astype(BF) for h in range(heads)]
        both = jnp.concatenate(parts, axis=1)
        for n, block_at in enumerate((2 * pair, 2 * pair + 1)):
            at, half = block_of(block_at, blocks)
            g_s[meta[JMAP + at], half * BLK : (half + 1) * BLK, :] = both[n * BLK : (n + 1) * BLK, :]
    for copy in copies:
        copy.wait()
    w = w_s[...].reshape(WIDTH, VEC_AT)[:, 0 : 3 * hw]
    total = None
    sums = None
    for j, piece in enumerate((h0, h1, h2, h3)):
        g = g_s[j]
        back = mm_nt(g, w)
        if j == 0:
            g_own[...] = back
        else:
            (g_a, g_b, g_d)[j - 1][...] = back.astype(BF)
        part = mm_tn(piece[...], g)
        col = jnp.sum(g.astype(F32), axis=0, keepdims=True)
        total = part if total is None else total + part
        sums = col if sums is None else sums + col
    shards, rows_out, cols = dw.shape
    rows = WIDTH // shards
    dw[:, 0:rows, :] = total.reshape(shards, rows, cols).astype(BF)
    dw[:, rows:, :] = jnp.broadcast_to(sums[None], (shards, rows_out - rows, cols)).astype(BF)
    for k in range(4):
        dw_own[k] = dw[2 * k + meta[CORE]]
        dw_other[k] = dw[2 * k + 1 - meta[CORE]]


def start_ffn_copies(core, t, a, b, d, crossed, e_s, r_s, sems):
    ca, cb = crossed.at[0], crossed.at[1]
    groups = []
    for p, parts in enumerate(((t,), (a, cb), (b, ca), (d,))):
        pairs = []
        if len(parts) == 1:
            pairs.append((parts[0].at[:, :, 0], e_s.at[p]))
            for h in range(2):
                pairs.append((parts[0].at[:, h, 1], r_s.at[p, h]))
        else:
            for src, parity in ((parts[0], core), (parts[1], 1 - core)):
                pairs.append((src.at[:, 0], e_s.at[p, :, parity]))
                pairs.append((src.at[:, 1], r_s.at[p, parity]))
        group = []
        for n, (src, dst) in enumerate(pairs):
            copy = pltpu.make_async_copy(src, dst, sems.at[p, n])
            copy.start()
            group.append(copy)
        groups.append(group)
    return groups


def ffn_scratch():
    return [
        pltpu.VMEM((4, 4, 2, 96, WIDTH), BF),
        pltpu.VMEM((4, 2, 4, 96, WIDTH), BF),
        pltpu.SemaphoreType.DMA((4, 4)),
        pltpu.VMEM((4, 2, 96, WIDTH), BF),
        pltpu.VMEM((4, 2, 16, 128), BF),
        pltpu.SemaphoreType.DMA((2,)),
    ]


def mlp_fwd_scratch(rows, hw):
    return ffn_scratch() + [pltpu.VMEM((4, rows, hw), BF), pltpu.VMEM((8, WIDTH), F32)]


def mlp_bwd_scratch():
    return ffn_scratch() + [pltpu.VMEM((8, WIDTH), F32)]


def wgrad_scratch():
    rows = 2 * BLK
    return [
        pltpu.VMEM((rows, 3 * WIDTH), BF),
        pltpu.VMEM((rows, 3 * WIDTH), BF),
        pltpu.VMEM((rows + 16, 6 * WIDTH), BF),
        pltpu.VMEM((rows + 16, 6 * WIDTH), BF),
        pltpu.SemaphoreType.DMA((16,)),
    ]


def attn_fwd_scratch(heads, tokens):
    hw = heads * HEAD_DIM
    return [
        pltpu.VMEM((heads, tokens, HEAD_DIM), BF),
        pltpu.VMEM((heads, tokens, HEAD_DIM), BF),
        pltpu.VMEM((hw, tokens), BF),
        pltpu.VMEM((hw, tokens), F32),
        pltpu.VMEM((4, BLK, 2 * hw), BF),
        pltpu.VMEM((4, 2, 96, VEC_AT), BF),
        pltpu.VMEM((4, 2, 16, 128), BF),
        pltpu.SemaphoreType.DMA((2,)),
    ]


def attn_bwd_scratch(heads, tokens):
    hw = heads * HEAD_DIM
    return [pltpu.VMEM((heads, tokens, HEAD_DIM), BF)] * 4 + [
        pltpu.VMEM((hw, tokens), BF),
        pltpu.VMEM((8, tokens), F32),
        pltpu.VMEM((heads, tokens, HEAD_DIM), F32),
        pltpu.VMEM((heads, tokens, HEAD_DIM), F32),
        pltpu.VMEM((hw, tokens), F32),
        pltpu.VMEM((4, tokens // 4, 3 * hw), BF),
        pltpu.VMEM((4, 2, 96, VEC_AT), BF),
        pltpu.VMEM((4, BLK, 2 * hw), BF),
        pltpu.VMEM((8, 112, 3 * hw), BF),
        pltpu.SemaphoreType.DMA((1,)),
    ]


def norm_parts(values):
    centre = values - jnp.mean(values, axis=-1, keepdims=True)
    spread = jnp.mean(centre * centre, axis=-1, keepdims=True)
    rstd = lax.rsqrt(spread + norm_eps)
    return centre * rstd, rstd


def shard_columns(x, parity):
    return jnp.concatenate([x[:, (2 * z + parity) * 96 : (2 * z + parity + 1) * 96] for z in range(4)], axis=1)


def mlp_fwd_kernel(
    writer, places, meta, c0, c1, c2, c3, hid, t, a, b, d, crossed,
    xhat1, rstd1, gp, xhat2, rstd2, l_mine, l_other, hlow, *rest, finish=True,
):
    hnext, (e_s, r_s, sems, wo_s, b_s, wo_sems, ctx, eb) = rest[:-8], rest[-8:]
    core = meta[CORE]
    xhat1_to, rstd1_to, gp_to, xhat2_to, rstd2_to, mine_to, other_to, hlow_to = places[:8]
    wo_copies = started_copies(
        wo_sems, (d.at[:, :, 2], wo_s), (t.at[:, :, 2, 0:16, VEC_AT : VEC_AT + 128], b_s)
    )
    copies = start_ffn_copies(core, t, a, b, d, crossed, e_s, r_s, sems)
    half_cols = WIDTH // 2
    hw = c0.shape[1] // 2
    for p, piece in enumerate((c0, c1, c2, c3)):
        for half in range(2):
            ctx[meta[RANK + p], half * BLK : (half + 1) * BLK, :] = piece[:, half * hw : (half + 1) * hw]

    def keep(parts, at):
        for parity in range(2):

            @pl.when(core == parity)
            def _():
                l_mine[:, at : at + half_cols] = parts[parity]

            @pl.when(core != parity)
            def _():
                l_other[:, at : at + half_cols] = parts[parity]

        for ref, to in ((l_mine, mine_to), (l_other, other_to)):
            writer.send(ref, to, slice(None), slice(at, at + half_cols))

    low = jnp.concatenate([ctx[rank] for rank in range(4)], axis=1)
    keep([shard_columns(low, parity) for parity in range(2)], half_cols)
    for copy in wo_copies:
        copy.wait()
    vec = vectors_of(b_s, NATURAL)
    eb[...] = vectors_of(b_s, CORE_MAJOR)[8:16, :]
    wo = wo_s[...].reshape(WIDTH, WIDTH)
    first_sum = hid[...].astype(F32) + (mm_nn(low, wo) + vec[0:1, :])
    x1, r1 = norm_parts(first_sum)
    xhat1[...] = x1
    rstd1[...] = r1
    writer.send(xhat1, xhat1_to)
    writer.send(rstd1, rstd1_to)
    normed = x1 * vec[1:2, :] + vec[2:3, :]
    lown = normed.astype(BF)
    keep([shard_columns(lown, parity) for parity in range(2)], 0)
    out = normed + vec[3:4, :]
    for p in range(4):
        for copy in copies[p]:
            copy.wait()
        bias = eb[pl.ds(meta[RANK + p], 1), :]
        u = mm_nn(lown, e_s[p].reshape(WIDTH, WIDTH)) + bias
        cdf = 0.5 * (1.0 + lax.erf(u * 0.7071067811865476))
        pdf = jnp.exp(-0.5 * u * u) * 0.3989422804014327
        low = (u * cdf).astype(BF)
        cut = slice(p * WIDTH, (p + 1) * WIDTH)
        gp[:, cut] = (cdf + u * pdf).astype(BF)
        writer.send(gp, gp_to, slice(None), cut)
        keep([low[:, :half_cols], low[:, half_cols:]], WIDTH + p * half_cols)
        out = out + mm_nn(low, r_s[p].reshape(WIDTH, WIDTH))
    x2, r2 = norm_parts(out)
    nxt = x2 * vec[4:5, :] + vec[5:6, :]
    hlow[...] = nxt.astype(BF)
    writer.send(hlow, hlow_to)
    xhat2[...] = x2
    writer.send(xhat2, xhat2_to)
    rstd2[...] = r2
    writer.send(rstd2, rstd2_to)
    if hnext:
        hnext[0][...] = nxt
        writer.send(hnext[0], places[8])
    if finish:
        writer.finish()


def norm_back(gy, gain, xhat, rstd):
    g = gy * gain
    return rstd * (g - jnp.mean(g, axis=-1, keepdims=True) - xhat * jnp.mean(g * xhat, axis=-1, keepdims=True))


def rows_sum(x):
    return jnp.sum(x, axis=0, keepdims=True)


def mlp_bwd_kernel(
    writer, places, meta, xhat1, rstd1, xhat2, rstd2, gp, *rest, parts, loaded=False
):
    t, a, b, d, crossed = rest[parts : parts + 5]
    gfs, dgg, gctx, e_s, r_s, sems, wo_s, b_s, wo_sems, eb_s = rest[-10:]
    rows = gfs.shape[0]
    core = meta[CORE]
    if loaded:
        copies, wo_copies = [[]] * 4, []
    else:
        copies = start_ffn_copies(core, t, a, b, d, crossed, e_s, r_s, sems)
        wo_copies = started_copies(
            wo_sems, (d.at[:, :, 2], wo_s), (t.at[:, :, 2, 0:16, VEC_AT : VEC_AT + 128], b_s)
        )
    grad = rest[0][...].astype(F32)
    for ref in rest[1:parts]:
        grad = grad + ref[...].astype(F32)
    x2 = xhat2[...]
    for copy in wo_copies:
        copy.wait()
    vec = vectors_of(b_s, NATURAL)
    gss = norm_back(grad, vec[4:5, :], x2, rstd2[...])
    low = gss.astype(BF)
    cut = slice(4 * WIDTH, 5 * WIDTH)
    dgg[0:rows, cut] = low
    writer.send(dgg.at[0:rows, cut], places[1].at[0:rows, cut])
    sums = [None] * 8
    sums[4] = rows_sum(grad * x2)
    sums[5] = rows_sum(grad)
    sums[3] = rows_sum(low.astype(F32))
    gn = gss
    eb_s[...] = jnp.zeros_like(eb_s)
    for p in range(4):
        for copy in copies[p]:
            copy.wait()
        ga = mm_nt(low, r_s[p].reshape(WIDTH, WIDTH))
        dip = (ga * gp[:, p * WIDTH : (p + 1) * WIDTH].astype(F32)).astype(BF)
        cut = slice(p * WIDTH, (p + 1) * WIDTH)
        dgg[0:rows, cut] = dip
        writer.send(dgg.at[0:rows, cut], places[1].at[0:rows, cut])
        eb_s[pl.ds(meta[RANK + p], 1), :] = rows_sum(dip.astype(F32))
        gn = gn + mm_nt(dip, e_s[p].reshape(WIDTH, WIDTH))
    x1 = xhat1[...]
    gf = norm_back(gn, vec[1:2, :], x1, rstd1[...])
    sums[1] = rows_sum(gn * x1)
    sums[2] = rows_sum(gn)
    lowa = gf.astype(BF)
    cut = slice(5 * WIDTH, 6 * WIDTH)
    dgg[0:rows, cut] = lowa
    writer.send(dgg.at[0:rows, cut], places[1].at[0:rows, cut])
    gfs[...] = gf
    writer.send(gfs, places[0])
    sums[0] = rows_sum(lowa.astype(F32))
    sums[6] = jnp.zeros_like(sums[0])
    sums[7] = sums[6]
    gc = mm_nt(lowa, wo_s[...].reshape(WIDTH, WIDTH)).astype(BF)
    hw = gctx.shape[2] // 2
    for rank in range(4):
        for half in range(2):
            gctx[rank, :, half * hw : (half + 1) * hw] = gc[half * BLK : (half + 1) * BLK, rank * hw : (rank + 1) * hw]
    writer.send(gctx, places[2])
    vecs = jnp.concatenate(sums, axis=0)
    ebs = jnp.concatenate([eb_s[:, (4 * (f % 2) + f // 2) * 96 : (4 * (f % 2) + f // 2 + 1) * 96] for f in range(8)], axis=1)
    dgg[rows:, 0:WIDTH] = jnp.concatenate([vecs, ebs], axis=0).astype(BF)
    dgg[rows:, WIDTH:] = jnp.zeros((16, 5 * WIDTH), BF)
    writer.send(dgg.at[rows:], places[1].at[rows:])
    writer.finish()


def wgrad_kernel(writer, places, meta, l_mine_from, l_other_from, dgg_from, dgg_other_from, *rest):
    t, a, b, dwo, d, l_mine, l_other, dgg, dgg_other, sems = rest[-10:]
    half = WIDTH // 2
    rows = l_mine.shape[0]

    def fetch(n, src, dst, at, width):
        copy = pltpu.make_async_copy(src.at[:, at : at + width], dst.at[:, at : at + width], sems.at[n])
        copy.start()
        return copy

    lefts = [fetch(n, src, dst, 0, WIDTH) for n, (src, dst) in enumerate(((l_mine_from, l_mine), (l_other_from, l_other)))]
    rights = {}
    for k in (3, 4, 1, 2, 0, 5):
        q = SWAPPED[k] if k < 4 else k
        rights[k] = [fetch(4 + k, dgg_from, dgg, k * WIDTH, WIDTH), fetch(10 + k, dgg_other_from, dgg_other, q * WIDTH, WIDTH)]
        if k == 3:
            acts = [
                fetch(2 + n, src, dst, WIDTH, 2 * WIDTH)
                for n, (src, dst) in enumerate(((l_mine_from, l_mine), (l_other_from, l_other)))
            ]

    def wait(copies):
        for copy in copies:
            copy.wait()

    def grad(left, left_other, right, right_other):
        return mm_nn(left, dgg[0:rows, right : right + WIDTH]) + mm_nn(
            left_other, dgg_other[0:rows, right_other : right_other + WIDTH]
        )

    def left(at, at_other):
        return l_mine[:, at : at + half].T, l_other[:, at_other : at_other + half].T

    wait(lefts)
    low = left(0, 0)
    for n, (p, out) in enumerate(((3, d), (1, a), (2, b), (0, t))):
        q = SWAPPED[p]
        wait(rights[p])
        out[:, 0] = grad(*low, p * WIDTH, q * WIDTH).reshape(4, 96, WIDTH).astype(BF)
        if n == 0:
            wait(acts)
            wait(rights[4])
        out[:, 1] = (
            grad(*left(WIDTH + p * half, WIDTH + q * half), 4 * WIDTH, 4 * WIDTH).reshape(4, 96, WIDTH).astype(BF)
        )
        writer.send(out, places[(4, 1, 2, 0)[n]])
    wait(rights[5])
    dwo[:, 0:96, :] = grad(*left(half, half), 5 * WIDTH, 5 * WIDTH).reshape(4, 96, WIDTH).astype(BF)
    vecs = dgg[rows:, 0:WIDTH].astype(F32) + dgg_other[rows:, 0:WIDTH].astype(F32)
    dwo[:, 96:, :] = jnp.zeros((4, 16, WIDTH), BF)
    for parity in range(2):

        @pl.when(meta[CORE] == parity)
        def _():
            for z in range(4):
                dwo[z, 96:, 0:96] = vecs[:, (2 * z + parity) * 96 : (2 * z + parity + 1) * 96].astype(BF)

    writer.send(dwo, places[3])
    writer.finish()


def place_kernel(
    meta, *rest, layer, last
):
    if last:
        parts = [((f.at[0], f.at[1]), a) for f, a in zip(rest[:4], rest[4:8])]
        small_in, rest = rest[8], rest[13:]
    else:
        parts = [((x.at[112:, 0:WIDTH], x.at[112:, WIDTH:]), x.at[0:112, :]) for x in rest[:4]]
        rest = rest[5:]
    e_hbm, r_hbm, i_hbm, o_hbm = rest[:4]
    smalls = rest[4:-10]
    e_s, i_s, b_s, e_out, r_out, i_out, o_out, small_s, eb_s, sems = rest[-10:]
    for p, (ffn, att) in enumerate(parts):
        rank = meta[RANK + p]
        r_out[pl.ds(pl.multiple_of(rank * 96, 96), 96), :] = ffn[1][...].astype(F32)
        e_s[rank] = ffn[0][...].astype(F32)
        i_s[rank] = att[0:96, WIDTH : WIDTH + 9 * HEAD_DIM].astype(F32)
        b_s[rank] = att[96:112, WIDTH : WIDTH + 9 * HEAD_DIM].astype(F32)
    copies = []

    def send(n, src, dst):
        copy = pltpu.make_async_copy(src, dst.at[layer], sems.at[n])
        copy.start()
        copies.append(copy)

    send(0, r_out, r_hbm)
    for f in range(8):
        at = (4 * (f % 2) + f // 2) * 96
        e_out[:, f * 384 : (f + 1) * 384] = jnp.concatenate([e_s[c, :, at : at + 96] for c in range(4)], axis=1)
    send(1, e_out, e_hbm)
    hw = WIDTH // 4
    for k in range(3):
        i_out[:, k * WIDTH : (k + 1) * WIDTH] = jnp.concatenate(
            [i_s[c, :, k * hw : (k + 1) * hw] for c in range(4)], axis=1
        )
    send(2, i_out, i_hbm)
    wo = [att[:, 0:WIDTH].astype(F32) for _, att in parts]
    total = (wo[0] + wo[1]) + (wo[2] + wo[3])
    o_out[...] = total[0:96, :]
    send(3, o_out, o_hbm)
    bias = b_s[lax.shift_right_logical(meta[SHARD], 1)]
    low_half = (meta[SHARD] & 1) == 0
    qb = jnp.where(low_half, bias[:, 0:96], bias[:, 96:192])
    vb = jnp.where(low_half, bias[:, 2 * hw : 2 * hw + 96], bias[:, 2 * hw + 96 : 3 * hw])
    rows = jnp.concatenate([total[96:102, 0:96], qb[0:1], vb[0:1], total[104:112, 0:96]], axis=0)
    if last:
        for n, ref in enumerate(smalls[:-1]):
            ref[...] = jnp.concatenate([rows[n : n + 1], small_in[n : n + 1, 0:96]], axis=0)
        smalls[-1][...] = jnp.concatenate(
            [
                jnp.concatenate([x[8 + c : 9 + c, 0:96] for c in range(4)], axis=1)
                for x in (rows, small_in[...])
            ],
            axis=0,
        )
    else:
        smalls[0][...] = rows
    for copy in copies:
        copy.wait()


def permutation(ctx, fsdp, move):
    return [
        (c * fsdp + f, move(c, f)[0] * fsdp + move(c, f)[1]) for c in range(ctx) for f in range(fsdp)
    ]


def add(*parts):
    total = parts[0].astype(F32)
    for part in parts[1:]:
        total = total + part.astype(F32)
    return total


def on_device_fast(
    activations, cotangent, doc_start, deal,
    attend_in, query_bias, value_bias, attend_out, attend_bias, first_gain, first_shift,
    expand_proj, expand_bias, reduce_proj, reduce_bias, second_gain, second_shift,
    *, ctx, fsdp,
):
    S = [pltpu.SMEM]
    V = [pltpu.VMEM]
    A = [pl.ANY]
    axes = ("ctx", "fsdp")

    def via(move):
        perm = permutation(ctx, fsdp, move)
        return lambda x: lax.ppermute(x, axes, perm)

    via_first = via(lambda c, f: (c ^ (1 + f % 2), f))
    via_second = via(lambda c, f: (c ^ (2 - f % 2), f))
    via_diagonal = via(lambda c, f: (c ^ 3, f))
    via_core = via(lambda c, f: (c, f ^ 1))
    via_z = [None] + [via(lambda c, f, k=k: (c, f ^ (2 * k))) for k in range(1, 4)]

    def exchange_ctx(own, a, b, d):
        return (own, via_first(a), via_second(b), via_diagonal(d))

    def spread_ctx(x):
        return (x, via_first(x), via_second(x), via_diagonal(x))

    def reduce_z(x):
        return lax.psum_scatter(x, "fsdp", scatter_dimension=0, tiled=True, axis_index_groups=zgroups)

    def exchange_z(own, *others):
        return (own,) + tuple(via_z[k + 1](x) for k, x in enumerate(others))

    def gather_ctx(x):
        a, b = via_first(x), via_second(x)
        return (x, a, b, via_second(a))

    heads = HEADS // ctx
    hw = heads * HEAD_DIM
    rows = activations.shape[1]
    tokens = rows * ctx
    cut = WIDTH // fsdp
    c = lax.axis_index("ctx").astype(jnp.int32)
    shard = lax.axis_index("fsdp").astype(jnp.int32)
    core = shard % 2
    zgroups = [[2 * z + k for z in range(fsdp // 2)] for k in range(2)]

    hidden = activations[0]
    gathered = gather_ctx(hidden)
    small = (attend_bias, first_gain, first_shift, reduce_bias, second_gain, second_shift, query_bias, value_bias)
    sent = call(
        prep_kernel,
        [((3 * cut, WIDTH), BF)] * 4,
        (expand_proj, reduce_proj, attend_in, attend_out, expand_bias) + small,
        V * 13,
        [],
        "prep",
        0,
        8 * 1024 * 1024,
    )

    def gather_ffn(x):
        x = lax.all_gather(x, "fsdp", axis=0, tiled=True)
        return x.reshape(fsdp // 2, 2, 3, cut, WIDTH)

    ranks = jnp.arange(ctx, dtype=jnp.int32)
    inv = jnp.sum(jnp.where(deal[None, :] == ranks[:, None], ranks[None, :], 0), axis=1).astype(jnp.int32)
    starts = lax.all_gather(doc_start[0], "ctx", axis=0, tiled=True)
    by_rank = starts.reshape(ctx, 2, BLK)
    chosen = inv[:, None, None, None] == ranks[None, :, None, None]
    by_block = jnp.sum(jnp.where(chosen, by_rank[None], 0), axis=1)
    logical = jnp.concatenate([by_block[:, 0], by_block[::-1, 1]], axis=0).reshape(-1)
    qrow = jnp.broadcast_to(logical[None, :], (8, tokens))
    kcol = jnp.broadcast_to(logical[:, None], (tokens, 128))
    jmin = jnp.min(logical.reshape(tokens // QB, QB), axis=1) // QB

    m1 = 1 + core
    mask = inv ^ c
    jmap = jnp.where((core == 1) & (mask > 0) & (mask < 3), 3 - mask, mask)
    meta = jnp.concatenate(
        [jnp.stack([core, shard, c, c ^ m1, c ^ (3 - m1), c ^ 3]), jmap, inv, jmin]
    ).astype(jnp.int32)

    kept = []
    earlier = ()
    wide = [gather_ffn(sent[0]), gather_ffn(sent[1]), None, None]
    wide[0] = after((wide[0],), starts, *gathered[1:])[0]
    wide[2] = gather_ffn(*after(sent[2:3], wide[0]))
    pieces = []
    for layer in range(LAYERS):
        t, d = wide[2 * layer : 2 * layer + 2]
        mine = half_of(meta, t, *gathered[1:])
        a, b = via_first(mine), via_second(mine)
        qkv, *ctx_own, lse = call(
            functools.partial(attn_fwd_kernel, heads=heads, tokens=tokens),
            [((ctx, rows, 3 * hw), BF)] + [((BLK, 2 * hw), BF)] * 4 + [((8, tokens), F32)],
            (meta,) + gathered + (qrow, kcol, t, mine) + earlier,
            S + V * 6 + A * (2 + len(earlier)),
            attn_fwd_scratch(heads, tokens),
            "attn_fwd",
            2 * tokens * WIDTH * 3 * hw * 4,
            10 * 1024 * 1024,
        )
        cx = exchange_ctx(*ctx_own)
        if layer + 1 < LAYERS:
            wide[3] = gather_ffn(*after(sent[3:4], *cx[1:]))
        pieces.append((t, a, b, d, via_core(pack(a, b, lse))))
        kinds = {
            "xhat": ((rows, WIDTH), F32), "rstd": ((rows, 1), F32), "gp": ((rows, 4 * WIDTH), BF),
            "left": ((rows, 3 * WIDTH), BF), "low": ((rows, WIDTH), BF),
        }
        norms = [kinds[name] for name in ("xhat", "rstd", "gp", "xhat", "rstd")]
        lows = [kinds[name] for name in ("left", "left", "low")]
        back_outs = [((rows, WIDTH), F32), ((rows + 16, 6 * WIDTH), BF), ((ctx, BLK, 2 * hw), BF)]
        if layer + 1 < LAYERS:
            xhat1, rstd1, gp, xhat2, rstd2, l_mine, l_other, hlow, hidden_next = call_writing(
                mlp_fwd_kernel,
                norms + lows + [kinds["xhat"]],
                (meta,) + cx + (hidden,) + pieces[layer],
                S + V * 5 + A * 5,
                mlp_fwd_scratch(rows, hw),
                "mlp_fwd",
                24,
            )
        else:
            xhat1 = rstd1 = gp = xhat2 = rstd2 = None
            l_mine, l_other, hlow, *last_back = call_writing(
                last_kernel,
                lows + back_outs,
                (meta,) + cx + (hidden, cotangent[0]) + pieces[layer],
                S + V * 6 + A * 5,
                [pltpu.VMEM(*kind) for kind in norms] + mlp_fwd_scratch(rows, hw) + [pltpu.VMEM((8, WIDTH), F32)],
                "last",
                36,
            )
        l_other = via_core(l_other)
        earlier = (l_other,)
        kept.append((gathered, qkv, ctx_own, lse, xhat1, rstd1, gp, xhat2, rstd2, l_mine, l_other))
        if layer + 1 < LAYERS:
            hidden = hidden_next
            gathered = gather_ctx(hlow)
    out_act = hlow[None]

    for layer in reversed(range(LAYERS)):
        gathered, qkv, ctx_own, lse, xhat1, rstd1, gp, xhat2, rstd2, l_mine, l_other = kept[layer]
        if layer + 1 == LAYERS:
            gfs, dgg, gctx = last_back
        else:
            gfs, dgg, gctx = call_writing(
                mlp_bwd_kernel,
                back_outs,
                (meta, xhat1, rstd1, xhat2, rstd2, gp) + grads + pieces[layer] + order,
                S + V * (5 + len(grads)) + A * (5 + len(order)),
                mlp_bwd_scratch(),
                "mlp_bwd",
                12,
                parts=len(grads),
            )
        gcx = lax.all_to_all(gctx, "ctx", 0, 0, tiled=True)
        piece = ((4, 2, cut, WIDTH), BF)

        def weight_grads(*before):
            return call_writing(
                wgrad_kernel,
                [piece] * 3 + [((4, cut + 16, WIDTH), BF), piece],
                (meta, l_mine, l_other, dgg, via_core(dgg)) + before,
                S + A * (4 + len(before)),
                wgrad_scratch(),
                "wgrad",
                5,
            )

        def attention_grads(*before):
            return call(
                functools.partial(attn_bwd_kernel, heads=heads, tokens=tokens),
                [
                    ((rows, WIDTH), F32), ((rows, WIDTH), BF), ((rows, WIDTH), BF), ((rows, WIDTH), BF),
                    ((4, cut + 16, 3 * hw), BF), ((4, cut + 16, 3 * hw), BF),
                ],
                (meta,) + gathered + (qrow, kcol, qkv) + tuple(ctx_own) + (gcx, lse, wide[2 * layer]) + before,
                S + V * 13 + A * (1 + len(before)),
                attn_bwd_scratch(heads, tokens),
                "attn_bwd",
                2 * tokens * WIDTH * 3 * hw * 8,
                10 * 1024 * 1024,
            )

        def attention_shards(dwo, dw, crossed, *others):
            shape = (4, cut + 16, WIDTH + 3 * hw)
            (merged,) = call(
                merge_kernel, [(shape, BF)], (dwo, dw, crossed) + others, V * 3 + A * len(others), [], "merge", 0, 0
            )
            return merged, reduce_z(merged).reshape(shape[1:])

        if layer > 0:
            g_own, g_a, g_b, g_d, dw, dw_other = attention_grads(l_other)
            t, a, b, dwo, d = weight_grads(g_d)
            d1 = reduce_z(d)
            over = via_first(sums([[(g_a, via_second(g_d))]])[0])
            merged, att1 = attention_shards(dwo, dw, via_core(dw_other))
            grads = (gfs, g_own, via_second(g_b), over)
            (t1,) = sums([[(t, via_first(a), via_second(b))]])
            order = (t1, merged)
            t1 = reduce_z(t1)
        else:
            t, a, b, dwo, d = weight_grads(gcx, att1)
            a, b = via_first(a), via_second(b)
            d0 = reduce_z(d)
            g_own, g_a, g_b, g_d, dw, dw_other = attention_grads(t, t1, d1)

    def shards(x):
        return x.reshape(2, cut, WIDTH)

    (t0,) = sums([[(t, a, b)]], g_d)
    merged, att0 = attention_shards(dwo, dw, via_core(dw_other), t0)
    t0 = reduce_z(t0)
    back = via_second(g_d), via_second(g_b)
    shape = (2 * cut + 16, 2 * WIDTH)
    (joined,) = call(
        join_kernel, [(shape, BF)], (att1, shards(t1), shards(via_diagonal(d1)), merged), V * 3 + A, [], "join", 0, 0
    )
    (over,) = sums([[(g_a, back[0])]], joined)
    joined = spread_ctx(joined)
    (ffn0,) = sums([[(shards(t0), shards(via_diagonal(d0)))]], over)
    over = via_first(over)

    small_out = None
    placed = []
    for layer in reversed(range(LAYERS)):
        if layer == 0:
            sent = spread_ctx(ffn0) + spread_ctx(att0)
            waits = ()
        else:
            sent = joined
            waits = (ffn0,)
        last = layer == 0
        big = [
            ((LAYERS, cut, 4 * WIDTH), F32), ((LAYERS, 4 * cut, WIDTH), F32),
            ((LAYERS, cut, 3 * WIDTH), F32), ((LAYERS, cut, WIDTH), F32),
        ]
        if last:
            smalls = [((LAYERS, cut), F32)] * 8 + [((LAYERS, 4 * cut), F32)]
        else:
            smalls = [((16, cut), F32)]
        args = (meta,) + sent + ((small_out,) + tuple(placed) if last else waits)
        spaces = S + V * len(sent) + (V + A * 4 if last else A)
        outs = pl.pallas_call(
            functools.partial(place_kernel, layer=layer, last=last),
            out_shape=[jax.ShapeDtypeStruct(shape, dtype) for shape, dtype in big + smalls],
            in_specs=[pl.BlockSpec(memory_space=space) for space in spaces],
            out_specs=[pl.BlockSpec(memory_space=space) for space in A * 4 + V * len(smalls)],
            scratch_shapes=[
                pltpu.VMEM((ctx, cut, WIDTH), F32), pltpu.VMEM((ctx, cut, 3 * hw), F32),
                pltpu.VMEM((ctx, 16, 3 * hw), F32),
                pltpu.VMEM((cut, 4 * WIDTH), F32), pltpu.VMEM((4 * cut, WIDTH), F32),
                pltpu.VMEM((cut, 3 * WIDTH), F32), pltpu.VMEM((cut, WIDTH), F32),
                pltpu.VMEM((16, 128), F32), pltpu.VMEM((8, 128), F32),
                pltpu.SemaphoreType.DMA((4,)),
            ],
            input_output_aliases={10 + n: n for n in range(4)} if last else {},
            compiler_params=pltpu.CompilerParams(vmem_limit_bytes=VMEM_LIMIT),
            cost_estimate=pl.CostEstimate(flops=0, bytes_accessed=10 * 1024 * 1024, transcendentals=0),
            name="place",
        )(*args)
        placed = outs[:4]
        small_out = outs[4]
        vectors = outs[4:]
    in_grad = add(gfs, g_own, back[1], over)[None]
    e_out, r_out, i_out, o_out = placed
    ab, fg, fs, rb, sg, ss, qb, vb, xb = vectors
    return (out_act, in_grad, i_out, qb, vb, o_out, ab, fg, fs, e_out, xb, r_out, rb, sg, ss)


def on_device(*args, ctx, fsdp):
    if ctx == 4 and fsdp == 8 and args[0].shape[1] == 2 * BLK:
        return on_device_fast(*args, ctx=ctx, fsdp=fsdp)
    return on_device_plain(*args)


def solution(mesh):
    placed = (
        P("fsdp", "ctx", None),
        P("fsdp", "ctx", None),
        P("fsdp", "ctx"),
        P(),
        P(None, "fsdp", None),
        P(None, "fsdp"),
        P(None, "fsdp"),
        P(None, "fsdp", None),
        P(None, "fsdp"),
        P(None, "fsdp"),
        P(None, "fsdp"),
        P(None, "fsdp", None),
        P(None, "fsdp"),
        P(None, "fsdp", None),
        P(None, "fsdp"),
        P(None, "fsdp"),
        P(None, "fsdp"),
    )
    return jax.shard_map(
        functools.partial(on_device, ctx=mesh.shape["ctx"], fsdp=mesh.shape["fsdp"]),
        mesh=mesh,
        in_specs=placed,
        out_specs=(
            P("fsdp", "ctx", None),
            P("fsdp", "ctx", None),
            P(None, "fsdp", None),
            P(None, "fsdp"),
            P(None, "fsdp"),
            P(None, "fsdp", None),
            P(None, "fsdp"),
            P(None, "fsdp"),
            P(None, "fsdp"),
            P(None, "fsdp", None),
            P(None, "fsdp"),
            P(None, "fsdp", None),
            P(None, "fsdp"),
            P(None, "fsdp"),
            P(None, "fsdp"),
        ),
        check_vma=False,
    )
```

```python
import functools

import jax
import jax.numpy as jnp
from jax import lax
from jax.experimental import pallas as pl
from jax.experimental.pallas import tpu as pltpu
from jax.sharding import PartitionSpec as P

HEADS = 12
HEAD_DIM = 64
LAYERS = 2
BLK = 192


norm_eps = 1e-05


def for_sending(x):
    return jax.tree.map(lambda a: a.astype(jnp.bfloat16) if a.dtype == jnp.float32 else a, x)


def layer_norm(values, gain, shift):
    centre = values - jnp.mean(values, axis=-1, keepdims=True)
    spread = jnp.mean(centre * centre, axis=-1, keepdims=True)
    return centre * lax.rsqrt(spread + norm_eps) * gain + shift


def gelu_exact(inputs):
    return 0.5 * inputs * (1.0 + jax.scipy.special.erf(inputs * 0.7071067811865476))


def key_positions(deal):
    pairs = deal.shape[0]
    offsets = jnp.arange(BLK, dtype=jnp.int32)
    first = deal[:, None] * BLK + offsets[None, :]
    second = (2 * pairs - 1 - deal)[:, None] * BLK + offsets[None, :]
    return jnp.concatenate([first, second], axis=1).reshape(-1)


def split_heads(matrix):
    return matrix.reshape(matrix.shape[0], HEADS, HEAD_DIM).transpose(1, 0, 2)


def join_heads(stacked):
    return stacked.transpose(1, 0, 2).reshape(stacked.shape[1], HEADS * HEAD_DIM)


def attend_forward(queries, keys_full, values_full, allowed):

    def one_head(items):
        head_q, head_k, head_v = items
        scores = jnp.einsum(
            "qd,kd->qk", head_q, head_k, preferred_element_type=jnp.float32
        ) * HEAD_DIM ** (-0.5)
        scores = jnp.where(allowed, scores, -1e30)
        top = jnp.max(scores, axis=-1, keepdims=True)
        weights = jnp.exp(scores - top)
        total = jnp.sum(weights, axis=-1, keepdims=True)
        probs = (weights / total).astype(jnp.bfloat16)
        output = jnp.einsum("qk,kd->qd", probs, head_v, preferred_element_type=jnp.float32)
        return (output, top[:, 0] + jnp.log(total[:, 0]))

    outputs, log_totals = lax.map(
        one_head, (split_heads(queries), split_heads(keys_full), split_heads(values_full))
    )
    return (join_heads(outputs), log_totals)


def attend_backward(queries, keys_full, values_full, log_totals, grad_context, allowed):

    def one_head(items):
        head_q, head_k, head_v, head_lse, head_grad = items
        scores = jnp.einsum(
            "qd,kd->qk", head_q, head_k, preferred_element_type=jnp.float32
        ) * HEAD_DIM ** (-0.5)
        scores = jnp.where(allowed, scores, -1e30)
        probs = jnp.exp(scores - head_lse[:, None])
        grad_probs = jnp.einsum("qd,kd->qk", head_grad, head_v, preferred_element_type=jnp.float32)
        inner_sum = jnp.sum(probs * grad_probs, axis=-1, keepdims=True)
        grad_scores = (probs * (grad_probs - inner_sum)).astype(jnp.bfloat16)
        grad_q = jnp.einsum(
            "qk,kd->qd", grad_scores, head_k, preferred_element_type=jnp.float32
        ) * HEAD_DIM ** (-0.5)
        grad_k = jnp.einsum(
            "qk,qd->kd", grad_scores, head_q, preferred_element_type=jnp.float32
        ) * HEAD_DIM ** (-0.5)
        grad_v = jnp.einsum(
            "qk,qd->kd", probs.astype(jnp.bfloat16), head_grad, preferred_element_type=jnp.float32
        )
        return (grad_q, grad_k, grad_v)

    grads = lax.map(
        one_head,
        (
            split_heads(queries),
            split_heads(keys_full),
            split_heads(values_full),
            log_totals,
            split_heads(grad_context),
        ),
    )
    return (join_heads(grads[0]), join_heads(grads[1]), join_heads(grads[2]))


def forward_layer(hidden, weights, allowed):
    (
        attend_in,
        query_bias,
        value_bias,
        attend_out,
        attend_bias,
        first_gain,
        first_shift,
        expand_proj,
        expand_bias,
        reduce_proj,
        reduce_bias,
        second_gain,
        second_shift,
    ) = weights
    width = hidden.shape[1]
    low_hidden = hidden.astype(jnp.bfloat16)
    projected = jnp.dot(low_hidden, attend_in, preferred_element_type=jnp.float32)
    queries = (projected[:, :width] + query_bias.astype(jnp.float32)).astype(jnp.bfloat16)
    keys_own = projected[:, width : 2 * width].astype(jnp.bfloat16)
    values_own = (projected[:, 2 * width :] + value_bias.astype(jnp.float32)).astype(jnp.bfloat16)
    keys_full, values_full = (
        lax.all_gather(keys_own, "ctx", axis=0, tiled=True),
        lax.all_gather(values_own, "ctx", axis=0, tiled=True),
    )
    context, log_totals = attend_forward(queries, keys_full, values_full, allowed)
    low_context = context.astype(jnp.bfloat16)
    branch = jnp.dot(
        low_context, attend_out, preferred_element_type=jnp.float32
    ) + attend_bias.astype(jnp.float32)
    first_sum = hidden + branch
    normed = layer_norm(first_sum, first_gain.astype(jnp.float32), first_shift.astype(jnp.float32))
    low_normed = normed.astype(jnp.bfloat16)
    inner_pre = jnp.dot(
        low_normed, expand_proj, preferred_element_type=jnp.float32
    ) + expand_bias.astype(jnp.float32)
    active = gelu_exact(inner_pre).astype(jnp.bfloat16)
    output_branch = jnp.dot(
        active, reduce_proj, preferred_element_type=jnp.float32
    ) + reduce_bias.astype(jnp.float32)
    second_sum = normed + output_branch
    output = layer_norm(
        second_sum, second_gain.astype(jnp.float32), second_shift.astype(jnp.float32)
    )
    saved = (
        low_hidden,
        queries,
        keys_full,
        values_full,
        log_totals,
        low_context,
        first_sum,
        low_normed,
        inner_pre,
        active,
        second_sum,
    )
    return (output, saved)


def column_sum(matrix):
    return jnp.sum(matrix.astype(jnp.float32), axis=0)


def backward_layer(grad_hidden, weights, saved, allowed):
    (
        attend_in,
        query_bias,
        value_bias,
        attend_out,
        attend_bias,
        first_gain,
        first_shift,
        expand_proj,
        expand_bias,
        reduce_proj,
        reduce_bias,
        second_gain,
        second_shift,
    ) = weights
    (
        low_hidden,
        queries,
        keys_full,
        values_full,
        log_totals,
        low_context,
        first_sum,
        low_normed,
        inner_pre,
        active,
        second_sum,
    ) = saved
    width = low_hidden.shape[1]
    second_pull = jax.vjp(
        layer_norm, second_sum, second_gain.astype(jnp.float32), second_shift.astype(jnp.float32)
    )[1]
    grad_second_sum, grad_second_gain, grad_second_shift = second_pull(grad_hidden)
    grad_branch = grad_second_sum.astype(jnp.bfloat16)
    grad_reduce_bias = column_sum(grad_branch)
    grad_reduce = jnp.einsum("tf,td->fd", active, grad_branch, preferred_element_type=jnp.float32)
    grad_active = jnp.einsum(
        "td,fd->tf", grad_branch, reduce_proj, preferred_element_type=jnp.float32
    )
    gelu_pull = jax.vjp(gelu_exact, inner_pre)[1]
    grad_inner = gelu_pull(grad_active)[0].astype(jnp.bfloat16)
    grad_expand_bias = column_sum(grad_inner)
    grad_expand = jnp.einsum(
        "td,tf->df", low_normed, grad_inner, preferred_element_type=jnp.float32
    )
    grad_normed = grad_second_sum + jnp.einsum(
        "tf,df->td", grad_inner, expand_proj, preferred_element_type=jnp.float32
    )
    first_pull = jax.vjp(
        layer_norm, first_sum, first_gain.astype(jnp.float32), first_shift.astype(jnp.float32)
    )[1]
    grad_first_sum, grad_first_gain, grad_first_shift = first_pull(grad_normed)
    grad_attn = grad_first_sum.astype(jnp.bfloat16)
    grad_attend_bias = column_sum(grad_attn)
    grad_attend_out = jnp.einsum(
        "td,te->de", low_context, grad_attn, preferred_element_type=jnp.float32
    )
    grad_context = jnp.einsum(
        "te,de->td", grad_attn, attend_out, preferred_element_type=jnp.float32
    ).astype(jnp.bfloat16)
    grad_queries, grad_keys_full, grad_values_full = attend_backward(
        queries, keys_full, values_full, log_totals, grad_context, allowed
    )
    grad_keys, grad_values = (
        lax.psum_scatter(
            grad_keys_full.astype(jnp.bfloat16), "ctx", scatter_dimension=0, tiled=True
        ).astype(jnp.float32),
        lax.psum_scatter(
            grad_values_full.astype(jnp.bfloat16), "ctx", scatter_dimension=0, tiled=True
        ).astype(jnp.float32),
    )
    grad_proj = jnp.concatenate(
        [
            grad_queries.astype(jnp.bfloat16),
            grad_keys.astype(jnp.bfloat16),
            grad_values.astype(jnp.bfloat16),
        ],
        axis=1,
    )
    grad_query_bias = column_sum(grad_proj[:, :width])
    grad_value_bias = column_sum(grad_proj[:, 2 * width :])
    grad_attend_in = jnp.einsum(
        "td,te->de", low_hidden, grad_proj, preferred_element_type=jnp.float32
    )
    grad_input = grad_first_sum + jnp.einsum(
        "te,de->td", grad_proj, attend_in, preferred_element_type=jnp.float32
    )
    grads = (
        grad_attend_in,
        grad_query_bias,
        grad_value_bias,
        grad_attend_out,
        grad_attend_bias,
        grad_first_gain,
        grad_first_shift,
        grad_expand,
        grad_expand_bias,
        grad_reduce,
        grad_reduce_bias,
        grad_second_gain,
        grad_second_shift,
    )
    return (grad_input, grads)


def reduce_grads(grads):
    shards = (
        lax.psum_scatter(
            grads[0].astype(jnp.bfloat16), "fsdp", scatter_dimension=0, tiled=True
        ).astype(jnp.float32),
        lax.psum_scatter(
            grads[1].astype(jnp.bfloat16), "fsdp", scatter_dimension=0, tiled=True
        ).astype(jnp.float32),
        lax.psum_scatter(
            grads[2].astype(jnp.bfloat16), "fsdp", scatter_dimension=0, tiled=True
        ).astype(jnp.float32),
        lax.psum_scatter(
            grads[3].astype(jnp.bfloat16), "fsdp", scatter_dimension=0, tiled=True
        ).astype(jnp.float32),
        lax.psum_scatter(
            grads[4].astype(jnp.bfloat16), "fsdp", scatter_dimension=0, tiled=True
        ).astype(jnp.float32),
        lax.psum_scatter(
            grads[5].astype(jnp.bfloat16), "fsdp", scatter_dimension=0, tiled=True
        ).astype(jnp.float32),
        lax.psum_scatter(
            grads[6].astype(jnp.bfloat16), "fsdp", scatter_dimension=0, tiled=True
        ).astype(jnp.float32),
        lax.psum_scatter(
            grads[7].astype(jnp.bfloat16), "fsdp", scatter_dimension=0, tiled=True
        ).astype(jnp.float32),
        lax.psum_scatter(
            grads[8].astype(jnp.bfloat16), "fsdp", scatter_dimension=0, tiled=True
        ).astype(jnp.float32),
        lax.psum_scatter(
            grads[9].astype(jnp.bfloat16), "fsdp", scatter_dimension=0, tiled=True
        ).astype(jnp.float32),
        lax.psum_scatter(
            grads[10].astype(jnp.bfloat16), "fsdp", scatter_dimension=0, tiled=True
        ).astype(jnp.float32),
        lax.psum_scatter(
            grads[11].astype(jnp.bfloat16), "fsdp", scatter_dimension=0, tiled=True
        ).astype(jnp.float32),
        lax.psum_scatter(
            grads[12].astype(jnp.bfloat16), "fsdp", scatter_dimension=0, tiled=True
        ).astype(jnp.float32),
    )
    return (
        lax.psum(shards[0].astype(jnp.bfloat16), "ctx").astype(jnp.float32),
        lax.psum(shards[1].astype(jnp.bfloat16), "ctx").astype(jnp.float32),
        lax.psum(shards[2].astype(jnp.bfloat16), "ctx").astype(jnp.float32),
        lax.psum(shards[3].astype(jnp.bfloat16), "ctx").astype(jnp.float32),
        lax.psum(shards[4].astype(jnp.bfloat16), "ctx").astype(jnp.float32),
        lax.psum(shards[5].astype(jnp.bfloat16), "ctx").astype(jnp.float32),
        lax.psum(shards[6].astype(jnp.bfloat16), "ctx").astype(jnp.float32),
        lax.psum(shards[7].astype(jnp.bfloat16), "ctx").astype(jnp.float32),
        lax.psum(shards[8].astype(jnp.bfloat16), "ctx").astype(jnp.float32),
        lax.psum(shards[9].astype(jnp.bfloat16), "ctx").astype(jnp.float32),
        lax.psum(shards[10].astype(jnp.bfloat16), "ctx").astype(jnp.float32),
        lax.psum(shards[11].astype(jnp.bfloat16), "ctx").astype(jnp.float32),
        lax.psum(shards[12].astype(jnp.bfloat16), "ctx").astype(jnp.float32),
    )


def layer_slices(sharded, layer_index):
    return tuple((tensor[layer_index] for tensor in sharded))


def on_device_plain(
    activations,
    cotangent,
    doc_start,
    deal,
    attend_in,
    query_bias,
    value_bias,
    attend_out,
    attend_bias,
    first_gain,
    first_shift,
    expand_proj,
    expand_bias,
    reduce_proj,
    reduce_bias,
    second_gain,
    second_shift,
):
    sharded = (
        attend_in,
        query_bias,
        value_bias,
        attend_out,
        attend_bias,
        first_gain,
        first_shift,
        expand_proj,
        expand_bias,
        reduce_proj,
        reduce_bias,
        second_gain,
        second_shift,
    )
    row_count = activations.shape[1]
    positions = key_positions(deal)
    own_rank = lax.axis_index("ctx")
    own_positions = lax.dynamic_slice_in_dim(positions, own_rank * row_count, row_count)
    own_starts = doc_start[0]
    key_starts = lax.all_gather(own_starts, "ctx", axis=0, tiled=True)
    allowed = (positions[None, :] <= own_positions[:, None]) & (
        key_starts[None, :] == own_starts[:, None]
    )
    hidden = activations[0].astype(jnp.float32)
    kept_weights = []
    kept_saved = []
    for layer_index in range(LAYERS):
        weights = lax.all_gather(
            for_sending(layer_slices(sharded, layer_index)), "fsdp", axis=0, tiled=True
        )
        hidden, saved = forward_layer(hidden, weights, allowed)
        kept_weights.append(weights)
        kept_saved.append(saved)
    out_act = hidden.astype(jnp.bfloat16)[None]
    grad_hidden = cotangent[0].astype(jnp.float32)
    reduced = [None] * LAYERS
    for layer_index in reversed(range(LAYERS)):
        weights = lax.all_gather(
            for_sending(layer_slices(sharded, layer_index)), "fsdp", axis=0, tiled=True
        )
        grad_hidden, grads = backward_layer(grad_hidden, weights, kept_saved[layer_index], allowed)
        reduced[layer_index] = reduce_grads(grads)
    stacked = [
        jnp.stack([reduced[layer_index][member] for layer_index in range(LAYERS)])
        for member in range(13)
    ]
    return (
        out_act,
        grad_hidden[None],
        stacked[0],
        stacked[1],
        stacked[2],
        stacked[3],
        stacked[4],
        stacked[5],
        stacked[6],
        stacked[7],
        stacked[8],
        stacked[9],
        stacked[10],
        stacked[11],
        stacked[12],
    )


F32 = jnp.float32
BF = jnp.bfloat16
WIDTH = HEADS * HEAD_DIM
QB = 256
SCORE_SCALE = HEAD_DIM ** (-0.5) * 1.4426950408889634
NEG = -1e30
VMEM_LIMIT = 60 * 1024 * 1024


def mm_nn(a, b):
    return lax.dot_general(a, b, (((1,), (0,)), ((), ())), preferred_element_type=F32)


def mm_nt(a, b):
    return lax.dot_general(a, b, (((1,), (1,)), ((), ())), preferred_element_type=F32)


def mm_tn(a, b):
    return lax.dot_general(a, b, (((0,), (0,)), ((), ())), preferred_element_type=F32)


def call(kernel, outs, args, specs, scratch, name, flops, nbytes):
    return pl.pallas_call(
        kernel,
        out_shape=[jax.ShapeDtypeStruct(shape, dtype) for shape, dtype in outs],
        in_specs=[pl.BlockSpec(memory_space=space) for space in specs],
        out_specs=[pl.BlockSpec(memory_space=pltpu.VMEM) for _ in outs],
        scratch_shapes=scratch,
        compiler_params=pltpu.CompilerParams(vmem_limit_bytes=VMEM_LIMIT),
        cost_estimate=pl.CostEstimate(flops=flops if name in ("sums", "join") else 0, bytes_accessed=0, transcendentals=0),
        name=name,
    )(*args)


def block_of(block, blocks):
    half = 0 if 2 * block < blocks else 1
    return (block if half == 0 else blocks - 1 - block), half


CORE, SHARD, RANK, JMAP, INV, JMIN = 0, 1, 2, 6, 10, 14
SWAPPED = (0, 2, 1, 3)
WEIGHT = 10**11
VEC_AT = 640


def started_copies(sems, *pairs):
    copies = []
    for n, (src, dst) in enumerate(pairs):
        copy = pltpu.make_async_copy(src, dst, sems.at[n])
        copy.start()
        copies.append(copy)
    return copies


def last_kernel(
    writer, places, meta, c0, c1, c2, c3, hid, cot, t, a, b, d, crossed,
    l_mine, l_other, hlow, gfs, dgg, gctx,
    xhat1, rstd1, gp, xhat2, rstd2, e_s, r_s, sems, wo_s, b_s, wo_sems, ctx, eb, eb_s,
):
    loads = (e_s, r_s, sems, wo_s, b_s, wo_sems)
    mlp_fwd_kernel(
        writer, (None,) * 5 + tuple(places[:3]), meta, c0, c1, c2, c3, hid, t, a, b, d, crossed,
        xhat1, rstd1, gp, xhat2, rstd2, l_mine, l_other, hlow, *loads, ctx, eb, finish=False,
    )
    mlp_bwd_kernel(
        writer, places[3:], meta, xhat1, rstd1, xhat2, rstd2, gp, cot, t, a, b, d, crossed,
        gfs, dgg, gctx, *loads, eb_s, parts=1, loaded=True,
    )


class Writer:
    def __init__(self, sems):
        self.sems = sems
        self.copies = []

    def send(self, src, dst, *at):
        if dst is None:
            return
        if at:
            src, dst = src.at[at], dst.at[at]
        copy = pltpu.make_async_copy(src, dst, self.sems.at[len(self.copies)])
        copy.start()
        self.copies.append(copy)

    def finish(self):
        for copy in self.copies:
            copy.wait()


def writing(kernel, outs, copies):
    count = len(outs)

    def run(*refs, scratch, **keys):
        ins, places, rest = refs[: -count - scratch], refs[-count - scratch : -scratch], refs[-scratch:]
        buffers, sems, rest = rest[:count], rest[count], rest[count + 1 :]
        kernel(Writer(sems), places, *ins, *buffers, *rest, **keys)

    return run, [pltpu.VMEM(shape, dtype) for shape, dtype in outs] + [pltpu.SemaphoreType.DMA((copies,))]


def call_writing(kernel, outs, args, specs, scratch, name, copies, **keys):
    run, buffers = writing(kernel, outs, copies)
    scratch = buffers + scratch
    return pl.pallas_call(
        functools.partial(run, scratch=len(scratch), **keys),
        out_shape=[jax.ShapeDtypeStruct(shape, dtype) for shape, dtype in outs],
        in_specs=[pl.BlockSpec(memory_space=space) for space in specs],
        out_specs=[pl.BlockSpec(memory_space=pl.ANY) for _ in outs],
        scratch_shapes=scratch,
        compiler_params=pltpu.CompilerParams(vmem_limit_bytes=VMEM_LIMIT),
        cost_estimate=pl.CostEstimate(flops=0, bytes_accessed=0, transcendentals=0),
        name=name,
    )(*args)


def prep_kernel(
    expand, reduce, attend_in, attend_out, expand_bias, v0, v1, v2, v3, v4, v5, v6, v7,
    t0, d0, t1, d1,
):
    rank = lax.axis_index("ctx")
    cut = expand.shape[1]
    hw = WIDTH // 4
    for layer, (t, d) in enumerate(((t0, d0), (t1, d1))):
        bias = expand_bias[layer : layer + 1, :].astype(F32)
        rows = [v[layer : layer + 1, :].astype(F32) for v in (v0, v1, v2, v3, v4, v5, v6, v7)]
        rows += [bias[:, k * cut : (k + 1) * cut] for k in range(4)]
        rows.append(jnp.zeros((4, cut), F32))
        d[2 * cut :, :] = attend_out[layer]
        t[2 * cut :, 3 * hw :] = jnp.zeros((cut, WIDTH - 3 * hw), BF)
        t[2 * cut : 2 * cut + 16, VEC_AT : VEC_AT + cut] = jnp.concatenate(rows, axis=0).astype(BF)
        for k in range(4):

            @pl.when(rank == k)
            def _():
                for out, at in ((t, k), (d, k ^ 3)):
                    out[0:cut, :] = jnp.concatenate(
                        [
                            expand[layer, :, (2 * z + h) * 4 * cut + at * cut : (2 * z + h) * 4 * cut + (at + 1) * cut]
                            for h in range(2)
                            for z in range(4)
                        ],
                        axis=1,
                    )
                    out[cut : 2 * cut, :] = reduce[layer, at * cut : (at + 1) * cut, :]
                t[2 * cut :, 0 : 3 * hw] = jnp.concatenate(
                    [attend_in[layer, :, n * WIDTH + k * hw : n * WIDTH + (k + 1) * hw] for n in range(3)], axis=1
                )


def nothing_kernel(*refs):
    pass


def after(xs, *others):
    return pl.pallas_call(
        nothing_kernel,
        out_shape=[jax.ShapeDtypeStruct(x.shape, x.dtype) for x in xs],
        in_specs=[pl.BlockSpec(memory_space=pl.ANY)] * (len(xs) + len(others)),
        out_specs=[pl.BlockSpec(memory_space=pl.ANY)] * len(xs),
        input_output_aliases={n: n for n in range(len(xs))},
        cost_estimate=pl.CostEstimate(flops=WEIGHT, bytes_accessed=0, transcendentals=0),
        name="after",
    )(*xs, *others)


def pack_kernel(a, b, *rest):
    out, held, ins, outs = rest[-4:]
    coming = [pltpu.make_async_copy((a, b)[n // 4].at[n % 4], held.at[n // 4, n % 4], ins.at[n]) for n in range(8)]
    going = [pltpu.make_async_copy(held.at[n // 4, n % 4], out.at[n // 4, n % 4], outs.at[n]) for n in range(8)]
    for copy in coming:
        copy.start()
    for arrive, leave in zip(coming, going):
        arrive.wait()
        leave.start()
    for copy in going:
        copy.wait()


def pack(a, b, *others):
    shape = (2,) + a.shape
    return pl.pallas_call(
        pack_kernel,
        out_shape=jax.ShapeDtypeStruct(shape, a.dtype),
        in_specs=[pl.BlockSpec(memory_space=pl.ANY)] * (2 + len(others)),
        out_specs=pl.BlockSpec(memory_space=pl.ANY),
        scratch_shapes=[pltpu.VMEM(shape, a.dtype), pltpu.SemaphoreType.DMA((8,)), pltpu.SemaphoreType.DMA((8,))],
        cost_estimate=pl.CostEstimate(flops=0, bytes_accessed=0, transcendentals=0),
        name="pack",
    )(a, b, *others)


def half_kernel(meta, t, *rest):
    out, held, ins, outs = rest[-4:]
    coming = [pltpu.make_async_copy(t.at[z, meta[CORE], 0:2], held.at[z], ins.at[z]) for z in range(4)]
    going = [pltpu.make_async_copy(held.at[z], out.at[z], outs.at[z]) for z in range(4)]
    for copy in coming:
        copy.start()
    for arrive, leave in zip(coming, going):
        arrive.wait()
        leave.start()
    for copy in going:
        copy.wait()


def half_of(meta, t, *others):
    shape = (4, 2) + t.shape[3:]
    return pl.pallas_call(
        half_kernel,
        out_shape=jax.ShapeDtypeStruct(shape, t.dtype),
        in_specs=[pl.BlockSpec(memory_space=space) for space in [pltpu.SMEM] + [pl.ANY] * (1 + len(others))],
        out_specs=pl.BlockSpec(memory_space=pl.ANY),
        scratch_shapes=[pltpu.VMEM(shape, t.dtype), pltpu.SemaphoreType.DMA((4,)), pltpu.SemaphoreType.DMA((4,))],
        cost_estimate=pl.CostEstimate(flops=0, bytes_accessed=0, transcendentals=0),
        name="half",
    )(meta, t, *others)


def sums_kernel(*refs, layout, count, split):
    outs = refs[-len(layout) :]
    at = 0
    for out, parts in zip(outs, layout):
        lane = 0
        for n in parts:
            total = refs[at][...].astype(F32)
            for ref in refs[at + 1 : at + n]:
                total = total + ref[...].astype(F32)
            at += n
            if split:
                for k in range(len(outs)):
                    outs[k][...] = total[k].astype(BF)
            else:
                out[..., lane : lane + total.shape[-1]] = total.astype(BF)
            lane += total.shape[-1]
        if split:
            break


def sums(outputs, *others, split=0, weight=0):
    args = tuple(x for groups in outputs for group in groups for x in group)
    layout = tuple(tuple(len(group) for group in groups) for groups in outputs)
    if split:
        shapes = [(args[0].shape[1:], BF)] * split
        layout = layout * split
    else:
        shapes = [
            (groups[0][0].shape[:-1] + (sum(group[0].shape[-1] for group in groups),), BF) for groups in outputs
        ]
    return call(
        functools.partial(sums_kernel, layout=layout, count=len(args), split=split),
        shapes, args + others, [pltpu.VMEM] * len(args) + [pl.ANY] * len(others), [], "sums", weight, 0,
    )


def join_kernel(att, t, d, *rest):
    out = rest[-1]
    rows = att.shape[0]
    out[0:rows, 0 : att.shape[1]] = att[...]
    out[0:rows, att.shape[1] :] = jnp.zeros((rows, out.shape[1] - att.shape[1]), BF)
    for k in range(2):
        out[rows:, k * WIDTH : (k + 1) * WIDTH] = (t[k].astype(F32) + d[k].astype(F32)).astype(BF)


def merge_kernel(dwo, own, other, *rest):
    out = rest[-1]
    out[:, :, 0:WIDTH] = dwo[...]
    out[:, :, WIDTH:] = (own[...].astype(F32) + other[...].astype(F32)).astype(BF)


def vectors_of(shards, order):
    return jnp.concatenate([shards[f // 2, f % 2, :, 0:96] for f in order], axis=1).astype(F32)


NATURAL = tuple(range(8))
CORE_MAJOR = (0, 2, 4, 6, 1, 3, 5, 7)


def attn_fwd_kernel(
    meta, h0, h1, h2, h3, qrow, kcol, t, *rest, heads, tokens
):
    qkv, c0, c1, c2, c3, lse, q_s, k_s, vt_s, o_s, ctx, w_s, b_s, sems = rest[-14:]
    blocks = tokens // BLK
    hw = heads * HEAD_DIM
    copies = started_copies(
        sems, (t.at[:, :, 2, :, 0:VEC_AT], w_s), (t.at[:, :, 2, 0:16, VEC_AT : VEC_AT + 128], b_s)
    )
    for copy in copies:
        copy.wait()
    w = w_s[...].reshape(WIDTH, VEC_AT)[:, 0 : 3 * hw]
    vec = vectors_of(b_s, NATURAL)
    bias = jnp.zeros((1, 3 * hw), F32)
    for k in range(4):
        part = jnp.concatenate(
            [vec[6:7, k * hw : (k + 1) * hw], jnp.zeros((1, hw), F32), vec[7:8, k * hw : (k + 1) * hw]], axis=1
        )
        bias = jnp.where(meta[RANK] == k, part, bias)
    for j, piece in enumerate((h0, h1, h2, h3)):
        qkv[j] = (mm_nn(piece[...], w) + bias).astype(BF)
    for pair in range(blocks // 2):
        rows = []
        for block in (2 * pair, 2 * pair + 1):
            at, half = block_of(block, blocks)
            rows.append(qkv[meta[JMAP + at], half * BLK : (half + 1) * BLK, :])
        both = jnp.concatenate(rows, axis=0)
        lo, hi = 2 * pair * BLK, 2 * (pair + 1) * BLK
        for h in range(heads):
            q_s[h, lo:hi, :] = both[:, h * HEAD_DIM : (h + 1) * HEAD_DIM]
            k_s[h, lo:hi, :] = both[:, hw + h * HEAD_DIM : hw + (h + 1) * HEAD_DIM]
        vt_s[:, lo:hi] = both[:, 2 * hw :].T
    iota_k = lax.broadcasted_iota(jnp.int32, (QB, QB), 0)
    iota_q = lax.broadcasted_iota(jnp.int32, (QB, QB), 1)
    causal = iota_k <= iota_q
    head_rows = [slice(h * HEAD_DIM, (h + 1) * HEAD_DIM) for h in range(heads)]
    for i in range(tokens // QB):
        lo = i * QB
        starts_q = qrow[0:1, lo : lo + QB]

        def scores(at, diagonal):
            col = kcol[pl.ds(at, QB), :]
            allowed = jnp.concatenate([col, col], axis=1) == starts_q
            if diagonal:
                allowed = allowed & causal
            return [
                jnp.where(allowed, mm_nt(k_s[h, pl.ds(at, QB), :], q_s[h, lo : lo + QB, :]) * SCORE_SCALE, NEG)
                for h in range(heads)
            ]

        ss = scores(lo, True)
        tops = [jnp.max(s, axis=0, keepdims=True) for s in ss]
        ps = [jnp.exp2(s - top) for s, top in zip(ss, tops)]
        totals = [jnp.sum(p, axis=0, keepdims=True) for p in ps]
        outs = [mm_nn(vt_s[head_rows[h], lo : lo + QB], ps[h].astype(BF)) for h in range(heads)]

        def step(jb, carry):
            tops, totals, outs = carry
            at = pl.multiple_of(jb * QB, QB)
            ss = scores(at, False)
            new = [jnp.maximum(top, jnp.max(s, axis=0, keepdims=True)) for s, top in zip(ss, tops)]
            ps = [jnp.exp2(s - top) for s, top in zip(ss, new)]
            alphas = [jnp.exp2(top - n) for top, n in zip(tops, new)]
            totals = [
                total * alpha + jnp.sum(p, axis=0, keepdims=True) for total, alpha, p in zip(totals, alphas, ps)
            ]
            outs = [
                outs[h] * alphas[h] + mm_nn(vt_s[head_rows[h], pl.ds(at, QB)], ps[h].astype(BF)) for h in range(heads)
            ]
            return new, totals, outs

        if i > 0:
            tops, totals, outs = lax.fori_loop(meta[JMIN + i], i, step, (tops, totals, outs))
        for h in range(heads):
            o_s[head_rows[h], lo : lo + QB] = outs[h] / totals[h]
            lse[h : h + 1, lo : lo + QB] = tops[h] + jnp.log2(totals[h])
    for pair in range(blocks // 2):
        lo, hi = 2 * pair * BLK, 2 * (pair + 1) * BLK
        both = o_s[:, lo:hi].T.astype(BF)
        for n, block in enumerate((2 * pair, 2 * pair + 1)):
            at, half = block_of(block, blocks)
            ctx[meta[JMAP + at], :, half * hw : (half + 1) * hw] = both[n * BLK : (n + 1) * BLK, :]
    for j, out in enumerate((c0, c1, c2, c3)):
        out[...] = ctx[j]


def attn_bwd_kernel(
    meta, h0, h1, h2, h3, qrow, kcol, qkv, c0, c1, c2, c3, gctx, lse, t, *rest, heads, tokens
):
    (
        g_own, g_a, g_b, g_d, dw_own, dw_other, q_s, k_s, v_s, do_s, kt_s, delta_s, dk_s, dv_s, dqt_s, g_s, w_s, ctx, dw, sems,
    ) = rest[-20:]
    blocks = tokens // BLK
    hw = heads * HEAD_DIM
    scale = HEAD_DIM ** (-0.5)
    copies = started_copies(sems, (t.at[:, :, 2, :, 0:VEC_AT], w_s))
    for j, c in enumerate((c0, c1, c2, c3)):
        ctx[j] = c[...]
    for pair in range(blocks // 2):
        rows, grads, outs = [], [], []
        for block in (2 * pair, 2 * pair + 1):
            at, half = block_of(block, blocks)
            rows.append(qkv[meta[JMAP + at], half * BLK : (half + 1) * BLK, :])
            grads.append(gctx[meta[INV + at], :, half * hw : (half + 1) * hw])
            outs.append(ctx[meta[JMAP + at], :, half * hw : (half + 1) * hw])
        both = jnp.concatenate(rows, axis=0)
        grad = jnp.concatenate(grads, axis=0)
        out = jnp.concatenate(outs, axis=0)
        lo, hi = 2 * pair * BLK, 2 * (pair + 1) * BLK
        prod = (grad.astype(F32) * out.astype(F32)).T
        kt_s[:, lo:hi] = both[:, hw : 2 * hw].T
        for h in range(heads):
            c0, c1 = h * HEAD_DIM, (h + 1) * HEAD_DIM
            q_s[h, lo:hi, :] = both[:, c0:c1]
            k_s[h, lo:hi, :] = both[:, hw + c0 : hw + c1]
            v_s[h, lo:hi, :] = both[:, 2 * hw + c0 : 2 * hw + c1]
            do_s[h, lo:hi, :] = grad[:, c0:c1]
            delta_s[h : h + 1, lo:hi] = jnp.sum(prod[c0:c1, :], axis=0, keepdims=True)
    dk_s[...] = jnp.zeros_like(dk_s)
    dv_s[...] = jnp.zeros_like(dv_s)
    iota_k = lax.broadcasted_iota(jnp.int32, (QB, QB), 0)
    iota_q = lax.broadcasted_iota(jnp.int32, (QB, QB), 1)
    causal = iota_k <= iota_q
    head_rows = [slice(h * HEAD_DIM, (h + 1) * HEAD_DIM) for h in range(heads)]
    for i in range(tokens // QB):
        lo = i * QB
        starts_q = qrow[0:1, lo : lo + QB]

        def block(at, diagonal):
            col = kcol[pl.ds(at, QB), :]
            allowed = jnp.concatenate([col, col], axis=1) == starts_q
            if diagonal:
                allowed = allowed & causal
            dqs = []
            for h in range(heads):
                q, do = q_s[h, lo : lo + QB, :], do_s[h, lo : lo + QB, :]
                s = mm_nt(k_s[h, pl.ds(at, QB), :], q) * SCORE_SCALE
                p = jnp.exp2(jnp.where(allowed, s, NEG) - lse[h : h + 1, lo : lo + QB])
                dp = mm_nt(v_s[h, pl.ds(at, QB), :], do)
                ds = (p * (dp - delta_s[h : h + 1, lo : lo + QB])).astype(BF)
                dv_s[h, pl.ds(at, QB), :] += mm_nn(p.astype(BF), do)
                dk_s[h, pl.ds(at, QB), :] += mm_nn(ds, q)
                dqs.append(mm_nn(kt_s[head_rows[h], pl.ds(at, QB)], ds))
            return dqs

        dqs = block(lo, True)
        if i > 0:
            dqs = lax.fori_loop(
                meta[JMIN + i],
                i,
                lambda jb, acc: [x + y for x, y in zip(acc, block(pl.multiple_of(jb * QB, QB), False))],
                dqs,
            )
        for h in range(heads):
            dqt_s[head_rows[h], lo : lo + QB] = dqs[h] * scale
    for pair in range(blocks // 2):
        lo, hi = 2 * pair * BLK, 2 * (pair + 1) * BLK
        parts = [dqt_s[:, lo:hi].T.astype(BF)]
        parts += [(dk_s[h, lo:hi, :] * scale).astype(BF) for h in range(heads)]
        parts += [dv_s[h, lo:hi, :].astype(BF) for h in range(heads)]
        both = jnp.concatenate(parts, axis=1)
        for n, block_at in enumerate((2 * pair, 2 * pair + 1)):
            at, half = block_of(block_at, blocks)
            g_s[meta[JMAP + at], half * BLK : (half + 1) * BLK, :] = both[n * BLK : (n + 1) * BLK, :]
    for copy in copies:
        copy.wait()
    w = w_s[...].reshape(WIDTH, VEC_AT)[:, 0 : 3 * hw]
    total = None
    sums = None
    for j, piece in enumerate((h0, h1, h2, h3)):
        g = g_s[j]
        back = mm_nt(g, w)
        if j == 0:
            g_own[...] = back
        else:
            (g_a, g_b, g_d)[j - 1][...] = back.astype(BF)
        part = mm_tn(piece[...], g)
        col = jnp.sum(g.astype(F32), axis=0, keepdims=True)
        total = part if total is None else total + part
        sums = col if sums is None else sums + col
    shards, rows_out, cols = dw.shape
    rows = WIDTH // shards
    dw[:, 0:rows, :] = total.reshape(shards, rows, cols).astype(BF)
    dw[:, rows:, :] = jnp.broadcast_to(sums[None], (shards, rows_out - rows, cols)).astype(BF)
    for k in range(4):
        dw_own[k] = dw[2 * k + meta[CORE]]
        dw_other[k] = dw[2 * k + 1 - meta[CORE]]


def start_ffn_copies(core, t, a, b, d, crossed, e_s, r_s, sems):
    ca, cb = crossed.at[0], crossed.at[1]
    groups = []
    for p, parts in enumerate(((t,), (a, cb), (b, ca), (d,))):
        pairs = []
        if len(parts) == 1:
            pairs.append((parts[0].at[:, :, 0], e_s.at[p]))
            for h in range(2):
                pairs.append((parts[0].at[:, h, 1], r_s.at[p, h]))
        else:
            for src, parity in ((parts[0], core), (parts[1], 1 - core)):
                pairs.append((src.at[:, 0], e_s.at[p, :, parity]))
                pairs.append((src.at[:, 1], r_s.at[p, parity]))
        group = []
        for n, (src, dst) in enumerate(pairs):
            copy = pltpu.make_async_copy(src, dst, sems.at[p, n])
            copy.start()
            group.append(copy)
        groups.append(group)
    return groups


def ffn_scratch():
    return [
        pltpu.VMEM((4, 4, 2, 96, WIDTH), BF),
        pltpu.VMEM((4, 2, 4, 96, WIDTH), BF),
        pltpu.SemaphoreType.DMA((4, 4)),
        pltpu.VMEM((4, 2, 96, WIDTH), BF),
        pltpu.VMEM((4, 2, 16, 128), BF),
        pltpu.SemaphoreType.DMA((2,)),
    ]


def mlp_fwd_scratch(rows, hw):
    return ffn_scratch() + [pltpu.VMEM((4, rows, hw), BF), pltpu.VMEM((8, WIDTH), F32)]


def mlp_bwd_scratch():
    return ffn_scratch() + [pltpu.VMEM((8, WIDTH), F32)]


def wgrad_scratch():
    rows = 2 * BLK
    return [
        pltpu.VMEM((rows, 3 * WIDTH), BF),
        pltpu.VMEM((rows, 3 * WIDTH), BF),
        pltpu.VMEM((rows + 16, 6 * WIDTH), BF),
        pltpu.VMEM((rows + 16, 6 * WIDTH), BF),
        pltpu.SemaphoreType.DMA((16,)),
    ]


def attn_fwd_scratch(heads, tokens):
    hw = heads * HEAD_DIM
    return [
        pltpu.VMEM((heads, tokens, HEAD_DIM), BF),
        pltpu.VMEM((heads, tokens, HEAD_DIM), BF),
        pltpu.VMEM((hw, tokens), BF),
        pltpu.VMEM((hw, tokens), F32),
        pltpu.VMEM((4, BLK, 2 * hw), BF),
        pltpu.VMEM((4, 2, 96, VEC_AT), BF),
        pltpu.VMEM((4, 2, 16, 128), BF),
        pltpu.SemaphoreType.DMA((2,)),
    ]


def attn_bwd_scratch(heads, tokens):
    hw = heads * HEAD_DIM
    return [pltpu.VMEM((heads, tokens, HEAD_DIM), BF)] * 4 + [
        pltpu.VMEM((hw, tokens), BF),
        pltpu.VMEM((8, tokens), F32),
        pltpu.VMEM((heads, tokens, HEAD_DIM), F32),
        pltpu.VMEM((heads, tokens, HEAD_DIM), F32),
        pltpu.VMEM((hw, tokens), F32),
        pltpu.VMEM((4, tokens // 4, 3 * hw), BF),
        pltpu.VMEM((4, 2, 96, VEC_AT), BF),
        pltpu.VMEM((4, BLK, 2 * hw), BF),
        pltpu.VMEM((8, 112, 3 * hw), BF),
        pltpu.SemaphoreType.DMA((1,)),
    ]


def norm_parts(values):
    centre = values - jnp.mean(values, axis=-1, keepdims=True)
    spread = jnp.mean(centre * centre, axis=-1, keepdims=True)
    rstd = lax.rsqrt(spread + norm_eps)
    return centre * rstd, rstd


def shard_columns(x, parity):
    return jnp.concatenate([x[:, (2 * z + parity) * 96 : (2 * z + parity + 1) * 96] for z in range(4)], axis=1)


def mlp_fwd_kernel(
    writer, places, meta, c0, c1, c2, c3, hid, t, a, b, d, crossed,
    xhat1, rstd1, gp, xhat2, rstd2, l_mine, l_other, hlow, *rest, finish=True,
):
    hnext, (e_s, r_s, sems, wo_s, b_s, wo_sems, ctx, eb) = rest[:-8], rest[-8:]
    core = meta[CORE]
    xhat1_to, rstd1_to, gp_to, xhat2_to, rstd2_to, mine_to, other_to, hlow_to = places[:8]
    wo_copies = started_copies(
        wo_sems, (d.at[:, :, 2], wo_s), (t.at[:, :, 2, 0:16, VEC_AT : VEC_AT + 128], b_s)
    )
    copies = start_ffn_copies(core, t, a, b, d, crossed, e_s, r_s, sems)
    half_cols = WIDTH // 2
    hw = c0.shape[1] // 2
    for p, piece in enumerate((c0, c1, c2, c3)):
        for half in range(2):
            ctx[meta[RANK + p], half * BLK : (half + 1) * BLK, :] = piece[:, half * hw : (half + 1) * hw]

    def keep(parts, at):
        for parity in range(2):

            @pl.when(core == parity)
            def _():
                l_mine[:, at : at + half_cols] = parts[parity]

            @pl.when(core != parity)
            def _():
                l_other[:, at : at + half_cols] = parts[parity]

        for ref, to in ((l_mine, mine_to), (l_other, other_to)):
            writer.send(ref, to, slice(None), slice(at, at + half_cols))

    low = jnp.concatenate([ctx[rank] for rank in range(4)], axis=1)
    keep([shard_columns(low, parity) for parity in range(2)], half_cols)
    for copy in wo_copies:
        copy.wait()
    vec = vectors_of(b_s, NATURAL)
    eb[...] = vectors_of(b_s, CORE_MAJOR)[8:16, :]
    wo = wo_s[...].reshape(WIDTH, WIDTH)
    first_sum = hid[...].astype(F32) + (mm_nn(low, wo) + vec[0:1, :])
    x1, r1 = norm_parts(first_sum)
    xhat1[...] = x1
    rstd1[...] = r1
    writer.send(xhat1, xhat1_to)
    writer.send(rstd1, rstd1_to)
    normed = x1 * vec[1:2, :] + vec[2:3, :]
    lown = normed.astype(BF)
    keep([shard_columns(lown, parity) for parity in range(2)], 0)
    out = normed + vec[3:4, :]
    for p in range(4):
        for copy in copies[p]:
            copy.wait()
        bias = eb[pl.ds(meta[RANK + p], 1), :]
        u = mm_nn(lown, e_s[p].reshape(WIDTH, WIDTH)) + bias
        cdf = 0.5 * (1.0 + lax.erf(u * 0.7071067811865476))
        pdf = jnp.exp(-0.5 * u * u) * 0.3989422804014327
        low = (u * cdf).astype(BF)
        cut = slice(p * WIDTH, (p + 1) * WIDTH)
        gp[:, cut] = (cdf + u * pdf).astype(BF)
        writer.send(gp, gp_to, slice(None), cut)
        keep([low[:, :half_cols], low[:, half_cols:]], WIDTH + p * half_cols)
        out = out + mm_nn(low, r_s[p].reshape(WIDTH, WIDTH))
    x2, r2 = norm_parts(out)
    nxt = x2 * vec[4:5, :] + vec[5:6, :]
    hlow[...] = nxt.astype(BF)
    writer.send(hlow, hlow_to)
    xhat2[...] = x2
    writer.send(xhat2, xhat2_to)
    rstd2[...] = r2
    writer.send(rstd2, rstd2_to)
    if hnext:
        hnext[0][...] = nxt
        writer.send(hnext[0], places[8])
    if finish:
        writer.finish()


def norm_back(gy, gain, xhat, rstd):
    g = gy * gain
    return rstd * (g - jnp.mean(g, axis=-1, keepdims=True) - xhat * jnp.mean(g * xhat, axis=-1, keepdims=True))


def rows_sum(x):
    return jnp.sum(x, axis=0, keepdims=True)


def mlp_bwd_kernel(
    writer, places, meta, xhat1, rstd1, xhat2, rstd2, gp, *rest, parts, loaded=False
):
    t, a, b, d, crossed = rest[parts : parts + 5]
    gfs, dgg, gctx, e_s, r_s, sems, wo_s, b_s, wo_sems, eb_s = rest[-10:]
    rows = gfs.shape[0]
    core = meta[CORE]
    if loaded:
        copies, wo_copies = [[]] * 4, []
    else:
        copies = start_ffn_copies(core, t, a, b, d, crossed, e_s, r_s, sems)
        wo_copies = started_copies(
            wo_sems, (d.at[:, :, 2], wo_s), (t.at[:, :, 2, 0:16, VEC_AT : VEC_AT + 128], b_s)
        )
    grad = rest[0][...].astype(F32)
    for ref in rest[1:parts]:
        grad = grad + ref[...].astype(F32)
    x2 = xhat2[...]
    for copy in wo_copies:
        copy.wait()
    vec = vectors_of(b_s, NATURAL)
    gss = norm_back(grad, vec[4:5, :], x2, rstd2[...])
    low = gss.astype(BF)
    cut = slice(4 * WIDTH, 5 * WIDTH)
    dgg[0:rows, cut] = low
    writer.send(dgg.at[0:rows, cut], places[1].at[0:rows, cut])
    sums = [None] * 8
    sums[4] = rows_sum(grad * x2)
    sums[5] = rows_sum(grad)
    sums[3] = rows_sum(low.astype(F32))
    gn = gss
    eb_s[...] = jnp.zeros_like(eb_s)
    for p in range(4):
        for copy in copies[p]:
            copy.wait()
        ga = mm_nt(low, r_s[p].reshape(WIDTH, WIDTH))
        dip = (ga * gp[:, p * WIDTH : (p + 1) * WIDTH].astype(F32)).astype(BF)
        cut = slice(p * WIDTH, (p + 1) * WIDTH)
        dgg[0:rows, cut] = dip
        writer.send(dgg.at[0:rows, cut], places[1].at[0:rows, cut])
        eb_s[pl.ds(meta[RANK + p], 1), :] = rows_sum(dip.astype(F32))
        gn = gn + mm_nt(dip, e_s[p].reshape(WIDTH, WIDTH))
    x1 = xhat1[...]
    gf = norm_back(gn, vec[1:2, :], x1, rstd1[...])
    sums[1] = rows_sum(gn * x1)
    sums[2] = rows_sum(gn)
    lowa = gf.astype(BF)
    cut = slice(5 * WIDTH, 6 * WIDTH)
    dgg[0:rows, cut] = lowa
    writer.send(dgg.at[0:rows, cut], places[1].at[0:rows, cut])
    gfs[...] = gf
    writer.send(gfs, places[0])
    sums[0] = rows_sum(lowa.astype(F32))
    sums[6] = jnp.zeros_like(sums[0])
    sums[7] = sums[6]
    gc = mm_nt(lowa, wo_s[...].reshape(WIDTH, WIDTH)).astype(BF)
    hw = gctx.shape[2] // 2
    for rank in range(4):
        for half in range(2):
            gctx[rank, :, half * hw : (half + 1) * hw] = gc[half * BLK : (half + 1) * BLK, rank * hw : (rank + 1) * hw]
    writer.send(gctx, places[2])
    vecs = jnp.concatenate(sums, axis=0)
    ebs = jnp.concatenate([eb_s[:, (4 * (f % 2) + f // 2) * 96 : (4 * (f % 2) + f // 2 + 1) * 96] for f in range(8)], axis=1)
    dgg[rows:, 0:WIDTH] = jnp.concatenate([vecs, ebs], axis=0).astype(BF)
    dgg[rows:, WIDTH:] = jnp.zeros((16, 5 * WIDTH), BF)
    writer.send(dgg.at[rows:], places[1].at[rows:])
    writer.finish()


def wgrad_kernel(writer, places, meta, l_mine_from, l_other_from, dgg_from, dgg_other_from, *rest):
    t, a, b, dwo, d, l_mine, l_other, dgg, dgg_other, sems = rest[-10:]
    half = WIDTH // 2
    rows = l_mine.shape[0]

    def fetch(n, src, dst, at, width):
        copy = pltpu.make_async_copy(src.at[:, at : at + width], dst.at[:, at : at + width], sems.at[n])
        copy.start()
        return copy

    lefts = [fetch(n, src, dst, 0, WIDTH) for n, (src, dst) in enumerate(((l_mine_from, l_mine), (l_other_from, l_other)))]
    rights = {}
    for k in (3, 4, 1, 2, 0, 5):
        q = SWAPPED[k] if k < 4 else k
        rights[k] = [fetch(4 + k, dgg_from, dgg, k * WIDTH, WIDTH), fetch(10 + k, dgg_other_from, dgg_other, q * WIDTH, WIDTH)]
        if k == 3:
            acts = [
                fetch(2 + n, src, dst, WIDTH, 2 * WIDTH)
                for n, (src, dst) in enumerate(((l_mine_from, l_mine), (l_other_from, l_other)))
            ]

    def wait(copies):
        for copy in copies:
            copy.wait()

    def grad(left, left_other, right, right_other):
        return mm_nn(left, dgg[0:rows, right : right + WIDTH]) + mm_nn(
            left_other, dgg_other[0:rows, right_other : right_other + WIDTH]
        )

    def left(at, at_other):
        return l_mine[:, at : at + half].T, l_other[:, at_other : at_other + half].T

    wait(lefts)
    low = left(0, 0)
    for n, (p, out) in enumerate(((3, d), (1, a), (2, b), (0, t))):
        q = SWAPPED[p]
        wait(rights[p])
        out[:, 0] = grad(*low, p * WIDTH, q * WIDTH).reshape(4, 96, WIDTH).astype(BF)
        if n == 0:
            wait(acts)
            wait(rights[4])
        out[:, 1] = (
            grad(*left(WIDTH + p * half, WIDTH + q * half), 4 * WIDTH, 4 * WIDTH).reshape(4, 96, WIDTH).astype(BF)
        )
        writer.send(out, places[(4, 1, 2, 0)[n]])
    wait(rights[5])
    dwo[:, 0:96, :] = grad(*left(half, half), 5 * WIDTH, 5 * WIDTH).reshape(4, 96, WIDTH).astype(BF)
    vecs = dgg[rows:, 0:WIDTH].astype(F32) + dgg_other[rows:, 0:WIDTH].astype(F32)
    dwo[:, 96:, :] = jnp.zeros((4, 16, WIDTH), BF)
    for parity in range(2):

        @pl.when(meta[CORE] == parity)
        def _():
            for z in range(4):
                dwo[z, 96:, 0:96] = vecs[:, (2 * z + parity) * 96 : (2 * z + parity + 1) * 96].astype(BF)

    writer.send(dwo, places[3])
    writer.finish()


def place_kernel(
    meta, *rest, layer, last
):
    if last:
        parts = [((f.at[0], f.at[1]), a) for f, a in zip(rest[:4], rest[4:8])]
        small_in, rest = rest[8], rest[13:]
    else:
        parts = [((x.at[112:, 0:WIDTH], x.at[112:, WIDTH:]), x.at[0:112, :]) for x in rest[:4]]
        rest = rest[5:]
    e_hbm, r_hbm, i_hbm, o_hbm = rest[:4]
    smalls = rest[4:-10]
    e_s, i_s, b_s, e_out, r_out, i_out, o_out, small_s, eb_s, sems = rest[-10:]
    for p, (ffn, att) in enumerate(parts):
        rank = meta[RANK + p]
        r_out[pl.ds(pl.multiple_of(rank * 96, 96), 96), :] = ffn[1][...].astype(F32)
        e_s[rank] = ffn[0][...].astype(F32)
        i_s[rank] = att[0:96, WIDTH : WIDTH + 9 * HEAD_DIM].astype(F32)
        b_s[rank] = att[96:112, WIDTH : WIDTH + 9 * HEAD_DIM].astype(F32)
    copies = []

    def send(n, src, dst):
        copy = pltpu.make_async_copy(src, dst.at[layer], sems.at[n])
        copy.start()
        copies.append(copy)

    send(0, r_out, r_hbm)
    for f in range(8):
        at = (4 * (f % 2) + f // 2) * 96
        e_out[:, f * 384 : (f + 1) * 384] = jnp.concatenate([e_s[c, :, at : at + 96] for c in range(4)], axis=1)
    send(1, e_out, e_hbm)
    hw = WIDTH // 4
    for k in range(3):
        i_out[:, k * WIDTH : (k + 1) * WIDTH] = jnp.concatenate(
            [i_s[c, :, k * hw : (k + 1) * hw] for c in range(4)], axis=1
        )
    send(2, i_out, i_hbm)
    wo = [att[:, 0:WIDTH].astype(F32) for _, att in parts]
    total = (wo[0] + wo[1]) + (wo[2] + wo[3])
    o_out[...] = total[0:96, :]
    send(3, o_out, o_hbm)
    bias = b_s[lax.shift_right_logical(meta[SHARD], 1)]
    low_half = (meta[SHARD] & 1) == 0
    qb = jnp.where(low_half, bias[:, 0:96], bias[:, 96:192])
    vb = jnp.where(low_half, bias[:, 2 * hw : 2 * hw + 96], bias[:, 2 * hw + 96 : 3 * hw])
    rows = jnp.concatenate([total[96:102, 0:96], qb[0:1], vb[0:1], total[104:112, 0:96]], axis=0)
    if last:
        for n, ref in enumerate(smalls[:-1]):
            ref[...] = jnp.concatenate([rows[n : n + 1], small_in[n : n + 1, 0:96]], axis=0)
        smalls[-1][...] = jnp.concatenate(
            [
                jnp.concatenate([x[8 + c : 9 + c, 0:96] for c in range(4)], axis=1)
                for x in (rows, small_in[...])
            ],
            axis=0,
        )
    else:
        smalls[0][...] = rows
    for copy in copies:
        copy.wait()


def permutation(ctx, fsdp, move):
    return [
        (c * fsdp + f, move(c, f)[0] * fsdp + move(c, f)[1]) for c in range(ctx) for f in range(fsdp)
    ]


def add(*parts):
    total = parts[0].astype(F32)
    for part in parts[1:]:
        total = total + part.astype(F32)
    return total


def on_device_fast(
    activations, cotangent, doc_start, deal,
    attend_in, query_bias, value_bias, attend_out, attend_bias, first_gain, first_shift,
    expand_proj, expand_bias, reduce_proj, reduce_bias, second_gain, second_shift,
    *, ctx, fsdp,
):
    S = [pltpu.SMEM]
    V = [pltpu.VMEM]
    A = [pl.ANY]
    axes = ("ctx", "fsdp")

    def via(move):
        perm = permutation(ctx, fsdp, move)
        return lambda x: lax.ppermute(x, axes, perm)

    via_first = via(lambda c, f: (c ^ (1 + f % 2), f))
    via_second = via(lambda c, f: (c ^ (2 - f % 2), f))
    via_diagonal = via(lambda c, f: (c ^ 3, f))
    via_core = via(lambda c, f: (c, f ^ 1))
    via_z = [None] + [via(lambda c, f, k=k: (c, f ^ (2 * k))) for k in range(1, 4)]

    def exchange_ctx(own, a, b, d):
        return (own, via_first(a), via_second(b), via_diagonal(d))

    def spread_ctx(x):
        return (x, via_first(x), via_second(x), via_diagonal(x))

    def reduce_z(x):
        return lax.psum_scatter(x, "fsdp", scatter_dimension=0, tiled=True, axis_index_groups=zgroups)

    def exchange_z(own, *others):
        return (own,) + tuple(via_z[k + 1](x) for k, x in enumerate(others))

    def gather_ctx(x):
        a, b = via_first(x), via_second(x)
        return (x, a, b, via_second(a))

    heads = HEADS // ctx
    hw = heads * HEAD_DIM
    rows = activations.shape[1]
    tokens = rows * ctx
    cut = WIDTH // fsdp
    c = lax.axis_index("ctx").astype(jnp.int32)
    shard = lax.axis_index("fsdp").astype(jnp.int32)
    core = shard % 2
    zgroups = [[2 * z + k for z in range(fsdp // 2)] for k in range(2)]

    hidden = activations[0]
    gathered = gather_ctx(hidden)
    small = (attend_bias, first_gain, first_shift, reduce_bias, second_gain, second_shift, query_bias, value_bias)
    sent = call(
        prep_kernel,
        [((3 * cut, WIDTH), BF)] * 4,
        (expand_proj, reduce_proj, attend_in, attend_out, expand_bias) + small,
        V * 13,
        [],
        "prep",
        0,
        8 * 1024 * 1024,
    )

    def gather_ffn(x):
        x = lax.all_gather(x, "fsdp", axis=0, tiled=True)
        return x.reshape(fsdp // 2, 2, 3, cut, WIDTH)

    ranks = jnp.arange(ctx, dtype=jnp.int32)
    inv = jnp.sum(jnp.where(deal[None, :] == ranks[:, None], ranks[None, :], 0), axis=1).astype(jnp.int32)
    starts = lax.all_gather(doc_start[0], "ctx", axis=0, tiled=True)
    by_rank = starts.reshape(ctx, 2, BLK)
    chosen = inv[:, None, None, None] == ranks[None, :, None, None]
    by_block = jnp.sum(jnp.where(chosen, by_rank[None], 0), axis=1)
    logical = jnp.concatenate([by_block[:, 0], by_block[::-1, 1]], axis=0).reshape(-1)
    qrow = jnp.broadcast_to(logical[None, :], (8, tokens))
    kcol = jnp.broadcast_to(logical[:, None], (tokens, 128))
    jmin = jnp.min(logical.reshape(tokens // QB, QB), axis=1) // QB

    m1 = 1 + core
    mask = inv ^ c
    jmap = jnp.where((core == 1) & (mask > 0) & (mask < 3), 3 - mask, mask)
    meta = jnp.concatenate(
        [jnp.stack([core, shard, c, c ^ m1, c ^ (3 - m1), c ^ 3]), jmap, inv, jmin]
    ).astype(jnp.int32)

    kept = []
    earlier = ()
    wide = [gather_ffn(sent[0]), gather_ffn(sent[1]), None, None]
    wide[0] = after((wide[0],), starts, *gathered[1:])[0]
    wide[2] = gather_ffn(*after(sent[2:3], wide[0]))
    pieces = []
    for layer in range(LAYERS):
        t, d = wide[2 * layer : 2 * layer + 2]
        mine = half_of(meta, t, *gathered[1:])
        a, b = via_first(mine), via_second(mine)
        qkv, *ctx_own, lse = call(
            functools.partial(attn_fwd_kernel, heads=heads, tokens=tokens),
            [((ctx, rows, 3 * hw), BF)] + [((BLK, 2 * hw), BF)] * 4 + [((8, tokens), F32)],
            (meta,) + gathered + (qrow, kcol, t, mine) + earlier,
            S + V * 6 + A * (2 + len(earlier)),
            attn_fwd_scratch(heads, tokens),
            "attn_fwd",
            2 * tokens * WIDTH * 3 * hw * 4,
            10 * 1024 * 1024,
        )
        cx = exchange_ctx(*ctx_own)
        if layer + 1 < LAYERS:
            wide[3] = gather_ffn(*after(sent[3:4], *cx[1:]))
        pieces.append((t, a, b, d, via_core(pack(a, b, lse))))
        kinds = {
            "xhat": ((rows, WIDTH), F32), "rstd": ((rows, 1), F32), "gp": ((rows, 4 * WIDTH), BF),
            "left": ((rows, 3 * WIDTH), BF), "low": ((rows, WIDTH), BF),
        }
        norms = [kinds[name] for name in ("xhat", "rstd", "gp", "xhat", "rstd")]
        lows = [kinds[name] for name in ("left", "left", "low")]
        back_outs = [((rows, WIDTH), F32), ((rows + 16, 6 * WIDTH), BF), ((ctx, BLK, 2 * hw), BF)]
        if layer + 1 < LAYERS:
            xhat1, rstd1, gp, xhat2, rstd2, l_mine, l_other, hlow, hidden_next = call_writing(
                mlp_fwd_kernel,
                norms + lows + [kinds["xhat"]],
                (meta,) + cx + (hidden,) + pieces[layer],
                S + V * 5 + A * 5,
                mlp_fwd_scratch(rows, hw),
                "mlp_fwd",
                24,
            )
        else:
            xhat1 = rstd1 = gp = xhat2 = rstd2 = None
            l_mine, l_other, hlow, *last_back = call_writing(
                last_kernel,
                lows + back_outs,
                (meta,) + cx + (hidden, cotangent[0]) + pieces[layer],
                S + V * 6 + A * 5,
                [pltpu.VMEM(*kind) for kind in norms] + mlp_fwd_scratch(rows, hw) + [pltpu.VMEM((8, WIDTH), F32)],
                "last",
                36,
            )
        l_other = via_core(l_other)
        earlier = (l_other,)
        kept.append((gathered, qkv, ctx_own, lse, xhat1, rstd1, gp, xhat2, rstd2, l_mine, l_other))
        if layer + 1 < LAYERS:
            hidden = hidden_next
            gathered = gather_ctx(hlow)
    out_act = hlow[None]

    for layer in reversed(range(LAYERS)):
        gathered, qkv, ctx_own, lse, xhat1, rstd1, gp, xhat2, rstd2, l_mine, l_other = kept[layer]
        if layer + 1 == LAYERS:
            gfs, dgg, gctx = last_back
        else:
            gfs, dgg, gctx = call_writing(
                mlp_bwd_kernel,
                back_outs,
                (meta, xhat1, rstd1, xhat2, rstd2, gp) + grads + pieces[layer] + order,
                S + V * (5 + len(grads)) + A * (5 + len(order)),
                mlp_bwd_scratch(),
                "mlp_bwd",
                12,
                parts=len(grads),
            )
        gcx = lax.all_to_all(gctx, "ctx", 0, 0, tiled=True)
        piece = ((4, 2, cut, WIDTH), BF)

        def weight_grads(*before):
            return call_writing(
                wgrad_kernel,
                [piece] * 3 + [((4, cut + 16, WIDTH), BF), piece],
                (meta, l_mine, l_other, dgg, via_core(dgg)) + before,
                S + A * (4 + len(before)),
                wgrad_scratch(),
                "wgrad",
                5,
            )

        def attention_grads(*before):
            return call(
                functools.partial(attn_bwd_kernel, heads=heads, tokens=tokens),
                [
                    ((rows, WIDTH), F32), ((rows, WIDTH), BF), ((rows, WIDTH), BF), ((rows, WIDTH), BF),
                    ((4, cut + 16, 3 * hw), BF), ((4, cut + 16, 3 * hw), BF),
                ],
                (meta,) + gathered + (qrow, kcol, qkv) + tuple(ctx_own) + (gcx, lse, wide[2 * layer]) + before,
                S + V * 13 + A * (1 + len(before)),
                attn_bwd_scratch(heads, tokens),
                "attn_bwd",
                2 * tokens * WIDTH * 3 * hw * 8,
                10 * 1024 * 1024,
            )

        def attention_shards(dwo, dw, crossed, *others):
            shape = (4, cut + 16, WIDTH + 3 * hw)
            (merged,) = call(
                merge_kernel, [(shape, BF)], (dwo, dw, crossed) + others, V * 3 + A * len(others), [], "merge", 0, 0
            )
            return merged, reduce_z(merged).reshape(shape[1:])

        if layer > 0:
            g_own, g_a, g_b, g_d, dw, dw_other = attention_grads(l_other)
            (over,) = sums([[(g_a, via_second(g_d))]])
            t, a, b, dwo, d = weight_grads(over)
            d1 = reduce_z(d)
            over = via_first(over)
            merged, att1 = attention_shards(dwo, dw, via_core(dw_other))
            back = via_second(g_b)
            grads = (gfs, g_own, back, over)
            a, b = after((a, b), over, back)
            order = (merged, a, b)
            parts1 = (t, via_first(a), via_second(b))
        else:
            (t1,) = sums([[parts1]], gcx, weight=WEIGHT)
            t, a, b, dwo, d = weight_grads(gcx, att1, t1)
            t1 = reduce_z(t1)
            from_b, from_d = via_second(b), via_second(d)
            g_own, g_a, g_b, g_d, dw, dw_other = attention_grads(t)

    def shards(x):
        return x.reshape(2, cut, WIDTH)

    a0, t0 = sums([[(a, from_d)], [(t, from_b)]], g_d, weight=WEIGHT)
    from_a = via_first(a0)
    merged, att0 = attention_shards(dwo, dw, via_core(dw_other), a0)
    back = via_second(g_d), via_second(g_b)
    shape = (2 * cut + 16, 2 * WIDTH)
    (joined,) = call(
        join_kernel, [(shape, BF)], (att1, shards(t1), shards(via_diagonal(d1)), merged), V * 3 + A, [], "join", WEIGHT, 0
    )
    (over,) = sums([[(g_a, back[0])]], joined)
    joined = spread_ctx(joined)
    (t0,) = sums([[(t0, from_a)]], over, weight=WEIGHT)
    over = via_first(over)
    ffn0 = shards(reduce_z(t0))

    small_out = None
    placed = []
    for layer in reversed(range(LAYERS)):
        if layer == 0:
            sent = spread_ctx(ffn0) + spread_ctx(att0)
            waits = ()
        else:
            sent = joined
            waits = (t0,)
        last = layer == 0
        big = [
            ((LAYERS, cut, 4 * WIDTH), F32), ((LAYERS, 4 * cut, WIDTH), F32),
            ((LAYERS, cut, 3 * WIDTH), F32), ((LAYERS, cut, WIDTH), F32),
        ]
        if last:
            smalls = [((LAYERS, cut), F32)] * 8 + [((LAYERS, 4 * cut), F32)]
        else:
            smalls = [((16, cut), F32)]
        args = (meta,) + sent + ((small_out,) + tuple(placed) if last else waits)
        spaces = S + V * len(sent) + (V + A * 4 if last else A)
        outs = pl.pallas_call(
            functools.partial(place_kernel, layer=layer, last=last),
            out_shape=[jax.ShapeDtypeStruct(shape, dtype) for shape, dtype in big + smalls],
            in_specs=[pl.BlockSpec(memory_space=space) for space in spaces],
            out_specs=[pl.BlockSpec(memory_space=space) for space in A * 4 + V * len(smalls)],
            scratch_shapes=[
                pltpu.VMEM((ctx, cut, WIDTH), F32), pltpu.VMEM((ctx, cut, 3 * hw), F32),
                pltpu.VMEM((ctx, 16, 3 * hw), F32),
                pltpu.VMEM((cut, 4 * WIDTH), F32), pltpu.VMEM((4 * cut, WIDTH), F32),
                pltpu.VMEM((cut, 3 * WIDTH), F32), pltpu.VMEM((cut, WIDTH), F32),
                pltpu.VMEM((16, 128), F32), pltpu.VMEM((8, 128), F32),
                pltpu.SemaphoreType.DMA((4,)),
            ],
            input_output_aliases={10 + n: n for n in range(4)} if last else {},
            compiler_params=pltpu.CompilerParams(vmem_limit_bytes=VMEM_LIMIT),
            cost_estimate=pl.CostEstimate(flops=0, bytes_accessed=10 * 1024 * 1024, transcendentals=0),
            name="place",
        )(*args)
        placed = outs[:4]
        small_out = outs[4]
        vectors = outs[4:]
    in_grad = add(gfs, g_own, back[1], over)[None]
    e_out, r_out, i_out, o_out = placed
    ab, fg, fs, rb, sg, ss, qb, vb, xb = vectors
    return (out_act, in_grad, i_out, qb, vb, o_out, ab, fg, fs, e_out, xb, r_out, rb, sg, ss)


def on_device(*args, ctx, fsdp):
    if ctx == 4 and fsdp == 8 and args[0].shape[1] == 2 * BLK:
        return on_device_fast(*args, ctx=ctx, fsdp=fsdp)
    return on_device_plain(*args)


def solution(mesh):
    placed = (
        P("fsdp", "ctx", None),
        P("fsdp", "ctx", None),
        P("fsdp", "ctx"),
        P(),
        P(None, "fsdp", None),
        P(None, "fsdp"),
        P(None, "fsdp"),
        P(None, "fsdp", None),
        P(None, "fsdp"),
        P(None, "fsdp"),
        P(None, "fsdp"),
        P(None, "fsdp", None),
        P(None, "fsdp"),
        P(None, "fsdp", None),
        P(None, "fsdp"),
        P(None, "fsdp"),
        P(None, "fsdp"),
    )
    return jax.shard_map(
        functools.partial(on_device, ctx=mesh.shape["ctx"], fsdp=mesh.shape["fsdp"]),
        mesh=mesh,
        in_specs=placed,
        out_specs=(
            P("fsdp", "ctx", None),
            P("fsdp", "ctx", None),
            P(None, "fsdp", None),
            P(None, "fsdp"),
            P(None, "fsdp"),
            P(None, "fsdp", None),
            P(None, "fsdp"),
            P(None, "fsdp"),
            P(None, "fsdp"),
            P(None, "fsdp", None),
            P(None, "fsdp"),
            P(None, "fsdp", None),
            P(None, "fsdp"),
            P(None, "fsdp"),
            P(None, "fsdp"),
        ),
        check_vma=False,
    )
```

```python
import functools

import jax
import jax.numpy as jnp
from jax import lax
from jax.experimental import pallas as pl
from jax.experimental.pallas import tpu as pltpu
from jax.sharding import PartitionSpec as P

HEADS = 12
HEAD_DIM = 64
LAYERS = 2
BLK = 192


norm_eps = 1e-05


def for_sending(x):
    return jax.tree.map(lambda a: a.astype(jnp.bfloat16) if a.dtype == jnp.float32 else a, x)


def layer_norm(values, gain, shift):
    centre = values - jnp.mean(values, axis=-1, keepdims=True)
    spread = jnp.mean(centre * centre, axis=-1, keepdims=True)
    return centre * lax.rsqrt(spread + norm_eps) * gain + shift


def gelu_exact(inputs):
    return 0.5 * inputs * (1.0 + jax.scipy.special.erf(inputs * 0.7071067811865476))


def key_positions(deal):
    pairs = deal.shape[0]
    offsets = jnp.arange(BLK, dtype=jnp.int32)
    first = deal[:, None] * BLK + offsets[None, :]
    second = (2 * pairs - 1 - deal)[:, None] * BLK + offsets[None, :]
    return jnp.concatenate([first, second], axis=1).reshape(-1)


def split_heads(matrix):
    return matrix.reshape(matrix.shape[0], HEADS, HEAD_DIM).transpose(1, 0, 2)


def join_heads(stacked):
    return stacked.transpose(1, 0, 2).reshape(stacked.shape[1], HEADS * HEAD_DIM)


def attend_forward(queries, keys_full, values_full, allowed):

    def one_head(items):
        head_q, head_k, head_v = items
        scores = jnp.einsum(
            "qd,kd->qk", head_q, head_k, preferred_element_type=jnp.float32
        ) * HEAD_DIM ** (-0.5)
        scores = jnp.where(allowed, scores, -1e30)
        top = jnp.max(scores, axis=-1, keepdims=True)
        weights = jnp.exp(scores - top)
        total = jnp.sum(weights, axis=-1, keepdims=True)
        probs = (weights / total).astype(jnp.bfloat16)
        output = jnp.einsum("qk,kd->qd", probs, head_v, preferred_element_type=jnp.float32)
        return (output, top[:, 0] + jnp.log(total[:, 0]))

    outputs, log_totals = lax.map(
        one_head, (split_heads(queries), split_heads(keys_full), split_heads(values_full))
    )
    return (join_heads(outputs), log_totals)


def attend_backward(queries, keys_full, values_full, log_totals, grad_context, allowed):

    def one_head(items):
        head_q, head_k, head_v, head_lse, head_grad = items
        scores = jnp.einsum(
            "qd,kd->qk", head_q, head_k, preferred_element_type=jnp.float32
        ) * HEAD_DIM ** (-0.5)
        scores = jnp.where(allowed, scores, -1e30)
        probs = jnp.exp(scores - head_lse[:, None])
        grad_probs = jnp.einsum("qd,kd->qk", head_grad, head_v, preferred_element_type=jnp.float32)
        inner_sum = jnp.sum(probs * grad_probs, axis=-1, keepdims=True)
        grad_scores = (probs * (grad_probs - inner_sum)).astype(jnp.bfloat16)
        grad_q = jnp.einsum(
            "qk,kd->qd", grad_scores, head_k, preferred_element_type=jnp.float32
        ) * HEAD_DIM ** (-0.5)
        grad_k = jnp.einsum(
            "qk,qd->kd", grad_scores, head_q, preferred_element_type=jnp.float32
        ) * HEAD_DIM ** (-0.5)
        grad_v = jnp.einsum(
            "qk,qd->kd", probs.astype(jnp.bfloat16), head_grad, preferred_element_type=jnp.float32
        )
        return (grad_q, grad_k, grad_v)

    grads = lax.map(
        one_head,
        (
            split_heads(queries),
            split_heads(keys_full),
            split_heads(values_full),
            log_totals,
            split_heads(grad_context),
        ),
    )
    return (join_heads(grads[0]), join_heads(grads[1]), join_heads(grads[2]))


def forward_layer(hidden, weights, allowed):
    (
        attend_in,
        query_bias,
        value_bias,
        attend_out,
        attend_bias,
        first_gain,
        first_shift,
        expand_proj,
        expand_bias,
        reduce_proj,
        reduce_bias,
        second_gain,
        second_shift,
    ) = weights
    width = hidden.shape[1]
    low_hidden = hidden.astype(jnp.bfloat16)
    projected = jnp.dot(low_hidden, attend_in, preferred_element_type=jnp.float32)
    queries = (projected[:, :width] + query_bias.astype(jnp.float32)).astype(jnp.bfloat16)
    keys_own = projected[:, width : 2 * width].astype(jnp.bfloat16)
    values_own = (projected[:, 2 * width :] + value_bias.astype(jnp.float32)).astype(jnp.bfloat16)
    keys_full, values_full = (
        lax.all_gather(keys_own, "ctx", axis=0, tiled=True),
        lax.all_gather(values_own, "ctx", axis=0, tiled=True),
    )
    context, log_totals = attend_forward(queries, keys_full, values_full, allowed)
    low_context = context.astype(jnp.bfloat16)
    branch = jnp.dot(
        low_context, attend_out, preferred_element_type=jnp.float32
    ) + attend_bias.astype(jnp.float32)
    first_sum = hidden + branch
    normed = layer_norm(first_sum, first_gain.astype(jnp.float32), first_shift.astype(jnp.float32))
    low_normed = normed.astype(jnp.bfloat16)
    inner_pre = jnp.dot(
        low_normed, expand_proj, preferred_element_type=jnp.float32
    ) + expand_bias.astype(jnp.float32)
    active = gelu_exact(inner_pre).astype(jnp.bfloat16)
    output_branch = jnp.dot(
        active, reduce_proj, preferred_element_type=jnp.float32
    ) + reduce_bias.astype(jnp.float32)
    second_sum = normed + output_branch
    output = layer_norm(
        second_sum, second_gain.astype(jnp.float32), second_shift.astype(jnp.float32)
    )
    saved = (
        low_hidden,
        queries,
        keys_full,
        values_full,
        log_totals,
        low_context,
        first_sum,
        low_normed,
        inner_pre,
        active,
        second_sum,
    )
    return (output, saved)


def column_sum(matrix):
    return jnp.sum(matrix.astype(jnp.float32), axis=0)


def backward_layer(grad_hidden, weights, saved, allowed):
    (
        attend_in,
        query_bias,
        value_bias,
        attend_out,
        attend_bias,
        first_gain,
        first_shift,
        expand_proj,
        expand_bias,
        reduce_proj,
        reduce_bias,
        second_gain,
        second_shift,
    ) = weights
    (
        low_hidden,
        queries,
        keys_full,
        values_full,
        log_totals,
        low_context,
        first_sum,
        low_normed,
        inner_pre,
        active,
        second_sum,
    ) = saved
    width = low_hidden.shape[1]
    second_pull = jax.vjp(
        layer_norm, second_sum, second_gain.astype(jnp.float32), second_shift.astype(jnp.float32)
    )[1]
    grad_second_sum, grad_second_gain, grad_second_shift = second_pull(grad_hidden)
    grad_branch = grad_second_sum.astype(jnp.bfloat16)
    grad_reduce_bias = column_sum(grad_branch)
    grad_reduce = jnp.einsum("tf,td->fd", active, grad_branch, preferred_element_type=jnp.float32)
    grad_active = jnp.einsum(
        "td,fd->tf", grad_branch, reduce_proj, preferred_element_type=jnp.float32
    )
    gelu_pull = jax.vjp(gelu_exact, inner_pre)[1]
    grad_inner = gelu_pull(grad_active)[0].astype(jnp.bfloat16)
    grad_expand_bias = column_sum(grad_inner)
    grad_expand = jnp.einsum(
        "td,tf->df", low_normed, grad_inner, preferred_element_type=jnp.float32
    )
    grad_normed = grad_second_sum + jnp.einsum(
        "tf,df->td", grad_inner, expand_proj, preferred_element_type=jnp.float32
    )
    first_pull = jax.vjp(
        layer_norm, first_sum, first_gain.astype(jnp.float32), first_shift.astype(jnp.float32)
    )[1]
    grad_first_sum, grad_first_gain, grad_first_shift = first_pull(grad_normed)
    grad_attn = grad_first_sum.astype(jnp.bfloat16)
    grad_attend_bias = column_sum(grad_attn)
    grad_attend_out = jnp.einsum(
        "td,te->de", low_context, grad_attn, preferred_element_type=jnp.float32
    )
    grad_context = jnp.einsum(
        "te,de->td", grad_attn, attend_out, preferred_element_type=jnp.float32
    ).astype(jnp.bfloat16)
    grad_queries, grad_keys_full, grad_values_full = attend_backward(
        queries, keys_full, values_full, log_totals, grad_context, allowed
    )
    grad_keys, grad_values = (
        lax.psum_scatter(
            grad_keys_full.astype(jnp.bfloat16), "ctx", scatter_dimension=0, tiled=True
        ).astype(jnp.float32),
        lax.psum_scatter(
            grad_values_full.astype(jnp.bfloat16), "ctx", scatter_dimension=0, tiled=True
        ).astype(jnp.float32),
    )
    grad_proj = jnp.concatenate(
        [
            grad_queries.astype(jnp.bfloat16),
            grad_keys.astype(jnp.bfloat16),
            grad_values.astype(jnp.bfloat16),
        ],
        axis=1,
    )
    grad_query_bias = column_sum(grad_proj[:, :width])
    grad_value_bias = column_sum(grad_proj[:, 2 * width :])
    grad_attend_in = jnp.einsum(
        "td,te->de", low_hidden, grad_proj, preferred_element_type=jnp.float32
    )
    grad_input = grad_first_sum + jnp.einsum(
        "te,de->td", grad_proj, attend_in, preferred_element_type=jnp.float32
    )
    grads = (
        grad_attend_in,
        grad_query_bias,
        grad_value_bias,
        grad_attend_out,
        grad_attend_bias,
        grad_first_gain,
        grad_first_shift,
        grad_expand,
        grad_expand_bias,
        grad_reduce,
        grad_reduce_bias,
        grad_second_gain,
        grad_second_shift,
    )
    return (grad_input, grads)


def reduce_grads(grads):
    shards = (
        lax.psum_scatter(
            grads[0].astype(jnp.bfloat16), "fsdp", scatter_dimension=0, tiled=True
        ).astype(jnp.float32),
        lax.psum_scatter(
            grads[1].astype(jnp.bfloat16), "fsdp", scatter_dimension=0, tiled=True
        ).astype(jnp.float32),
        lax.psum_scatter(
            grads[2].astype(jnp.bfloat16), "fsdp", scatter_dimension=0, tiled=True
        ).astype(jnp.float32),
        lax.psum_scatter(
            grads[3].astype(jnp.bfloat16), "fsdp", scatter_dimension=0, tiled=True
        ).astype(jnp.float32),
        lax.psum_scatter(
            grads[4].astype(jnp.bfloat16), "fsdp", scatter_dimension=0, tiled=True
        ).astype(jnp.float32),
        lax.psum_scatter(
            grads[5].astype(jnp.bfloat16), "fsdp", scatter_dimension=0, tiled=True
        ).astype(jnp.float32),
        lax.psum_scatter(
            grads[6].astype(jnp.bfloat16), "fsdp", scatter_dimension=0, tiled=True
        ).astype(jnp.float32),
        lax.psum_scatter(
            grads[7].astype(jnp.bfloat16), "fsdp", scatter_dimension=0, tiled=True
        ).astype(jnp.float32),
        lax.psum_scatter(
            grads[8].astype(jnp.bfloat16), "fsdp", scatter_dimension=0, tiled=True
        ).astype(jnp.float32),
        lax.psum_scatter(
            grads[9].astype(jnp.bfloat16), "fsdp", scatter_dimension=0, tiled=True
        ).astype(jnp.float32),
        lax.psum_scatter(
            grads[10].astype(jnp.bfloat16), "fsdp", scatter_dimension=0, tiled=True
        ).astype(jnp.float32),
        lax.psum_scatter(
            grads[11].astype(jnp.bfloat16), "fsdp", scatter_dimension=0, tiled=True
        ).astype(jnp.float32),
        lax.psum_scatter(
            grads[12].astype(jnp.bfloat16), "fsdp", scatter_dimension=0, tiled=True
        ).astype(jnp.float32),
    )
    return (
        lax.psum(shards[0].astype(jnp.bfloat16), "ctx").astype(jnp.float32),
        lax.psum(shards[1].astype(jnp.bfloat16), "ctx").astype(jnp.float32),
        lax.psum(shards[2].astype(jnp.bfloat16), "ctx").astype(jnp.float32),
        lax.psum(shards[3].astype(jnp.bfloat16), "ctx").astype(jnp.float32),
        lax.psum(shards[4].astype(jnp.bfloat16), "ctx").astype(jnp.float32),
        lax.psum(shards[5].astype(jnp.bfloat16), "ctx").astype(jnp.float32),
        lax.psum(shards[6].astype(jnp.bfloat16), "ctx").astype(jnp.float32),
        lax.psum(shards[7].astype(jnp.bfloat16), "ctx").astype(jnp.float32),
        lax.psum(shards[8].astype(jnp.bfloat16), "ctx").astype(jnp.float32),
        lax.psum(shards[9].astype(jnp.bfloat16), "ctx").astype(jnp.float32),
        lax.psum(shards[10].astype(jnp.bfloat16), "ctx").astype(jnp.float32),
        lax.psum(shards[11].astype(jnp.bfloat16), "ctx").astype(jnp.float32),
        lax.psum(shards[12].astype(jnp.bfloat16), "ctx").astype(jnp.float32),
    )


def layer_slices(sharded, layer_index):
    return tuple((tensor[layer_index] for tensor in sharded))


def on_device_plain(
    activations,
    cotangent,
    doc_start,
    deal,
    attend_in,
    query_bias,
    value_bias,
    attend_out,
    attend_bias,
    first_gain,
    first_shift,
    expand_proj,
    expand_bias,
    reduce_proj,
    reduce_bias,
    second_gain,
    second_shift,
):
    sharded = (
        attend_in,
        query_bias,
        value_bias,
        attend_out,
        attend_bias,
        first_gain,
        first_shift,
        expand_proj,
        expand_bias,
        reduce_proj,
        reduce_bias,
        second_gain,
        second_shift,
    )
    row_count = activations.shape[1]
    positions = key_positions(deal)
    own_rank = lax.axis_index("ctx")
    own_positions = lax.dynamic_slice_in_dim(positions, own_rank * row_count, row_count)
    own_starts = doc_start[0]
    key_starts = lax.all_gather(own_starts, "ctx", axis=0, tiled=True)
    allowed = (positions[None, :] <= own_positions[:, None]) & (
        key_starts[None, :] == own_starts[:, None]
    )
    hidden = activations[0].astype(jnp.float32)
    kept_weights = []
    kept_saved = []
    for layer_index in range(LAYERS):
        weights = lax.all_gather(
            for_sending(layer_slices(sharded, layer_index)), "fsdp", axis=0, tiled=True
        )
        hidden, saved = forward_layer(hidden, weights, allowed)
        kept_weights.append(weights)
        kept_saved.append(saved)
    out_act = hidden.astype(jnp.bfloat16)[None]
    grad_hidden = cotangent[0].astype(jnp.float32)
    reduced = [None] * LAYERS
    for layer_index in reversed(range(LAYERS)):
        weights = lax.all_gather(
            for_sending(layer_slices(sharded, layer_index)), "fsdp", axis=0, tiled=True
        )
        grad_hidden, grads = backward_layer(grad_hidden, weights, kept_saved[layer_index], allowed)
        reduced[layer_index] = reduce_grads(grads)
    stacked = [
        jnp.stack([reduced[layer_index][member] for layer_index in range(LAYERS)])
        for member in range(13)
    ]
    return (
        out_act,
        grad_hidden[None],
        stacked[0],
        stacked[1],
        stacked[2],
        stacked[3],
        stacked[4],
        stacked[5],
        stacked[6],
        stacked[7],
        stacked[8],
        stacked[9],
        stacked[10],
        stacked[11],
        stacked[12],
    )


F32 = jnp.float32
BF = jnp.bfloat16
WIDTH = HEADS * HEAD_DIM
QB = 256
SCORE_SCALE = HEAD_DIM ** (-0.5) * 1.4426950408889634
NEG = -1e30
VMEM_LIMIT = 60 * 1024 * 1024


def mm_nn(a, b):
    return lax.dot_general(a, b, (((1,), (0,)), ((), ())), preferred_element_type=F32)


def mm_nt(a, b):
    return lax.dot_general(a, b, (((1,), (1,)), ((), ())), preferred_element_type=F32)


def mm_tn(a, b):
    return lax.dot_general(a, b, (((0,), (0,)), ((), ())), preferred_element_type=F32)


def call(kernel, outs, args, specs, scratch, name, flops, nbytes):
    return pl.pallas_call(
        kernel,
        out_shape=[jax.ShapeDtypeStruct(shape, dtype) for shape, dtype in outs],
        in_specs=[pl.BlockSpec(memory_space=space) for space in specs],
        out_specs=[pl.BlockSpec(memory_space=pltpu.VMEM) for _ in outs],
        scratch_shapes=scratch,
        compiler_params=pltpu.CompilerParams(vmem_limit_bytes=VMEM_LIMIT),
        cost_estimate=pl.CostEstimate(flops=flops if name in ("sums", "join") else 0, bytes_accessed=0, transcendentals=0),
        name=name,
    )(*args)


def block_of(block, blocks):
    half = 0 if 2 * block < blocks else 1
    return (block if half == 0 else blocks - 1 - block), half


CORE, SHARD, RANK, JMAP, INV, JMIN = 0, 1, 2, 6, 10, 14
SWAPPED = (0, 2, 1, 3)
WEIGHT = 10**11
VEC_AT = 640


def started_copies(sems, *pairs):
    copies = []
    for n, (src, dst) in enumerate(pairs):
        copy = pltpu.make_async_copy(src, dst, sems.at[n])
        copy.start()
        copies.append(copy)
    return copies


def last_kernel(
    writer, places, meta, c0, c1, c2, c3, hid, cot, t, a, b, d, crossed,
    l_mine, l_other, hlow, gfs, dgg, gctx,
    xhat1, rstd1, gp, xhat2, rstd2, e_s, r_s, sems, wo_s, b_s, wo_sems, ctx, eb, eb_s,
):
    loads = (e_s, r_s, sems, wo_s, b_s, wo_sems)
    mlp_fwd_kernel(
        writer, (None,) * 5 + tuple(places[:3]), meta, c0, c1, c2, c3, hid, t, a, b, d, crossed,
        xhat1, rstd1, gp, xhat2, rstd2, l_mine, l_other, hlow, *loads, ctx, eb, finish=False,
    )
    mlp_bwd_kernel(
        writer, places[3:], meta, xhat1, rstd1, xhat2, rstd2, gp, cot, t, a, b, d, crossed,
        gfs, dgg, gctx, *loads, eb_s, parts=1, loaded=True,
    )


class Writer:
    def __init__(self, sems):
        self.sems = sems
        self.copies = []

    def send(self, src, dst, *at):
        if dst is None:
            return
        if at:
            src, dst = src.at[at], dst.at[at]
        copy = pltpu.make_async_copy(src, dst, self.sems.at[len(self.copies)])
        copy.start()
        self.copies.append(copy)

    def finish(self):
        for copy in self.copies:
            copy.wait()


def writing(kernel, outs, copies):
    count = len(outs)

    def run(*refs, scratch, **keys):
        ins, places, rest = refs[: -count - scratch], refs[-count - scratch : -scratch], refs[-scratch:]
        buffers, sems, rest = rest[:count], rest[count], rest[count + 1 :]
        kernel(Writer(sems), places, *ins, *buffers, *rest, **keys)

    return run, [pltpu.VMEM(shape, dtype) for shape, dtype in outs] + [pltpu.SemaphoreType.DMA((copies,))]


def call_writing(kernel, outs, args, specs, scratch, name, copies, **keys):
    run, buffers = writing(kernel, outs, copies)
    scratch = buffers + scratch
    return pl.pallas_call(
        functools.partial(run, scratch=len(scratch), **keys),
        out_shape=[jax.ShapeDtypeStruct(shape, dtype) for shape, dtype in outs],
        in_specs=[pl.BlockSpec(memory_space=space) for space in specs],
        out_specs=[pl.BlockSpec(memory_space=pl.ANY) for _ in outs],
        scratch_shapes=scratch,
        compiler_params=pltpu.CompilerParams(vmem_limit_bytes=VMEM_LIMIT),
        cost_estimate=pl.CostEstimate(flops=0, bytes_accessed=0, transcendentals=0),
        name=name,
    )(*args)


def prep_kernel(
    expand, reduce, attend_in, attend_out, expand_bias, v0, v1, v2, v3, v4, v5, v6, v7,
    t0, d0, t1, d1,
):
    rank = lax.axis_index("ctx")
    cut = expand.shape[1]
    hw = WIDTH // 4
    for layer, (t, d) in enumerate(((t0, d0), (t1, d1))):
        bias = expand_bias[layer : layer + 1, :].astype(F32)
        rows = [v[layer : layer + 1, :].astype(F32) for v in (v0, v1, v2, v3, v4, v5, v6, v7)]
        rows += [bias[:, k * cut : (k + 1) * cut] for k in range(4)]
        rows.append(jnp.zeros((4, cut), F32))
        d[2 * cut :, :] = attend_out[layer]
        t[2 * cut :, 3 * hw :] = jnp.zeros((cut, WIDTH - 3 * hw), BF)
        t[2 * cut : 2 * cut + 16, VEC_AT : VEC_AT + cut] = jnp.concatenate(rows, axis=0).astype(BF)
        for k in range(4):

            @pl.when(rank == k)
            def _():
                for out, at in ((t, k), (d, k ^ 3)):
                    out[0:cut, :] = jnp.concatenate(
                        [
                            expand[layer, :, (2 * z + h) * 4 * cut + at * cut : (2 * z + h) * 4 * cut + (at + 1) * cut]
                            for h in range(2)
                            for z in range(4)
                        ],
                        axis=1,
                    )
                    out[cut : 2 * cut, :] = reduce[layer, at * cut : (at + 1) * cut, :]
                t[2 * cut :, 0 : 3 * hw] = jnp.concatenate(
                    [attend_in[layer, :, n * WIDTH + k * hw : n * WIDTH + (k + 1) * hw] for n in range(3)], axis=1
                )


def nothing_kernel(*refs):
    pass


def after(xs, *others):
    return pl.pallas_call(
        nothing_kernel,
        out_shape=[jax.ShapeDtypeStruct(x.shape, x.dtype) for x in xs],
        in_specs=[pl.BlockSpec(memory_space=pl.ANY)] * (len(xs) + len(others)),
        out_specs=[pl.BlockSpec(memory_space=pl.ANY)] * len(xs),
        input_output_aliases={n: n for n in range(len(xs))},
        cost_estimate=pl.CostEstimate(flops=WEIGHT, bytes_accessed=0, transcendentals=0),
        name="after",
    )(*xs, *others)


def pack_kernel(a, b, *rest):
    out, held, ins, outs = rest[-4:]
    coming = [pltpu.make_async_copy((a, b)[n // 4].at[n % 4], held.at[n // 4, n % 4], ins.at[n]) for n in range(8)]
    going = [pltpu.make_async_copy(held.at[n // 4, n % 4], out.at[n // 4, n % 4], outs.at[n]) for n in range(8)]
    for copy in coming:
        copy.start()
    for arrive, leave in zip(coming, going):
        arrive.wait()
        leave.start()
    for copy in going:
        copy.wait()


def pack(a, b, *others):
    shape = (2,) + a.shape
    return pl.pallas_call(
        pack_kernel,
        out_shape=jax.ShapeDtypeStruct(shape, a.dtype),
        in_specs=[pl.BlockSpec(memory_space=pl.ANY)] * (2 + len(others)),
        out_specs=pl.BlockSpec(memory_space=pl.ANY),
        scratch_shapes=[pltpu.VMEM(shape, a.dtype), pltpu.SemaphoreType.DMA((8,)), pltpu.SemaphoreType.DMA((8,))],
        cost_estimate=pl.CostEstimate(flops=0, bytes_accessed=0, transcendentals=0),
        name="pack",
    )(a, b, *others)


def half_kernel(meta, t, *rest):
    out, held, ins, outs = rest[-4:]
    coming = [pltpu.make_async_copy(t.at[z, meta[CORE], 0:2], held.at[z], ins.at[z]) for z in range(4)]
    going = [pltpu.make_async_copy(held.at[z], out.at[z], outs.at[z]) for z in range(4)]
    for copy in coming:
        copy.start()
    for arrive, leave in zip(coming, going):
        arrive.wait()
        leave.start()
    for copy in going:
        copy.wait()


def half_of(meta, t, *others):
    shape = (4, 2) + t.shape[3:]
    return pl.pallas_call(
        half_kernel,
        out_shape=jax.ShapeDtypeStruct(shape, t.dtype),
        in_specs=[pl.BlockSpec(memory_space=space) for space in [pltpu.SMEM] + [pl.ANY] * (1 + len(others))],
        out_specs=pl.BlockSpec(memory_space=pl.ANY),
        scratch_shapes=[pltpu.VMEM(shape, t.dtype), pltpu.SemaphoreType.DMA((4,)), pltpu.SemaphoreType.DMA((4,))],
        cost_estimate=pl.CostEstimate(flops=0, bytes_accessed=0, transcendentals=0),
        name="half",
    )(meta, t, *others)


def sums_kernel(*refs, layout, count, split):
    outs = refs[-len(layout) :]
    at = 0
    for out, parts in zip(outs, layout):
        lane = 0
        for n in parts:
            total = refs[at][...].astype(F32)
            for ref in refs[at + 1 : at + n]:
                total = total + ref[...].astype(F32)
            at += n
            if split:
                for k in range(len(outs)):
                    outs[k][...] = total[k].astype(BF)
            else:
                out[..., lane : lane + total.shape[-1]] = total.astype(BF)
            lane += total.shape[-1]
        if split:
            break


def sums(outputs, *others, split=0, weight=0):
    args = tuple(x for groups in outputs for group in groups for x in group)
    layout = tuple(tuple(len(group) for group in groups) for groups in outputs)
    if split:
        shapes = [(args[0].shape[1:], BF)] * split
        layout = layout * split
    else:
        shapes = [
            (groups[0][0].shape[:-1] + (sum(group[0].shape[-1] for group in groups),), BF) for groups in outputs
        ]
    return call(
        functools.partial(sums_kernel, layout=layout, count=len(args), split=split),
        shapes, args + others, [pltpu.VMEM] * len(args) + [pl.ANY] * len(others), [], "sums", weight, 0,
    )


def join_kernel(att, t, d, *rest):
    out = rest[-1]
    rows = att.shape[0]
    out[0:rows, 0 : att.shape[1]] = att[...]
    out[0:rows, att.shape[1] :] = jnp.zeros((rows, out.shape[1] - att.shape[1]), BF)
    for k in range(2):
        out[rows:, k * WIDTH : (k + 1) * WIDTH] = (t[k].astype(F32) + d[k].astype(F32)).astype(BF)


def merge_kernel(dwo, own, other, *rest):
    out = rest[-1]
    out[:, :, 0:WIDTH] = dwo[...]
    out[:, :, WIDTH:] = (own[...].astype(F32) + other[...].astype(F32)).astype(BF)


def vectors_of(shards, order):
    return jnp.concatenate([shards[f // 2, f % 2, :, 0:96] for f in order], axis=1).astype(F32)


NATURAL = tuple(range(8))
CORE_MAJOR = (0, 2, 4, 6, 1, 3, 5, 7)


def attn_fwd_kernel(
    meta, h0, h1, h2, h3, qrow, kcol, t, *rest, heads, tokens
):
    qkv, c0, c1, c2, c3, lse, q_s, k_s, vt_s, o_s, ctx, w_s, b_s, sems = rest[-14:]
    blocks = tokens // BLK
    hw = heads * HEAD_DIM
    copies = started_copies(
        sems, (t.at[:, :, 2, :, 0:VEC_AT], w_s), (t.at[:, :, 2, 0:16, VEC_AT : VEC_AT + 128], b_s)
    )
    for copy in copies:
        copy.wait()
    w = w_s[...].reshape(WIDTH, VEC_AT)[:, 0 : 3 * hw]
    vec = vectors_of(b_s, NATURAL)
    bias = jnp.zeros((1, 3 * hw), F32)
    for k in range(4):
        part = jnp.concatenate(
            [vec[6:7, k * hw : (k + 1) * hw], jnp.zeros((1, hw), F32), vec[7:8, k * hw : (k + 1) * hw]], axis=1
        )
        bias = jnp.where(meta[RANK] == k, part, bias)
    for j, piece in enumerate((h0, h1, h2, h3)):
        qkv[j] = (mm_nn(piece[...], w) + bias).astype(BF)
    for pair in range(blocks // 2):
        rows = []
        for block in (2 * pair, 2 * pair + 1):
            at, half = block_of(block, blocks)
            rows.append(qkv[meta[JMAP + at], half * BLK : (half + 1) * BLK, :])
        both = jnp.concatenate(rows, axis=0)
        lo, hi = 2 * pair * BLK, 2 * (pair + 1) * BLK
        for h in range(heads):
            q_s[h, lo:hi, :] = both[:, h * HEAD_DIM : (h + 1) * HEAD_DIM]
            k_s[h, lo:hi, :] = both[:, hw + h * HEAD_DIM : hw + (h + 1) * HEAD_DIM]
        vt_s[:, lo:hi] = both[:, 2 * hw :].T
    iota_k = lax.broadcasted_iota(jnp.int32, (QB, QB), 0)
    iota_q = lax.broadcasted_iota(jnp.int32, (QB, QB), 1)
    causal = iota_k <= iota_q
    head_rows = [slice(h * HEAD_DIM, (h + 1) * HEAD_DIM) for h in range(heads)]
    for i in range(tokens // QB):
        lo = i * QB
        starts_q = qrow[0:1, lo : lo + QB]

        def scores(at, diagonal):
            col = kcol[pl.ds(at, QB), :]
            allowed = jnp.concatenate([col, col], axis=1) == starts_q
            if diagonal:
                allowed = allowed & causal
            return [
                jnp.where(allowed, mm_nt(k_s[h, pl.ds(at, QB), :], q_s[h, lo : lo + QB, :]) * SCORE_SCALE, NEG)
                for h in range(heads)
            ]

        ss = scores(lo, True)
        tops = [jnp.max(s, axis=0, keepdims=True) for s in ss]
        ps = [jnp.exp2(s - top) for s, top in zip(ss, tops)]
        totals = [jnp.sum(p, axis=0, keepdims=True) for p in ps]
        outs = [mm_nn(vt_s[head_rows[h], lo : lo + QB], ps[h].astype(BF)) for h in range(heads)]

        def step(jb, carry):
            tops, totals, outs = carry
            at = pl.multiple_of(jb * QB, QB)
            ss = scores(at, False)
            new = [jnp.maximum(top, jnp.max(s, axis=0, keepdims=True)) for s, top in zip(ss, tops)]
            ps = [jnp.exp2(s - top) for s, top in zip(ss, new)]
            alphas = [jnp.exp2(top - n) for top, n in zip(tops, new)]
            totals = [
                total * alpha + jnp.sum(p, axis=0, keepdims=True) for total, alpha, p in zip(totals, alphas, ps)
            ]
            outs = [
                outs[h] * alphas[h] + mm_nn(vt_s[head_rows[h], pl.ds(at, QB)], ps[h].astype(BF)) for h in range(heads)
            ]
            return new, totals, outs

        if i > 0:
            tops, totals, outs = lax.fori_loop(meta[JMIN + i], i, step, (tops, totals, outs))
        for h in range(heads):
            o_s[head_rows[h], lo : lo + QB] = outs[h] / totals[h]
            lse[h : h + 1, lo : lo + QB] = tops[h] + jnp.log2(totals[h])
    for pair in range(blocks // 2):
        lo, hi = 2 * pair * BLK, 2 * (pair + 1) * BLK
        both = o_s[:, lo:hi].T.astype(BF)
        for n, block in enumerate((2 * pair, 2 * pair + 1)):
            at, half = block_of(block, blocks)
            ctx[meta[JMAP + at], :, half * hw : (half + 1) * hw] = both[n * BLK : (n + 1) * BLK, :]
    for j, out in enumerate((c0, c1, c2, c3)):
        out[...] = ctx[j]


def attn_bwd_kernel(
    meta, h0, h1, h2, h3, qrow, kcol, qkv, c0, c1, c2, c3, gctx, lse, t, *rest, heads, tokens
):
    (
        g_own, g_a, g_b, g_d, dw_own, dw_other, q_s, k_s, v_s, do_s, kt_s, delta_s, dk_s, dv_s, dqt_s, g_s, w_s, ctx, dw, sems,
    ) = rest[-20:]
    blocks = tokens // BLK
    hw = heads * HEAD_DIM
    scale = HEAD_DIM ** (-0.5)
    copies = started_copies(sems, (t.at[:, :, 2, :, 0:VEC_AT], w_s))
    for j, c in enumerate((c0, c1, c2, c3)):
        ctx[j] = c[...]
    for pair in range(blocks // 2):
        rows, grads, outs = [], [], []
        for block in (2 * pair, 2 * pair + 1):
            at, half = block_of(block, blocks)
            rows.append(qkv[meta[JMAP + at], half * BLK : (half + 1) * BLK, :])
            grads.append(gctx[meta[INV + at], :, half * hw : (half + 1) * hw])
            outs.append(ctx[meta[JMAP + at], :, half * hw : (half + 1) * hw])
        both = jnp.concatenate(rows, axis=0)
        grad = jnp.concatenate(grads, axis=0)
        out = jnp.concatenate(outs, axis=0)
        lo, hi = 2 * pair * BLK, 2 * (pair + 1) * BLK
        prod = (grad.astype(F32) * out.astype(F32)).T
        kt_s[:, lo:hi] = both[:, hw : 2 * hw].T
        for h in range(heads):
            c0, c1 = h * HEAD_DIM, (h + 1) * HEAD_DIM
            q_s[h, lo:hi, :] = both[:, c0:c1]
            k_s[h, lo:hi, :] = both[:, hw + c0 : hw + c1]
            v_s[h, lo:hi, :] = both[:, 2 * hw + c0 : 2 * hw + c1]
            do_s[h, lo:hi, :] = grad[:, c0:c1]
            delta_s[h : h + 1, lo:hi] = jnp.sum(prod[c0:c1, :], axis=0, keepdims=True)
    dk_s[...] = jnp.zeros_like(dk_s)
    dv_s[...] = jnp.zeros_like(dv_s)
    iota_k = lax.broadcasted_iota(jnp.int32, (QB, QB), 0)
    iota_q = lax.broadcasted_iota(jnp.int32, (QB, QB), 1)
    causal = iota_k <= iota_q
    head_rows = [slice(h * HEAD_DIM, (h + 1) * HEAD_DIM) for h in range(heads)]
    for i in range(tokens // QB):
        lo = i * QB
        starts_q = qrow[0:1, lo : lo + QB]

        def block(at, diagonal):
            col = kcol[pl.ds(at, QB), :]
            allowed = jnp.concatenate([col, col], axis=1) == starts_q
            if diagonal:
                allowed = allowed & causal
            keys = pl.ds(at, QB)
            cols = slice(lo, lo + QB)
            ss = [mm_nt(k_s[h, keys, :], q_s[h, cols, :]) for h in range(heads)]
            dps = [mm_nt(v_s[h, keys, :], do_s[h, cols, :]) for h in range(heads)]
            ps = [
                jnp.exp2(jnp.where(allowed, s * SCORE_SCALE, NEG) - lse[h : h + 1, cols]) for h, s in enumerate(ss)
            ]
            dss = [
                (p * (dp - delta_s[h : h + 1, cols])).astype(BF) for h, (p, dp) in enumerate(zip(ps, dps))
            ]
            for h in range(heads):
                dv_s[h, keys, :] += mm_nn(ps[h].astype(BF), do_s[h, cols, :])
            for h in range(heads):
                dk_s[h, keys, :] += mm_nn(dss[h], q_s[h, cols, :])
            return [mm_nn(kt_s[head_rows[h], keys], dss[h]) for h in range(heads)]

        dqs = block(lo, True)
        if i > 0:
            dqs = lax.fori_loop(
                meta[JMIN + i],
                i,
                lambda jb, acc: [x + y for x, y in zip(acc, block(pl.multiple_of(jb * QB, QB), False))],
                dqs,
            )
        for h in range(heads):
            dqt_s[head_rows[h], lo : lo + QB] = dqs[h] * scale
    for pair in range(blocks // 2):
        lo, hi = 2 * pair * BLK, 2 * (pair + 1) * BLK
        parts = [dqt_s[:, lo:hi].T.astype(BF)]
        parts += [(dk_s[h, lo:hi, :] * scale).astype(BF) for h in range(heads)]
        parts += [dv_s[h, lo:hi, :].astype(BF) for h in range(heads)]
        both = jnp.concatenate(parts, axis=1)
        for n, block_at in enumerate((2 * pair, 2 * pair + 1)):
            at, half = block_of(block_at, blocks)
            g_s[meta[JMAP + at], half * BLK : (half + 1) * BLK, :] = both[n * BLK : (n + 1) * BLK, :]
    for copy in copies:
        copy.wait()
    w = w_s[...].reshape(WIDTH, VEC_AT)[:, 0 : 3 * hw]
    total = None
    sums = None
    for j, piece in enumerate((h0, h1, h2, h3)):
        g = g_s[j]
        back = mm_nt(g, w)
        if j == 0:
            g_own[...] = back
        else:
            (g_a, g_b, g_d)[j - 1][...] = back.astype(BF)
        part = mm_tn(piece[...], g)
        col = jnp.sum(g.astype(F32), axis=0, keepdims=True)
        total = part if total is None else total + part
        sums = col if sums is None else sums + col
    shards, rows_out, cols = dw.shape
    rows = WIDTH // shards
    dw[:, 0:rows, :] = total.reshape(shards, rows, cols).astype(BF)
    dw[:, rows:, :] = jnp.broadcast_to(sums[None], (shards, rows_out - rows, cols)).astype(BF)
    for k in range(4):
        dw_own[k] = dw[2 * k + meta[CORE]]
        dw_other[k] = dw[2 * k + 1 - meta[CORE]]


def start_ffn_copies(core, t, a, b, d, crossed, e_s, r_s, sems):
    ca, cb = crossed.at[0], crossed.at[1]
    groups = []
    for p, parts in enumerate(((t,), (a, cb), (b, ca), (d,))):
        pairs = []
        if len(parts) == 1:
            pairs.append((parts[0].at[:, :, 0], e_s.at[p]))
            for h in range(2):
                pairs.append((parts[0].at[:, h, 1], r_s.at[p, h]))
        else:
            for src, parity in ((parts[0], core), (parts[1], 1 - core)):
                pairs.append((src.at[:, 0], e_s.at[p, :, parity]))
                pairs.append((src.at[:, 1], r_s.at[p, parity]))
        group = []
        for n, (src, dst) in enumerate(pairs):
            copy = pltpu.make_async_copy(src, dst, sems.at[p, n])
            copy.start()
            group.append(copy)
        groups.append(group)
    return groups


def ffn_scratch():
    return [
        pltpu.VMEM((4, 4, 2, 96, WIDTH), BF),
        pltpu.VMEM((4, 2, 4, 96, WIDTH), BF),
        pltpu.SemaphoreType.DMA((4, 4)),
        pltpu.VMEM((4, 2, 96, WIDTH), BF),
        pltpu.VMEM((4, 2, 16, 128), BF),
        pltpu.SemaphoreType.DMA((2,)),
    ]


def mlp_fwd_scratch(rows, hw):
    return ffn_scratch() + [pltpu.VMEM((4, rows, hw), BF), pltpu.VMEM((8, WIDTH), F32)]


def mlp_bwd_scratch():
    return ffn_scratch() + [pltpu.VMEM((8, WIDTH), F32)]


def wgrad_scratch():
    rows = 2 * BLK
    return [
        pltpu.VMEM((rows, 3 * WIDTH), BF),
        pltpu.VMEM((rows, 3 * WIDTH), BF),
        pltpu.VMEM((rows + 16, 6 * WIDTH), BF),
        pltpu.VMEM((rows + 16, 6 * WIDTH), BF),
        pltpu.SemaphoreType.DMA((16,)),
    ]


def attn_fwd_scratch(heads, tokens):
    hw = heads * HEAD_DIM
    return [
        pltpu.VMEM((heads, tokens, HEAD_DIM), BF),
        pltpu.VMEM((heads, tokens, HEAD_DIM), BF),
        pltpu.VMEM((hw, tokens), BF),
        pltpu.VMEM((hw, tokens), F32),
        pltpu.VMEM((4, BLK, 2 * hw), BF),
        pltpu.VMEM((4, 2, 96, VEC_AT), BF),
        pltpu.VMEM((4, 2, 16, 128), BF),
        pltpu.SemaphoreType.DMA((2,)),
    ]


def attn_bwd_scratch(heads, tokens):
    hw = heads * HEAD_DIM
    return [pltpu.VMEM((heads, tokens, HEAD_DIM), BF)] * 4 + [
        pltpu.VMEM((hw, tokens), BF),
        pltpu.VMEM((8, tokens), F32),
        pltpu.VMEM((heads, tokens, HEAD_DIM), F32),
        pltpu.VMEM((heads, tokens, HEAD_DIM), F32),
        pltpu.VMEM((hw, tokens), F32),
        pltpu.VMEM((4, tokens // 4, 3 * hw), BF),
        pltpu.VMEM((4, 2, 96, VEC_AT), BF),
        pltpu.VMEM((4, BLK, 2 * hw), BF),
        pltpu.VMEM((8, 112, 3 * hw), BF),
        pltpu.SemaphoreType.DMA((1,)),
    ]


def norm_parts(values):
    centre = values - jnp.mean(values, axis=-1, keepdims=True)
    spread = jnp.mean(centre * centre, axis=-1, keepdims=True)
    rstd = lax.rsqrt(spread + norm_eps)
    return centre * rstd, rstd


def shard_columns(x, parity):
    return jnp.concatenate([x[:, (2 * z + parity) * 96 : (2 * z + parity + 1) * 96] for z in range(4)], axis=1)


def mlp_fwd_kernel(
    writer, places, meta, c0, c1, c2, c3, hid, t, a, b, d, crossed,
    xhat1, rstd1, gp, xhat2, rstd2, l_mine, l_other, hlow, *rest, finish=True,
):
    hnext, (e_s, r_s, sems, wo_s, b_s, wo_sems, ctx, eb) = rest[:-8], rest[-8:]
    core = meta[CORE]
    xhat1_to, rstd1_to, gp_to, xhat2_to, rstd2_to, mine_to, other_to, hlow_to = places[:8]
    wo_copies = started_copies(
        wo_sems, (d.at[:, :, 2], wo_s), (t.at[:, :, 2, 0:16, VEC_AT : VEC_AT + 128], b_s)
    )
    copies = start_ffn_copies(core, t, a, b, d, crossed, e_s, r_s, sems)
    half_cols = WIDTH // 2
    hw = c0.shape[1] // 2
    for p, piece in enumerate((c0, c1, c2, c3)):
        for half in range(2):
            ctx[meta[RANK + p], half * BLK : (half + 1) * BLK, :] = piece[:, half * hw : (half + 1) * hw]

    def keep(parts, at):
        for parity in range(2):

            @pl.when(core == parity)
            def _():
                l_mine[:, at : at + half_cols] = parts[parity]

            @pl.when(core != parity)
            def _():
                l_other[:, at : at + half_cols] = parts[parity]

        for ref, to in ((l_mine, mine_to), (l_other, other_to)):
            writer.send(ref, to, slice(None), slice(at, at + half_cols))

    low = jnp.concatenate([ctx[rank] for rank in range(4)], axis=1)
    keep([shard_columns(low, parity) for parity in range(2)], half_cols)
    for copy in wo_copies:
        copy.wait()
    vec = vectors_of(b_s, NATURAL)
    eb[...] = vectors_of(b_s, CORE_MAJOR)[8:16, :]
    wo = wo_s[...].reshape(WIDTH, WIDTH)
    first_sum = hid[...].astype(F32) + (mm_nn(low, wo) + vec[0:1, :])
    x1, r1 = norm_parts(first_sum)
    xhat1[...] = x1
    rstd1[...] = r1
    writer.send(xhat1, xhat1_to)
    writer.send(rstd1, rstd1_to)
    normed = x1 * vec[1:2, :] + vec[2:3, :]
    lown = normed.astype(BF)
    keep([shard_columns(lown, parity) for parity in range(2)], 0)
    out = normed + vec[3:4, :]
    for p in range(4):
        for copy in copies[p]:
            copy.wait()
        bias = eb[pl.ds(meta[RANK + p], 1), :]
        u = mm_nn(lown, e_s[p].reshape(WIDTH, WIDTH)) + bias
        cdf = 0.5 * (1.0 + lax.erf(u * 0.7071067811865476))
        pdf = jnp.exp(-0.5 * u * u) * 0.3989422804014327
        low = (u * cdf).astype(BF)
        cut = slice(p * WIDTH, (p + 1) * WIDTH)
        gp[:, cut] = (cdf + u * pdf).astype(BF)
        writer.send(gp, gp_to, slice(None), cut)
        keep([low[:, :half_cols], low[:, half_cols:]], WIDTH + p * half_cols)
        out = out + mm_nn(low, r_s[p].reshape(WIDTH, WIDTH))
    x2, r2 = norm_parts(out)
    nxt = x2 * vec[4:5, :] + vec[5:6, :]
    hlow[...] = nxt.astype(BF)
    writer.send(hlow, hlow_to)
    xhat2[...] = x2
    writer.send(xhat2, xhat2_to)
    rstd2[...] = r2
    writer.send(rstd2, rstd2_to)
    if hnext:
        hnext[0][...] = nxt
        writer.send(hnext[0], places[8])
    if finish:
        writer.finish()


def norm_back(gy, gain, xhat, rstd):
    g = gy * gain
    return rstd * (g - jnp.mean(g, axis=-1, keepdims=True) - xhat * jnp.mean(g * xhat, axis=-1, keepdims=True))


def rows_sum(x):
    return jnp.sum(x, axis=0, keepdims=True)


def mlp_bwd_kernel(
    writer, places, meta, xhat1, rstd1, xhat2, rstd2, gp, *rest, parts, loaded=False
):
    t, a, b, d, crossed = rest[parts : parts + 5]
    gfs, dgg, gctx, e_s, r_s, sems, wo_s, b_s, wo_sems, eb_s = rest[-10:]
    rows = gfs.shape[0]
    core = meta[CORE]
    if loaded:
        copies, wo_copies = [[]] * 4, []
    else:
        copies = start_ffn_copies(core, t, a, b, d, crossed, e_s, r_s, sems)
        wo_copies = started_copies(
            wo_sems, (d.at[:, :, 2], wo_s), (t.at[:, :, 2, 0:16, VEC_AT : VEC_AT + 128], b_s)
        )
    grad = rest[0][...].astype(F32)
    for ref in rest[1:parts]:
        grad = grad + ref[...].astype(F32)
    x2 = xhat2[...]
    for copy in wo_copies:
        copy.wait()
    vec = vectors_of(b_s, NATURAL)
    gss = norm_back(grad, vec[4:5, :], x2, rstd2[...])
    low = gss.astype(BF)
    cut = slice(4 * WIDTH, 5 * WIDTH)
    dgg[0:rows, cut] = low
    writer.send(dgg.at[0:rows, cut], places[1].at[0:rows, cut])
    sums = [None] * 8
    sums[4] = rows_sum(grad * x2)
    sums[5] = rows_sum(grad)
    sums[3] = rows_sum(low.astype(F32))
    gn = gss
    eb_s[...] = jnp.zeros_like(eb_s)
    for p in range(4):
        for copy in copies[p]:
            copy.wait()
        ga = mm_nt(low, r_s[p].reshape(WIDTH, WIDTH))
        dip = (ga * gp[:, p * WIDTH : (p + 1) * WIDTH].astype(F32)).astype(BF)
        cut = slice(p * WIDTH, (p + 1) * WIDTH)
        dgg[0:rows, cut] = dip
        writer.send(dgg.at[0:rows, cut], places[1].at[0:rows, cut])
        eb_s[pl.ds(meta[RANK + p], 1), :] = rows_sum(dip.astype(F32))
        gn = gn + mm_nt(dip, e_s[p].reshape(WIDTH, WIDTH))
    x1 = xhat1[...]
    gf = norm_back(gn, vec[1:2, :], x1, rstd1[...])
    sums[1] = rows_sum(gn * x1)
    sums[2] = rows_sum(gn)
    lowa = gf.astype(BF)
    cut = slice(5 * WIDTH, 6 * WIDTH)
    dgg[0:rows, cut] = lowa
    writer.send(dgg.at[0:rows, cut], places[1].at[0:rows, cut])
    gfs[...] = gf
    writer.send(gfs, places[0])
    sums[0] = rows_sum(lowa.astype(F32))
    sums[6] = jnp.zeros_like(sums[0])
    sums[7] = sums[6]
    gc = mm_nt(lowa, wo_s[...].reshape(WIDTH, WIDTH)).astype(BF)
    hw = gctx.shape[2] // 2
    for rank in range(4):
        for half in range(2):
            gctx[rank, :, half * hw : (half + 1) * hw] = gc[half * BLK : (half + 1) * BLK, rank * hw : (rank + 1) * hw]
    writer.send(gctx, places[2])
    vecs = jnp.concatenate(sums, axis=0)
    ebs = jnp.concatenate([eb_s[:, (4 * (f % 2) + f // 2) * 96 : (4 * (f % 2) + f // 2 + 1) * 96] for f in range(8)], axis=1)
    dgg[rows:, 0:WIDTH] = jnp.concatenate([vecs, ebs], axis=0).astype(BF)
    dgg[rows:, WIDTH:] = jnp.zeros((16, 5 * WIDTH), BF)
    writer.send(dgg.at[rows:], places[1].at[rows:])
    writer.finish()


def wgrad_kernel(writer, places, meta, l_mine_from, l_other_from, dgg_from, dgg_other_from, *rest):
    t, a, b, dwo, d, l_mine, l_other, dgg, dgg_other, sems = rest[-10:]
    half = WIDTH // 2
    rows = l_mine.shape[0]

    def fetch(n, src, dst, at, width):
        copy = pltpu.make_async_copy(src.at[:, at : at + width], dst.at[:, at : at + width], sems.at[n])
        copy.start()
        return copy

    lefts = [fetch(n, src, dst, 0, WIDTH) for n, (src, dst) in enumerate(((l_mine_from, l_mine), (l_other_from, l_other)))]
    rights = {}
    for k in (3, 4, 1, 2, 0, 5):
        q = SWAPPED[k] if k < 4 else k
        rights[k] = [fetch(4 + k, dgg_from, dgg, k * WIDTH, WIDTH), fetch(10 + k, dgg_other_from, dgg_other, q * WIDTH, WIDTH)]
        if k == 3:
            acts = [
                fetch(2 + n, src, dst, WIDTH, 2 * WIDTH)
                for n, (src, dst) in enumerate(((l_mine_from, l_mine), (l_other_from, l_other)))
            ]

    def wait(copies):
        for copy in copies:
            copy.wait()

    def grad(left, left_other, right, right_other):
        return mm_nn(left, dgg[0:rows, right : right + WIDTH]) + mm_nn(
            left_other, dgg_other[0:rows, right_other : right_other + WIDTH]
        )

    def left(at, at_other):
        return l_mine[:, at : at + half].T, l_other[:, at_other : at_other + half].T

    wait(lefts)
    low = left(0, 0)
    for n, (p, out) in enumerate(((3, d), (1, a), (2, b), (0, t))):
        q = SWAPPED[p]
        wait(rights[p])
        out[:, 0] = grad(*low, p * WIDTH, q * WIDTH).reshape(4, 96, WIDTH).astype(BF)
        if n == 0:
            wait(acts)
            wait(rights[4])
        out[:, 1] = (
            grad(*left(WIDTH + p * half, WIDTH + q * half), 4 * WIDTH, 4 * WIDTH).reshape(4, 96, WIDTH).astype(BF)
        )
        writer.send(out, places[(4, 1, 2, 0)[n]])
    wait(rights[5])
    dwo[:, 0:96, :] = grad(*left(half, half), 5 * WIDTH, 5 * WIDTH).reshape(4, 96, WIDTH).astype(BF)
    vecs = dgg[rows:, 0:WIDTH].astype(F32) + dgg_other[rows:, 0:WIDTH].astype(F32)
    dwo[:, 96:, :] = jnp.zeros((4, 16, WIDTH), BF)
    for parity in range(2):

        @pl.when(meta[CORE] == parity)
        def _():
            for z in range(4):
                dwo[z, 96:, 0:96] = vecs[:, (2 * z + parity) * 96 : (2 * z + parity + 1) * 96].astype(BF)

    writer.send(dwo, places[3])
    writer.finish()


def place_kernel(
    meta, *rest, layer, last
):
    if last:
        parts = [((f.at[0], f.at[1]), a) for f, a in zip(rest[:4], rest[4:8])]
        small_in, rest = rest[8], rest[13:]
    else:
        parts = [((x.at[112:, 0:WIDTH], x.at[112:, WIDTH:]), x.at[0:112, :]) for x in rest[:4]]
        rest = rest[5:]
    e_hbm, r_hbm, i_hbm, o_hbm = rest[:4]
    smalls = rest[4:-10]
    e_s, i_s, b_s, e_out, r_out, i_out, o_out, small_s, eb_s, sems = rest[-10:]
    for p, (ffn, att) in enumerate(parts):
        rank = meta[RANK + p]
        r_out[pl.ds(pl.multiple_of(rank * 96, 96), 96), :] = ffn[1][...].astype(F32)
        e_s[rank] = ffn[0][...].astype(F32)
        i_s[rank] = att[0:96, WIDTH : WIDTH + 9 * HEAD_DIM].astype(F32)
        b_s[rank] = att[96:112, WIDTH : WIDTH + 9 * HEAD_DIM].astype(F32)
    copies = []

    def send(n, src, dst):
        copy = pltpu.make_async_copy(src, dst.at[layer], sems.at[n])
        copy.start()
        copies.append(copy)

    send(0, r_out, r_hbm)
    for f in range(8):
        at = (4 * (f % 2) + f // 2) * 96
        e_out[:, f * 384 : (f + 1) * 384] = jnp.concatenate([e_s[c, :, at : at + 96] for c in range(4)], axis=1)
    send(1, e_out, e_hbm)
    hw = WIDTH // 4
    for k in range(3):
        i_out[:, k * WIDTH : (k + 1) * WIDTH] = jnp.concatenate(
            [i_s[c, :, k * hw : (k + 1) * hw] for c in range(4)], axis=1
        )
    send(2, i_out, i_hbm)
    wo = [att[:, 0:WIDTH].astype(F32) for _, att in parts]
    total = (wo[0] + wo[1]) + (wo[2] + wo[3])
    o_out[...] = total[0:96, :]
    send(3, o_out, o_hbm)
    bias = b_s[lax.shift_right_logical(meta[SHARD], 1)]
    low_half = (meta[SHARD] & 1) == 0
    qb = jnp.where(low_half, bias[:, 0:96], bias[:, 96:192])
    vb = jnp.where(low_half, bias[:, 2 * hw : 2 * hw + 96], bias[:, 2 * hw + 96 : 3 * hw])
    rows = jnp.concatenate([total[96:102, 0:96], qb[0:1], vb[0:1], total[104:112, 0:96]], axis=0)
    if last:
        for n, ref in enumerate(smalls[:-1]):
            ref[...] = jnp.concatenate([rows[n : n + 1], small_in[n : n + 1, 0:96]], axis=0)
        smalls[-1][...] = jnp.concatenate(
            [
                jnp.concatenate([x[8 + c : 9 + c, 0:96] for c in range(4)], axis=1)
                for x in (rows, small_in[...])
            ],
            axis=0,
        )
    else:
        smalls[0][...] = rows
    for copy in copies:
        copy.wait()


def permutation(ctx, fsdp, move):
    return [
        (c * fsdp + f, move(c, f)[0] * fsdp + move(c, f)[1]) for c in range(ctx) for f in range(fsdp)
    ]


def add(*parts):
    total = parts[0].astype(F32)
    for part in parts[1:]:
        total = total + part.astype(F32)
    return total


def on_device_fast(
    activations, cotangent, doc_start, deal,
    attend_in, query_bias, value_bias, attend_out, attend_bias, first_gain, first_shift,
    expand_proj, expand_bias, reduce_proj, reduce_bias, second_gain, second_shift,
    *, ctx, fsdp,
):
    S = [pltpu.SMEM]
    V = [pltpu.VMEM]
    A = [pl.ANY]
    axes = ("ctx", "fsdp")

    def via(move):
        perm = permutation(ctx, fsdp, move)
        return lambda x: lax.ppermute(x, axes, perm)

    via_first = via(lambda c, f: (c ^ (1 + f % 2), f))
    via_second = via(lambda c, f: (c ^ (2 - f % 2), f))
    via_diagonal = via(lambda c, f: (c ^ 3, f))
    via_core = via(lambda c, f: (c, f ^ 1))
    via_z = [None] + [via(lambda c, f, k=k: (c, f ^ (2 * k))) for k in range(1, 4)]

    def exchange_ctx(own, a, b, d):
        return (own, via_first(a), via_second(b), via_diagonal(d))

    def spread_ctx(x):
        return (x, via_first(x), via_second(x), via_diagonal(x))

    def reduce_z(x):
        return lax.psum_scatter(x, "fsdp", scatter_dimension=0, tiled=True, axis_index_groups=zgroups)

    def exchange_z(own, *others):
        return (own,) + tuple(via_z[k + 1](x) for k, x in enumerate(others))

    def gather_ctx(x):
        a, b = via_first(x), via_second(x)
        return (x, a, b, via_second(a))

    heads = HEADS // ctx
    hw = heads * HEAD_DIM
    rows = activations.shape[1]
    tokens = rows * ctx
    cut = WIDTH // fsdp
    c = lax.axis_index("ctx").astype(jnp.int32)
    shard = lax.axis_index("fsdp").astype(jnp.int32)
    core = shard % 2
    zgroups = [[2 * z + k for z in range(fsdp // 2)] for k in range(2)]

    hidden = activations[0]
    gathered = gather_ctx(hidden)
    small = (attend_bias, first_gain, first_shift, reduce_bias, second_gain, second_shift, query_bias, value_bias)
    sent = call(
        prep_kernel,
        [((3 * cut, WIDTH), BF)] * 4,
        (expand_proj, reduce_proj, attend_in, attend_out, expand_bias) + small,
        V * 13,
        [],
        "prep",
        0,
        8 * 1024 * 1024,
    )

    def gather_ffn(x):
        x = lax.all_gather(x, "fsdp", axis=0, tiled=True)
        return x.reshape(fsdp // 2, 2, 3, cut, WIDTH)

    ranks = jnp.arange(ctx, dtype=jnp.int32)
    inv = jnp.sum(jnp.where(deal[None, :] == ranks[:, None], ranks[None, :], 0), axis=1).astype(jnp.int32)
    starts = lax.all_gather(doc_start[0], "ctx", axis=0, tiled=True)
    by_rank = starts.reshape(ctx, 2, BLK)
    chosen = inv[:, None, None, None] == ranks[None, :, None, None]
    by_block = jnp.sum(jnp.where(chosen, by_rank[None], 0), axis=1)
    logical = jnp.concatenate([by_block[:, 0], by_block[::-1, 1]], axis=0).reshape(-1)
    qrow = jnp.broadcast_to(logical[None, :], (8, tokens))
    kcol = jnp.broadcast_to(logical[:, None], (tokens, 128))
    jmin = jnp.min(logical.reshape(tokens // QB, QB), axis=1) // QB

    m1 = 1 + core
    mask = inv ^ c
    jmap = jnp.where((core == 1) & (mask > 0) & (mask < 3), 3 - mask, mask)
    meta = jnp.concatenate(
        [jnp.stack([core, shard, c, c ^ m1, c ^ (3 - m1), c ^ 3]), jmap, inv, jmin]
    ).astype(jnp.int32)

    kept = []
    earlier = ()
    wide = [gather_ffn(sent[0]), gather_ffn(sent[1]), None, None]
    wide[0] = after((wide[0],), starts, *gathered[1:])[0]
    wide[2] = gather_ffn(*after(sent[2:3], wide[0]))
    pieces = []
    for layer in range(LAYERS):
        t, d = wide[2 * layer : 2 * layer + 2]
        mine = half_of(meta, t, *gathered[1:])
        a, b = via_first(mine), via_second(mine)
        qkv, *ctx_own, lse = call(
            functools.partial(attn_fwd_kernel, heads=heads, tokens=tokens),
            [((ctx, rows, 3 * hw), BF)] + [((BLK, 2 * hw), BF)] * 4 + [((8, tokens), F32)],
            (meta,) + gathered + (qrow, kcol, t, mine) + earlier,
            S + V * 6 + A * (2 + len(earlier)),
            attn_fwd_scratch(heads, tokens),
            "attn_fwd",
            2 * tokens * WIDTH * 3 * hw * 4,
            10 * 1024 * 1024,
        )
        cx = exchange_ctx(*ctx_own)
        if layer + 1 < LAYERS:
            wide[3] = gather_ffn(*after(sent[3:4], *cx[1:]))
        pieces.append((t, a, b, d, via_core(pack(a, b, lse))))
        kinds = {
            "xhat": ((rows, WIDTH), F32), "rstd": ((rows, 1), F32), "gp": ((rows, 4 * WIDTH), BF),
            "left": ((rows, 3 * WIDTH), BF), "low": ((rows, WIDTH), BF),
        }
        norms = [kinds[name] for name in ("xhat", "rstd", "gp", "xhat", "rstd")]
        lows = [kinds[name] for name in ("left", "left", "low")]
        back_outs = [((rows, WIDTH), F32), ((rows + 16, 6 * WIDTH), BF), ((ctx, BLK, 2 * hw), BF)]
        if layer + 1 < LAYERS:
            xhat1, rstd1, gp, xhat2, rstd2, l_mine, l_other, hlow, hidden_next = call_writing(
                mlp_fwd_kernel,
                norms + lows + [kinds["xhat"]],
                (meta,) + cx + (hidden,) + pieces[layer],
                S + V * 5 + A * 5,
                mlp_fwd_scratch(rows, hw),
                "mlp_fwd",
                24,
            )
        else:
            xhat1 = rstd1 = gp = xhat2 = rstd2 = None
            l_mine, l_other, hlow, *last_back = call_writing(
                last_kernel,
                lows + back_outs,
                (meta,) + cx + (hidden, cotangent[0]) + pieces[layer],
                S + V * 6 + A * 5,
                [pltpu.VMEM(*kind) for kind in norms] + mlp_fwd_scratch(rows, hw) + [pltpu.VMEM((8, WIDTH), F32)],
                "last",
                36,
            )
        l_other = via_core(l_other)
        earlier = (l_other,)
        kept.append((gathered, qkv, ctx_own, lse, xhat1, rstd1, gp, xhat2, rstd2, l_mine, l_other))
        if layer + 1 < LAYERS:
            hidden = hidden_next
            gathered = gather_ctx(hlow)
    out_act = hlow[None]

    for layer in reversed(range(LAYERS)):
        gathered, qkv, ctx_own, lse, xhat1, rstd1, gp, xhat2, rstd2, l_mine, l_other = kept[layer]
        if layer + 1 == LAYERS:
            gfs, dgg, gctx = last_back
        else:
            gfs, dgg, gctx = call_writing(
                mlp_bwd_kernel,
                back_outs,
                (meta, xhat1, rstd1, xhat2, rstd2, gp) + grads + pieces[layer] + order,
                S + V * (5 + len(grads)) + A * (5 + len(order)),
                mlp_bwd_scratch(),
                "mlp_bwd",
                12,
                parts=len(grads),
            )
        gcx = lax.all_to_all(gctx, "ctx", 0, 0, tiled=True)
        piece = ((4, 2, cut, WIDTH), BF)

        def weight_grads(*before):
            return call_writing(
                wgrad_kernel,
                [piece] * 3 + [((4, cut + 16, WIDTH), BF), piece],
                (meta, l_mine, l_other, dgg, via_core(dgg)) + before,
                S + A * (4 + len(before)),
                wgrad_scratch(),
                "wgrad",
                5,
            )

        def attention_grads(*before):
            return call(
                functools.partial(attn_bwd_kernel, heads=heads, tokens=tokens),
                [
                    ((rows, WIDTH), F32), ((rows, WIDTH), BF), ((rows, WIDTH), BF), ((rows, WIDTH), BF),
                    ((4, cut + 16, 3 * hw), BF), ((4, cut + 16, 3 * hw), BF),
                ],
                (meta,) + gathered + (qrow, kcol, qkv) + tuple(ctx_own) + (gcx, lse, wide[2 * layer]) + before,
                S + V * 13 + A * (1 + len(before)),
                attn_bwd_scratch(heads, tokens),
                "attn_bwd",
                2 * tokens * WIDTH * 3 * hw * 8,
                10 * 1024 * 1024,
            )

        def attention_shards(dwo, dw, crossed, *others):
            shape = (4, cut + 16, WIDTH + 3 * hw)
            (merged,) = call(
                merge_kernel, [(shape, BF)], (dwo, dw, crossed) + others, V * 3 + A * len(others), [], "merge", 0, 0
            )
            return merged, reduce_z(merged).reshape(shape[1:])

        if layer > 0:
            g_own, g_a, g_b, g_d, dw, dw_other = attention_grads(l_other)
            (over,) = sums([[(g_a, via_second(g_d))]])
            t, a, b, dwo, d = weight_grads(over)
            d1 = reduce_z(d)
            over = via_first(over)
            merged, att1 = attention_shards(dwo, dw, via_core(dw_other))
            back = via_second(g_b)
            grads = (gfs, g_own, back, over)
            a, b = after((a, b), over, back)
            order = (merged, a, b)
            parts1 = (t, via_first(a), via_second(b))
        else:
            (t1,) = sums([[parts1]], gcx, weight=WEIGHT)
            t, a, b, dwo, d = weight_grads(gcx, att1, t1)
            t1 = reduce_z(t1)
            from_b, from_d = via_second(b), via_second(d)
            g_own, g_a, g_b, g_d, dw, dw_other = attention_grads(t)

    def shards(x):
        return x.reshape(2, cut, WIDTH)

    a0, t0 = sums([[(a, from_d)], [(t, from_b)]], g_d, weight=WEIGHT)
    from_a = via_first(a0)
    merged, att0 = attention_shards(dwo, dw, via_core(dw_other), a0)
    back = via_second(g_d), via_second(g_b)
    shape = (2 * cut + 16, 2 * WIDTH)
    (joined,) = call(
        join_kernel, [(shape, BF)], (att1, shards(t1), shards(via_diagonal(d1)), merged), V * 3 + A, [], "join", WEIGHT, 0
    )
    (over,) = sums([[(g_a, back[0])]], joined)
    joined = spread_ctx(joined)
    (t0,) = sums([[(t0, from_a)]], over, weight=WEIGHT)
    over = via_first(over)
    ffn0 = shards(reduce_z(t0))

    small_out = None
    placed = []
    for layer in reversed(range(LAYERS)):
        if layer == 0:
            sent = spread_ctx(ffn0) + spread_ctx(att0)
            waits = ()
        else:
            sent = joined
            waits = (t0,)
        last = layer == 0
        big = [
            ((LAYERS, cut, 4 * WIDTH), F32), ((LAYERS, 4 * cut, WIDTH), F32),
            ((LAYERS, cut, 3 * WIDTH), F32), ((LAYERS, cut, WIDTH), F32),
        ]
        if last:
            smalls = [((LAYERS, cut), F32)] * 8 + [((LAYERS, 4 * cut), F32)]
        else:
            smalls = [((16, cut), F32)]
        args = (meta,) + sent + ((small_out,) + tuple(placed) if last else waits)
        spaces = S + V * len(sent) + (V + A * 4 if last else A)
        outs = pl.pallas_call(
            functools.partial(place_kernel, layer=layer, last=last),
            out_shape=[jax.ShapeDtypeStruct(shape, dtype) for shape, dtype in big + smalls],
            in_specs=[pl.BlockSpec(memory_space=space) for space in spaces],
            out_specs=[pl.BlockSpec(memory_space=space) for space in A * 4 + V * len(smalls)],
            scratch_shapes=[
                pltpu.VMEM((ctx, cut, WIDTH), F32), pltpu.VMEM((ctx, cut, 3 * hw), F32),
                pltpu.VMEM((ctx, 16, 3 * hw), F32),
                pltpu.VMEM((cut, 4 * WIDTH), F32), pltpu.VMEM((4 * cut, WIDTH), F32),
                pltpu.VMEM((cut, 3 * WIDTH), F32), pltpu.VMEM((cut, WIDTH), F32),
                pltpu.VMEM((16, 128), F32), pltpu.VMEM((8, 128), F32),
                pltpu.SemaphoreType.DMA((4,)),
            ],
            input_output_aliases={10 + n: n for n in range(4)} if last else {},
            compiler_params=pltpu.CompilerParams(vmem_limit_bytes=VMEM_LIMIT),
            cost_estimate=pl.CostEstimate(flops=0, bytes_accessed=10 * 1024 * 1024, transcendentals=0),
            name="place",
        )(*args)
        placed = outs[:4]
        small_out = outs[4]
        vectors = outs[4:]
    in_grad = add(gfs, g_own, back[1], over)[None]
    e_out, r_out, i_out, o_out = placed
    ab, fg, fs, rb, sg, ss, qb, vb, xb = vectors
    return (out_act, in_grad, i_out, qb, vb, o_out, ab, fg, fs, e_out, xb, r_out, rb, sg, ss)


def on_device(*args, ctx, fsdp):
    if ctx == 4 and fsdp == 8 and args[0].shape[1] == 2 * BLK:
        return on_device_fast(*args, ctx=ctx, fsdp=fsdp)
    return on_device_plain(*args)


def solution(mesh):
    placed = (
        P("fsdp", "ctx", None),
        P("fsdp", "ctx", None),
        P("fsdp", "ctx"),
        P(),
        P(None, "fsdp", None),
        P(None, "fsdp"),
        P(None, "fsdp"),
        P(None, "fsdp", None),
        P(None, "fsdp"),
        P(None, "fsdp"),
        P(None, "fsdp"),
        P(None, "fsdp", None),
        P(None, "fsdp"),
        P(None, "fsdp", None),
        P(None, "fsdp"),
        P(None, "fsdp"),
        P(None, "fsdp"),
    )
    return jax.shard_map(
        functools.partial(on_device, ctx=mesh.shape["ctx"], fsdp=mesh.shape["fsdp"]),
        mesh=mesh,
        in_specs=placed,
        out_specs=(
            P("fsdp", "ctx", None),
            P("fsdp", "ctx", None),
            P(None, "fsdp", None),
            P(None, "fsdp"),
            P(None, "fsdp"),
            P(None, "fsdp", None),
            P(None, "fsdp"),
            P(None, "fsdp"),
            P(None, "fsdp"),
            P(None, "fsdp", None),
            P(None, "fsdp"),
            P(None, "fsdp", None),
            P(None, "fsdp"),
            P(None, "fsdp"),
            P(None, "fsdp"),
        ),
        check_vma=False,
    )
```

```python
import functools

import jax
import jax.numpy as jnp
from jax import lax
from jax.experimental import pallas as pl
from jax.experimental.pallas import tpu as pltpu
from jax.sharding import PartitionSpec as P

HEADS = 12
HEAD_DIM = 64
LAYERS = 2
BLK = 192


norm_eps = 1e-05


def for_sending(x):
    return jax.tree.map(lambda a: a.astype(jnp.bfloat16) if a.dtype == jnp.float32 else a, x)


def layer_norm(values, gain, shift):
    centre = values - jnp.mean(values, axis=-1, keepdims=True)
    spread = jnp.mean(centre * centre, axis=-1, keepdims=True)
    return centre * lax.rsqrt(spread + norm_eps) * gain + shift


def gelu_exact(inputs):
    return 0.5 * inputs * (1.0 + jax.scipy.special.erf(inputs * 0.7071067811865476))


def key_positions(deal):
    pairs = deal.shape[0]
    offsets = jnp.arange(BLK, dtype=jnp.int32)
    first = deal[:, None] * BLK + offsets[None, :]
    second = (2 * pairs - 1 - deal)[:, None] * BLK + offsets[None, :]
    return jnp.concatenate([first, second], axis=1).reshape(-1)


def split_heads(matrix):
    return matrix.reshape(matrix.shape[0], HEADS, HEAD_DIM).transpose(1, 0, 2)


def join_heads(stacked):
    return stacked.transpose(1, 0, 2).reshape(stacked.shape[1], HEADS * HEAD_DIM)


def attend_forward(queries, keys_full, values_full, allowed):

    def one_head(items):
        head_q, head_k, head_v = items
        scores = jnp.einsum(
            "qd,kd->qk", head_q, head_k, preferred_element_type=jnp.float32
        ) * HEAD_DIM ** (-0.5)
        scores = jnp.where(allowed, scores, -1e30)
        top = jnp.max(scores, axis=-1, keepdims=True)
        weights = jnp.exp(scores - top)
        total = jnp.sum(weights, axis=-1, keepdims=True)
        probs = (weights / total).astype(jnp.bfloat16)
        output = jnp.einsum("qk,kd->qd", probs, head_v, preferred_element_type=jnp.float32)
        return (output, top[:, 0] + jnp.log(total[:, 0]))

    outputs, log_totals = lax.map(
        one_head, (split_heads(queries), split_heads(keys_full), split_heads(values_full))
    )
    return (join_heads(outputs), log_totals)


def attend_backward(queries, keys_full, values_full, log_totals, grad_context, allowed):

    def one_head(items):
        head_q, head_k, head_v, head_lse, head_grad = items
        scores = jnp.einsum(
            "qd,kd->qk", head_q, head_k, preferred_element_type=jnp.float32
        ) * HEAD_DIM ** (-0.5)
        scores = jnp.where(allowed, scores, -1e30)
        probs = jnp.exp(scores - head_lse[:, None])
        grad_probs = jnp.einsum("qd,kd->qk", head_grad, head_v, preferred_element_type=jnp.float32)
        inner_sum = jnp.sum(probs * grad_probs, axis=-1, keepdims=True)
        grad_scores = (probs * (grad_probs - inner_sum)).astype(jnp.bfloat16)
        grad_q = jnp.einsum(
            "qk,kd->qd", grad_scores, head_k, preferred_element_type=jnp.float32
        ) * HEAD_DIM ** (-0.5)
        grad_k = jnp.einsum(
            "qk,qd->kd", grad_scores, head_q, preferred_element_type=jnp.float32
        ) * HEAD_DIM ** (-0.5)
        grad_v = jnp.einsum(
            "qk,qd->kd", probs.astype(jnp.bfloat16), head_grad, preferred_element_type=jnp.float32
        )
        return (grad_q, grad_k, grad_v)

    grads = lax.map(
        one_head,
        (
            split_heads(queries),
            split_heads(keys_full),
            split_heads(values_full),
            log_totals,
            split_heads(grad_context),
        ),
    )
    return (join_heads(grads[0]), join_heads(grads[1]), join_heads(grads[2]))


def forward_layer(hidden, weights, allowed):
    (
        attend_in,
        query_bias,
        value_bias,
        attend_out,
        attend_bias,
        first_gain,
        first_shift,
        expand_proj,
        expand_bias,
        reduce_proj,
        reduce_bias,
        second_gain,
        second_shift,
    ) = weights
    width = hidden.shape[1]
    low_hidden = hidden.astype(jnp.bfloat16)
    projected = jnp.dot(low_hidden, attend_in, preferred_element_type=jnp.float32)
    queries = (projected[:, :width] + query_bias.astype(jnp.float32)).astype(jnp.bfloat16)
    keys_own = projected[:, width : 2 * width].astype(jnp.bfloat16)
    values_own = (projected[:, 2 * width :] + value_bias.astype(jnp.float32)).astype(jnp.bfloat16)
    keys_full, values_full = (
        lax.all_gather(keys_own, "ctx", axis=0, tiled=True),
        lax.all_gather(values_own, "ctx", axis=0, tiled=True),
    )
    context, log_totals = attend_forward(queries, keys_full, values_full, allowed)
    low_context = context.astype(jnp.bfloat16)
    branch = jnp.dot(
        low_context, attend_out, preferred_element_type=jnp.float32
    ) + attend_bias.astype(jnp.float32)
    first_sum = hidden + branch
    normed = layer_norm(first_sum, first_gain.astype(jnp.float32), first_shift.astype(jnp.float32))
    low_normed = normed.astype(jnp.bfloat16)
    inner_pre = jnp.dot(
        low_normed, expand_proj, preferred_element_type=jnp.float32
    ) + expand_bias.astype(jnp.float32)
    active = gelu_exact(inner_pre).astype(jnp.bfloat16)
    output_branch = jnp.dot(
        active, reduce_proj, preferred_element_type=jnp.float32
    ) + reduce_bias.astype(jnp.float32)
    second_sum = normed + output_branch
    output = layer_norm(
        second_sum, second_gain.astype(jnp.float32), second_shift.astype(jnp.float32)
    )
    saved = (
        low_hidden,
        queries,
        keys_full,
        values_full,
        log_totals,
        low_context,
        first_sum,
        low_normed,
        inner_pre,
        active,
        second_sum,
    )
    return (output, saved)


def column_sum(matrix):
    return jnp.sum(matrix.astype(jnp.float32), axis=0)


def backward_layer(grad_hidden, weights, saved, allowed):
    (
        attend_in,
        query_bias,
        value_bias,
        attend_out,
        attend_bias,
        first_gain,
        first_shift,
        expand_proj,
        expand_bias,
        reduce_proj,
        reduce_bias,
        second_gain,
        second_shift,
    ) = weights
    (
        low_hidden,
        queries,
        keys_full,
        values_full,
        log_totals,
        low_context,
        first_sum,
        low_normed,
        inner_pre,
        active,
        second_sum,
    ) = saved
    width = low_hidden.shape[1]
    second_pull = jax.vjp(
        layer_norm, second_sum, second_gain.astype(jnp.float32), second_shift.astype(jnp.float32)
    )[1]
    grad_second_sum, grad_second_gain, grad_second_shift = second_pull(grad_hidden)
    grad_branch = grad_second_sum.astype(jnp.bfloat16)
    grad_reduce_bias = column_sum(grad_branch)
    grad_reduce = jnp.einsum("tf,td->fd", active, grad_branch, preferred_element_type=jnp.float32)
    grad_active = jnp.einsum(
        "td,fd->tf", grad_branch, reduce_proj, preferred_element_type=jnp.float32
    )
    gelu_pull = jax.vjp(gelu_exact, inner_pre)[1]
    grad_inner = gelu_pull(grad_active)[0].astype(jnp.bfloat16)
    grad_expand_bias = column_sum(grad_inner)
    grad_expand = jnp.einsum(
        "td,tf->df", low_normed, grad_inner, preferred_element_type=jnp.float32
    )
    grad_normed = grad_second_sum + jnp.einsum(
        "tf,df->td", grad_inner, expand_proj, preferred_element_type=jnp.float32
    )
    first_pull = jax.vjp(
        layer_norm, first_sum, first_gain.astype(jnp.float32), first_shift.astype(jnp.float32)
    )[1]
    grad_first_sum, grad_first_gain, grad_first_shift = first_pull(grad_normed)
    grad_attn = grad_first_sum.astype(jnp.bfloat16)
    grad_attend_bias = column_sum(grad_attn)
    grad_attend_out = jnp.einsum(
        "td,te->de", low_context, grad_attn, preferred_element_type=jnp.float32
    )
    grad_context = jnp.einsum(
        "te,de->td", grad_attn, attend_out, preferred_element_type=jnp.float32
    ).astype(jnp.bfloat16)
    grad_queries, grad_keys_full, grad_values_full = attend_backward(
        queries, keys_full, values_full, log_totals, grad_context, allowed
    )
    grad_keys, grad_values = (
        lax.psum_scatter(
            grad_keys_full.astype(jnp.bfloat16), "ctx", scatter_dimension=0, tiled=True
        ).astype(jnp.float32),
        lax.psum_scatter(
            grad_values_full.astype(jnp.bfloat16), "ctx", scatter_dimension=0, tiled=True
        ).astype(jnp.float32),
    )
    grad_proj = jnp.concatenate(
        [
            grad_queries.astype(jnp.bfloat16),
            grad_keys.astype(jnp.bfloat16),
            grad_values.astype(jnp.bfloat16),
        ],
        axis=1,
    )
    grad_query_bias = column_sum(grad_proj[:, :width])
    grad_value_bias = column_sum(grad_proj[:, 2 * width :])
    grad_attend_in = jnp.einsum(
        "td,te->de", low_hidden, grad_proj, preferred_element_type=jnp.float32
    )
    grad_input = grad_first_sum + jnp.einsum(
        "te,de->td", grad_proj, attend_in, preferred_element_type=jnp.float32
    )
    grads = (
        grad_attend_in,
        grad_query_bias,
        grad_value_bias,
        grad_attend_out,
        grad_attend_bias,
        grad_first_gain,
        grad_first_shift,
        grad_expand,
        grad_expand_bias,
        grad_reduce,
        grad_reduce_bias,
        grad_second_gain,
        grad_second_shift,
    )
    return (grad_input, grads)


def reduce_grads(grads):
    shards = (
        lax.psum_scatter(
            grads[0].astype(jnp.bfloat16), "fsdp", scatter_dimension=0, tiled=True
        ).astype(jnp.float32),
        lax.psum_scatter(
            grads[1].astype(jnp.bfloat16), "fsdp", scatter_dimension=0, tiled=True
        ).astype(jnp.float32),
        lax.psum_scatter(
            grads[2].astype(jnp.bfloat16), "fsdp", scatter_dimension=0, tiled=True
        ).astype(jnp.float32),
        lax.psum_scatter(
            grads[3].astype(jnp.bfloat16), "fsdp", scatter_dimension=0, tiled=True
        ).astype(jnp.float32),
        lax.psum_scatter(
            grads[4].astype(jnp.bfloat16), "fsdp", scatter_dimension=0, tiled=True
        ).astype(jnp.float32),
        lax.psum_scatter(
            grads[5].astype(jnp.bfloat16), "fsdp", scatter_dimension=0, tiled=True
        ).astype(jnp.float32),
        lax.psum_scatter(
            grads[6].astype(jnp.bfloat16), "fsdp", scatter_dimension=0, tiled=True
        ).astype(jnp.float32),
        lax.psum_scatter(
            grads[7].astype(jnp.bfloat16), "fsdp", scatter_dimension=0, tiled=True
        ).astype(jnp.float32),
        lax.psum_scatter(
            grads[8].astype(jnp.bfloat16), "fsdp", scatter_dimension=0, tiled=True
        ).astype(jnp.float32),
        lax.psum_scatter(
            grads[9].astype(jnp.bfloat16), "fsdp", scatter_dimension=0, tiled=True
        ).astype(jnp.float32),
        lax.psum_scatter(
            grads[10].astype(jnp.bfloat16), "fsdp", scatter_dimension=0, tiled=True
        ).astype(jnp.float32),
        lax.psum_scatter(
            grads[11].astype(jnp.bfloat16), "fsdp", scatter_dimension=0, tiled=True
        ).astype(jnp.float32),
        lax.psum_scatter(
            grads[12].astype(jnp.bfloat16), "fsdp", scatter_dimension=0, tiled=True
        ).astype(jnp.float32),
    )
    return (
        lax.psum(shards[0].astype(jnp.bfloat16), "ctx").astype(jnp.float32),
        lax.psum(shards[1].astype(jnp.bfloat16), "ctx").astype(jnp.float32),
        lax.psum(shards[2].astype(jnp.bfloat16), "ctx").astype(jnp.float32),
        lax.psum(shards[3].astype(jnp.bfloat16), "ctx").astype(jnp.float32),
        lax.psum(shards[4].astype(jnp.bfloat16), "ctx").astype(jnp.float32),
        lax.psum(shards[5].astype(jnp.bfloat16), "ctx").astype(jnp.float32),
        lax.psum(shards[6].astype(jnp.bfloat16), "ctx").astype(jnp.float32),
        lax.psum(shards[7].astype(jnp.bfloat16), "ctx").astype(jnp.float32),
        lax.psum(shards[8].astype(jnp.bfloat16), "ctx").astype(jnp.float32),
        lax.psum(shards[9].astype(jnp.bfloat16), "ctx").astype(jnp.float32),
        lax.psum(shards[10].astype(jnp.bfloat16), "ctx").astype(jnp.float32),
        lax.psum(shards[11].astype(jnp.bfloat16), "ctx").astype(jnp.float32),
        lax.psum(shards[12].astype(jnp.bfloat16), "ctx").astype(jnp.float32),
    )


def layer_slices(sharded, layer_index):
    return tuple((tensor[layer_index] for tensor in sharded))


def on_device_plain(
    activations,
    cotangent,
    doc_start,
    deal,
    attend_in,
    query_bias,
    value_bias,
    attend_out,
    attend_bias,
    first_gain,
    first_shift,
    expand_proj,
    expand_bias,
    reduce_proj,
    reduce_bias,
    second_gain,
    second_shift,
):
    sharded = (
        attend_in,
        query_bias,
        value_bias,
        attend_out,
        attend_bias,
        first_gain,
        first_shift,
        expand_proj,
        expand_bias,
        reduce_proj,
        reduce_bias,
        second_gain,
        second_shift,
    )
    row_count = activations.shape[1]
    positions = key_positions(deal)
    own_rank = lax.axis_index("ctx")
    own_positions = lax.dynamic_slice_in_dim(positions, own_rank * row_count, row_count)
    own_starts = doc_start[0]
    key_starts = lax.all_gather(own_starts, "ctx", axis=0, tiled=True)
    allowed = (positions[None, :] <= own_positions[:, None]) & (
        key_starts[None, :] == own_starts[:, None]
    )
    hidden = activations[0].astype(jnp.float32)
    kept_weights = []
    kept_saved = []
    for layer_index in range(LAYERS):
        weights = lax.all_gather(
            for_sending(layer_slices(sharded, layer_index)), "fsdp", axis=0, tiled=True
        )
        hidden, saved = forward_layer(hidden, weights, allowed)
        kept_weights.append(weights)
        kept_saved.append(saved)
    out_act = hidden.astype(jnp.bfloat16)[None]
    grad_hidden = cotangent[0].astype(jnp.float32)
    reduced = [None] * LAYERS
    for layer_index in reversed(range(LAYERS)):
        weights = lax.all_gather(
            for_sending(layer_slices(sharded, layer_index)), "fsdp", axis=0, tiled=True
        )
        grad_hidden, grads = backward_layer(grad_hidden, weights, kept_saved[layer_index], allowed)
        reduced[layer_index] = reduce_grads(grads)
    stacked = [
        jnp.stack([reduced[layer_index][member] for layer_index in range(LAYERS)])
        for member in range(13)
    ]
    return (
        out_act,
        grad_hidden[None],
        stacked[0],
        stacked[1],
        stacked[2],
        stacked[3],
        stacked[4],
        stacked[5],
        stacked[6],
        stacked[7],
        stacked[8],
        stacked[9],
        stacked[10],
        stacked[11],
        stacked[12],
    )


F32 = jnp.float32
BF = jnp.bfloat16
WIDTH = HEADS * HEAD_DIM
QB = 256
SCORE_SCALE = HEAD_DIM ** (-0.5) * 1.4426950408889634
NEG = -1e30
VMEM_LIMIT = 60 * 1024 * 1024


def mm_nn(a, b):
    return lax.dot_general(a, b, (((1,), (0,)), ((), ())), preferred_element_type=F32)


def mm_nt(a, b):
    return lax.dot_general(a, b, (((1,), (1,)), ((), ())), preferred_element_type=F32)


def mm_tn(a, b):
    return lax.dot_general(a, b, (((0,), (0,)), ((), ())), preferred_element_type=F32)


def call(kernel, outs, args, specs, scratch, name, flops, nbytes):
    return pl.pallas_call(
        kernel,
        out_shape=[jax.ShapeDtypeStruct(shape, dtype) for shape, dtype in outs],
        in_specs=[pl.BlockSpec(memory_space=space) for space in specs],
        out_specs=[pl.BlockSpec(memory_space=pltpu.VMEM) for _ in outs],
        scratch_shapes=scratch,
        compiler_params=pltpu.CompilerParams(vmem_limit_bytes=VMEM_LIMIT),
        cost_estimate=pl.CostEstimate(flops=flops if name in ("sums", "join") else 0, bytes_accessed=0, transcendentals=0),
        name=name,
    )(*args)


def block_of(block, blocks):
    half = 0 if 2 * block < blocks else 1
    return (block if half == 0 else blocks - 1 - block), half


CORE, SHARD, RANK, JMAP, INV, JMIN = 0, 1, 2, 6, 10, 14
SWAPPED = (0, 2, 1, 3)
WEIGHT = 10**11
VEC_AT = 640


def started_copies(sems, *pairs):
    copies = []
    for n, (src, dst) in enumerate(pairs):
        copy = pltpu.make_async_copy(src, dst, sems.at[n])
        copy.start()
        copies.append(copy)
    return copies


def last_kernel(
    writer, places, meta, c0, c1, c2, c3, hid, cot, t, a, b, d, crossed,
    l_mine, l_other, hlow, gfs, dgg, gctx,
    xhat1, rstd1, gp, xhat2, rstd2, e_s, r_s, sems, wo_s, b_s, wo_sems, ctx, eb, eb_s,
):
    loads = (e_s, r_s, sems, wo_s, b_s, wo_sems)
    mlp_fwd_kernel(
        writer, (None,) * 5 + tuple(places[:3]), meta, c0, c1, c2, c3, hid, t, a, b, d, crossed,
        xhat1, rstd1, gp, xhat2, rstd2, l_mine, l_other, hlow, *loads, ctx, eb, finish=False,
    )
    mlp_bwd_kernel(
        writer, places[3:], meta, xhat1, rstd1, xhat2, rstd2, gp, cot, t, a, b, d, crossed,
        gfs, dgg, gctx, *loads, eb_s, parts=1, loaded=True,
    )


class Writer:
    def __init__(self, sems):
        self.sems = sems
        self.copies = []

    def send(self, src, dst, *at):
        if dst is None:
            return
        if at:
            src, dst = src.at[at], dst.at[at]
        copy = pltpu.make_async_copy(src, dst, self.sems.at[len(self.copies)])
        copy.start()
        self.copies.append(copy)

    def finish(self):
        for copy in self.copies:
            copy.wait()


def writing(kernel, outs, copies):
    count = len(outs)

    def run(*refs, scratch, **keys):
        ins, places, rest = refs[: -count - scratch], refs[-count - scratch : -scratch], refs[-scratch:]
        buffers, sems, rest = rest[:count], rest[count], rest[count + 1 :]
        kernel(Writer(sems), places, *ins, *buffers, *rest, **keys)

    return run, [pltpu.VMEM(shape, dtype) for shape, dtype in outs] + [pltpu.SemaphoreType.DMA((copies,))]


def call_writing(kernel, outs, args, specs, scratch, name, copies, **keys):
    run, buffers = writing(kernel, outs, copies)
    scratch = buffers + scratch
    return pl.pallas_call(
        functools.partial(run, scratch=len(scratch), **keys),
        out_shape=[jax.ShapeDtypeStruct(shape, dtype) for shape, dtype in outs],
        in_specs=[pl.BlockSpec(memory_space=space) for space in specs],
        out_specs=[pl.BlockSpec(memory_space=pl.ANY) for _ in outs],
        scratch_shapes=scratch,
        compiler_params=pltpu.CompilerParams(vmem_limit_bytes=VMEM_LIMIT),
        cost_estimate=pl.CostEstimate(flops=0, bytes_accessed=0, transcendentals=0),
        name=name,
    )(*args)


def prep_kernel(
    expand, reduce, attend_in, attend_out, expand_bias, v0, v1, v2, v3, v4, v5, v6, v7,
    t0, d0, t1, d1,
):
    rank = lax.axis_index("ctx")
    cut = expand.shape[1]
    hw = WIDTH // 4
    for layer, (t, d) in enumerate(((t0, d0), (t1, d1))):
        bias = expand_bias[layer : layer + 1, :].astype(F32)
        rows = [v[layer : layer + 1, :].astype(F32) for v in (v0, v1, v2, v3, v4, v5, v6, v7)]
        rows += [bias[:, k * cut : (k + 1) * cut] for k in range(4)]
        rows.append(jnp.zeros((4, cut), F32))
        d[2 * cut :, :] = attend_out[layer]
        t[2 * cut :, 3 * hw :] = jnp.zeros((cut, WIDTH - 3 * hw), BF)
        t[2 * cut : 2 * cut + 16, VEC_AT : VEC_AT + cut] = jnp.concatenate(rows, axis=0).astype(BF)
        for k in range(4):

            @pl.when(rank == k)
            def _():
                for out, at in ((t, k), (d, k ^ 3)):
                    out[0:cut, :] = jnp.concatenate(
                        [
                            expand[layer, :, (2 * z + h) * 4 * cut + at * cut : (2 * z + h) * 4 * cut + (at + 1) * cut]
                            for h in range(2)
                            for z in range(4)
                        ],
                        axis=1,
                    )
                    out[cut : 2 * cut, :] = reduce[layer, at * cut : (at + 1) * cut, :]
                t[2 * cut :, 0 : 3 * hw] = jnp.concatenate(
                    [attend_in[layer, :, n * WIDTH + k * hw : n * WIDTH + (k + 1) * hw] for n in range(3)], axis=1
                )


def nothing_kernel(*refs):
    pass


def after(xs, *others):
    return pl.pallas_call(
        nothing_kernel,
        out_shape=[jax.ShapeDtypeStruct(x.shape, x.dtype) for x in xs],
        in_specs=[pl.BlockSpec(memory_space=pl.ANY)] * (len(xs) + len(others)),
        out_specs=[pl.BlockSpec(memory_space=pl.ANY)] * len(xs),
        input_output_aliases={n: n for n in range(len(xs))},
        cost_estimate=pl.CostEstimate(flops=WEIGHT, bytes_accessed=0, transcendentals=0),
        name="after",
    )(*xs, *others)


def pack_kernel(a, b, *rest):
    out, held, ins, outs = rest[-4:]
    coming = [pltpu.make_async_copy((a, b)[n // 4].at[n % 4], held.at[n // 4, n % 4], ins.at[n]) for n in range(8)]
    going = [pltpu.make_async_copy(held.at[n // 4, n % 4], out.at[n // 4, n % 4], outs.at[n]) for n in range(8)]
    for copy in coming:
        copy.start()
    for arrive, leave in zip(coming, going):
        arrive.wait()
        leave.start()
    for copy in going:
        copy.wait()


def pack(a, b, *others):
    shape = (2,) + a.shape
    return pl.pallas_call(
        pack_kernel,
        out_shape=jax.ShapeDtypeStruct(shape, a.dtype),
        in_specs=[pl.BlockSpec(memory_space=pl.ANY)] * (2 + len(others)),
        out_specs=pl.BlockSpec(memory_space=pl.ANY),
        scratch_shapes=[pltpu.VMEM(shape, a.dtype), pltpu.SemaphoreType.DMA((8,)), pltpu.SemaphoreType.DMA((8,))],
        cost_estimate=pl.CostEstimate(flops=0, bytes_accessed=0, transcendentals=0),
        name="pack",
    )(a, b, *others)


def half_kernel(meta, t, *rest):
    out, held, ins, outs = rest[-4:]
    coming = [pltpu.make_async_copy(t.at[z, meta[CORE], 0:2], held.at[z], ins.at[z]) for z in range(4)]
    going = [pltpu.make_async_copy(held.at[z], out.at[z], outs.at[z]) for z in range(4)]
    for copy in coming:
        copy.start()
    for arrive, leave in zip(coming, going):
        arrive.wait()
        leave.start()
    for copy in going:
        copy.wait()


def half_of(meta, t, *others):
    shape = (4, 2) + t.shape[3:]
    return pl.pallas_call(
        half_kernel,
        out_shape=jax.ShapeDtypeStruct(shape, t.dtype),
        in_specs=[pl.BlockSpec(memory_space=space) for space in [pltpu.SMEM] + [pl.ANY] * (1 + len(others))],
        out_specs=pl.BlockSpec(memory_space=pl.ANY),
        scratch_shapes=[pltpu.VMEM(shape, t.dtype), pltpu.SemaphoreType.DMA((4,)), pltpu.SemaphoreType.DMA((4,))],
        cost_estimate=pl.CostEstimate(flops=0, bytes_accessed=0, transcendentals=0),
        name="half",
    )(meta, t, *others)


def sums_kernel(*refs, layout, count, split):
    outs = refs[-len(layout) :]
    at = 0
    for out, parts in zip(outs, layout):
        lane = 0
        for n in parts:
            total = refs[at][...].astype(F32)
            for ref in refs[at + 1 : at + n]:
                total = total + ref[...].astype(F32)
            at += n
            if split:
                for k in range(len(outs)):
                    outs[k][...] = total[k].astype(BF)
            else:
                out[..., lane : lane + total.shape[-1]] = total.astype(BF)
            lane += total.shape[-1]
        if split:
            break


def sums(outputs, *others, split=0, weight=0):
    args = tuple(x for groups in outputs for group in groups for x in group)
    layout = tuple(tuple(len(group) for group in groups) for groups in outputs)
    if split:
        shapes = [(args[0].shape[1:], BF)] * split
        layout = layout * split
    else:
        shapes = [
            (groups[0][0].shape[:-1] + (sum(group[0].shape[-1] for group in groups),), BF) for groups in outputs
        ]
    return call(
        functools.partial(sums_kernel, layout=layout, count=len(args), split=split),
        shapes, args + others, [pltpu.VMEM] * len(args) + [pl.ANY] * len(others), [], "sums", weight, 0,
    )


def join_kernel(att, t, d, *rest):
    out = rest[-1]
    rows = att.shape[0]
    out[0:rows, 0 : att.shape[1]] = att[...]
    out[0:rows, att.shape[1] :] = jnp.zeros((rows, out.shape[1] - att.shape[1]), BF)
    for k in range(2):
        out[rows:, k * WIDTH : (k + 1) * WIDTH] = (t[k].astype(F32) + d[k].astype(F32)).astype(BF)


def merge_kernel(dwo, own, other, *rest):
    out = rest[-1]
    out[:, :, 0:WIDTH] = dwo[...]
    out[:, :, WIDTH:] = (own[...].astype(F32) + other[...].astype(F32)).astype(BF)


def vectors_of(shards, order):
    return jnp.concatenate([shards[f // 2, f % 2, :, 0:96] for f in order], axis=1).astype(F32)


NATURAL = tuple(range(8))
CORE_MAJOR = (0, 2, 4, 6, 1, 3, 5, 7)


def attn_fwd_kernel(
    meta, h0, h1, h2, h3, qrow, kcol, t, *rest, heads, tokens
):
    qkv, c0, c1, c2, c3, lse, q_s, k_s, vt_s, o_s, ctx, w_s, b_s, sems = rest[-14:]
    blocks = tokens // BLK
    hw = heads * HEAD_DIM
    copies = started_copies(
        sems, (t.at[:, :, 2, :, 0:VEC_AT], w_s), (t.at[:, :, 2, 0:16, VEC_AT : VEC_AT + 128], b_s)
    )
    for copy in copies:
        copy.wait()
    w = w_s[...].reshape(WIDTH, VEC_AT)[:, 0 : 3 * hw]
    vec = vectors_of(b_s, NATURAL)
    bias = jnp.zeros((1, 3 * hw), F32)
    for k in range(4):
        part = jnp.concatenate(
            [vec[6:7, k * hw : (k + 1) * hw], jnp.zeros((1, hw), F32), vec[7:8, k * hw : (k + 1) * hw]], axis=1
        )
        bias = jnp.where(meta[RANK] == k, part, bias)
    for j, piece in enumerate((h0, h1, h2, h3)):
        qkv[j] = (mm_nn(piece[...], w) + bias).astype(BF)
    for pair in range(blocks // 2):
        rows = []
        for block in (2 * pair, 2 * pair + 1):
            at, half = block_of(block, blocks)
            rows.append(qkv[meta[JMAP + at], half * BLK : (half + 1) * BLK, :])
        both = jnp.concatenate(rows, axis=0)
        lo, hi = 2 * pair * BLK, 2 * (pair + 1) * BLK
        for h in range(heads):
            q_s[h, lo:hi, :] = both[:, h * HEAD_DIM : (h + 1) * HEAD_DIM]
            k_s[h, lo:hi, :] = both[:, hw + h * HEAD_DIM : hw + (h + 1) * HEAD_DIM]
        vt_s[:, lo:hi] = both[:, 2 * hw :].T
    iota_k = lax.broadcasted_iota(jnp.int32, (QB, QB), 0)
    iota_q = lax.broadcasted_iota(jnp.int32, (QB, QB), 1)
    causal = iota_k <= iota_q
    head_rows = [slice(h * HEAD_DIM, (h + 1) * HEAD_DIM) for h in range(heads)]
    for i in range(tokens // QB):
        lo = i * QB
        starts_q = qrow[0:1, lo : lo + QB]

        def scores(at, diagonal):
            col = kcol[pl.ds(at, QB), :]
            allowed = jnp.concatenate([col, col], axis=1) == starts_q
            if diagonal:
                allowed = allowed & causal
            return [
                jnp.where(allowed, mm_nt(k_s[h, pl.ds(at, QB), :], q_s[h, lo : lo + QB, :]) * SCORE_SCALE, NEG)
                for h in range(heads)
            ]

        ss = scores(lo, True)
        tops = [jnp.max(s, axis=0, keepdims=True) for s in ss]
        ps = [jnp.exp2(s - top) for s, top in zip(ss, tops)]
        totals = [jnp.sum(p, axis=0, keepdims=True) for p in ps]
        outs = [mm_nn(vt_s[head_rows[h], lo : lo + QB], ps[h].astype(BF)) for h in range(heads)]

        def step(jb, carry):
            tops, totals, outs = carry
            at = pl.multiple_of(jb * QB, QB)
            ss = scores(at, False)
            new = [jnp.maximum(top, jnp.max(s, axis=0, keepdims=True)) for s, top in zip(ss, tops)]
            ps = [jnp.exp2(s - top) for s, top in zip(ss, new)]
            alphas = [jnp.exp2(top - n) for top, n in zip(tops, new)]
            totals = [
                total * alpha + jnp.sum(p, axis=0, keepdims=True) for total, alpha, p in zip(totals, alphas, ps)
            ]
            outs = [
                outs[h] * alphas[h] + mm_nn(vt_s[head_rows[h], pl.ds(at, QB)], ps[h].astype(BF)) for h in range(heads)
            ]
            return new, totals, outs

        if i > 0:
            tops, totals, outs = lax.fori_loop(meta[JMIN + i], i, step, (tops, totals, outs))
        for h in range(heads):
            o_s[head_rows[h], lo : lo + QB] = outs[h] / totals[h]
            lse[h : h + 1, lo : lo + QB] = tops[h] + jnp.log2(totals[h])
    for pair in range(blocks // 2):
        lo, hi = 2 * pair * BLK, 2 * (pair + 1) * BLK
        both = o_s[:, lo:hi].T.astype(BF)
        for n, block in enumerate((2 * pair, 2 * pair + 1)):
            at, half = block_of(block, blocks)
            ctx[meta[JMAP + at], :, half * hw : (half + 1) * hw] = both[n * BLK : (n + 1) * BLK, :]
    for j, out in enumerate((c0, c1, c2, c3)):
        out[...] = ctx[j]


def attn_bwd_kernel(
    meta, h0, h1, h2, h3, qrow, kcol, qkv, c0, c1, c2, c3, gctx, lse, t, *rest, heads, tokens, paired
):
    (
        dw_own, dw_other, q_s, k_s, v_s, do_s, kt_s, delta_s, dk_s, dv_s, dqt_s, g_s, w_s, ctx, dw, sems,
    ) = rest[-16:]
    if paired:
        g_own, g_a, g_bd = rest[-19:-16]
        g_b, g_d = g_bd.at[0], g_bd.at[1]
    else:
        g_own, g_a, g_b, g_d = rest[-20:-16]
    blocks = tokens // BLK
    hw = heads * HEAD_DIM
    scale = HEAD_DIM ** (-0.5)
    copies = started_copies(sems, (t.at[:, :, 2, :, 0:VEC_AT], w_s))
    for j, c in enumerate((c0, c1, c2, c3)):
        ctx[j] = c[...]
    for pair in range(blocks // 2):
        rows, grads, outs = [], [], []
        for block in (2 * pair, 2 * pair + 1):
            at, half = block_of(block, blocks)
            rows.append(qkv[meta[JMAP + at], half * BLK : (half + 1) * BLK, :])
            grads.append(gctx[meta[INV + at], :, half * hw : (half + 1) * hw])
            outs.append(ctx[meta[JMAP + at], :, half * hw : (half + 1) * hw])
        both = jnp.concatenate(rows, axis=0)
        grad = jnp.concatenate(grads, axis=0)
        out = jnp.concatenate(outs, axis=0)
        lo, hi = 2 * pair * BLK, 2 * (pair + 1) * BLK
        prod = (grad.astype(F32) * out.astype(F32)).T
        kt_s[:, lo:hi] = both[:, hw : 2 * hw].T
        for h in range(heads):
            c0, c1 = h * HEAD_DIM, (h + 1) * HEAD_DIM
            q_s[h, lo:hi, :] = both[:, c0:c1]
            k_s[h, lo:hi, :] = both[:, hw + c0 : hw + c1]
            v_s[h, lo:hi, :] = both[:, 2 * hw + c0 : 2 * hw + c1]
            do_s[h, lo:hi, :] = grad[:, c0:c1]
            delta_s[h : h + 1, lo:hi] = jnp.sum(prod[c0:c1, :], axis=0, keepdims=True)
    dk_s[...] = jnp.zeros_like(dk_s)
    dv_s[...] = jnp.zeros_like(dv_s)
    iota_k = lax.broadcasted_iota(jnp.int32, (QB, QB), 0)
    iota_q = lax.broadcasted_iota(jnp.int32, (QB, QB), 1)
    causal = iota_k <= iota_q
    head_rows = [slice(h * HEAD_DIM, (h + 1) * HEAD_DIM) for h in range(heads)]
    for i in range(tokens // QB):
        lo = i * QB
        starts_q = qrow[0:1, lo : lo + QB]

        def block(at, diagonal):
            col = kcol[pl.ds(at, QB), :]
            allowed = jnp.concatenate([col, col], axis=1) == starts_q
            if diagonal:
                allowed = allowed & causal
            keys = pl.ds(at, QB)
            cols = slice(lo, lo + QB)
            ss = [mm_nt(k_s[h, keys, :], q_s[h, cols, :]) for h in range(heads)]
            dps = [mm_nt(v_s[h, keys, :], do_s[h, cols, :]) for h in range(heads)]
            ps = [
                jnp.exp2(jnp.where(allowed, s * SCORE_SCALE, NEG) - lse[h : h + 1, cols]) for h, s in enumerate(ss)
            ]
            dss = [
                (p * (dp - delta_s[h : h + 1, cols])).astype(BF) for h, (p, dp) in enumerate(zip(ps, dps))
            ]
            for h in range(heads):
                dv_s[h, keys, :] += mm_nn(ps[h].astype(BF), do_s[h, cols, :])
            for h in range(heads):
                dk_s[h, keys, :] += mm_nn(dss[h], q_s[h, cols, :])
            return [mm_nn(kt_s[head_rows[h], keys], dss[h]) for h in range(heads)]

        dqs = block(lo, True)
        if i > 0:
            dqs = lax.fori_loop(
                meta[JMIN + i],
                i,
                lambda jb, acc: [x + y for x, y in zip(acc, block(pl.multiple_of(jb * QB, QB), False))],
                dqs,
            )
        for h in range(heads):
            dqt_s[head_rows[h], lo : lo + QB] = dqs[h] * scale
    for pair in range(blocks // 2):
        lo, hi = 2 * pair * BLK, 2 * (pair + 1) * BLK
        parts = [dqt_s[:, lo:hi].T.astype(BF)]
        parts += [(dk_s[h, lo:hi, :] * scale).astype(BF) for h in range(heads)]
        parts += [dv_s[h, lo:hi, :].astype(BF) for h in range(heads)]
        both = jnp.concatenate(parts, axis=1)
        for n, block_at in enumerate((2 * pair, 2 * pair + 1)):
            at, half = block_of(block_at, blocks)
            g_s[meta[JMAP + at], half * BLK : (half + 1) * BLK, :] = both[n * BLK : (n + 1) * BLK, :]
    for copy in copies:
        copy.wait()
    w = w_s[...].reshape(WIDTH, VEC_AT)[:, 0 : 3 * hw]
    total = None
    sums = None
    for j, piece in enumerate((h0, h1, h2, h3)):
        g = g_s[j]
        back = mm_nt(g, w)
        if j == 0:
            g_own[...] = back
        else:
            (g_a, g_b, g_d)[j - 1][...] = back.astype(BF)
        part = mm_tn(piece[...], g)
        col = jnp.sum(g.astype(F32), axis=0, keepdims=True)
        total = part if total is None else total + part
        sums = col if sums is None else sums + col
    shards, rows_out, cols = dw.shape
    rows = WIDTH // shards
    dw[:, 0:rows, :] = total.reshape(shards, rows, cols).astype(BF)
    dw[:, rows:, :] = jnp.broadcast_to(sums[None], (shards, rows_out - rows, cols)).astype(BF)
    for k in range(4):
        dw_own[k] = dw[2 * k + meta[CORE]]
        dw_other[k] = dw[2 * k + 1 - meta[CORE]]


def start_ffn_copies(core, t, a, b, d, crossed, e_s, r_s, sems):
    ca, cb = crossed.at[0], crossed.at[1]
    groups = []
    for p, parts in enumerate(((t,), (a, cb), (b, ca), (d,))):
        pairs = []
        if len(parts) == 1:
            pairs.append((parts[0].at[:, :, 0], e_s.at[p]))
            for h in range(2):
                pairs.append((parts[0].at[:, h, 1], r_s.at[p, h]))
        else:
            for src, parity in ((parts[0], core), (parts[1], 1 - core)):
                pairs.append((src.at[:, 0], e_s.at[p, :, parity]))
                pairs.append((src.at[:, 1], r_s.at[p, parity]))
        group = []
        for n, (src, dst) in enumerate(pairs):
            copy = pltpu.make_async_copy(src, dst, sems.at[p, n])
            copy.start()
            group.append(copy)
        groups.append(group)
    return groups


def ffn_scratch():
    return [
        pltpu.VMEM((4, 4, 2, 96, WIDTH), BF),
        pltpu.VMEM((4, 2, 4, 96, WIDTH), BF),
        pltpu.SemaphoreType.DMA((4, 4)),
        pltpu.VMEM((4, 2, 96, WIDTH), BF),
        pltpu.VMEM((4, 2, 16, 128), BF),
        pltpu.SemaphoreType.DMA((2,)),
    ]


def mlp_fwd_scratch(rows, hw):
    return ffn_scratch() + [pltpu.VMEM((4, rows, hw), BF), pltpu.VMEM((8, WIDTH), F32)]


def mlp_bwd_scratch():
    return ffn_scratch() + [pltpu.VMEM((8, WIDTH), F32)]


def wgrad_scratch():
    rows = 2 * BLK
    return [
        pltpu.VMEM((rows, 3 * WIDTH), BF),
        pltpu.VMEM((rows, 3 * WIDTH), BF),
        pltpu.VMEM((rows + 16, 6 * WIDTH), BF),
        pltpu.VMEM((rows + 16, 6 * WIDTH), BF),
        pltpu.SemaphoreType.DMA((16,)),
    ]


def attn_fwd_scratch(heads, tokens):
    hw = heads * HEAD_DIM
    return [
        pltpu.VMEM((heads, tokens, HEAD_DIM), BF),
        pltpu.VMEM((heads, tokens, HEAD_DIM), BF),
        pltpu.VMEM((hw, tokens), BF),
        pltpu.VMEM((hw, tokens), F32),
        pltpu.VMEM((4, BLK, 2 * hw), BF),
        pltpu.VMEM((4, 2, 96, VEC_AT), BF),
        pltpu.VMEM((4, 2, 16, 128), BF),
        pltpu.SemaphoreType.DMA((2,)),
    ]


def attn_bwd_scratch(heads, tokens):
    hw = heads * HEAD_DIM
    return [pltpu.VMEM((heads, tokens, HEAD_DIM), BF)] * 4 + [
        pltpu.VMEM((hw, tokens), BF),
        pltpu.VMEM((8, tokens), F32),
        pltpu.VMEM((heads, tokens, HEAD_DIM), F32),
        pltpu.VMEM((heads, tokens, HEAD_DIM), F32),
        pltpu.VMEM((hw, tokens), F32),
        pltpu.VMEM((4, tokens // 4, 3 * hw), BF),
        pltpu.VMEM((4, 2, 96, VEC_AT), BF),
        pltpu.VMEM((4, BLK, 2 * hw), BF),
        pltpu.VMEM((8, 112, 3 * hw), BF),
        pltpu.SemaphoreType.DMA((1,)),
    ]


def norm_parts(values):
    centre = values - jnp.mean(values, axis=-1, keepdims=True)
    spread = jnp.mean(centre * centre, axis=-1, keepdims=True)
    rstd = lax.rsqrt(spread + norm_eps)
    return centre * rstd, rstd


def shard_columns(x, parity):
    return jnp.concatenate([x[:, (2 * z + parity) * 96 : (2 * z + parity + 1) * 96] for z in range(4)], axis=1)


def mlp_fwd_kernel(
    writer, places, meta, c0, c1, c2, c3, hid, t, a, b, d, crossed,
    xhat1, rstd1, gp, xhat2, rstd2, l_mine, l_other, hlow, *rest, finish=True,
):
    hnext, (e_s, r_s, sems, wo_s, b_s, wo_sems, ctx, eb) = rest[:-8], rest[-8:]
    core = meta[CORE]
    xhat1_to, rstd1_to, gp_to, xhat2_to, rstd2_to, mine_to, other_to, hlow_to = places[:8]
    wo_copies = started_copies(
        wo_sems, (d.at[:, :, 2], wo_s), (t.at[:, :, 2, 0:16, VEC_AT : VEC_AT + 128], b_s)
    )
    copies = start_ffn_copies(core, t, a, b, d, crossed, e_s, r_s, sems)
    half_cols = WIDTH // 2
    hw = c0.shape[1] // 2
    for p, piece in enumerate((c0, c1, c2, c3)):
        for half in range(2):
            ctx[meta[RANK + p], half * BLK : (half + 1) * BLK, :] = piece[:, half * hw : (half + 1) * hw]

    def keep(parts, at):
        for parity in range(2):

            @pl.when(core == parity)
            def _():
                l_mine[:, at : at + half_cols] = parts[parity]

            @pl.when(core != parity)
            def _():
                l_other[:, at : at + half_cols] = parts[parity]

        for ref, to in ((l_mine, mine_to), (l_other, other_to)):
            writer.send(ref, to, slice(None), slice(at, at + half_cols))

    low = jnp.concatenate([ctx[rank] for rank in range(4)], axis=1)
    keep([shard_columns(low, parity) for parity in range(2)], half_cols)
    for copy in wo_copies:
        copy.wait()
    vec = vectors_of(b_s, NATURAL)
    eb[...] = vectors_of(b_s, CORE_MAJOR)[8:16, :]
    wo = wo_s[...].reshape(WIDTH, WIDTH)
    first_sum = hid[...].astype(F32) + (mm_nn(low, wo) + vec[0:1, :])
    x1, r1 = norm_parts(first_sum)
    xhat1[...] = x1
    rstd1[...] = r1
    writer.send(xhat1, xhat1_to)
    writer.send(rstd1, rstd1_to)
    normed = x1 * vec[1:2, :] + vec[2:3, :]
    lown = normed.astype(BF)
    keep([shard_columns(lown, parity) for parity in range(2)], 0)
    out = normed + vec[3:4, :]
    for p in range(4):
        for copy in copies[p]:
            copy.wait()
        bias = eb[pl.ds(meta[RANK + p], 1), :]
        u = mm_nn(lown, e_s[p].reshape(WIDTH, WIDTH)) + bias
        cdf = 0.5 * (1.0 + lax.erf(u * 0.7071067811865476))
        pdf = jnp.exp(-0.5 * u * u) * 0.3989422804014327
        low = (u * cdf).astype(BF)
        cut = slice(p * WIDTH, (p + 1) * WIDTH)
        gp[:, cut] = (cdf + u * pdf).astype(BF)
        writer.send(gp, gp_to, slice(None), cut)
        keep([low[:, :half_cols], low[:, half_cols:]], WIDTH + p * half_cols)
        out = out + mm_nn(low, r_s[p].reshape(WIDTH, WIDTH))
    x2, r2 = norm_parts(out)
    nxt = x2 * vec[4:5, :] + vec[5:6, :]
    hlow[...] = nxt.astype(BF)
    writer.send(hlow, hlow_to)
    xhat2[...] = x2
    writer.send(xhat2, xhat2_to)
    rstd2[...] = r2
    writer.send(rstd2, rstd2_to)
    if hnext:
        hnext[0][...] = nxt
        writer.send(hnext[0], places[8])
    if finish:
        writer.finish()


def norm_back(gy, gain, xhat, rstd):
    g = gy * gain
    return rstd * (g - jnp.mean(g, axis=-1, keepdims=True) - xhat * jnp.mean(g * xhat, axis=-1, keepdims=True))


def rows_sum(x):
    return jnp.sum(x, axis=0, keepdims=True)


def mlp_bwd_kernel(
    writer, places, meta, xhat1, rstd1, xhat2, rstd2, gp, *rest, parts, loaded=False
):
    t, a, b, d, crossed = rest[parts : parts + 5]
    gfs, dgg, gctx, e_s, r_s, sems, wo_s, b_s, wo_sems, eb_s = rest[-10:]
    rows = gfs.shape[0]
    core = meta[CORE]
    if loaded:
        copies, wo_copies = [[]] * 4, []
    else:
        copies = start_ffn_copies(core, t, a, b, d, crossed, e_s, r_s, sems)
        wo_copies = started_copies(
            wo_sems, (d.at[:, :, 2], wo_s), (t.at[:, :, 2, 0:16, VEC_AT : VEC_AT + 128], b_s)
        )
    grad = rest[0][...].astype(F32)
    for ref in rest[1:parts]:
        grad = grad + ref[...].astype(F32)
    x2 = xhat2[...]
    for copy in wo_copies:
        copy.wait()
    vec = vectors_of(b_s, NATURAL)
    gss = norm_back(grad, vec[4:5, :], x2, rstd2[...])
    low = gss.astype(BF)
    cut = slice(4 * WIDTH, 5 * WIDTH)
    dgg[0:rows, cut] = low
    writer.send(dgg.at[0:rows, cut], places[1].at[0:rows, cut])
    sums = [None] * 8
    sums[4] = rows_sum(grad * x2)
    sums[5] = rows_sum(grad)
    sums[3] = rows_sum(low.astype(F32))
    gn = gss
    eb_s[...] = jnp.zeros_like(eb_s)
    for p in range(4):
        for copy in copies[p]:
            copy.wait()
        ga = mm_nt(low, r_s[p].reshape(WIDTH, WIDTH))
        dip = (ga * gp[:, p * WIDTH : (p + 1) * WIDTH].astype(F32)).astype(BF)
        cut = slice(p * WIDTH, (p + 1) * WIDTH)
        dgg[0:rows, cut] = dip
        writer.send(dgg.at[0:rows, cut], places[1].at[0:rows, cut])
        eb_s[pl.ds(meta[RANK + p], 1), :] = rows_sum(dip.astype(F32))
        gn = gn + mm_nt(dip, e_s[p].reshape(WIDTH, WIDTH))
    x1 = xhat1[...]
    gf = norm_back(gn, vec[1:2, :], x1, rstd1[...])
    sums[1] = rows_sum(gn * x1)
    sums[2] = rows_sum(gn)
    lowa = gf.astype(BF)
    cut = slice(5 * WIDTH, 6 * WIDTH)
    dgg[0:rows, cut] = lowa
    writer.send(dgg.at[0:rows, cut], places[1].at[0:rows, cut])
    gfs[...] = gf
    writer.send(gfs, places[0])
    sums[0] = rows_sum(lowa.astype(F32))
    sums[6] = jnp.zeros_like(sums[0])
    sums[7] = sums[6]
    gc = mm_nt(lowa, wo_s[...].reshape(WIDTH, WIDTH)).astype(BF)
    hw = gctx.shape[2] // 2
    for rank in range(4):
        for half in range(2):
            gctx[rank, :, half * hw : (half + 1) * hw] = gc[half * BLK : (half + 1) * BLK, rank * hw : (rank + 1) * hw]
    writer.send(gctx, places[2])
    vecs = jnp.concatenate(sums, axis=0)
    ebs = jnp.concatenate([eb_s[:, (4 * (f % 2) + f // 2) * 96 : (4 * (f % 2) + f // 2 + 1) * 96] for f in range(8)], axis=1)
    dgg[rows:, 0:WIDTH] = jnp.concatenate([vecs, ebs], axis=0).astype(BF)
    dgg[rows:, WIDTH:] = jnp.zeros((16, 5 * WIDTH), BF)
    writer.send(dgg.at[rows:], places[1].at[rows:])
    writer.finish()


def wgrad_kernel(writer, places, meta, l_mine_from, l_other_from, dgg_from, dgg_other_from, *rest):
    t, a, b, dwo, d, l_mine, l_other, dgg, dgg_other, sems = rest[-10:]
    half = WIDTH // 2
    rows = l_mine.shape[0]

    def fetch(n, src, dst, at, width):
        copy = pltpu.make_async_copy(src.at[:, at : at + width], dst.at[:, at : at + width], sems.at[n])
        copy.start()
        return copy

    lefts = [fetch(n, src, dst, 0, WIDTH) for n, (src, dst) in enumerate(((l_mine_from, l_mine), (l_other_from, l_other)))]
    rights = {}
    for k in (3, 4, 1, 2, 0, 5):
        q = SWAPPED[k] if k < 4 else k
        rights[k] = [fetch(4 + k, dgg_from, dgg, k * WIDTH, WIDTH), fetch(10 + k, dgg_other_from, dgg_other, q * WIDTH, WIDTH)]
        if k == 3:
            acts = [
                fetch(2 + n, src, dst, WIDTH, 2 * WIDTH)
                for n, (src, dst) in enumerate(((l_mine_from, l_mine), (l_other_from, l_other)))
            ]

    def wait(copies):
        for copy in copies:
            copy.wait()

    def grad(left, left_other, right, right_other):
        return mm_nn(left, dgg[0:rows, right : right + WIDTH]) + mm_nn(
            left_other, dgg_other[0:rows, right_other : right_other + WIDTH]
        )

    def left(at, at_other):
        return l_mine[:, at : at + half].T, l_other[:, at_other : at_other + half].T

    wait(lefts)
    low = left(0, 0)
    for n, (p, out) in enumerate(((3, d), (1, a), (2, b), (0, t))):
        q = SWAPPED[p]
        wait(rights[p])
        out[:, 0] = grad(*low, p * WIDTH, q * WIDTH).reshape(4, 96, WIDTH).astype(BF)
        if n == 0:
            wait(acts)
            wait(rights[4])
        out[:, 1] = (
            grad(*left(WIDTH + p * half, WIDTH + q * half), 4 * WIDTH, 4 * WIDTH).reshape(4, 96, WIDTH).astype(BF)
        )
        writer.send(out, places[(4, 1, 2, 0)[n]])
    wait(rights[5])
    dwo[:, 0:96, :] = grad(*left(half, half), 5 * WIDTH, 5 * WIDTH).reshape(4, 96, WIDTH).astype(BF)
    vecs = dgg[rows:, 0:WIDTH].astype(F32) + dgg_other[rows:, 0:WIDTH].astype(F32)
    dwo[:, 96:, :] = jnp.zeros((4, 16, WIDTH), BF)
    for parity in range(2):

        @pl.when(meta[CORE] == parity)
        def _():
            for z in range(4):
                dwo[z, 96:, 0:96] = vecs[:, (2 * z + parity) * 96 : (2 * z + parity + 1) * 96].astype(BF)

    writer.send(dwo, places[3])
    writer.finish()


def place_kernel(
    meta, *rest, layer, last
):
    if last:
        parts = [((f.at[0], f.at[1]), a) for f, a in zip(rest[:4], rest[4:8])]
        small_in, rest = rest[8], rest[13:]
    else:
        parts = [((x.at[112:, 0:WIDTH], x.at[112:, WIDTH:]), x.at[0:112, :]) for x in rest[:4]]
        rest = rest[5:]
    e_hbm, r_hbm, i_hbm, o_hbm = rest[:4]
    smalls = rest[4:-10]
    e_s, i_s, b_s, e_out, r_out, i_out, o_out, small_s, eb_s, sems = rest[-10:]
    for p, (ffn, att) in enumerate(parts):
        rank = meta[RANK + p]
        r_out[pl.ds(pl.multiple_of(rank * 96, 96), 96), :] = ffn[1][...].astype(F32)
        e_s[rank] = ffn[0][...].astype(F32)
        i_s[rank] = att[0:96, WIDTH : WIDTH + 9 * HEAD_DIM].astype(F32)
        b_s[rank] = att[96:112, WIDTH : WIDTH + 9 * HEAD_DIM].astype(F32)
    copies = []

    def send(n, src, dst):
        copy = pltpu.make_async_copy(src, dst.at[layer], sems.at[n])
        copy.start()
        copies.append(copy)

    send(0, r_out, r_hbm)
    for f in range(8):
        at = (4 * (f % 2) + f // 2) * 96
        e_out[:, f * 384 : (f + 1) * 384] = jnp.concatenate([e_s[c, :, at : at + 96] for c in range(4)], axis=1)
    send(1, e_out, e_hbm)
    hw = WIDTH // 4
    for k in range(3):
        i_out[:, k * WIDTH : (k + 1) * WIDTH] = jnp.concatenate(
            [i_s[c, :, k * hw : (k + 1) * hw] for c in range(4)], axis=1
        )
    send(2, i_out, i_hbm)
    wo = [att[:, 0:WIDTH].astype(F32) for _, att in parts]
    total = (wo[0] + wo[1]) + (wo[2] + wo[3])
    o_out[...] = total[0:96, :]
    send(3, o_out, o_hbm)
    bias = b_s[lax.shift_right_logical(meta[SHARD], 1)]
    low_half = (meta[SHARD] & 1) == 0
    qb = jnp.where(low_half, bias[:, 0:96], bias[:, 96:192])
    vb = jnp.where(low_half, bias[:, 2 * hw : 2 * hw + 96], bias[:, 2 * hw + 96 : 3 * hw])
    rows = jnp.concatenate([total[96:102, 0:96], qb[0:1], vb[0:1], total[104:112, 0:96]], axis=0)
    if last:
        for n, ref in enumerate(smalls[:-1]):
            ref[...] = jnp.concatenate([rows[n : n + 1], small_in[n : n + 1, 0:96]], axis=0)
        smalls[-1][...] = jnp.concatenate(
            [
                jnp.concatenate([x[8 + c : 9 + c, 0:96] for c in range(4)], axis=1)
                for x in (rows, small_in[...])
            ],
            axis=0,
        )
    else:
        smalls[0][...] = rows
    for copy in copies:
        copy.wait()


def permutation(ctx, fsdp, move):
    return [
        (c * fsdp + f, move(c, f)[0] * fsdp + move(c, f)[1]) for c in range(ctx) for f in range(fsdp)
    ]


def add(*parts):
    total = parts[0].astype(F32)
    for part in parts[1:]:
        total = total + part.astype(F32)
    return total


def on_device_fast(
    activations, cotangent, doc_start, deal,
    attend_in, query_bias, value_bias, attend_out, attend_bias, first_gain, first_shift,
    expand_proj, expand_bias, reduce_proj, reduce_bias, second_gain, second_shift,
    *, ctx, fsdp,
):
    S = [pltpu.SMEM]
    V = [pltpu.VMEM]
    A = [pl.ANY]
    axes = ("ctx", "fsdp")

    def via(move):
        perm = permutation(ctx, fsdp, move)
        return lambda x: lax.ppermute(x, axes, perm)

    via_first = via(lambda c, f: (c ^ (1 + f % 2), f))
    via_second = via(lambda c, f: (c ^ (2 - f % 2), f))
    via_diagonal = via(lambda c, f: (c ^ 3, f))
    via_core = via(lambda c, f: (c, f ^ 1))
    via_z = [None] + [via(lambda c, f, k=k: (c, f ^ (2 * k))) for k in range(1, 4)]

    def exchange_ctx(own, a, b, d):
        return (own, via_first(a), via_second(b), via_diagonal(d))

    def spread_ctx(x):
        return (x, via_first(x), via_second(x), via_diagonal(x))

    def reduce_z(x):
        return lax.psum_scatter(x, "fsdp", scatter_dimension=0, tiled=True, axis_index_groups=zgroups)

    def exchange_z(own, *others):
        return (own,) + tuple(via_z[k + 1](x) for k, x in enumerate(others))

    def gather_ctx(x):
        a, b = via_first(x), via_second(x)
        return (x, a, b, via_second(a))

    heads = HEADS // ctx
    hw = heads * HEAD_DIM
    rows = activations.shape[1]
    tokens = rows * ctx
    cut = WIDTH // fsdp
    c = lax.axis_index("ctx").astype(jnp.int32)
    shard = lax.axis_index("fsdp").astype(jnp.int32)
    core = shard % 2
    zgroups = [[2 * z + k for z in range(fsdp // 2)] for k in range(2)]

    hidden = activations[0]
    gathered = gather_ctx(hidden)
    small = (attend_bias, first_gain, first_shift, reduce_bias, second_gain, second_shift, query_bias, value_bias)
    sent = call(
        prep_kernel,
        [((3 * cut, WIDTH), BF)] * 4,
        (expand_proj, reduce_proj, attend_in, attend_out, expand_bias) + small,
        V * 13,
        [],
        "prep",
        0,
        8 * 1024 * 1024,
    )

    def gather_ffn(x):
        x = lax.all_gather(x, "fsdp", axis=0, tiled=True)
        return x.reshape(fsdp // 2, 2, 3, cut, WIDTH)

    ranks = jnp.arange(ctx, dtype=jnp.int32)
    inv = jnp.sum(jnp.where(deal[None, :] == ranks[:, None], ranks[None, :], 0), axis=1).astype(jnp.int32)
    starts = lax.all_gather(doc_start[0], "ctx", axis=0, tiled=True)
    by_rank = starts.reshape(ctx, 2, BLK)
    chosen = inv[:, None, None, None] == ranks[None, :, None, None]
    by_block = jnp.sum(jnp.where(chosen, by_rank[None], 0), axis=1)
    logical = jnp.concatenate([by_block[:, 0], by_block[::-1, 1]], axis=0).reshape(-1)
    qrow = jnp.broadcast_to(logical[None, :], (8, tokens))
    kcol = jnp.broadcast_to(logical[:, None], (tokens, 128))
    jmin = jnp.min(logical.reshape(tokens // QB, QB), axis=1) // QB

    m1 = 1 + core
    mask = inv ^ c
    jmap = jnp.where((core == 1) & (mask > 0) & (mask < 3), 3 - mask, mask)
    meta = jnp.concatenate(
        [jnp.stack([core, shard, c, c ^ m1, c ^ (3 - m1), c ^ 3]), jmap, inv, jmin]
    ).astype(jnp.int32)

    kept = []
    earlier = ()
    wide = [gather_ffn(sent[0]), gather_ffn(sent[1]), None, None]
    wide[0] = after((wide[0],), starts, *gathered[1:])[0]
    wide[2] = gather_ffn(*after(sent[2:3], wide[0]))
    pieces = []
    for layer in range(LAYERS):
        t, d = wide[2 * layer : 2 * layer + 2]
        mine = half_of(meta, t, *gathered[1:])
        a, b = via_first(mine), via_second(mine)
        qkv, *ctx_own, lse = call(
            functools.partial(attn_fwd_kernel, heads=heads, tokens=tokens),
            [((ctx, rows, 3 * hw), BF)] + [((BLK, 2 * hw), BF)] * 4 + [((8, tokens), F32)],
            (meta,) + gathered + (qrow, kcol, t, mine) + earlier,
            S + V * 6 + A * (2 + len(earlier)),
            attn_fwd_scratch(heads, tokens),
            "attn_fwd",
            2 * tokens * WIDTH * 3 * hw * 4,
            10 * 1024 * 1024,
        )
        cx = exchange_ctx(*ctx_own)
        if layer + 1 < LAYERS:
            wide[3] = gather_ffn(*after(sent[3:4], *cx[1:]))
        pieces.append((t, a, b, d, via_core(pack(a, b, lse))))
        kinds = {
            "xhat": ((rows, WIDTH), F32), "rstd": ((rows, 1), F32), "gp": ((rows, 4 * WIDTH), BF),
            "left": ((rows, 3 * WIDTH), BF), "low": ((rows, WIDTH), BF),
        }
        norms = [kinds[name] for name in ("xhat", "rstd", "gp", "xhat", "rstd")]
        lows = [kinds[name] for name in ("left", "left", "low")]
        back_outs = [((rows, WIDTH), F32), ((rows + 16, 6 * WIDTH), BF), ((ctx, BLK, 2 * hw), BF)]
        if layer + 1 < LAYERS:
            xhat1, rstd1, gp, xhat2, rstd2, l_mine, l_other, hlow, hidden_next = call_writing(
                mlp_fwd_kernel,
                norms + lows + [kinds["xhat"]],
                (meta,) + cx + (hidden,) + pieces[layer],
                S + V * 5 + A * 5,
                mlp_fwd_scratch(rows, hw),
                "mlp_fwd",
                24,
            )
        else:
            xhat1 = rstd1 = gp = xhat2 = rstd2 = None
            l_mine, l_other, hlow, *last_back = call_writing(
                last_kernel,
                lows + back_outs,
                (meta,) + cx + (hidden, cotangent[0]) + pieces[layer],
                S + V * 6 + A * 5,
                [pltpu.VMEM(*kind) for kind in norms] + mlp_fwd_scratch(rows, hw) + [pltpu.VMEM((8, WIDTH), F32)],
                "last",
                36,
            )
        l_other = via_core(l_other)
        earlier = (l_other,)
        kept.append((gathered, qkv, ctx_own, lse, xhat1, rstd1, gp, xhat2, rstd2, l_mine, l_other))
        if layer + 1 < LAYERS:
            hidden = hidden_next
            gathered = gather_ctx(hlow)
    out_act = hlow[None]

    for layer in reversed(range(LAYERS)):
        gathered, qkv, ctx_own, lse, xhat1, rstd1, gp, xhat2, rstd2, l_mine, l_other = kept[layer]
        if layer + 1 == LAYERS:
            gfs, dgg, gctx = last_back
        else:
            gfs, dgg, gctx = call_writing(
                mlp_bwd_kernel,
                back_outs,
                (meta, xhat1, rstd1, xhat2, rstd2, gp) + grads + pieces[layer] + order,
                S + V * (5 + len(grads)) + A * (5 + len(order)),
                mlp_bwd_scratch(),
                "mlp_bwd",
                12,
                parts=len(grads),
            )
        gcx = lax.all_to_all(gctx, "ctx", 0, 0, tiled=True)
        piece = ((4, 2, cut, WIDTH), BF)

        def weight_grads(*before):
            return call_writing(
                wgrad_kernel,
                [piece] * 3 + [((4, cut + 16, WIDTH), BF), piece],
                (meta, l_mine, l_other, dgg, via_core(dgg)) + before,
                S + A * (4 + len(before)),
                wgrad_scratch(),
                "wgrad",
                5,
            )

        def attention_grads(*before):
            return call(
                functools.partial(attn_bwd_kernel, heads=heads, tokens=tokens, paired=layer == 0),
                [((rows, WIDTH), F32), ((rows, WIDTH), BF)]
                + ([((2, rows, WIDTH), BF)] if layer == 0 else [((rows, WIDTH), BF)] * 2)
                + [
                    ((4, cut + 16, 3 * hw), BF), ((4, cut + 16, 3 * hw), BF),
                ],
                (meta,) + gathered + (qrow, kcol, qkv) + tuple(ctx_own) + (gcx, lse, wide[2 * layer]) + before,
                S + V * 13 + A * (1 + len(before)),
                attn_bwd_scratch(heads, tokens),
                "attn_bwd",
                2 * tokens * WIDTH * 3 * hw * 8,
                10 * 1024 * 1024,
            )

        def attention_shards(dwo, dw, crossed, *others):
            shape = (4, cut + 16, WIDTH + 3 * hw)
            (merged,) = call(
                merge_kernel, [(shape, BF)], (dwo, dw, crossed) + others, V * 3 + A * len(others), [], "merge", 0, 0
            )
            return merged, reduce_z(merged).reshape(shape[1:])

        if layer > 0:
            g_own, g_a, g_b, g_d, dw, dw_other = attention_grads(l_other)
            (over,) = sums([[(g_a, via_second(g_d))]])
            t, a, b, dwo, d = weight_grads(over)
            d1 = reduce_z(d)
            over = via_first(over)
            merged, att1 = attention_shards(dwo, dw, via_core(dw_other))
            back = via_second(g_b)
            grads = (gfs, g_own, back, over)
            a, b = after((a, b), over, back)
            order = (merged, a, b)
            parts1 = (t, via_first(a), via_second(b))
        else:
            (t1,) = sums([[parts1]], gcx, weight=WEIGHT)
            t, a, b, dwo, d = weight_grads(gcx, att1, t1)
            t1 = reduce_z(t1)
            from_b, from_d = via_second(b), via_second(d)
            g_own, g_a, g_bd, dw, dw_other = attention_grads(t)

    def shards(x):
        return x.reshape(2, cut, WIDTH)

    a0, t0 = sums([[(a, from_d)], [(t, from_b)]], g_bd, weight=WEIGHT)
    from_a = via_first(a0)
    (d1,) = after((d1,), a0)
    merged, att0 = attention_shards(dwo, dw, via_core(dw_other), a0)
    back = via_second(g_bd)
    shape = (2 * cut + 16, 2 * WIDTH)
    (joined,) = call(
        join_kernel, [(shape, BF)], (att1, shards(t1), shards(via_diagonal(d1)), merged), V * 3 + A, [], "join", WEIGHT, 0
    )
    (over,) = sums([[(g_a, back[1])]], joined)
    joined = spread_ctx(joined)
    (t0,) = sums([[(t0, from_a)]], over, weight=WEIGHT)
    over = via_first(over)
    ffn0 = shards(reduce_z(t0))

    small_out = None
    placed = []
    for layer in reversed(range(LAYERS)):
        if layer == 0:
            sent = spread_ctx(ffn0) + spread_ctx(att0)
            waits = ()
        else:
            sent = joined
            waits = (t0,)
        last = layer == 0
        big = [
            ((LAYERS, cut, 4 * WIDTH), F32), ((LAYERS, 4 * cut, WIDTH), F32),
            ((LAYERS, cut, 3 * WIDTH), F32), ((LAYERS, cut, WIDTH), F32),
        ]
        if last:
            smalls = [((LAYERS, cut), F32)] * 8 + [((LAYERS, 4 * cut), F32)]
        else:
            smalls = [((16, cut), F32)]
        args = (meta,) + sent + ((small_out,) + tuple(placed) if last else waits)
        spaces = S + V * len(sent) + (V + A * 4 if last else A)
        outs = pl.pallas_call(
            functools.partial(place_kernel, layer=layer, last=last),
            out_shape=[jax.ShapeDtypeStruct(shape, dtype) for shape, dtype in big + smalls],
            in_specs=[pl.BlockSpec(memory_space=space) for space in spaces],
            out_specs=[pl.BlockSpec(memory_space=space) for space in A * 4 + V * len(smalls)],
            scratch_shapes=[
                pltpu.VMEM((ctx, cut, WIDTH), F32), pltpu.VMEM((ctx, cut, 3 * hw), F32),
                pltpu.VMEM((ctx, 16, 3 * hw), F32),
                pltpu.VMEM((cut, 4 * WIDTH), F32), pltpu.VMEM((4 * cut, WIDTH), F32),
                pltpu.VMEM((cut, 3 * WIDTH), F32), pltpu.VMEM((cut, WIDTH), F32),
                pltpu.VMEM((16, 128), F32), pltpu.VMEM((8, 128), F32),
                pltpu.SemaphoreType.DMA((4,)),
            ],
            input_output_aliases={10 + n: n for n in range(4)} if last else {},
            compiler_params=pltpu.CompilerParams(vmem_limit_bytes=VMEM_LIMIT),
            cost_estimate=pl.CostEstimate(flops=0, bytes_accessed=10 * 1024 * 1024, transcendentals=0),
            name="place",
        )(*args)
        placed = outs[:4]
        small_out = outs[4]
        vectors = outs[4:]
    in_grad = add(gfs, g_own, back[0], over)[None]
    e_out, r_out, i_out, o_out = placed
    ab, fg, fs, rb, sg, ss, qb, vb, xb = vectors
    return (out_act, in_grad, i_out, qb, vb, o_out, ab, fg, fs, e_out, xb, r_out, rb, sg, ss)


def on_device(*args, ctx, fsdp):
    if ctx == 4 and fsdp == 8 and args[0].shape[1] == 2 * BLK:
        return on_device_fast(*args, ctx=ctx, fsdp=fsdp)
    return on_device_plain(*args)


def solution(mesh):
    placed = (
        P("fsdp", "ctx", None),
        P("fsdp", "ctx", None),
        P("fsdp", "ctx"),
        P(),
        P(None, "fsdp", None),
        P(None, "fsdp"),
        P(None, "fsdp"),
        P(None, "fsdp", None),
        P(None, "fsdp"),
        P(None, "fsdp"),
        P(None, "fsdp"),
        P(None, "fsdp", None),
        P(None, "fsdp"),
        P(None, "fsdp", None),
        P(None, "fsdp"),
        P(None, "fsdp"),
        P(None, "fsdp"),
    )
    return jax.shard_map(
        functools.partial(on_device, ctx=mesh.shape["ctx"], fsdp=mesh.shape["fsdp"]),
        mesh=mesh,
        in_specs=placed,
        out_specs=(
            P("fsdp", "ctx", None),
            P("fsdp", "ctx", None),
            P(None, "fsdp", None),
            P(None, "fsdp"),
            P(None, "fsdp"),
            P(None, "fsdp", None),
            P(None, "fsdp"),
            P(None, "fsdp"),
            P(None, "fsdp"),
            P(None, "fsdp", None),
            P(None, "fsdp"),
            P(None, "fsdp", None),
            P(None, "fsdp"),
            P(None, "fsdp"),
            P(None, "fsdp"),
        ),
        check_vma=False,
    )
```

```python
import functools

import jax
import jax.numpy as jnp
from jax import lax
from jax.experimental import pallas as pl
from jax.experimental.pallas import tpu as pltpu
from jax.sharding import PartitionSpec as P

HEADS = 12
HEAD_DIM = 64
LAYERS = 2
BLK = 192


norm_eps = 1e-05


def for_sending(x):
    return jax.tree.map(lambda a: a.astype(jnp.bfloat16) if a.dtype == jnp.float32 else a, x)


def layer_norm(values, gain, shift):
    centre = values - jnp.mean(values, axis=-1, keepdims=True)
    spread = jnp.mean(centre * centre, axis=-1, keepdims=True)
    return centre * lax.rsqrt(spread + norm_eps) * gain + shift


def gelu_exact(inputs):
    return 0.5 * inputs * (1.0 + jax.scipy.special.erf(inputs * 0.7071067811865476))


def key_positions(deal):
    pairs = deal.shape[0]
    offsets = jnp.arange(BLK, dtype=jnp.int32)
    first = deal[:, None] * BLK + offsets[None, :]
    second = (2 * pairs - 1 - deal)[:, None] * BLK + offsets[None, :]
    return jnp.concatenate([first, second], axis=1).reshape(-1)


def split_heads(matrix):
    return matrix.reshape(matrix.shape[0], HEADS, HEAD_DIM).transpose(1, 0, 2)


def join_heads(stacked):
    return stacked.transpose(1, 0, 2).reshape(stacked.shape[1], HEADS * HEAD_DIM)


def attend_forward(queries, keys_full, values_full, allowed):

    def one_head(items):
        head_q, head_k, head_v = items
        scores = jnp.einsum(
            "qd,kd->qk", head_q, head_k, preferred_element_type=jnp.float32
        ) * HEAD_DIM ** (-0.5)
        scores = jnp.where(allowed, scores, -1e30)
        top = jnp.max(scores, axis=-1, keepdims=True)
        weights = jnp.exp(scores - top)
        total = jnp.sum(weights, axis=-1, keepdims=True)
        probs = (weights / total).astype(jnp.bfloat16)
        output = jnp.einsum("qk,kd->qd", probs, head_v, preferred_element_type=jnp.float32)
        return (output, top[:, 0] + jnp.log(total[:, 0]))

    outputs, log_totals = lax.map(
        one_head, (split_heads(queries), split_heads(keys_full), split_heads(values_full))
    )
    return (join_heads(outputs), log_totals)


def attend_backward(queries, keys_full, values_full, log_totals, grad_context, allowed):

    def one_head(items):
        head_q, head_k, head_v, head_lse, head_grad = items
        scores = jnp.einsum(
            "qd,kd->qk", head_q, head_k, preferred_element_type=jnp.float32
        ) * HEAD_DIM ** (-0.5)
        scores = jnp.where(allowed, scores, -1e30)
        probs = jnp.exp(scores - head_lse[:, None])
        grad_probs = jnp.einsum("qd,kd->qk", head_grad, head_v, preferred_element_type=jnp.float32)
        inner_sum = jnp.sum(probs * grad_probs, axis=-1, keepdims=True)
        grad_scores = (probs * (grad_probs - inner_sum)).astype(jnp.bfloat16)
        grad_q = jnp.einsum(
            "qk,kd->qd", grad_scores, head_k, preferred_element_type=jnp.float32
        ) * HEAD_DIM ** (-0.5)
        grad_k = jnp.einsum(
            "qk,qd->kd", grad_scores, head_q, preferred_element_type=jnp.float32
        ) * HEAD_DIM ** (-0.5)
        grad_v = jnp.einsum(
            "qk,qd->kd", probs.astype(jnp.bfloat16), head_grad, preferred_element_type=jnp.float32
        )
        return (grad_q, grad_k, grad_v)

    grads = lax.map(
        one_head,
        (
            split_heads(queries),
            split_heads(keys_full),
            split_heads(values_full),
            log_totals,
            split_heads(grad_context),
        ),
    )
    return (join_heads(grads[0]), join_heads(grads[1]), join_heads(grads[2]))


def forward_layer(hidden, weights, allowed):
    (
        attend_in,
        query_bias,
        value_bias,
        attend_out,
        attend_bias,
        first_gain,
        first_shift,
        expand_proj,
        expand_bias,
        reduce_proj,
        reduce_bias,
        second_gain,
        second_shift,
    ) = weights
    width = hidden.shape[1]
    low_hidden = hidden.astype(jnp.bfloat16)
    projected = jnp.dot(low_hidden, attend_in, preferred_element_type=jnp.float32)
    queries = (projected[:, :width] + query_bias.astype(jnp.float32)).astype(jnp.bfloat16)
    keys_own = projected[:, width : 2 * width].astype(jnp.bfloat16)
    values_own = (projected[:, 2 * width :] + value_bias.astype(jnp.float32)).astype(jnp.bfloat16)
    keys_full, values_full = (
        lax.all_gather(keys_own, "ctx", axis=0, tiled=True),
        lax.all_gather(values_own, "ctx", axis=0, tiled=True),
    )
    context, log_totals = attend_forward(queries, keys_full, values_full, allowed)
    low_context = context.astype(jnp.bfloat16)
    branch = jnp.dot(
        low_context, attend_out, preferred_element_type=jnp.float32
    ) + attend_bias.astype(jnp.float32)
    first_sum = hidden + branch
    normed = layer_norm(first_sum, first_gain.astype(jnp.float32), first_shift.astype(jnp.float32))
    low_normed = normed.astype(jnp.bfloat16)
    inner_pre = jnp.dot(
        low_normed, expand_proj, preferred_element_type=jnp.float32
    ) + expand_bias.astype(jnp.float32)
    active = gelu_exact(inner_pre).astype(jnp.bfloat16)
    output_branch = jnp.dot(
        active, reduce_proj, preferred_element_type=jnp.float32
    ) + reduce_bias.astype(jnp.float32)
    second_sum = normed + output_branch
    output = layer_norm(
        second_sum, second_gain.astype(jnp.float32), second_shift.astype(jnp.float32)
    )
    saved = (
        low_hidden,
        queries,
        keys_full,
        values_full,
        log_totals,
        low_context,
        first_sum,
        low_normed,
        inner_pre,
        active,
        second_sum,
    )
    return (output, saved)


def column_sum(matrix):
    return jnp.sum(matrix.astype(jnp.float32), axis=0)


def backward_layer(grad_hidden, weights, saved, allowed):
    (
        attend_in,
        query_bias,
        value_bias,
        attend_out,
        attend_bias,
        first_gain,
        first_shift,
        expand_proj,
        expand_bias,
        reduce_proj,
        reduce_bias,
        second_gain,
        second_shift,
    ) = weights
    (
        low_hidden,
        queries,
        keys_full,
        values_full,
        log_totals,
        low_context,
        first_sum,
        low_normed,
        inner_pre,
        active,
        second_sum,
    ) = saved
    width = low_hidden.shape[1]
    second_pull = jax.vjp(
        layer_norm, second_sum, second_gain.astype(jnp.float32), second_shift.astype(jnp.float32)
    )[1]
    grad_second_sum, grad_second_gain, grad_second_shift = second_pull(grad_hidden)
    grad_branch = grad_second_sum.astype(jnp.bfloat16)
    grad_reduce_bias = column_sum(grad_branch)
    grad_reduce = jnp.einsum("tf,td->fd", active, grad_branch, preferred_element_type=jnp.float32)
    grad_active = jnp.einsum(
        "td,fd->tf", grad_branch, reduce_proj, preferred_element_type=jnp.float32
    )
    gelu_pull = jax.vjp(gelu_exact, inner_pre)[1]
    grad_inner = gelu_pull(grad_active)[0].astype(jnp.bfloat16)
    grad_expand_bias = column_sum(grad_inner)
    grad_expand = jnp.einsum(
        "td,tf->df", low_normed, grad_inner, preferred_element_type=jnp.float32
    )
    grad_normed = grad_second_sum + jnp.einsum(
        "tf,df->td", grad_inner, expand_proj, preferred_element_type=jnp.float32
    )
    first_pull = jax.vjp(
        layer_norm, first_sum, first_gain.astype(jnp.float32), first_shift.astype(jnp.float32)
    )[1]
    grad_first_sum, grad_first_gain, grad_first_shift = first_pull(grad_normed)
    grad_attn = grad_first_sum.astype(jnp.bfloat16)
    grad_attend_bias = column_sum(grad_attn)
    grad_attend_out = jnp.einsum(
        "td,te->de", low_context, grad_attn, preferred_element_type=jnp.float32
    )
    grad_context = jnp.einsum(
        "te,de->td", grad_attn, attend_out, preferred_element_type=jnp.float32
    ).astype(jnp.bfloat16)
    grad_queries, grad_keys_full, grad_values_full = attend_backward(
        queries, keys_full, values_full, log_totals, grad_context, allowed
    )
    grad_keys, grad_values = (
        lax.psum_scatter(
            grad_keys_full.astype(jnp.bfloat16), "ctx", scatter_dimension=0, tiled=True
        ).astype(jnp.float32),
        lax.psum_scatter(
            grad_values_full.astype(jnp.bfloat16), "ctx", scatter_dimension=0, tiled=True
        ).astype(jnp.float32),
    )
    grad_proj = jnp.concatenate(
        [
            grad_queries.astype(jnp.bfloat16),
            grad_keys.astype(jnp.bfloat16),
            grad_values.astype(jnp.bfloat16),
        ],
        axis=1,
    )
    grad_query_bias = column_sum(grad_proj[:, :width])
    grad_value_bias = column_sum(grad_proj[:, 2 * width :])
    grad_attend_in = jnp.einsum(
        "td,te->de", low_hidden, grad_proj, preferred_element_type=jnp.float32
    )
    grad_input = grad_first_sum + jnp.einsum(
        "te,de->td", grad_proj, attend_in, preferred_element_type=jnp.float32
    )
    grads = (
        grad_attend_in,
        grad_query_bias,
        grad_value_bias,
        grad_attend_out,
        grad_attend_bias,
        grad_first_gain,
        grad_first_shift,
        grad_expand,
        grad_expand_bias,
        grad_reduce,
        grad_reduce_bias,
        grad_second_gain,
        grad_second_shift,
    )
    return (grad_input, grads)


def reduce_grads(grads):
    shards = (
        lax.psum_scatter(
            grads[0].astype(jnp.bfloat16), "fsdp", scatter_dimension=0, tiled=True
        ).astype(jnp.float32),
        lax.psum_scatter(
            grads[1].astype(jnp.bfloat16), "fsdp", scatter_dimension=0, tiled=True
        ).astype(jnp.float32),
        lax.psum_scatter(
            grads[2].astype(jnp.bfloat16), "fsdp", scatter_dimension=0, tiled=True
        ).astype(jnp.float32),
        lax.psum_scatter(
            grads[3].astype(jnp.bfloat16), "fsdp", scatter_dimension=0, tiled=True
        ).astype(jnp.float32),
        lax.psum_scatter(
            grads[4].astype(jnp.bfloat16), "fsdp", scatter_dimension=0, tiled=True
        ).astype(jnp.float32),
        lax.psum_scatter(
            grads[5].astype(jnp.bfloat16), "fsdp", scatter_dimension=0, tiled=True
        ).astype(jnp.float32),
        lax.psum_scatter(
            grads[6].astype(jnp.bfloat16), "fsdp", scatter_dimension=0, tiled=True
        ).astype(jnp.float32),
        lax.psum_scatter(
            grads[7].astype(jnp.bfloat16), "fsdp", scatter_dimension=0, tiled=True
        ).astype(jnp.float32),
        lax.psum_scatter(
            grads[8].astype(jnp.bfloat16), "fsdp", scatter_dimension=0, tiled=True
        ).astype(jnp.float32),
        lax.psum_scatter(
            grads[9].astype(jnp.bfloat16), "fsdp", scatter_dimension=0, tiled=True
        ).astype(jnp.float32),
        lax.psum_scatter(
            grads[10].astype(jnp.bfloat16), "fsdp", scatter_dimension=0, tiled=True
        ).astype(jnp.float32),
        lax.psum_scatter(
            grads[11].astype(jnp.bfloat16), "fsdp", scatter_dimension=0, tiled=True
        ).astype(jnp.float32),
        lax.psum_scatter(
            grads[12].astype(jnp.bfloat16), "fsdp", scatter_dimension=0, tiled=True
        ).astype(jnp.float32),
    )
    return (
        lax.psum(shards[0].astype(jnp.bfloat16), "ctx").astype(jnp.float32),
        lax.psum(shards[1].astype(jnp.bfloat16), "ctx").astype(jnp.float32),
        lax.psum(shards[2].astype(jnp.bfloat16), "ctx").astype(jnp.float32),
        lax.psum(shards[3].astype(jnp.bfloat16), "ctx").astype(jnp.float32),
        lax.psum(shards[4].astype(jnp.bfloat16), "ctx").astype(jnp.float32),
        lax.psum(shards[5].astype(jnp.bfloat16), "ctx").astype(jnp.float32),
        lax.psum(shards[6].astype(jnp.bfloat16), "ctx").astype(jnp.float32),
        lax.psum(shards[7].astype(jnp.bfloat16), "ctx").astype(jnp.float32),
        lax.psum(shards[8].astype(jnp.bfloat16), "ctx").astype(jnp.float32),
        lax.psum(shards[9].astype(jnp.bfloat16), "ctx").astype(jnp.float32),
        lax.psum(shards[10].astype(jnp.bfloat16), "ctx").astype(jnp.float32),
        lax.psum(shards[11].astype(jnp.bfloat16), "ctx").astype(jnp.float32),
        lax.psum(shards[12].astype(jnp.bfloat16), "ctx").astype(jnp.float32),
    )


def layer_slices(sharded, layer_index):
    return tuple((tensor[layer_index] for tensor in sharded))


def on_device_plain(
    activations,
    cotangent,
    doc_start,
    deal,
    attend_in,
    query_bias,
    value_bias,
    attend_out,
    attend_bias,
    first_gain,
    first_shift,
    expand_proj,
    expand_bias,
    reduce_proj,
    reduce_bias,
    second_gain,
    second_shift,
):
    sharded = (
        attend_in,
        query_bias,
        value_bias,
        attend_out,
        attend_bias,
        first_gain,
        first_shift,
        expand_proj,
        expand_bias,
        reduce_proj,
        reduce_bias,
        second_gain,
        second_shift,
    )
    row_count = activations.shape[1]
    positions = key_positions(deal)
    own_rank = lax.axis_index("ctx")
    own_positions = lax.dynamic_slice_in_dim(positions, own_rank * row_count, row_count)
    own_starts = doc_start[0]
    key_starts = lax.all_gather(own_starts, "ctx", axis=0, tiled=True)
    allowed = (positions[None, :] <= own_positions[:, None]) & (
        key_starts[None, :] == own_starts[:, None]
    )
    hidden = activations[0].astype(jnp.float32)
    kept_weights = []
    kept_saved = []
    for layer_index in range(LAYERS):
        weights = lax.all_gather(
            for_sending(layer_slices(sharded, layer_index)), "fsdp", axis=0, tiled=True
        )
        hidden, saved = forward_layer(hidden, weights, allowed)
        kept_weights.append(weights)
        kept_saved.append(saved)
    out_act = hidden.astype(jnp.bfloat16)[None]
    grad_hidden = cotangent[0].astype(jnp.float32)
    reduced = [None] * LAYERS
    for layer_index in reversed(range(LAYERS)):
        weights = lax.all_gather(
            for_sending(layer_slices(sharded, layer_index)), "fsdp", axis=0, tiled=True
        )
        grad_hidden, grads = backward_layer(grad_hidden, weights, kept_saved[layer_index], allowed)
        reduced[layer_index] = reduce_grads(grads)
    stacked = [
        jnp.stack([reduced[layer_index][member] for layer_index in range(LAYERS)])
        for member in range(13)
    ]
    return (
        out_act,
        grad_hidden[None],
        stacked[0],
        stacked[1],
        stacked[2],
        stacked[3],
        stacked[4],
        stacked[5],
        stacked[6],
        stacked[7],
        stacked[8],
        stacked[9],
        stacked[10],
        stacked[11],
        stacked[12],
    )


F32 = jnp.float32
BF = jnp.bfloat16
WIDTH = HEADS * HEAD_DIM
QB = 256
SCORE_SCALE = HEAD_DIM ** (-0.5) * 1.4426950408889634
NEG = -1e30
VMEM_LIMIT = 60 * 1024 * 1024


def mm_nn(a, b):
    return lax.dot_general(a, b, (((1,), (0,)), ((), ())), preferred_element_type=F32)


def mm_nt(a, b):
    return lax.dot_general(a, b, (((1,), (1,)), ((), ())), preferred_element_type=F32)


def mm_tn(a, b):
    return lax.dot_general(a, b, (((0,), (0,)), ((), ())), preferred_element_type=F32)


def call(kernel, outs, args, specs, scratch, name, flops, nbytes):
    return pl.pallas_call(
        kernel,
        out_shape=[jax.ShapeDtypeStruct(shape, dtype) for shape, dtype in outs],
        in_specs=[pl.BlockSpec(memory_space=space) for space in specs],
        out_specs=[pl.BlockSpec(memory_space=pltpu.VMEM) for _ in outs],
        scratch_shapes=scratch,
        compiler_params=pltpu.CompilerParams(vmem_limit_bytes=VMEM_LIMIT),
        cost_estimate=pl.CostEstimate(flops=flops if name in ("sums", "join") else 0, bytes_accessed=0, transcendentals=0),
        name=name,
    )(*args)


def block_of(block, blocks):
    half = 0 if 2 * block < blocks else 1
    return (block if half == 0 else blocks - 1 - block), half


CORE, SHARD, RANK, JMAP, INV, JMIN = 0, 1, 2, 6, 10, 14
SWAPPED = (0, 2, 1, 3)
WEIGHT = 10**11
VEC_AT = 640


def started_copies(sems, *pairs):
    copies = []
    for n, (src, dst) in enumerate(pairs):
        copy = pltpu.make_async_copy(src, dst, sems.at[n])
        copy.start()
        copies.append(copy)
    return copies


def last_kernel(
    writer, places, meta, c0, c1, c2, c3, hid, cot, t, a, b, d, crossed,
    l_mine, l_other, hlow, gfs, dgg, gctx,
    xhat1, rstd1, gp, xhat2, rstd2, e_s, r_s, sems, wo_s, b_s, wo_sems, ctx, eb, eb_s,
):
    loads = (e_s, r_s, sems, wo_s, b_s, wo_sems)
    mlp_fwd_kernel(
        writer, (None,) * 5 + tuple(places[:3]), meta, c0, c1, c2, c3, hid, t, a, b, d, crossed,
        xhat1, rstd1, gp, xhat2, rstd2, l_mine, l_other, hlow, *loads, ctx, eb, finish=False,
    )
    mlp_bwd_kernel(
        writer, places[3:], meta, xhat1, rstd1, xhat2, rstd2, gp, cot, t, a, b, d, crossed,
        gfs, dgg, gctx, *loads, eb_s, parts=1, loaded=True,
    )


class Writer:
    def __init__(self, sems):
        self.sems = sems
        self.copies = []

    def send(self, src, dst, *at):
        if dst is None:
            return
        if at:
            src, dst = src.at[at], dst.at[at]
        copy = pltpu.make_async_copy(src, dst, self.sems.at[len(self.copies)])
        copy.start()
        self.copies.append(copy)

    def finish(self):
        for copy in self.copies:
            copy.wait()


def writing(kernel, outs, copies):
    count = len(outs)

    def run(*refs, scratch, **keys):
        ins, places, rest = refs[: -count - scratch], refs[-count - scratch : -scratch], refs[-scratch:]
        buffers, sems, rest = rest[:count], rest[count], rest[count + 1 :]
        kernel(Writer(sems), places, *ins, *buffers, *rest, **keys)

    return run, [pltpu.VMEM(shape, dtype) for shape, dtype in outs] + [pltpu.SemaphoreType.DMA((copies,))]


def call_writing(kernel, outs, args, specs, scratch, name, copies, **keys):
    run, buffers = writing(kernel, outs, copies)
    scratch = buffers + scratch
    return pl.pallas_call(
        functools.partial(run, scratch=len(scratch), **keys),
        out_shape=[jax.ShapeDtypeStruct(shape, dtype) for shape, dtype in outs],
        in_specs=[pl.BlockSpec(memory_space=space) for space in specs],
        out_specs=[pl.BlockSpec(memory_space=pl.ANY) for _ in outs],
        scratch_shapes=scratch,
        compiler_params=pltpu.CompilerParams(vmem_limit_bytes=VMEM_LIMIT),
        cost_estimate=pl.CostEstimate(flops=0, bytes_accessed=0, transcendentals=0),
        name=name,
    )(*args)


def prep_kernel(
    expand, reduce, attend_in, attend_out, expand_bias, v0, v1, v2, v3, v4, v5, v6, v7,
    t0, d0, t1, d1,
):
    rank = lax.axis_index("ctx")
    cut = expand.shape[1]
    hw = WIDTH // 4
    for layer, (t, d) in enumerate(((t0, d0), (t1, d1))):
        bias = expand_bias[layer : layer + 1, :].astype(F32)
        rows = [v[layer : layer + 1, :].astype(F32) for v in (v0, v1, v2, v3, v4, v5, v6, v7)]
        rows += [bias[:, k * cut : (k + 1) * cut] for k in range(4)]
        rows.append(jnp.zeros((4, cut), F32))
        d[2 * cut :, :] = attend_out[layer]
        t[2 * cut :, 3 * hw :] = jnp.zeros((cut, WIDTH - 3 * hw), BF)
        t[2 * cut : 2 * cut + 16, VEC_AT : VEC_AT + cut] = jnp.concatenate(rows, axis=0).astype(BF)
        for k in range(4):

            @pl.when(rank == k)
            def _():
                for out, at in ((t, k), (d, k ^ 3)):
                    out[0:cut, :] = jnp.concatenate(
                        [
                            expand[layer, :, (2 * z + h) * 4 * cut + at * cut : (2 * z + h) * 4 * cut + (at + 1) * cut]
                            for h in range(2)
                            for z in range(4)
                        ],
                        axis=1,
                    )
                    out[cut : 2 * cut, :] = reduce[layer, at * cut : (at + 1) * cut, :]
                t[2 * cut :, 0 : 3 * hw] = jnp.concatenate(
                    [attend_in[layer, :, n * WIDTH + k * hw : n * WIDTH + (k + 1) * hw] for n in range(3)], axis=1
                )


def nothing_kernel(*refs):
    pass


def after(xs, *others):
    return pl.pallas_call(
        nothing_kernel,
        out_shape=[jax.ShapeDtypeStruct(x.shape, x.dtype) for x in xs],
        in_specs=[pl.BlockSpec(memory_space=pl.ANY)] * (len(xs) + len(others)),
        out_specs=[pl.BlockSpec(memory_space=pl.ANY)] * len(xs),
        input_output_aliases={n: n for n in range(len(xs))},
        cost_estimate=pl.CostEstimate(flops=WEIGHT, bytes_accessed=0, transcendentals=0),
        name="after",
    )(*xs, *others)


def pack_kernel(a, b, *rest):
    out, held, ins, outs = rest[-4:]
    coming = [pltpu.make_async_copy((a, b)[n // 4].at[n % 4], held.at[n // 4, n % 4], ins.at[n]) for n in range(8)]
    going = [pltpu.make_async_copy(held.at[n // 4, n % 4], out.at[n // 4, n % 4], outs.at[n]) for n in range(8)]
    for copy in coming:
        copy.start()
    for arrive, leave in zip(coming, going):
        arrive.wait()
        leave.start()
    for copy in going:
        copy.wait()


def pack(a, b, *others):
    shape = (2,) + a.shape
    return pl.pallas_call(
        pack_kernel,
        out_shape=jax.ShapeDtypeStruct(shape, a.dtype),
        in_specs=[pl.BlockSpec(memory_space=pl.ANY)] * (2 + len(others)),
        out_specs=pl.BlockSpec(memory_space=pl.ANY),
        scratch_shapes=[pltpu.VMEM(shape, a.dtype), pltpu.SemaphoreType.DMA((8,)), pltpu.SemaphoreType.DMA((8,))],
        cost_estimate=pl.CostEstimate(flops=0, bytes_accessed=0, transcendentals=0),
        name="pack",
    )(a, b, *others)


def half_kernel(meta, t, *rest):
    out, held, ins, outs = rest[-4:]
    coming = [pltpu.make_async_copy(t.at[z, meta[CORE], 0:2], held.at[z], ins.at[z]) for z in range(4)]
    going = [pltpu.make_async_copy(held.at[z], out.at[z], outs.at[z]) for z in range(4)]
    for copy in coming:
        copy.start()
    for arrive, leave in zip(coming, going):
        arrive.wait()
        leave.start()
    for copy in going:
        copy.wait()


def half_of(meta, t, *others):
    shape = (4, 2) + t.shape[3:]
    return pl.pallas_call(
        half_kernel,
        out_shape=jax.ShapeDtypeStruct(shape, t.dtype),
        in_specs=[pl.BlockSpec(memory_space=space) for space in [pltpu.SMEM] + [pl.ANY] * (1 + len(others))],
        out_specs=pl.BlockSpec(memory_space=pl.ANY),
        scratch_shapes=[pltpu.VMEM(shape, t.dtype), pltpu.SemaphoreType.DMA((4,)), pltpu.SemaphoreType.DMA((4,))],
        cost_estimate=pl.CostEstimate(flops=0, bytes_accessed=0, transcendentals=0),
        name="half",
    )(meta, t, *others)


def sums_kernel(*refs, layout, count, split):
    outs = refs[-len(layout) :]
    at = 0
    for out, parts in zip(outs, layout):
        lane = 0
        for n in parts:
            total = refs[at][...].astype(F32)
            for ref in refs[at + 1 : at + n]:
                total = total + ref[...].astype(F32)
            at += n
            if split:
                for k in range(len(outs)):
                    outs[k][...] = total[k].astype(BF)
            else:
                out[..., lane : lane + total.shape[-1]] = total.astype(BF)
            lane += total.shape[-1]
        if split:
            break


def parts_kernel(*refs, layout, count, skip):
    sums_kernel(*refs[:count], *refs[count + skip :], layout=layout, count=count, split=0)


def sums(outputs, *others, split=0, weight=0):
    args = tuple(x for groups in outputs for group in groups for x in group)
    layout = tuple(tuple(len(group) for group in groups) for groups in outputs)
    if split:
        shapes = [(args[0].shape[1:], BF)] * split
        layout = layout * split
    else:
        shapes = [
            (groups[0][0].shape[:-1] + (sum(group[0].shape[-1] for group in groups),), BF) for groups in outputs
        ]
    if not split and args[0].ndim == 4:
        part = pl.BlockSpec((1,) + args[0].shape[1:], lambda n: (n, 0, 0, 0))
        return pl.pallas_call(
            functools.partial(parts_kernel, layout=layout, count=len(args), skip=len(others)),
            grid=(args[0].shape[0],),
            out_shape=[jax.ShapeDtypeStruct(shape, dtype) for shape, dtype in shapes],
            in_specs=[part] * len(args) + [pl.BlockSpec(memory_space=pl.ANY)] * len(others),
            out_specs=[part] * len(shapes),
            compiler_params=pltpu.CompilerParams(vmem_limit_bytes=VMEM_LIMIT),
            cost_estimate=pl.CostEstimate(flops=weight, bytes_accessed=0, transcendentals=0),
            name="sums",
        )(*args, *others)
    return call(
        functools.partial(sums_kernel, layout=layout, count=len(args), split=split),
        shapes, args + others, [pltpu.VMEM] * len(args) + [pl.ANY] * len(others), [], "sums", weight, 0,
    )


def join_kernel(att, t, d, *rest):
    out = rest[-1]
    rows = att.shape[0]
    out[0:rows, 0 : att.shape[1]] = att[...]
    out[0:rows, att.shape[1] :] = jnp.zeros((rows, out.shape[1] - att.shape[1]), BF)
    for k in range(2):
        out[rows:, k * WIDTH : (k + 1) * WIDTH] = (t[k].astype(F32) + d[k].astype(F32)).astype(BF)


def merge_kernel(dwo, own, other, *rest):
    out = rest[-1]
    out[:, :, 0:WIDTH] = dwo[...]
    out[:, :, WIDTH:] = (own[...].astype(F32) + other[...].astype(F32)).astype(BF)


def vectors_of(shards, order):
    return jnp.concatenate([shards[f // 2, f % 2, :, 0:96] for f in order], axis=1).astype(F32)


NATURAL = tuple(range(8))
CORE_MAJOR = (0, 2, 4, 6, 1, 3, 5, 7)


def attn_fwd_kernel(
    meta, h0, h1, h2, h3, qrow, kcol, t, *rest, heads, tokens
):
    qkv, c0, c1, c2, c3, lse, q_s, k_s, vt_s, o_s, ctx, w_s, b_s, sems = rest[-14:]
    blocks = tokens // BLK
    hw = heads * HEAD_DIM
    copies = started_copies(
        sems, (t.at[:, :, 2, :, 0:VEC_AT], w_s), (t.at[:, :, 2, 0:16, VEC_AT : VEC_AT + 128], b_s)
    )
    for copy in copies:
        copy.wait()
    w = w_s[...].reshape(WIDTH, VEC_AT)[:, 0 : 3 * hw]
    vec = vectors_of(b_s, NATURAL)
    bias = jnp.zeros((1, 3 * hw), F32)
    for k in range(4):
        part = jnp.concatenate(
            [vec[6:7, k * hw : (k + 1) * hw], jnp.zeros((1, hw), F32), vec[7:8, k * hw : (k + 1) * hw]], axis=1
        )
        bias = jnp.where(meta[RANK] == k, part, bias)
    for j, piece in enumerate((h0, h1, h2, h3)):
        qkv[j] = (mm_nn(piece[...], w) + bias).astype(BF)
    for pair in range(blocks // 2):
        rows = []
        for block in (2 * pair, 2 * pair + 1):
            at, half = block_of(block, blocks)
            rows.append(qkv[meta[JMAP + at], half * BLK : (half + 1) * BLK, :])
        both = jnp.concatenate(rows, axis=0)
        lo, hi = 2 * pair * BLK, 2 * (pair + 1) * BLK
        for h in range(heads):
            q_s[h, lo:hi, :] = both[:, h * HEAD_DIM : (h + 1) * HEAD_DIM]
            k_s[h, lo:hi, :] = both[:, hw + h * HEAD_DIM : hw + (h + 1) * HEAD_DIM]
        vt_s[:, lo:hi] = both[:, 2 * hw :].T
    iota_k = lax.broadcasted_iota(jnp.int32, (QB, QB), 0)
    iota_q = lax.broadcasted_iota(jnp.int32, (QB, QB), 1)
    causal = iota_k <= iota_q
    head_rows = [slice(h * HEAD_DIM, (h + 1) * HEAD_DIM) for h in range(heads)]
    for i in range(tokens // QB):
        lo = i * QB
        starts_q = qrow[0:1, lo : lo + QB]

        def scores(at, diagonal):
            col = kcol[pl.ds(at, QB), :]
            allowed = jnp.concatenate([col, col], axis=1) == starts_q
            if diagonal:
                allowed = allowed & causal
            return [
                jnp.where(allowed, mm_nt(k_s[h, pl.ds(at, QB), :], q_s[h, lo : lo + QB, :]) * SCORE_SCALE, NEG)
                for h in range(heads)
            ]

        ss = scores(lo, True)
        tops = [jnp.max(s, axis=0, keepdims=True) for s in ss]
        ps = [jnp.exp2(s - top) for s, top in zip(ss, tops)]
        totals = [jnp.sum(p, axis=0, keepdims=True) for p in ps]
        outs = [mm_nn(vt_s[head_rows[h], lo : lo + QB], ps[h].astype(BF)) for h in range(heads)]

        def step(jb, carry):
            tops, totals, outs = carry
            at = pl.multiple_of(jb * QB, QB)
            ss = scores(at, False)
            new = [jnp.maximum(top, jnp.max(s, axis=0, keepdims=True)) for s, top in zip(ss, tops)]
            ps = [jnp.exp2(s - top) for s, top in zip(ss, new)]
            alphas = [jnp.exp2(top - n) for top, n in zip(tops, new)]
            totals = [
                total * alpha + jnp.sum(p, axis=0, keepdims=True) for total, alpha, p in zip(totals, alphas, ps)
            ]
            outs = [
                outs[h] * alphas[h] + mm_nn(vt_s[head_rows[h], pl.ds(at, QB)], ps[h].astype(BF)) for h in range(heads)
            ]
            return new, totals, outs

        if i > 0:
            tops, totals, outs = lax.fori_loop(meta[JMIN + i], i, step, (tops, totals, outs))
        for h in range(heads):
            o_s[head_rows[h], lo : lo + QB] = outs[h] / totals[h]
            lse[h : h + 1, lo : lo + QB] = tops[h] + jnp.log2(totals[h])
    for pair in range(blocks // 2):
        lo, hi = 2 * pair * BLK, 2 * (pair + 1) * BLK
        both = o_s[:, lo:hi].T.astype(BF)
        for n, block in enumerate((2 * pair, 2 * pair + 1)):
            at, half = block_of(block, blocks)
            ctx[meta[JMAP + at], :, half * hw : (half + 1) * hw] = both[n * BLK : (n + 1) * BLK, :]
    for j, out in enumerate((c0, c1, c2, c3)):
        out[...] = ctx[j]


def attn_bwd_kernel(
    meta, h0, h1, h2, h3, qrow, kcol, qkv, c0, c1, c2, c3, gctx, lse, t, *rest, heads, tokens
):
    (
        g_own, g_a, g_b, g_d, dw_own, dw_other, q_s, k_s, v_s, do_s, kt_s, delta_s, dk_s, dv_s, dqt_s, g_s, w_s, ctx, dw, sems,
    ) = rest[-20:]
    blocks = tokens // BLK
    hw = heads * HEAD_DIM
    scale = HEAD_DIM ** (-0.5)
    copies = started_copies(sems, (t.at[:, :, 2, :, 0:VEC_AT], w_s))
    for j, c in enumerate((c0, c1, c2, c3)):
        ctx[j] = c[...]
    for pair in range(blocks // 2):
        rows, grads, outs = [], [], []
        for block in (2 * pair, 2 * pair + 1):
            at, half = block_of(block, blocks)
            rows.append(qkv[meta[JMAP + at], half * BLK : (half + 1) * BLK, :])
            grads.append(gctx[meta[INV + at], :, half * hw : (half + 1) * hw])
            outs.append(ctx[meta[JMAP + at], :, half * hw : (half + 1) * hw])
        both = jnp.concatenate(rows, axis=0)
        grad = jnp.concatenate(grads, axis=0)
        out = jnp.concatenate(outs, axis=0)
        lo, hi = 2 * pair * BLK, 2 * (pair + 1) * BLK
        prod = (grad.astype(F32) * out.astype(F32)).T
        kt_s[:, lo:hi] = both[:, hw : 2 * hw].T
        for h in range(heads):
            c0, c1 = h * HEAD_DIM, (h + 1) * HEAD_DIM
            q_s[h, lo:hi, :] = both[:, c0:c1]
            k_s[h, lo:hi, :] = both[:, hw + c0 : hw + c1]
            v_s[h, lo:hi, :] = both[:, 2 * hw + c0 : 2 * hw + c1]
            do_s[h, lo:hi, :] = grad[:, c0:c1]
            delta_s[h : h + 1, lo:hi] = jnp.sum(prod[c0:c1, :], axis=0, keepdims=True)
    dk_s[...] = jnp.zeros_like(dk_s)
    dv_s[...] = jnp.zeros_like(dv_s)
    iota_k = lax.broadcasted_iota(jnp.int32, (QB, QB), 0)
    iota_q = lax.broadcasted_iota(jnp.int32, (QB, QB), 1)
    causal = iota_k <= iota_q
    head_rows = [slice(h * HEAD_DIM, (h + 1) * HEAD_DIM) for h in range(heads)]
    for i in range(tokens // QB):
        lo = i * QB
        starts_q = qrow[0:1, lo : lo + QB]

        def block(at, diagonal):
            col = kcol[pl.ds(at, QB), :]
            allowed = jnp.concatenate([col, col], axis=1) == starts_q
            if diagonal:
                allowed = allowed & causal
            keys = pl.ds(at, QB)
            cols = slice(lo, lo + QB)
            ss = [mm_nt(k_s[h, keys, :], q_s[h, cols, :]) for h in range(heads)]
            dps = [mm_nt(v_s[h, keys, :], do_s[h, cols, :]) for h in range(heads)]
            ps = [
                jnp.exp2(jnp.where(allowed, s * SCORE_SCALE, NEG) - lse[h : h + 1, cols]) for h, s in enumerate(ss)
            ]
            dss = [
                (p * (dp - delta_s[h : h + 1, cols])).astype(BF) for h, (p, dp) in enumerate(zip(ps, dps))
            ]
            for h in range(heads):
                dv_s[h, keys, :] += mm_nn(ps[h].astype(BF), do_s[h, cols, :])
            for h in range(heads):
                dk_s[h, keys, :] += mm_nn(dss[h], q_s[h, cols, :])
            return [mm_nn(kt_s[head_rows[h], keys], dss[h]) for h in range(heads)]

        dqs = block(lo, True)
        if i > 0:
            dqs = lax.fori_loop(
                meta[JMIN + i],
                i,
                lambda jb, acc: [x + y for x, y in zip(acc, block(pl.multiple_of(jb * QB, QB), False))],
                dqs,
            )
        for h in range(heads):
            dqt_s[head_rows[h], lo : lo + QB] = dqs[h] * scale
    for pair in range(blocks // 2):
        lo, hi = 2 * pair * BLK, 2 * (pair + 1) * BLK
        parts = [dqt_s[:, lo:hi].T.astype(BF)]
        parts += [(dk_s[h, lo:hi, :] * scale).astype(BF) for h in range(heads)]
        parts += [dv_s[h, lo:hi, :].astype(BF) for h in range(heads)]
        both = jnp.concatenate(parts, axis=1)
        for n, block_at in enumerate((2 * pair, 2 * pair + 1)):
            at, half = block_of(block_at, blocks)
            g_s[meta[JMAP + at], half * BLK : (half + 1) * BLK, :] = both[n * BLK : (n + 1) * BLK, :]
    for copy in copies:
        copy.wait()
    w = w_s[...].reshape(WIDTH, VEC_AT)[:, 0 : 3 * hw]
    total = None
    sums = None
    for j, piece in enumerate((h0, h1, h2, h3)):
        g = g_s[j]
        back = mm_nt(g, w)
        if j == 0:
            g_own[...] = back
        else:
            (g_a, g_b, g_d)[j - 1][...] = back.astype(BF)
        part = mm_tn(piece[...], g)
        col = jnp.sum(g.astype(F32), axis=0, keepdims=True)
        total = part if total is None else total + part
        sums = col if sums is None else sums + col
    shards, rows_out, cols = dw.shape
    rows = WIDTH // shards
    dw[:, 0:rows, :] = total.reshape(shards, rows, cols).astype(BF)
    dw[:, rows:, :] = jnp.broadcast_to(sums[None], (shards, rows_out - rows, cols)).astype(BF)
    for k in range(4):
        dw_own[k] = dw[2 * k + meta[CORE]]
        dw_other[k] = dw[2 * k + 1 - meta[CORE]]


def start_ffn_copies(core, t, a, b, d, crossed, e_s, r_s, sems):
    ca, cb = crossed.at[0], crossed.at[1]
    groups = []
    for p, parts in enumerate(((t,), (a, cb), (b, ca), (d,))):
        pairs = []
        if len(parts) == 1:
            pairs.append((parts[0].at[:, :, 0], e_s.at[p]))
            for h in range(2):
                pairs.append((parts[0].at[:, h, 1], r_s.at[p, h]))
        else:
            for src, parity in ((parts[0], core), (parts[1], 1 - core)):
                pairs.append((src.at[:, 0], e_s.at[p, :, parity]))
                pairs.append((src.at[:, 1], r_s.at[p, parity]))
        group = []
        for n, (src, dst) in enumerate(pairs):
            copy = pltpu.make_async_copy(src, dst, sems.at[p, n])
            copy.start()
            group.append(copy)
        groups.append(group)
    return groups


def ffn_scratch():
    return [
        pltpu.VMEM((4, 4, 2, 96, WIDTH), BF),
        pltpu.VMEM((4, 2, 4, 96, WIDTH), BF),
        pltpu.SemaphoreType.DMA((4, 4)),
        pltpu.VMEM((4, 2, 96, WIDTH), BF),
        pltpu.VMEM((4, 2, 16, 128), BF),
        pltpu.SemaphoreType.DMA((2,)),
    ]


def mlp_fwd_scratch(rows, hw):
    return ffn_scratch() + [pltpu.VMEM((4, rows, hw), BF), pltpu.VMEM((8, WIDTH), F32)]


def mlp_bwd_scratch():
    return ffn_scratch() + [pltpu.VMEM((8, WIDTH), F32)]


def wgrad_scratch():
    rows = 2 * BLK
    return [
        pltpu.VMEM((rows, 3 * WIDTH), BF),
        pltpu.VMEM((rows, 3 * WIDTH), BF),
        pltpu.VMEM((rows + 16, 6 * WIDTH), BF),
        pltpu.VMEM((rows + 16, 6 * WIDTH), BF),
        pltpu.SemaphoreType.DMA((16,)),
    ]


def attn_fwd_scratch(heads, tokens):
    hw = heads * HEAD_DIM
    return [
        pltpu.VMEM((heads, tokens, HEAD_DIM), BF),
        pltpu.VMEM((heads, tokens, HEAD_DIM), BF),
        pltpu.VMEM((hw, tokens), BF),
        pltpu.VMEM((hw, tokens), F32),
        pltpu.VMEM((4, BLK, 2 * hw), BF),
        pltpu.VMEM((4, 2, 96, VEC_AT), BF),
        pltpu.VMEM((4, 2, 16, 128), BF),
        pltpu.SemaphoreType.DMA((2,)),
    ]


def attn_bwd_scratch(heads, tokens):
    hw = heads * HEAD_DIM
    return [pltpu.VMEM((heads, tokens, HEAD_DIM), BF)] * 4 + [
        pltpu.VMEM((hw, tokens), BF),
        pltpu.VMEM((8, tokens), F32),
        pltpu.VMEM((heads, tokens, HEAD_DIM), F32),
        pltpu.VMEM((heads, tokens, HEAD_DIM), F32),
        pltpu.VMEM((hw, tokens), F32),
        pltpu.VMEM((4, tokens // 4, 3 * hw), BF),
        pltpu.VMEM((4, 2, 96, VEC_AT), BF),
        pltpu.VMEM((4, BLK, 2 * hw), BF),
        pltpu.VMEM((8, 112, 3 * hw), BF),
        pltpu.SemaphoreType.DMA((1,)),
    ]


def norm_parts(values):
    centre = values - jnp.mean(values, axis=-1, keepdims=True)
    spread = jnp.mean(centre * centre, axis=-1, keepdims=True)
    rstd = lax.rsqrt(spread + norm_eps)
    return centre * rstd, rstd


def shard_columns(x, parity):
    return jnp.concatenate([x[:, (2 * z + parity) * 96 : (2 * z + parity + 1) * 96] for z in range(4)], axis=1)


def mlp_fwd_kernel(
    writer, places, meta, c0, c1, c2, c3, hid, t, a, b, d, crossed,
    xhat1, rstd1, gp, xhat2, rstd2, l_mine, l_other, hlow, *rest, finish=True,
):
    hnext, (e_s, r_s, sems, wo_s, b_s, wo_sems, ctx, eb) = rest[:-8], rest[-8:]
    core = meta[CORE]
    xhat1_to, rstd1_to, gp_to, xhat2_to, rstd2_to, mine_to, other_to, hlow_to = places[:8]
    wo_copies = started_copies(
        wo_sems, (d.at[:, :, 2], wo_s), (t.at[:, :, 2, 0:16, VEC_AT : VEC_AT + 128], b_s)
    )
    copies = start_ffn_copies(core, t, a, b, d, crossed, e_s, r_s, sems)
    half_cols = WIDTH // 2
    hw = c0.shape[1] // 2
    for p, piece in enumerate((c0, c1, c2, c3)):
        for half in range(2):
            ctx[meta[RANK + p], half * BLK : (half + 1) * BLK, :] = piece[:, half * hw : (half + 1) * hw]

    def keep(parts, at):
        for parity in range(2):

            @pl.when(core == parity)
            def _():
                l_mine[:, at : at + half_cols] = parts[parity]

            @pl.when(core != parity)
            def _():
                l_other[:, at : at + half_cols] = parts[parity]

        for ref, to in ((l_mine, mine_to), (l_other, other_to)):
            writer.send(ref, to, slice(None), slice(at, at + half_cols))

    low = jnp.concatenate([ctx[rank] for rank in range(4)], axis=1)
    keep([shard_columns(low, parity) for parity in range(2)], half_cols)
    for copy in wo_copies:
        copy.wait()
    vec = vectors_of(b_s, NATURAL)
    eb[...] = vectors_of(b_s, CORE_MAJOR)[8:16, :]
    wo = wo_s[...].reshape(WIDTH, WIDTH)
    first_sum = hid[...].astype(F32) + (mm_nn(low, wo) + vec[0:1, :])
    x1, r1 = norm_parts(first_sum)
    xhat1[...] = x1
    rstd1[...] = r1
    writer.send(xhat1, xhat1_to)
    writer.send(rstd1, rstd1_to)
    normed = x1 * vec[1:2, :] + vec[2:3, :]
    lown = normed.astype(BF)
    keep([shard_columns(lown, parity) for parity in range(2)], 0)
    out = normed + vec[3:4, :]
    for p in range(4):
        for copy in copies[p]:
            copy.wait()
        bias = eb[pl.ds(meta[RANK + p], 1), :]
        u = mm_nn(lown, e_s[p].reshape(WIDTH, WIDTH)) + bias
        cdf = 0.5 * (1.0 + lax.erf(u * 0.7071067811865476))
        pdf = jnp.exp(-0.5 * u * u) * 0.3989422804014327
        low = (u * cdf).astype(BF)
        cut = slice(p * WIDTH, (p + 1) * WIDTH)
        gp[:, cut] = (cdf + u * pdf).astype(BF)
        writer.send(gp, gp_to, slice(None), cut)
        keep([low[:, :half_cols], low[:, half_cols:]], WIDTH + p * half_cols)
        out = out + mm_nn(low, r_s[p].reshape(WIDTH, WIDTH))
    x2, r2 = norm_parts(out)
    nxt = x2 * vec[4:5, :] + vec[5:6, :]
    hlow[...] = nxt.astype(BF)
    writer.send(hlow, hlow_to)
    xhat2[...] = x2
    writer.send(xhat2, xhat2_to)
    rstd2[...] = r2
    writer.send(rstd2, rstd2_to)
    if hnext:
        hnext[0][...] = nxt
        writer.send(hnext[0], places[8])
    if finish:
        writer.finish()


def norm_back(gy, gain, xhat, rstd):
    g = gy * gain
    return rstd * (g - jnp.mean(g, axis=-1, keepdims=True) - xhat * jnp.mean(g * xhat, axis=-1, keepdims=True))


def rows_sum(x):
    return jnp.sum(x, axis=0, keepdims=True)


def mlp_bwd_kernel(
    writer, places, meta, xhat1, rstd1, xhat2, rstd2, gp, *rest, parts, loaded=False
):
    t, a, b, d, crossed = rest[parts : parts + 5]
    gfs, dgg, gctx, e_s, r_s, sems, wo_s, b_s, wo_sems, eb_s = rest[-10:]
    rows = gfs.shape[0]
    core = meta[CORE]
    if loaded:
        copies, wo_copies = [[]] * 4, []
    else:
        copies = start_ffn_copies(core, t, a, b, d, crossed, e_s, r_s, sems)
        wo_copies = started_copies(
            wo_sems, (d.at[:, :, 2], wo_s), (t.at[:, :, 2, 0:16, VEC_AT : VEC_AT + 128], b_s)
        )
    grad = rest[0][...].astype(F32)
    for ref in rest[1:parts]:
        grad = grad + ref[...].astype(F32)
    x2 = xhat2[...]
    for copy in wo_copies:
        copy.wait()
    vec = vectors_of(b_s, NATURAL)
    gss = norm_back(grad, vec[4:5, :], x2, rstd2[...])
    low = gss.astype(BF)
    cut = slice(4 * WIDTH, 5 * WIDTH)
    dgg[0:rows, cut] = low
    writer.send(dgg.at[0:rows, cut], places[1].at[0:rows, cut])
    sums = [None] * 8
    sums[4] = rows_sum(grad * x2)
    sums[5] = rows_sum(grad)
    sums[3] = rows_sum(low.astype(F32))
    gn = gss
    eb_s[...] = jnp.zeros_like(eb_s)
    for p in range(4):
        for copy in copies[p]:
            copy.wait()
        ga = mm_nt(low, r_s[p].reshape(WIDTH, WIDTH))
        dip = (ga * gp[:, p * WIDTH : (p + 1) * WIDTH].astype(F32)).astype(BF)
        cut = slice(p * WIDTH, (p + 1) * WIDTH)
        dgg[0:rows, cut] = dip
        writer.send(dgg.at[0:rows, cut], places[1].at[0:rows, cut])
        eb_s[pl.ds(meta[RANK + p], 1), :] = rows_sum(dip.astype(F32))
        gn = gn + mm_nt(dip, e_s[p].reshape(WIDTH, WIDTH))
    x1 = xhat1[...]
    gf = norm_back(gn, vec[1:2, :], x1, rstd1[...])
    sums[1] = rows_sum(gn * x1)
    sums[2] = rows_sum(gn)
    lowa = gf.astype(BF)
    cut = slice(5 * WIDTH, 6 * WIDTH)
    dgg[0:rows, cut] = lowa
    writer.send(dgg.at[0:rows, cut], places[1].at[0:rows, cut])
    gfs[...] = gf
    writer.send(gfs, places[0])
    sums[0] = rows_sum(lowa.astype(F32))
    sums[6] = jnp.zeros_like(sums[0])
    sums[7] = sums[6]
    gc = mm_nt(lowa, wo_s[...].reshape(WIDTH, WIDTH)).astype(BF)
    hw = gctx.shape[2] // 2
    for rank in range(4):
        for half in range(2):
            gctx[rank, :, half * hw : (half + 1) * hw] = gc[half * BLK : (half + 1) * BLK, rank * hw : (rank + 1) * hw]
    writer.send(gctx, places[2])
    vecs = jnp.concatenate(sums, axis=0)
    ebs = jnp.concatenate([eb_s[:, (4 * (f % 2) + f // 2) * 96 : (4 * (f % 2) + f // 2 + 1) * 96] for f in range(8)], axis=1)
    dgg[rows:, 0:WIDTH] = jnp.concatenate([vecs, ebs], axis=0).astype(BF)
    dgg[rows:, WIDTH:] = jnp.zeros((16, 5 * WIDTH), BF)
    writer.send(dgg.at[rows:], places[1].at[rows:])
    writer.finish()


def wgrad_kernel(writer, places, meta, l_mine_from, l_other_from, dgg_from, dgg_other_from, *rest):
    t, a, b, dwo, d, l_mine, l_other, dgg, dgg_other, sems = rest[-10:]
    half = WIDTH // 2
    rows = l_mine.shape[0]

    def fetch(n, src, dst, at, width):
        copy = pltpu.make_async_copy(src.at[:, at : at + width], dst.at[:, at : at + width], sems.at[n])
        copy.start()
        return copy

    lefts = [fetch(n, src, dst, 0, WIDTH) for n, (src, dst) in enumerate(((l_mine_from, l_mine), (l_other_from, l_other)))]
    rights = {}
    for k in (3, 4, 1, 2, 0, 5):
        q = SWAPPED[k] if k < 4 else k
        rights[k] = [fetch(4 + k, dgg_from, dgg, k * WIDTH, WIDTH), fetch(10 + k, dgg_other_from, dgg_other, q * WIDTH, WIDTH)]
        if k == 3:
            acts = [
                fetch(2 + n, src, dst, WIDTH, 2 * WIDTH)
                for n, (src, dst) in enumerate(((l_mine_from, l_mine), (l_other_from, l_other)))
            ]

    def wait(copies):
        for copy in copies:
            copy.wait()

    def grad(left, left_other, right, right_other):
        return mm_nn(left, dgg[0:rows, right : right + WIDTH]) + mm_nn(
            left_other, dgg_other[0:rows, right_other : right_other + WIDTH]
        )

    def left(at, at_other):
        return l_mine[:, at : at + half].T, l_other[:, at_other : at_other + half].T

    wait(lefts)
    low = left(0, 0)
    for n, (p, out) in enumerate(((3, d), (1, a), (2, b), (0, t))):
        q = SWAPPED[p]
        wait(rights[p])
        out[:, 0] = grad(*low, p * WIDTH, q * WIDTH).reshape(4, 96, WIDTH).astype(BF)
        if n == 0:
            wait(acts)
            wait(rights[4])
        out[:, 1] = (
            grad(*left(WIDTH + p * half, WIDTH + q * half), 4 * WIDTH, 4 * WIDTH).reshape(4, 96, WIDTH).astype(BF)
        )
        writer.send(out, places[(4, 1, 2, 0)[n]])
    wait(rights[5])
    dwo[:, 0:96, :] = grad(*left(half, half), 5 * WIDTH, 5 * WIDTH).reshape(4, 96, WIDTH).astype(BF)
    vecs = dgg[rows:, 0:WIDTH].astype(F32) + dgg_other[rows:, 0:WIDTH].astype(F32)
    dwo[:, 96:, :] = jnp.zeros((4, 16, WIDTH), BF)
    for parity in range(2):

        @pl.when(meta[CORE] == parity)
        def _():
            for z in range(4):
                dwo[z, 96:, 0:96] = vecs[:, (2 * z + parity) * 96 : (2 * z + parity + 1) * 96].astype(BF)

    writer.send(dwo, places[3])
    writer.finish()


def place_kernel(
    meta, *rest, layer, last
):
    if last:
        parts = [((f.at[0], f.at[1]), a) for f, a in zip(rest[:4], rest[4:8])]
        small_in, rest = rest[8], rest[13:]
    else:
        parts = [((x.at[112:, 0:WIDTH], x.at[112:, WIDTH:]), x.at[0:112, :]) for x in rest[:4]]
        rest = rest[5:]
    e_hbm, r_hbm, i_hbm, o_hbm = rest[:4]
    smalls = rest[4:-10]
    e_s, i_s, b_s, e_out, r_out, i_out, o_out, small_s, eb_s, sems = rest[-10:]
    for p, (ffn, att) in enumerate(parts):
        rank = meta[RANK + p]
        r_out[pl.ds(pl.multiple_of(rank * 96, 96), 96), :] = ffn[1][...].astype(F32)
        e_s[rank] = ffn[0][...].astype(F32)
        i_s[rank] = att[0:96, WIDTH : WIDTH + 9 * HEAD_DIM].astype(F32)
        b_s[rank] = att[96:112, WIDTH : WIDTH + 9 * HEAD_DIM].astype(F32)
    copies = []

    def send(n, src, dst):
        copy = pltpu.make_async_copy(src, dst.at[layer], sems.at[n])
        copy.start()
        copies.append(copy)

    send(0, r_out, r_hbm)
    for f in range(8):
        at = (4 * (f % 2) + f // 2) * 96
        e_out[:, f * 384 : (f + 1) * 384] = jnp.concatenate([e_s[c, :, at : at + 96] for c in range(4)], axis=1)
    send(1, e_out, e_hbm)
    hw = WIDTH // 4
    for k in range(3):
        i_out[:, k * WIDTH : (k + 1) * WIDTH] = jnp.concatenate(
            [i_s[c, :, k * hw : (k + 1) * hw] for c in range(4)], axis=1
        )
    send(2, i_out, i_hbm)
    wo = [att[:, 0:WIDTH].astype(F32) for _, att in parts]
    total = (wo[0] + wo[1]) + (wo[2] + wo[3])
    o_out[...] = total[0:96, :]
    send(3, o_out, o_hbm)
    bias = b_s[lax.shift_right_logical(meta[SHARD], 1)]
    low_half = (meta[SHARD] & 1) == 0
    qb = jnp.where(low_half, bias[:, 0:96], bias[:, 96:192])
    vb = jnp.where(low_half, bias[:, 2 * hw : 2 * hw + 96], bias[:, 2 * hw + 96 : 3 * hw])
    rows = jnp.concatenate([total[96:102, 0:96], qb[0:1], vb[0:1], total[104:112, 0:96]], axis=0)
    if last:
        for n, ref in enumerate(smalls[:-1]):
            ref[...] = jnp.concatenate([rows[n : n + 1], small_in[n : n + 1, 0:96]], axis=0)
        smalls[-1][...] = jnp.concatenate(
            [
                jnp.concatenate([x[8 + c : 9 + c, 0:96] for c in range(4)], axis=1)
                for x in (rows, small_in[...])
            ],
            axis=0,
        )
    else:
        smalls[0][...] = rows
    for copy in copies:
        copy.wait()


def permutation(ctx, fsdp, move):
    return [
        (c * fsdp + f, move(c, f)[0] * fsdp + move(c, f)[1]) for c in range(ctx) for f in range(fsdp)
    ]


def add(*parts):
    total = parts[0].astype(F32)
    for part in parts[1:]:
        total = total + part.astype(F32)
    return total


def on_device_fast(
    activations, cotangent, doc_start, deal,
    attend_in, query_bias, value_bias, attend_out, attend_bias, first_gain, first_shift,
    expand_proj, expand_bias, reduce_proj, reduce_bias, second_gain, second_shift,
    *, ctx, fsdp,
):
    S = [pltpu.SMEM]
    V = [pltpu.VMEM]
    A = [pl.ANY]
    axes = ("ctx", "fsdp")

    def via(move):
        perm = permutation(ctx, fsdp, move)
        return lambda x: lax.ppermute(x, axes, perm)

    via_first = via(lambda c, f: (c ^ (1 + f % 2), f))
    via_second = via(lambda c, f: (c ^ (2 - f % 2), f))
    via_diagonal = via(lambda c, f: (c ^ 3, f))
    via_core = via(lambda c, f: (c, f ^ 1))
    via_z = [None] + [via(lambda c, f, k=k: (c, f ^ (2 * k))) for k in range(1, 4)]

    def exchange_ctx(own, a, b, d):
        return (own, via_first(a), via_second(b), via_diagonal(d))

    def spread_ctx(x):
        return (x, via_first(x), via_second(x), via_diagonal(x))

    def reduce_z(x):
        return lax.psum_scatter(x, "fsdp", scatter_dimension=0, tiled=True, axis_index_groups=zgroups)

    def exchange_z(own, *others):
        return (own,) + tuple(via_z[k + 1](x) for k, x in enumerate(others))

    def gather_ctx(x):
        a, b = via_first(x), via_second(x)
        return (x, a, b, via_second(a))

    heads = HEADS // ctx
    hw = heads * HEAD_DIM
    rows = activations.shape[1]
    tokens = rows * ctx
    cut = WIDTH // fsdp
    c = lax.axis_index("ctx").astype(jnp.int32)
    shard = lax.axis_index("fsdp").astype(jnp.int32)
    core = shard % 2
    zgroups = [[2 * z + k for z in range(fsdp // 2)] for k in range(2)]

    hidden = activations[0]
    gathered = gather_ctx(hidden)
    small = (attend_bias, first_gain, first_shift, reduce_bias, second_gain, second_shift, query_bias, value_bias)
    sent = call(
        prep_kernel,
        [((3 * cut, WIDTH), BF)] * 4,
        (expand_proj, reduce_proj, attend_in, attend_out, expand_bias) + small,
        V * 13,
        [],
        "prep",
        0,
        8 * 1024 * 1024,
    )

    def gather_ffn(x):
        x = lax.all_gather(x, "fsdp", axis=0, tiled=True)
        return x.reshape(fsdp // 2, 2, 3, cut, WIDTH)

    ranks = jnp.arange(ctx, dtype=jnp.int32)
    inv = jnp.sum(jnp.where(deal[None, :] == ranks[:, None], ranks[None, :], 0), axis=1).astype(jnp.int32)
    starts = lax.all_gather(doc_start[0], "ctx", axis=0, tiled=True)
    by_rank = starts.reshape(ctx, 2, BLK)
    chosen = inv[:, None, None, None] == ranks[None, :, None, None]
    by_block = jnp.sum(jnp.where(chosen, by_rank[None], 0), axis=1)
    logical = jnp.concatenate([by_block[:, 0], by_block[::-1, 1]], axis=0).reshape(-1)
    qrow = jnp.broadcast_to(logical[None, :], (8, tokens))
    kcol = jnp.broadcast_to(logical[:, None], (tokens, 128))
    jmin = jnp.min(logical.reshape(tokens // QB, QB), axis=1) // QB

    m1 = 1 + core
    mask = inv ^ c
    jmap = jnp.where((core == 1) & (mask > 0) & (mask < 3), 3 - mask, mask)
    meta = jnp.concatenate(
        [jnp.stack([core, shard, c, c ^ m1, c ^ (3 - m1), c ^ 3]), jmap, inv, jmin]
    ).astype(jnp.int32)

    kept = []
    earlier = ()
    wide = [gather_ffn(sent[0]), gather_ffn(sent[1]), None, None]
    wide[0] = after((wide[0],), starts, *gathered[1:])[0]
    wide[2] = gather_ffn(*after(sent[2:3], wide[0]))
    pieces = []
    for layer in range(LAYERS):
        t, d = wide[2 * layer : 2 * layer + 2]
        mine = half_of(meta, t, *gathered[1:])
        a, b = via_first(mine), via_second(mine)
        qkv, *ctx_own, lse = call(
            functools.partial(attn_fwd_kernel, heads=heads, tokens=tokens),
            [((ctx, rows, 3 * hw), BF)] + [((BLK, 2 * hw), BF)] * 4 + [((8, tokens), F32)],
            (meta,) + gathered + (qrow, kcol, t, mine) + earlier,
            S + V * 6 + A * (2 + len(earlier)),
            attn_fwd_scratch(heads, tokens),
            "attn_fwd",
            2 * tokens * WIDTH * 3 * hw * 4,
            10 * 1024 * 1024,
        )
        cx = exchange_ctx(*ctx_own)
        if layer + 1 < LAYERS:
            wide[3] = gather_ffn(*after(sent[3:4], *cx[1:]))
        pieces.append((t, a, b, d, via_core(pack(a, b, lse))))
        kinds = {
            "xhat": ((rows, WIDTH), F32), "rstd": ((rows, 1), F32), "gp": ((rows, 4 * WIDTH), BF),
            "left": ((rows, 3 * WIDTH), BF), "low": ((rows, WIDTH), BF),
        }
        norms = [kinds[name] for name in ("xhat", "rstd", "gp", "xhat", "rstd")]
        lows = [kinds[name] for name in ("left", "left", "low")]
        back_outs = [((rows, WIDTH), F32), ((rows + 16, 6 * WIDTH), BF), ((ctx, BLK, 2 * hw), BF)]
        if layer + 1 < LAYERS:
            xhat1, rstd1, gp, xhat2, rstd2, l_mine, l_other, hlow, hidden_next = call_writing(
                mlp_fwd_kernel,
                norms + lows + [kinds["xhat"]],
                (meta,) + cx + (hidden,) + pieces[layer],
                S + V * 5 + A * 5,
                mlp_fwd_scratch(rows, hw),
                "mlp_fwd",
                24,
            )
        else:
            xhat1 = rstd1 = gp = xhat2 = rstd2 = None
            l_mine, l_other, hlow, *last_back = call_writing(
                last_kernel,
                lows + back_outs,
                (meta,) + cx + (hidden, cotangent[0]) + pieces[layer],
                S + V * 6 + A * 5,
                [pltpu.VMEM(*kind) for kind in norms] + mlp_fwd_scratch(rows, hw) + [pltpu.VMEM((8, WIDTH), F32)],
                "last",
                36,
            )
        l_other = via_core(l_other)
        earlier = (l_other,)
        kept.append((gathered, qkv, ctx_own, lse, xhat1, rstd1, gp, xhat2, rstd2, l_mine, l_other))
        if layer + 1 < LAYERS:
            hidden = hidden_next
            gathered = gather_ctx(hlow)
    out_act = hlow[None]

    for layer in reversed(range(LAYERS)):
        gathered, qkv, ctx_own, lse, xhat1, rstd1, gp, xhat2, rstd2, l_mine, l_other = kept[layer]
        if layer + 1 == LAYERS:
            gfs, dgg, gctx = last_back
        else:
            gfs, dgg, gctx = call_writing(
                mlp_bwd_kernel,
                back_outs,
                (meta, xhat1, rstd1, xhat2, rstd2, gp) + grads + pieces[layer] + order,
                S + V * (5 + len(grads)) + A * (5 + len(order)),
                mlp_bwd_scratch(),
                "mlp_bwd",
                12,
                parts=len(grads),
            )
        gcx = lax.all_to_all(gctx, "ctx", 0, 0, tiled=True)
        piece = ((4, 2, cut, WIDTH), BF)

        def weight_grads(*before):
            return call_writing(
                wgrad_kernel,
                [piece] * 3 + [((4, cut + 16, WIDTH), BF), piece],
                (meta, l_mine, l_other, dgg, via_core(dgg)) + before,
                S + A * (4 + len(before)),
                wgrad_scratch(),
                "wgrad",
                5,
            )

        def attention_grads(*before):
            return call(
                functools.partial(attn_bwd_kernel, heads=heads, tokens=tokens),
                [
                    ((rows, WIDTH), F32), ((rows, WIDTH), BF), ((rows, WIDTH), BF), ((rows, WIDTH), BF),
                    ((4, cut + 16, 3 * hw), BF), ((4, cut + 16, 3 * hw), BF),
                ],
                (meta,) + gathered + (qrow, kcol, qkv) + tuple(ctx_own) + (gcx, lse, wide[2 * layer]) + before,
                S + V * 13 + A * (1 + len(before)),
                attn_bwd_scratch(heads, tokens),
                "attn_bwd",
                2 * tokens * WIDTH * 3 * hw * 8,
                10 * 1024 * 1024,
            )

        def attention_shards(dwo, dw, crossed, *others):
            shape = (4, cut + 16, WIDTH + 3 * hw)
            (merged,) = call(
                merge_kernel, [(shape, BF)], (dwo, dw, crossed) + others, V * 3 + A * len(others), [], "merge", 0, 0
            )
            return merged, reduce_z(merged).reshape(shape[1:])

        if layer > 0:
            g_own, g_a, g_b, g_d, dw, dw_other = attention_grads(l_other)
            (over,) = sums([[(g_a, via_second(g_d))]])
            t, a, b, dwo, d = weight_grads(over)
            d1 = reduce_z(d)
            over = via_first(over)
            merged, att1 = attention_shards(dwo, dw, via_core(dw_other))
            back = via_second(g_b)
            grads = (gfs, g_own, back, over)
            a, b = after((a, b), over, back)
            order = (merged, a, b)
            parts1 = (t, via_first(a), via_second(b))
        else:
            (t1,) = sums([[parts1]], gcx, weight=WEIGHT)
            t, a, b, dwo, d = weight_grads(gcx, att1, t1)
            t1 = reduce_z(t1)
            from_b, from_d = via_second(b), via_second(d)
            g_own, g_a, g_b, g_d, dw, dw_other = attention_grads(t)

    def shards(x):
        return x.reshape(2, cut, WIDTH)

    a0, t0 = sums([[(a, from_d)], [(t, from_b)]], g_d, weight=WEIGHT)
    from_a = via_first(a0)
    merged, att0 = attention_shards(dwo, dw, via_core(dw_other), a0)
    back = via_second(g_d), via_second(g_b)
    shape = (2 * cut + 16, 2 * WIDTH)
    (joined,) = call(
        join_kernel, [(shape, BF)], (att1, shards(t1), shards(via_diagonal(d1)), merged), V * 3 + A, [], "join", WEIGHT, 0
    )
    (over,) = sums([[(g_a, back[0])]], joined)
    joined = spread_ctx(joined)
    (t0,) = sums([[(t0, from_a)]], over, weight=WEIGHT)
    over = via_first(over)
    ffn0 = shards(reduce_z(t0))

    small_out = None
    placed = []
    for layer in reversed(range(LAYERS)):
        if layer == 0:
            sent = spread_ctx(ffn0) + spread_ctx(att0)
            waits = ()
        else:
            sent = joined
            waits = (t0,)
        last = layer == 0
        big = [
            ((LAYERS, cut, 4 * WIDTH), F32), ((LAYERS, 4 * cut, WIDTH), F32),
            ((LAYERS, cut, 3 * WIDTH), F32), ((LAYERS, cut, WIDTH), F32),
        ]
        if last:
            smalls = [((LAYERS, cut), F32)] * 8 + [((LAYERS, 4 * cut), F32)]
        else:
            smalls = [((16, cut), F32)]
        args = (meta,) + sent + ((small_out,) + tuple(placed) if last else waits)
        spaces = S + V * len(sent) + (V + A * 4 if last else A)
        outs = pl.pallas_call(
            functools.partial(place_kernel, layer=layer, last=last),
            out_shape=[jax.ShapeDtypeStruct(shape, dtype) for shape, dtype in big + smalls],
            in_specs=[pl.BlockSpec(memory_space=space) for space in spaces],
            out_specs=[pl.BlockSpec(memory_space=space) for space in A * 4 + V * len(smalls)],
            scratch_shapes=[
                pltpu.VMEM((ctx, cut, WIDTH), F32), pltpu.VMEM((ctx, cut, 3 * hw), F32),
                pltpu.VMEM((ctx, 16, 3 * hw), F32),
                pltpu.VMEM((cut, 4 * WIDTH), F32), pltpu.VMEM((4 * cut, WIDTH), F32),
                pltpu.VMEM((cut, 3 * WIDTH), F32), pltpu.VMEM((cut, WIDTH), F32),
                pltpu.VMEM((16, 128), F32), pltpu.VMEM((8, 128), F32),
                pltpu.SemaphoreType.DMA((4,)),
            ],
            input_output_aliases={10 + n: n for n in range(4)} if last else {},
            compiler_params=pltpu.CompilerParams(vmem_limit_bytes=VMEM_LIMIT),
            cost_estimate=pl.CostEstimate(flops=0, bytes_accessed=10 * 1024 * 1024, transcendentals=0),
            name="place",
        )(*args)
        placed = outs[:4]
        small_out = outs[4]
        vectors = outs[4:]
    in_grad = add(gfs, g_own, back[1], over)[None]
    e_out, r_out, i_out, o_out = placed
    ab, fg, fs, rb, sg, ss, qb, vb, xb = vectors
    return (out_act, in_grad, i_out, qb, vb, o_out, ab, fg, fs, e_out, xb, r_out, rb, sg, ss)


def on_device(*args, ctx, fsdp):
    if ctx == 4 and fsdp == 8 and args[0].shape[1] == 2 * BLK:
        return on_device_fast(*args, ctx=ctx, fsdp=fsdp)
    return on_device_plain(*args)


def solution(mesh):
    placed = (
        P("fsdp", "ctx", None),
        P("fsdp", "ctx", None),
        P("fsdp", "ctx"),
        P(),
        P(None, "fsdp", None),
        P(None, "fsdp"),
        P(None, "fsdp"),
        P(None, "fsdp", None),
        P(None, "fsdp"),
        P(None, "fsdp"),
        P(None, "fsdp"),
        P(None, "fsdp", None),
        P(None, "fsdp"),
        P(None, "fsdp", None),
        P(None, "fsdp"),
        P(None, "fsdp"),
        P(None, "fsdp"),
    )
    return jax.shard_map(
        functools.partial(on_device, ctx=mesh.shape["ctx"], fsdp=mesh.shape["fsdp"]),
        mesh=mesh,
        in_specs=placed,
        out_specs=(
            P("fsdp", "ctx", None),
            P("fsdp", "ctx", None),
            P(None, "fsdp", None),
            P(None, "fsdp"),
            P(None, "fsdp"),
            P(None, "fsdp", None),
            P(None, "fsdp"),
            P(None, "fsdp"),
            P(None, "fsdp"),
            P(None, "fsdp", None),
            P(None, "fsdp"),
            P(None, "fsdp", None),
            P(None, "fsdp"),
            P(None, "fsdp"),
            P(None, "fsdp"),
        ),
        check_vma=False,
    )
```
